32 devices in a mesh: dp: 8 (over y, x, core), tensor: 4 (over z).
Axes of the slice: x: 2, y: 2, z: 4, core: 2. Of those that a mesh axis runs over, the one named last changes fastest.
Arguments:
- tokens: bfloat16 [18432, 1536], P(('dp', 'tensor')), may hold values from -6 to 6
- teacher: bfloat16 [18432, 1536], P(('dp', 'tensor')), may hold values from -13 to 13
- valid_mask: int32 [18432], P('dp'), may hold values from 0 to 1, as said below
- norm1_gain: float32 [1536], replicated, may hold values from 0.5 to 1.5
- w_query: bfloat16 [1536, 1536], P(None, 'tensor'), may hold values from -0.15625 to 0.15625
- w_key: bfloat16 [1536, 1536], P(None, 'tensor'), may hold values from -0.15625 to 0.15625
- w_value: bfloat16 [1536, 1536], P(None, 'tensor'), may hold values from -0.15625 to 0.15625
- conv_weight: float32 [16, 6, 11], P('tensor'), may hold values from -0.6 to 2.1
- head_mix: float32 [8, 2, 2], P('tensor'), may hold values from -1.2 to 2
- gn_gain: float32 [16, 96], P('tensor'), may hold values from 0.5 to 1.5
- w_out: bfloat16 [1536, 1536], P(None, 'tensor'), may hold values from -0.15625 to 0.15625
- norm2_gain: float32 [1536], replicated, may hold values from 0.5 to 1.5
- w_gate: bfloat16 [1536, 4096], P(None, 'tensor'), may hold values from -0.15625 to 0.15625
- w_up: bfloat16 [1536, 4096], P(None, 'tensor'), may hold values from -0.15625 to 0.15625
- w_down: bfloat16 [1536, 4096], P(None, 'tensor'), may hold values from -0.09375 to 0.09375
Outputs:
- output: bfloat16 [18432, 1536], P(('dp', 'tensor'))
- loss: float32 [], replicated
- grad_input: float32 [18432, 1536], P(('dp', 'tensor'))
- grad_norm1_gain: float32 [1536], P('tensor')
- grad_w_query: float32 [1536, 1536], P(None, 'tensor')
- grad_w_key: float32 [1536, 1536], P(None, 'tensor')
- grad_w_value: float32 [1536, 1536], P(None, 'tensor')
- grad_conv_weight: float32 [16, 6, 11], P('tensor')
- grad_head_mix: float32 [8, 2, 2], P('tensor')
- grad_gn_gain: float32 [16, 96], P('tensor')
- grad_w_out: float32 [1536, 1536], P(None, 'tensor')
- grad_norm2_gain: float32 [1536], P('tensor')
- grad_w_gate: float32 [1536, 4096], P(None, 'tensor')
- grad_w_up: float32 [1536, 4096], P(None, 'tensor')
- grad_w_down: float32 [1536, 4096], P(None, 'tensor')
The draws below stay inside these ranges and needn't reach their ends.
Inputs may be any that keep to these rules, and one draw needn't show every extreme that they name: `valid_mask`: in every tree the valid slots of the trunk and of each branch and leaf form a prefix of it of one slot or more.
All inputs are finite; a program needn't handle non-finite values.
Results may differ from the reference program's by a relative error of at most 0.018.
Values may be sent and summed in bfloat16 or wider, within the bound.
A program may use at most 448 MiB of HBM per device.

```python
import math
import jax
import jax.numpy as jnp
from jax import lax

D = 1536
H = 16
HD = 96
FF = 4096
CQ = 6
CK = 11
TRUNK = 192
SEG = 32
TREE = 576
TREES = 32
TOKENS = 18432
GROUPS = 8


def draw_valid_mask(key, part):
    last_tree = max(TREES - 1, 1)
    tree_ids = jnp.arange(TREES, dtype=jnp.int32)[:, None]
    segment_sizes = jnp.array([TRUNK] + [SEG] * 12, dtype=jnp.int32)[None, :]
    upper_len = jnp.maximum(1, segment_sizes * (last_tree + 2 * tree_ids) // (3 * last_tree))
    lengths = jax.random.randint(key, (TREES, 13), 1, upper_len + 1)
    position = jnp.arange(TREE, dtype=jnp.int32)
    segment = jnp.where(position < TRUNK, 0, 1 + (position - TRUNK) // SEG)
    within = jnp.where(position < TRUNK, position, (position - TRUNK) % SEG)
    limits = lengths[:, segment]
    return (within[None, :] < limits).astype(jnp.int32).reshape(TREES * TREE)


def draw_teacher(key, part):
    key_base = jax.random.fold_in(key, 0)
    tree_scale = 1.0 + 2.0 * jnp.arange(TREES, dtype=jnp.float32) / max(TREES - 1, 1)
    row_scale = jnp.repeat(tree_scale, TREE)[:, None]
    return (jax.random.truncated_normal(key_base, -4.0, 4.0, (TOKENS, D), jnp.float32) * row_scale).astype(jnp.bfloat16)


def draw_conv_weight(key, part):
    centre = (jnp.arange(CQ)[:, None] == 0) & (jnp.arange(CK)[None, :] == CK // 2)
    noise = 0.15 * jax.random.truncated_normal(key, -4.0, 4.0, (H, CQ, CK), jnp.float32)
    return jnp.where(centre[None], 1.5, 0.0) + noise


def draw_head_mix(key, part):
    identity = jnp.eye(2, dtype=jnp.float32)[None]
    noise = 0.3 * jax.random.truncated_normal(key, -4.0, 4.0, (GROUPS, 2, 2), jnp.float32)
    return 0.8 * identity + noise


def level_of(own_key, shape, shards, smallest, high):
    def one(dim, blocks):
        draws = jax.random.uniform(jax.random.fold_in(jax.random.fold_in(own_key, 6), dim), (blocks,), jnp.float32, smallest / len(shards), high / len(shards))
        return jnp.repeat(jnp.exp(draws), shape[dim] // blocks).reshape((-1,) + (1,) * (len(shape) - dim - 1))

    loudness = one(*shards[0])
    for cut in shards[1:]:
        loudness = loudness * one(*cut)
    return loudness


def bell_draw(key, shape, deviation, most, cuts=(), kind=jnp.bfloat16):
    gain = level_of(key, shape, cuts, -0.22, 0.18) if cuts else 1.0
    values = jax.random.normal(key, shape, jnp.float32) * deviation * gain
    return jnp.minimum(jnp.maximum(values, -most), most).astype(kind)


def setup_inputs(seed: int = 0) -> dict:
    key_list = jax.random.split(jax.random.key(seed), 16)
    return {
        "tokens": bell_draw(key_list[0], (TOKENS, D), 1.0, 6.0, ((0, 32),)),
        "teacher": draw_teacher(jax.random.fold_in(key_list[15], 71), 0),
        "valid_mask": draw_valid_mask(jax.random.fold_in(key_list[15], 71), 0),
        "norm1_gain": jnp.clip(1.0 + 0.1 * jax.random.normal(key_list[3], (D,), jnp.float32), 0.5, 1.5),
        "w_query": bell_draw(key_list[4], (D, H * HD), D ** -0.5, 0.15625, ((1, 4),)),
        "w_key": bell_draw(key_list[5], (D, H * HD), D ** -0.5, 0.15625, ((1, 4),)),
        "w_value": bell_draw(key_list[6], (D, H * HD), D ** -0.5, 0.15625, ((1, 4),)),
        "conv_weight": draw_conv_weight(jax.random.fold_in(key_list[15], 71), 0),
        "head_mix": draw_head_mix(jax.random.fold_in(key_list[15], 71), 0),
        "gn_gain": jnp.clip(1.0 + 0.1 * jax.random.normal(key_list[9], (H, HD), jnp.float32), 0.5, 1.5),
        "w_out": bell_draw(key_list[10], (D, H * HD), (H * HD) ** -0.5, 0.15625, ((1, 4),)),
        "norm2_gain": jnp.clip(1.0 + 0.1 * jax.random.normal(key_list[11], (D,), jnp.float32), 0.5, 1.5),
        "w_gate": bell_draw(key_list[12], (D, FF), D ** -0.5, 0.15625, ((1, 4),)),
        "w_up": bell_draw(key_list[13], (D, FF), D ** -0.5, 0.15625, ((1, 4),)),
        "w_down": bell_draw(key_list[14], (D, FF), FF ** -0.5, 0.09375, ((1, 4),)),
    }


@jax.custom_vjp
def low(v):
    return lax.optimization_barrier(v.astype(jnp.bfloat16)).astype(jnp.float32)

@jax.custom_vjp
def low_back(v):
    return v

def low_keep(v):
    return (low(v), None)

def low_pass(kept, grad):
    return (grad,)

def back_keep(v):
    return (v, None)

def back_low(kept, grad):
    return (low(grad),)
low.defvjp(low_keep, low_pass)
low_back.defvjp(back_keep, back_low)

def matmul(left, right):
    return jnp.dot(left, right, precision=lax.Precision.HIGHEST, preferred_element_type=jnp.float32)

def along_paths(array_in):
    tail_shape = array_in.shape[1:]
    trunk_part = array_in[:TRUNK]
    branch_part = array_in[TRUNK:TRUNK + 4 * SEG].reshape((4, SEG) + tail_shape)
    leaf_part = array_in[TRUNK + 4 * SEG:].reshape((8, SEG) + tail_shape)
    trunk_wide = jnp.broadcast_to(trunk_part[None], (8,) + trunk_part.shape)
    branch_wide = jnp.repeat(branch_part, 2, axis=0)
    return jnp.concatenate([trunk_wide, branch_wide, leaf_part], axis=1)

def owned_rows(trunk_out, path_out):
    tail_shape = path_out.shape[2:]
    branch_rows = path_out[0::2, :SEG].reshape((4 * SEG,) + tail_shape)
    leaf_rows = path_out[:, SEG:].reshape((8 * SEG,) + tail_shape)
    return jnp.concatenate([trunk_out, branch_rows, leaf_rows], axis=0)

def convolve(pre_scores, conv_w):
    out_rows = pre_scores.shape[1] - (CQ - 1)
    key_width = pre_scores.shape[2]
    half_width = CK // 2
    padded = jnp.pad(pre_scores, ((0, 0), (0, 0), (half_width, half_width)))
    conv_total = jnp.zeros((pre_scores.shape[0], out_rows, key_width), jnp.float32)
    for shift_q in range(CQ):
        for shift_k in range(CK):
            window = padded[:, CQ - 1 - shift_q:CQ - 1 - shift_q + out_rows, 2 * half_width - shift_k:2 * half_width - shift_k + key_width]
            conv_total = conv_total + conv_w[:, shift_q, shift_k][:, None, None] * window
    return conv_total

def attend(q_rows, k_rows, v_rows, q_pos, k_valid, conv_w, mix_w):
    raw_scores = jnp.einsum('rhd,khd->hrk', q_rows, k_rows, precision=lax.Precision.HIGHEST) / math.sqrt(HD)
    raw_scores = low_back(raw_scores)
    key_index = jnp.arange(k_rows.shape[0], dtype=jnp.int32)
    allowed = (key_index[None, :] <= q_pos[:, None]) & k_valid[None, :] & (q_pos[:, None] >= 0)
    pre_scores = jnp.where(allowed[None], raw_scores, 0.0)
    conv_out = convolve(pre_scores, conv_w)
    logits = jnp.where(allowed[CQ - 1:][None], conv_out, -1e+30)
    probabilities = jax.nn.softmax(logits, axis=-1)
    mixed_probs = low(lax.optimization_barrier(jnp.sum(mix_w[:, :, None, None] * probabilities[None], axis=1)))
    return jnp.einsum('hrk,khd->rhd', mixed_probs, v_rows, precision=lax.Precision.HIGHEST)

def group_attention(q_grp, k_grp, v_grp, conv_grp, mix_grp, valid_tree):
    trunk_pos = jnp.arange(-(CQ - 1), TRUNK, dtype=jnp.int32)
    path_pos = jnp.arange(TRUNK - (CQ - 1), TRUNK + 2 * SEG, dtype=jnp.int32)
    trunk_q = jnp.concatenate([jnp.zeros((CQ - 1,) + q_grp.shape[1:], jnp.float32), q_grp[:TRUNK]], axis=0)
    trunk_out = attend(trunk_q, k_grp[:TRUNK], v_grp[:TRUNK], trunk_pos, valid_tree[:TRUNK], conv_grp, mix_grp)
    path_attend = jax.vmap(attend, in_axes=(0, 0, 0, None, 0, None, None))
    path_out = path_attend(along_paths(q_grp)[:, TRUNK - (CQ - 1):], along_paths(k_grp), along_paths(v_grp), path_pos, along_paths(valid_tree), conv_grp, mix_grp)
    return owned_rows(trunk_out, path_out)

def residual_block(inputs, gain_one, w_query, w_key, w_value, conv_weight, head_mix, gn_gain, w_out, gain_two, w_gate, w_up, w_down, valid_tree, target):
    row_total = inputs.shape[0]
    inv_one = lax.rsqrt(lax.optimization_barrier(jnp.mean(inputs * inputs, axis=-1, keepdims=True)) + 1e-06)
    normed_one = low(inputs * inv_one * gain_one)
    queries = low(low_back(matmul(normed_one, w_query)))
    keys_all = low(low_back(matmul(normed_one, w_key)))
    values_all = low(low_back(matmul(normed_one, w_value)))

    def by_group(array_in):
        return array_in.reshape(row_total, H // 2, 2, HD).transpose(1, 0, 2, 3)

    def per_group(group_items):
        q_grp, k_grp, v_grp, conv_grp, mix_grp = group_items
        return group_attention(q_grp, k_grp, v_grp, conv_grp, mix_grp, valid_tree)
    head_out = lax.map(jax.checkpoint(per_group), (by_group(queries), by_group(keys_all), by_group(values_all), conv_weight.reshape(H // 2, 2, CQ, CK), head_mix))
    head_out = head_out.transpose(1, 0, 2, 3).reshape(row_total, H, HD)
    head_out = low_back(head_out)
    centered = head_out - lax.optimization_barrier(jnp.mean(head_out, axis=-1, keepdims=True))
    inv_gn = lax.rsqrt(lax.optimization_barrier(jnp.mean(centered * centered, axis=-1, keepdims=True)) + 1e-05)
    normed_heads = low((centered * inv_gn * gn_gain).reshape(row_total, H * HD))
    attn_rows = low_back(matmul(normed_heads, w_out.T))
    hidden_in = inputs + attn_rows
    inv_two = lax.rsqrt(lax.optimization_barrier(jnp.mean(hidden_in * hidden_in, axis=-1, keepdims=True)) + 1e-06)
    normed_two = low(hidden_in * inv_two * gain_two)
    gate_val = low_back(matmul(normed_two, w_gate))
    up_val = low_back(matmul(normed_two, w_up))
    hidden_low = low(jax.nn.silu(gate_val) * up_val)
    ffn_rows = low_back(matmul(hidden_low, w_down.T))
    final_rows = hidden_in + ffn_rows
    error_rows = valid_tree.astype(jnp.float32)[:, None] * (final_rows - target)
    squared = jnp.sum(error_rows * error_rows)
    return (0.5 * squared, (final_rows, squared))

def reference(tokens, teacher, valid_mask, norm1_gain, w_query, w_key, w_value, conv_weight, head_mix, gn_gain, w_out, norm2_gain, w_gate, w_up, w_down):
    weights = (norm1_gain.astype(jnp.float32), w_query.astype(jnp.float32), w_key.astype(jnp.float32), w_value.astype(jnp.float32), conv_weight.astype(jnp.float32), head_mix.astype(jnp.float32), gn_gain.astype(jnp.float32), w_out.astype(jnp.float32), norm2_gain.astype(jnp.float32), w_gate.astype(jnp.float32), w_up.astype(jnp.float32), w_down.astype(jnp.float32))
    tree_tokens = tokens.astype(jnp.float32).reshape(TREES, TREE, D)
    tree_teacher = teacher.astype(jnp.float32).reshape(TREES, TREE, D)
    tree_valid = valid_mask.reshape(TREES, TREE)

    def per_tree(running, tree_items):
        tok_tree, teach_tree, valid_tree = tree_items
        valid_bool = valid_tree > 0

        def energy(inputs, *params):
            return residual_block(inputs, *params, valid_bool, teach_tree)
        energy_value, pullback, aux_values = jax.vjp(energy, tok_tree, *weights, has_aux=True)
        tree_grads = pullback(jnp.ones_like(energy_value))
        updated = tuple((acc + grad for acc, grad in zip(running, tree_grads[1:])))
        count_tree = jnp.sum(valid_bool.astype(jnp.float32))
        return (updated, (aux_values[0], tree_grads[0], aux_values[1], count_tree))
    initial = tuple((jnp.zeros_like(weight) for weight in weights))
    totals, (finals, d_inputs, squares, counts) = lax.scan(per_tree, initial, (tree_tokens, tree_teacher, tree_valid))
    loss = jnp.sum(squares) / (jnp.sum(counts) * D)
    return (finals.reshape(TOKENS, D).astype(jnp.bfloat16), loss, d_inputs.reshape(TOKENS, D), totals[0], totals[1], totals[2], totals[3], totals[4], totals[5], totals[6], totals[7], totals[8], totals[9], totals[10], totals[11])
```

```python
import math
import jax
import jax.numpy as jnp
from jax import lax
from jax.experimental import pallas as pl
from jax.experimental.pallas import tpu as pltpu
from jax.sharding import PartitionSpec as P

HD = 96
CQ = 6
CK = 11
TRUNK = 192
SEG = 32
TREE = 576
WIN = 256
FAM = 96
EXT = 680
F32 = jnp.float32
BF16 = jnp.bfloat16


def segments():
    rows = [(0, TRUNK, 0, 0, -1)]
    for b in range(4):
        base, ext = TRUNK + FAM * b, 200 + 120 * b
        rows.append((TRUNK + SEG * b, SEG, base, ext, TRUNK - 8))
        for c in range(2):
            rows.append((320 + 64 * b + SEG * c, SEG, base + SEG * (c + 1), ext + 40 * (c + 1), TRUNK + SEG * b + SEG - 8))
    return rows


SEGS = segments()


def nn(a, b):
    return lax.dot_general(a, b, (((1,), (0,)), ((), ())), preferred_element_type=F32)


def nt(a, b):
    return lax.dot_general(a, b, (((1,), (1,)), ((), ())), preferred_element_type=F32)


def tn(a, b):
    return lax.dot_general(a, b, (((0,), (0,)), ((), ())), preferred_element_type=F32)


def head_masks(g):
    lane = lax.broadcasted_iota(jnp.int32, (1, WIN), 1)
    first = 64 * g
    m0 = (lane >= first) & (lane < first + HD)
    m1 = (lane >= first + HD) & (lane < first + 2 * HD)
    return m0, m1, lane >= first


def fill_distance(jj_ref, dist_ref):
    for index, (_, size, row, _, _) in enumerate(SEGS):
        start = 0 if index == 0 else (TRUNK if (index - 1) % 3 == 0 else TRUNK + SEG)
        pos = lax.broadcasted_iota(jnp.int32, (size, WIN), 0) + start
        dist_ref[row : row + size] = pos - jj_ref[index : index + 1, :]


def path_rows(ref, b, c, column):
    if b is None:
        parts = [ref[0:TRUNK, pl.ds(column, WIN)], ref[TRUNK : TRUNK + SEG, pl.ds(column, WIN)], ref[320 : 320 + SEG, pl.ds(column, WIN)]]
    else:
        parts = [
            ref[0:TRUNK, pl.ds(column, WIN)],
            ref[pl.ds(pl.multiple_of(TRUNK + SEG * b, SEG), SEG), pl.ds(column, WIN)],
            ref[pl.ds(pl.multiple_of(320 + 64 * b + SEG * c, SEG), SEG), pl.ds(column, WIN)],
        ]
    return jnp.concatenate(parts, axis=0)


def fam_rows(b, c):
    base = TRUNK + FAM * b
    return (pl.ds(pl.multiple_of(base, 32), 64), 64) if c == 0 else (pl.ds(pl.multiple_of(base + 64, 32), SEG), SEG)


def group_norm(ho, m0, m1):
    def stat(v):
        s0 = jnp.sum(jnp.where(m0, v, 0.0), axis=-1, keepdims=True) * (1.0 / HD)
        s1 = jnp.sum(jnp.where(m1, v, 0.0), axis=-1, keepdims=True) * (1.0 / HD)
        return jnp.where(m0, s0, s1)

    centered = jnp.where(m0 | m1, ho - stat(ho), 0.0)
    inv = lax.rsqrt(stat(centered * centered) + 1e-05)
    return centered * inv, inv, stat


def fwd_kernel(mix_ref, qkv_ref, t_ref, gn_ref, jj_ref, nh_ref, att_ref, pre_ref, qs_ref, ho_ref, dist_ref, qx_ref, mx_ref):
    g = pl.program_id(1)
    w0 = pl.multiple_of(g * 128, 128)
    m0, m1, from_first = head_masks(g)
    m0f, m1f = m0.astype(F32), m1.astype(F32)
    fill_distance(jj_ref, dist_ref)
    qx_ref[0:8] = jnp.zeros((8, WIN), F32)
    for token, size, _, ext, parent in SEGS:
        if parent >= 0:
            low = qkv_ref[parent - 8 : parent + 8, pl.ds(w0, WIN)].astype(F32)
            qx_ref[ext : ext + 8] = low[8:16]
        qx_ref[ext + 8 : ext + 8 + size] = qkv_ref[token : token + size, pl.ds(w0, WIN)].astype(F32)
    for a in range(CQ):
        for _, size, row, ext, _ in SEGS:
            part = qx_ref[ext + 8 - a : ext + 8 - a + size]
            qs_ref[0, a, row : row + size] = (part * m0f).astype(BF16)
            qs_ref[1, a, row : row + size] = (part * m1f).astype(BF16)
    k0, v0 = w0 + 384, w0 + 768
    k_trunk = path_rows(qkv_ref, None, 0, k0)

    def trunk_scores(a, carry):
        scores = nt(qs_ref[:, a, 0:TRUNK].reshape(2 * TRUNK, WIN), k_trunk).reshape(2, TRUNK, WIN)
        kept = dist_ref[0:TRUNK] >= a
        for e in range(2):
            pre_ref[e, 0:TRUNK, pl.ds(pl.multiple_of(a * WIN, WIN), WIN)] = jnp.where(kept, scores[e], 0.0).astype(BF16)
        return carry

    lax.fori_loop(0, CQ, trunk_scores, 0)

    def fam_scores(b, carry):
        for c in range(2):
            rows, size = fam_rows(b, c)
            keys = path_rows(qkv_ref, b, c, k0)
            scores = nt(qs_ref[:, :, rows].reshape(2 * CQ * size, WIN), keys).reshape(2, CQ, size, WIN)
            dist = dist_ref[rows]
            for a in range(CQ):
                kept = dist >= a
                for e in range(2):
                    pre_ref[e, rows, a * WIN : (a + 1) * WIN] = jnp.where(kept, scores[e, a], 0.0).astype(BF16)
        return carry

    lax.fori_loop(0, 4, fam_scores, 0)
    for e in range(2):
        conv = nn(pre_ref[e], t_ref[e])
        logits = jnp.where(dist_ref[...] >= 0, conv, -1e30)
        shifted = jnp.exp(logits - jnp.max(logits, axis=-1, keepdims=True))
        att_ref[e] = shifted / jnp.sum(shifted, axis=-1, keepdims=True)
    for c in range(2):
        mx_ref[c] = (mix_ref[4 * g + 2 * c] * att_ref[0] + mix_ref[4 * g + 2 * c + 1] * att_ref[1]).astype(BF16)

    def put_out(rows, size, values):
        out = nn(mx_ref[:, rows].reshape(2 * size, WIN), values).reshape(2, size, WIN)
        ho_ref[rows] = jnp.where(m0, out[0], jnp.where(m1, out[1], 0.0))

    put_out(pl.ds(0, TRUNK), TRUNK, path_rows(qkv_ref, None, 0, v0))

    def fam_out(b, carry):
        for c in range(2):
            rows, size = fam_rows(b, c)
            put_out(rows, size, path_rows(qkv_ref, b, c, v0))
        return carry

    lax.fori_loop(0, 4, fam_out, 0)
    gain = gn_ref[0:1, pl.ds(w0, WIN)]
    for token, size, row, _, _ in SEGS:
        unit, _, _ = group_norm(ho_ref[row : row + size], m0, m1)
        old = nh_ref[token : token + size, pl.ds(w0, WIN)].astype(F32)
        nh_ref[token : token + size, pl.ds(w0, WIN)] = jnp.where(from_first, unit * gain, old).astype(BF16)


def bwd_kernel(
    mix_ref, qkv_ref, t_ref, gn_ref, jj_ref, dn_ref, att_ref, pre_ref, qs_ref, ho_ref,
    dqkv_ref, ggn_ref, gmix_ref, gconv_ref,
    dist_ref, dh_ref, mx_ref, dm_ref, dc_ref, es_ref, dqx_ref, dk_ref, dv_ref,
):
    t, g = pl.program_id(0), pl.program_id(1)
    w0 = pl.multiple_of(g * 128, 128)
    m0, m1, from_first = head_masks(g)
    both = m0 | m1
    fill_distance(jj_ref, dist_ref)
    gain = gn_ref[0:1, pl.ds(w0, WIN)]
    gn_sum = jnp.zeros((1, WIN), F32)
    for token, size, row, _, _ in SEGS:
        unit, inv, stat = group_norm(ho_ref[row : row + size], m0, m1)
        dn = jnp.where(both, dn_ref[token : token + size, pl.ds(w0, WIN)].astype(F32), 0.0)
        gn_sum = gn_sum + jnp.sum(dn * unit, axis=0, keepdims=True)
        scaled = dn * gain
        d_head = inv * (scaled - stat(scaled) - unit * stat(scaled * unit))
        dh_ref[0, row : row + size] = jnp.where(m0, d_head, 0.0).astype(BF16)
        dh_ref[1, row : row + size] = jnp.where(m1, d_head, 0.0).astype(BF16)

    @pl.when((t == 0) & (g == 0))
    def _():
        ggn_ref[...] = jnp.zeros_like(ggn_ref)

    ggn_ref[0:1, pl.ds(w0, WIN)] += gn_sum
    k0, v0 = w0 + 384, w0 + 768
    for c in range(2):
        mx_ref[c] = (mix_ref[4 * g + 2 * c] * att_ref[0] + mix_ref[4 * g + 2 * c + 1] * att_ref[1]).astype(BF16)

    def add_keys(acc_ref, b, c, grads):
        acc_ref[0:TRUNK] += grads[0:TRUNK]
        branch = pl.ds(pl.multiple_of(TRUNK + SEG * b, SEG), SEG)
        if c == 0:
            acc_ref[branch] = grads[TRUNK : TRUNK + SEG]
        else:
            acc_ref[branch] += grads[TRUNK : TRUNK + SEG]
        acc_ref[pl.ds(pl.multiple_of(320 + 64 * b + SEG * c, SEG), SEG)] = grads[TRUNK + SEG :]

    def value_part(rows, size, values):
        heads = dh_ref[:, rows].reshape(2 * size, WIN)
        dm_ref[:, rows] = nt(heads, values).reshape(2, size, WIN)
        return tn(mx_ref[:, rows].reshape(2 * size, WIN), heads)

    dv_ref[0:TRUNK] = value_part(pl.ds(0, TRUNK), TRUNK, path_rows(qkv_ref, None, 0, v0))[0:TRUNK]

    def fam_values(b, carry):
        for c in range(2):
            rows, size = fam_rows(b, c)
            add_keys(dv_ref, b, c, value_part(rows, size, path_rows(qkv_ref, b, c, v0)))
        return carry

    lax.fori_loop(0, 4, fam_values, 0)

    def soft_part(block, sums):
        rows = pl.ds(pl.multiple_of(block * FAM, 32), FAM)
        dm = [dm_ref[c, rows] for c in range(2)]
        att = [att_ref[e, rows] for e in range(2)]
        out = []
        for e in range(2):
            d_att = mix_ref[4 * g + e] * dm[0] + mix_ref[4 * g + 2 + e] * dm[1]
            d_conv = att[e] * (d_att - jnp.sum(d_att * att[e], axis=-1, keepdims=True))
            dc_ref[e, rows] = d_conv.astype(BF16)
        for c in range(2):
            for e in range(2):
                out.append(sums[2 * c + e] + jnp.sum(dm[c] * att[e], axis=0, keepdims=True))
        return tuple(out)

    mix_sums = lax.fori_loop(0, 6, soft_part, tuple(jnp.zeros((1, WIN), F32) for _ in range(4)))
    gmix_ref[...] = jnp.zeros_like(gmix_ref)
    gconv_ref[...] = jnp.zeros_like(gconv_ref)
    for index in range(4):
        gmix_ref[index : index + 1] = mix_sums[index]
    mirror = lax.broadcasted_iota(jnp.int32, (WIN, WIN), 0) + lax.broadcasted_iota(jnp.int32, (WIN, WIN), 1) - (WIN - 1)
    band = jnp.abs(mirror) <= CK // 2
    flip = jnp.where(mirror == 0, 1.0, 0.0).astype(BF16)
    for e in range(2):
        flipped = nn(dc_ref[e], flip).astype(BF16)
        for a in range(CQ):
            cols = slice(a * WIN, (a + 1) * WIN)
            products = jnp.where(band, tn(flipped, pre_ref[e, :, cols]), 0.0)
            rolled = pltpu.roll(products, 24, 1, stride=1, stride_axis=0)
            gconv_ref[e, a : a + 1] = jnp.sum(rolled, axis=0, keepdims=True)
            grads = nt(dc_ref[e], t_ref[e, cols, :])
            es_ref[e, a] = jnp.where(dist_ref[...] >= a, grads, 0.0).astype(BF16)

    def score_part(rows, size, keys):
        grads = es_ref[:, :, rows].reshape(2 * CQ * size, WIN)
        back = nn(grads, keys).reshape(2, CQ, size, WIN)
        d_query = [jnp.where(m0, back[0, a], jnp.where(m1, back[1, a], 0.0)) for a in range(CQ)]
        return d_query, tn(grads, qs_ref[:, :, rows].reshape(2 * CQ * size, WIN))

    def shifted_sum(parts, start, size):
        zeros = jnp.zeros((8, WIN), F32)
        total = None
        for a in range(CQ):
            padded = jnp.concatenate([zeros, parts[a][start : start + size]], axis=0)
            if a:
                padded = pltpu.roll(padded, size + 8 - a, 0)
            total = padded if total is None else total + padded
        return total

    d_query, d_keys = score_part(pl.ds(0, TRUNK), TRUNK, path_rows(qkv_ref, None, 0, k0))
    dqx_ref[0:200] = shifted_sum(d_query, 0, TRUNK)
    dk_ref[0:TRUNK] = d_keys[0:TRUNK]

    def fam_scores(b, carry):
        ext = 200 + 120 * b
        for c in range(2):
            rows, size = fam_rows(b, c)
            d_query, d_keys = score_part(rows, size, path_rows(qkv_ref, b, c, k0))
            add_keys(dk_ref, b, c, d_keys)
            if c == 0:
                dqx_ref[pl.ds(pl.multiple_of(ext, 8), 40)] = shifted_sum(d_query, 0, SEG)
                dqx_ref[pl.ds(pl.multiple_of(ext + 40, 8), 40)] = shifted_sum(d_query, SEG, SEG)
            else:
                dqx_ref[pl.ds(pl.multiple_of(ext + 80, 8), 40)] = shifted_sum(d_query, 0, SEG)
        return carry

    lax.fori_loop(0, 4, fam_scores, 0)
    for b in range(4):
        ext = 200 + 120 * b
        dqx_ref[192:200] += dqx_ref[ext : ext + 8]
        dqx_ref[ext + 32 : ext + 40] += dqx_ref[ext + 40 : ext + 48] + dqx_ref[ext + 80 : ext + 88]

    def put(token, size, column, value):
        old = dqkv_ref[token : token + size, pl.ds(column, WIN)].astype(F32)
        dqkv_ref[token : token + size, pl.ds(column, WIN)] = jnp.where(from_first, value, old).astype(BF16)

    for token, size, _, ext, _ in SEGS:
        put(token, size, w0, dqx_ref[ext + 8 : ext + 8 + size])
        put(token, size, k0, dk_ref[token : token + size])
        put(token, size, v0, dv_ref[token : token + size])


def by_tree(shape, last):
    return pl.BlockSpec(shape, lambda t, g: (t,) + (0,) * last)


def by_group(shape):
    tail = (0,) * (len(shape) - 2)
    return pl.BlockSpec((None, None) + shape[2:], lambda t, g: (t, g) + tail)


def common_specs():
    return [
        pl.BlockSpec(memory_space=pltpu.SMEM),
        pl.BlockSpec((TREE, 1152), lambda t, g: (t, 0)),
        pl.BlockSpec((None, 2, CQ * WIN, WIN), lambda t, g: (g, 0, 0, 0)),
        pl.BlockSpec((8, 384), lambda t, g: (0, 0)),
        pl.BlockSpec((None, 16, WIN), lambda t, g: (t, 0, 0)),
    ]


PARAMS = dict(vmem_limit_bytes=60 * 1024 * 1024, dimension_semantics=("arbitrary", "arbitrary"))


def saved_shapes(trees):
    return [(trees, 2, 2, TREE, WIN), (trees, 2, 2, TREE, CQ * WIN), (trees, 2, 2, CQ, TREE, WIN), (trees, 2, TREE, WIN)]


def attention_forward(mix, qkv, toeplitz, gains, jj):
    trees = qkv.shape[0] // TREE
    shapes = saved_shapes(trees)
    kinds = (F32, BF16, BF16, F32)
    return pl.pallas_call(
        fwd_kernel,
        grid=(trees, 2),
        in_specs=common_specs(),
        out_specs=[pl.BlockSpec((TREE, 384), lambda t, g: (t, 0))] + [by_group(s) for s in shapes],
        out_shape=[jax.ShapeDtypeStruct((trees * TREE, 384), BF16)] + [jax.ShapeDtypeStruct(s, k) for s, k in zip(shapes, kinds)],
        scratch_shapes=[pltpu.VMEM((TREE, WIN), jnp.int32), pltpu.VMEM((EXT, WIN), F32), pltpu.VMEM((2, TREE, WIN), BF16)],
        compiler_params=pltpu.CompilerParams(**PARAMS),
        cost_estimate=pl.CostEstimate(flops=40_000_000_000, bytes_accessed=60_000_000, transcendentals=0),
    )(mix, qkv, toeplitz, gains, jj)


def attention_backward(mix, qkv, toeplitz, gains, jj, d_normed, saved):
    trees = qkv.shape[0] // TREE
    shapes = saved_shapes(trees)
    return pl.pallas_call(
        bwd_kernel,
        grid=(trees, 2),
        in_specs=common_specs() + [pl.BlockSpec((TREE, 384), lambda t, g: (t, 0))] + [by_group(s) for s in shapes],
        out_specs=[
            pl.BlockSpec((TREE, 1152), lambda t, g: (t, 0)),
            pl.BlockSpec((8, 384), lambda t, g: (0, 0)),
            by_group((trees, 2, 8, WIN)),
            by_group((trees, 2, 2, 8, WIN)),
        ],
        out_shape=[
            jax.ShapeDtypeStruct((trees * TREE, 1152), BF16),
            jax.ShapeDtypeStruct((8, 384), F32),
            jax.ShapeDtypeStruct((trees, 2, 8, WIN), F32),
            jax.ShapeDtypeStruct((trees, 2, 2, 8, WIN), F32),
        ],
        scratch_shapes=[
            pltpu.VMEM((TREE, WIN), jnp.int32),
            pltpu.VMEM((2, TREE, WIN), BF16),
            pltpu.VMEM((2, TREE, WIN), BF16),
            pltpu.VMEM((2, TREE, WIN), F32),
            pltpu.VMEM((2, TREE, WIN), BF16),
            pltpu.VMEM((2, CQ, TREE, WIN), BF16),
            pltpu.VMEM((EXT, WIN), F32),
            pltpu.VMEM((TREE, WIN), F32),
            pltpu.VMEM((TREE, WIN), F32),
        ],
        compiler_params=pltpu.CompilerParams(**PARAMS),
        cost_estimate=pl.CostEstimate(flops=80_000_000_000, bytes_accessed=60_000_000, transcendentals=0),
    )(mix, qkv, toeplitz, gains, jj, d_normed, *saved)


def toeplitz_of(conv_w):
    heads = conv_w.shape[0]
    offset = lax.broadcasted_iota(jnp.int32, (WIN, WIN), 1) - lax.broadcasted_iota(jnp.int32, (WIN, WIN), 0) + CK // 2
    total = jnp.zeros((heads, CQ, WIN, WIN), F32)
    for b in range(CK):
        total = total + jnp.where(offset == b, 1.0, 0.0) * (conv_w[:, :, b] * (1.0 / math.sqrt(HD)))[:, :, None, None]
    return total.astype(BF16).reshape(heads // 2, 2, CQ * WIN, WIN)


def key_positions(valid):
    trees = valid.shape[0] // TREE
    valid = valid.reshape(trees, TREE)
    far = jnp.int32(1 << 20)

    def places(part, start):
        return jnp.where(part > 0, lax.broadcasted_iota(jnp.int32, part.shape, 1) + start, far)

    trunk = places(valid[:, :TRUNK], 0)
    empty = jnp.full((trees, SEG), far, jnp.int32)
    rows = [jnp.concatenate([trunk, empty, empty], axis=1)]
    for b in range(4):
        branch = places(valid[:, TRUNK + SEG * b : TRUNK + SEG * (b + 1)], TRUNK)
        rows.append(jnp.concatenate([trunk, branch, empty], axis=1))
        for c in range(2):
            first = 320 + 64 * b + SEG * c
            leaf = places(valid[:, first : first + SEG], TRUNK + SEG)
            rows.append(jnp.concatenate([trunk, branch, leaf], axis=1))
    rows += [jnp.zeros((trees, WIN), jnp.int32)] * 3
    return jnp.stack(rows, axis=1)


def conv_grads(gconv):
    lanes = gconv[..., :CQ, 18:29][..., ::-1] * (1.0 / math.sqrt(HD))
    return jnp.sum(lanes, axis=0).reshape(-1, CQ, CK)


def mix_grads(gmix):
    return jnp.sum(gmix[:, :, :4], axis=(0, 3)).reshape(-1, 2, 2)


BACK = (0, 2, 1, 3)


def rows_dot(lhs, rhs):
    return tn(lhs, rhs).astype(BF16)


def unfused(value):
    return lax.optimization_barrier(value)


def make_local(planes, tensors):
    every = ("plane", "core", "tensor")
    sides = [(c, z) for c in range(2) for z in range(tensors)]

    def spot(q, c, z):
        return (q * 2 + c) * tensors + z

    def is_home(c, z):
        return z // 2 == c

    far_pairs = [(spot(q, c, z), spot(q, 1 - c, z ^ 2)) for q in range(planes) for c, z in sides if not is_home(c, z)]
    near_pairs = [
        (spot(q, c, z), spot(q, c, z ^ 1) if is_home(c, z) else spot(q, 1 - c, z ^ 3)) for q in range(planes) for c, z in sides
    ]

    def plane_pairs(flip, away_only):
        return [(spot(q, c, z), spot(q ^ flip, c, z)) for q in range(planes) for c, z in sides if not (away_only and is_home(c, z))]

    def over_plane(value, flip, away_only=False):
        return lax.ppermute(value, every, plane_pairs(flip, away_only))

    def over_core(value):
        return lax.ppermute(value, "core", [(0, 1), (1, 0)])

    def first_from(value):
        return lax.ppermute(value, every, far_pairs)

    def second_from(value):
        return lax.ppermute(value, every, near_pairs)

    square = planes == 4

    def local(
        tokens, teacher, valid_mask, norm1_gain, w_query, w_key, w_value, conv_weight, head_mix, gn_gain, w_out, norm2_gain,
        w_gate, w_up, w_down,
    ):
        q, c, z = lax.axis_index("plane"), lax.axis_index("core"), lax.axis_index("tensor")
        own_rows, width = tokens.shape
        home = (z // 2) == c
        chunk = width // planes
        heads = conv_weight.shape[0]
        wide = w_query.shape[1]

        def place(k):
            return jnp.bitwise_xor(q, k)

        def cut(value, index, axis):
            return lax.dynamic_slice_in_dim(value, index * chunk, chunk, axis)

        def turn(value, axis):
            if not square:
                return value
            return jnp.concatenate([cut(value, place(k), axis) for k in BACK], axis=axis)

        def turn_back(value, axis):
            if not square:
                return value
            parts = []
            for j in range(4):
                k = place(j)
                parts.append(cut(value, (k % 2) * 2 + k // 2, axis))
            return jnp.concatenate(parts, axis=axis)

        def spread(piece, away_only):
            if not square:
                return lax.all_gather(piece, "plane", axis=0, tiled=True)
            half = piece.shape[0] // 2
            by_x = over_plane(piece, 1, away_only)
            by_y = over_plane(piece, 2, away_only)
            top = over_plane(by_x[:half], 2, away_only)
            low = over_plane(by_y[half:], 1, away_only)
            return jnp.concatenate([piece, by_y, by_x, top, low], axis=0)

        def collect(parts):
            piece = jnp.concatenate([cut(p, q, 0) for p in parts], axis=1)
            second = spread(second_from(piece), False)
            first = spread(first_from(piece), True)
            mine = turn(jnp.concatenate(parts, axis=1), 0)
            return jnp.where(home, mine, first), second

        def reduce(lhs, rhs_first, rhs_second):
            if square:
                order = [lhs[:, k * chunk : (k + 1) * chunk] for k in range(4)]
                other = jnp.concatenate([order[1], order[3]], axis=1)
                keep = jnp.concatenate([order[0], order[2]], axis=1)
                recv_a = over_plane(rows_dot(lhs[:, 2 * chunk :], rhs_first), 1)
                recv_b = over_plane(rows_dot(other, rhs_second), 2)
                top_a = unfused(rows_dot(lhs[:, : 2 * chunk], rhs_first))
                top_b = unfused(rows_dot(keep, rhs_second))
                sum_a = top_a.astype(F32) + recv_a.astype(F32)
                sum_b = top_b.astype(F32) + recv_b.astype(F32)
                last_a = over_plane(sum_a[chunk:].astype(BF16), 2)
                last_b = over_plane(sum_b[chunk:].astype(BF16), 1)
                part_a = (sum_a[:chunk] + last_a.astype(F32)).astype(BF16)
                part_b = (sum_b[:chunk] + last_b.astype(F32)).astype(BF16)
            else:
                part_a = lax.psum_scatter(rows_dot(lhs, rhs_first), "plane", scatter_dimension=0, tiled=True)
                part_b = lax.psum_scatter(rows_dot(lhs, rhs_second), "plane", scatter_dimension=0, tiled=True)
            from_a = first_from(part_a)
            from_b = second_from(part_b)
            here = (jnp.where(home, part_a, from_a).astype(F32) + from_b.astype(F32)).astype(BF16)
            there = over_core(here)
            total = (here.astype(F32) + there.astype(F32)).astype(BF16)
            if not square:
                return lax.all_gather(total, "plane", axis=0, tiled=True).astype(F32)
            half = chunk // 2
            mine = spread(lax.dynamic_slice_in_dim(total, c * half, half, 0), False)
            theirs = over_core(mine)
            low = jnp.where(c == 0, mine, theirs).reshape(4, half, -1)
            high = jnp.where(c == 0, theirs, mine).reshape(4, half, -1)
            whole = jnp.concatenate([low, high], axis=1).reshape(width, -1)
            return turn_back(whole, 0).astype(F32)

        small = jnp.concatenate([conv_weight.reshape(-1), head_mix.reshape(-1), gn_gain.reshape(-1)])
        small_first = jnp.where(home, small, first_from(small))
        small_second = second_from(small)
        conv_size, mix_size = conv_weight.size, head_mix.size

        tokens = turn(tokens, 1)
        teacher = turn(teacher, 1)
        gain_one = turn(norm1_gain, 0)
        gain_two = turn(norm2_gain, 0)
        own_valid = lax.dynamic_slice_in_dim(valid_mask, z * own_rows, own_rows, 0)
        jj = key_positions(jnp.concatenate([own_valid, over_core(own_valid)]))

        qkv_weights = collect([w_query, w_key, w_value])
        out_weights = collect([w_out])
        gu_weights = collect([w_gate, w_up])
        down_weights = collect([w_down])

        def with_partner(value):
            return jnp.concatenate([value, over_core(value)], axis=0)

        def summed(lefts, rights):
            def half(rows):
                total = nt(lefts[0][rows], rights[0])
                return total + nt(lefts[1][rows], rights[1])

            sent = over_core(half(slice(own_rows, None)).astype(BF16))
            return half(slice(0, own_rows)) + sent.astype(F32)

        inputs = tokens.astype(F32)
        inv_one = lax.rsqrt(jnp.mean(inputs * inputs, axis=-1, keepdims=True) + 1e-06)
        normed_one = with_partner((inputs * inv_one * gain_one).astype(BF16))
        sides_small = []
        for vec in (small_first, small_second):
            conv = vec[:conv_size].reshape(conv_weight.shape)
            mix = vec[conv_size : conv_size + mix_size]
            gains = jnp.broadcast_to(vec[conv_size + mix_size :][None], (8, wide))
            sides_small.append((mix, toeplitz_of(conv), gains))
        qkv, heads_out, saved = [], [], []
        for (mix, toep, gains), weight in zip(sides_small, qkv_weights):
            projected = nn(normed_one, weight).astype(BF16)
            result = attention_forward(mix, projected, toep, gains, jj)
            qkv.append(projected)
            heads_out.append(result[0])
            saved.append(result[1:])
        hidden_in = inputs + summed(heads_out, out_weights)
        inv_two = lax.rsqrt(jnp.mean(hidden_in * hidden_in, axis=-1, keepdims=True) + 1e-06)
        normed_two = with_partner((hidden_in * inv_two * gain_two).astype(BF16))
        units = w_gate.shape[1]
        gates, ups, hiddens = [], [], []
        for weight in gu_weights:
            both = nn(normed_two, weight)
            gate, up = both[:, :units], both[:, units:]
            gates.append(gate.astype(BF16))
            ups.append(up.astype(BF16))
            hiddens.append((jax.nn.silu(gate) * up).astype(BF16))
        final_rows = hidden_in + summed(hiddens, down_weights)
        output = turn_back(final_rows.astype(BF16), 1)
        own_mask = own_valid.astype(F32)
        error = own_mask[:, None] * (final_rows - teacher.astype(F32))
        squared_sum = jnp.sum(error * error)
        count_sum = jnp.sum(own_mask)

        d_all = with_partner(error.astype(BF16))
        grad_down = reduce(d_all, hiddens[0], hiddens[1])
        d_gus = []
        for index, weight in enumerate(down_weights):
            d_hidden = nn(d_all, weight)
            gate, up = gates[index].astype(F32), ups[index].astype(F32)
            s = jax.nn.sigmoid(gate)
            d_gate = (d_hidden * up * s * (1.0 + gate * (1.0 - s))).astype(BF16)
            d_up = (d_hidden * gate * s).astype(BF16)
            d_gus.append(jnp.concatenate([d_gate, d_up], axis=1))
        grad_gu = reduce(normed_two, d_gus[0], d_gus[1])
        d_normed_two = summed(d_gus, gu_weights)
        scaled_two = d_normed_two * gain_two
        grad_gain_two = jnp.sum(d_normed_two * hidden_in * inv_two, axis=0)
        d_hidden_in = (
            error + inv_two * scaled_two - hidden_in * inv_two**3 * jnp.mean(scaled_two * hidden_in, axis=-1, keepdims=True)
        )
        d_attn = with_partner(d_hidden_in.astype(BF16))
        grad_out = reduce(d_attn, heads_out[0], heads_out[1])
        d_qkv, small_grads = [], []
        for index, (mix, toep, gains) in enumerate(sides_small):
            d_normed = nn(d_attn, out_weights[index])
            dqkv, ggn, gmix, gconv = attention_backward(mix, qkv[index], toep, gains, jj, d_normed, saved[index])
            d_qkv.append(dqkv)
            small_grads.append(jnp.concatenate([conv_grads(gconv).reshape(-1), mix_grads(gmix).reshape(-1), ggn[0]]))
        grad_qkv = reduce(normed_one, d_qkv[0], d_qkv[1])
        d_normed_one = summed(d_qkv, qkv_weights)
        scaled_one = d_normed_one * gain_one
        grad_gain_one = jnp.sum(d_normed_one * inputs * inv_one, axis=0)
        grad_input = (
            d_hidden_in + inv_one * scaled_one - inputs * inv_one**3 * jnp.mean(scaled_one * inputs, axis=-1, keepdims=True)
        )
        grad_input = turn_back(grad_input, 1)

        table = jnp.zeros((tensors, small.size), F32)
        table = lax.dynamic_update_slice(table, small_grads[0][None], (2 * c + z % 2, 0))
        table = lax.dynamic_update_slice(table, small_grads[1][None], (2 * c + 1 - z % 2, 0))
        packed = jnp.concatenate(
            [table.reshape(-1), turn_back(grad_gain_one, 0), turn_back(grad_gain_two, 0), squared_sum[None], count_sum[None]]
        )
        packed = lax.psum(packed, every)
        table_size = tensors * small.size
        small_sum = lax.dynamic_slice_in_dim(packed, z * small.size, small.size, 0)
        gain_slice = width // tensors
        gain_one_out = lax.dynamic_slice_in_dim(packed, table_size + z * gain_slice, gain_slice, 0)
        gain_two_out = lax.dynamic_slice_in_dim(packed, table_size + width + z * gain_slice, gain_slice, 0)
        loss = packed[-2] / (packed[-1] * width)
        return (
            output,
            loss,
            grad_input,
            gain_one_out,
            grad_qkv[:, :wide],
            grad_qkv[:, wide : 2 * wide],
            grad_qkv[:, 2 * wide :],
            small_sum[:conv_size].reshape(conv_weight.shape),
            small_sum[conv_size : conv_size + mix_size].reshape(head_mix.shape),
            small_sum[conv_size + mix_size :].reshape(gn_gain.shape),
            grad_out,
            gain_two_out,
            grad_gu[:, :units],
            grad_gu[:, units:],
            grad_down,
        )

    return local


def solution(mesh):
    tensors = mesh.shape["tensor"]
    planes = mesh.shape["dp"] // 2
    inner = jax.sharding.Mesh(mesh.devices.reshape(planes, 2, tensors), ("plane", "core", "tensor"))
    rows = P(("plane", "core", "tensor"), None)
    columns = P(None, "tensor")
    cube = P("tensor", None, None)
    return jax.shard_map(
        make_local(planes, tensors),
        mesh=inner,
        in_specs=(
            rows, rows, P(("plane", "core")), P(), columns, columns, columns, cube, cube, P("tensor", None), columns, P(),
            columns, columns, columns,
        ),
        out_specs=(
            rows, P(), rows, P("tensor"), columns, columns, columns, cube, cube, P("tensor", None), columns, P("tensor"),
            columns, columns, columns,
        ),
        check_vma=False,
    )
```

```python
import math
import jax
import jax.numpy as jnp
from jax import lax
from jax.experimental import pallas as pl
from jax.experimental.pallas import tpu as pltpu
from jax.sharding import PartitionSpec as P

HD = 96
CQ = 6
CK = 11
TRUNK = 192
SEG = 32
TREE = 576
WIN = 256
FAM = 96
EXT = 680
F32 = jnp.float32
BF16 = jnp.bfloat16


def segments():
    rows = [(0, TRUNK, 0, 0, -1)]
    for b in range(4):
        base, ext = TRUNK + FAM * b, 200 + 120 * b
        rows.append((TRUNK + SEG * b, SEG, base, ext, TRUNK - 8))
        for c in range(2):
            rows.append((320 + 64 * b + SEG * c, SEG, base + SEG * (c + 1), ext + 40 * (c + 1), TRUNK + SEG * b + SEG - 8))
    return rows


SEGS = segments()


def nn(a, b):
    return lax.dot_general(a, b, (((1,), (0,)), ((), ())), preferred_element_type=F32)


def nt(a, b):
    return lax.dot_general(a, b, (((1,), (1,)), ((), ())), preferred_element_type=F32)


def tn(a, b):
    return lax.dot_general(a, b, (((0,), (0,)), ((), ())), preferred_element_type=F32)


def head_masks(g):
    lane = lax.broadcasted_iota(jnp.int32, (1, WIN), 1)
    first = 64 * g
    m0 = (lane >= first) & (lane < first + HD)
    m1 = (lane >= first + HD) & (lane < first + 2 * HD)
    return m0, m1, lane >= first


def fill_distance(jj_ref, dist_ref):
    for index, (_, size, row, _, _) in enumerate(SEGS):
        start = 0 if index == 0 else (TRUNK if (index - 1) % 3 == 0 else TRUNK + SEG)
        pos = lax.broadcasted_iota(jnp.int32, (size, WIN), 0) + start
        dist_ref[row : row + size] = pos - jj_ref[index : index + 1, :]


def path_rows(ref, b, c, column):
    if b is None:
        parts = [ref[0:TRUNK, pl.ds(column, WIN)], ref[TRUNK : TRUNK + SEG, pl.ds(column, WIN)], ref[320 : 320 + SEG, pl.ds(column, WIN)]]
    else:
        parts = [
            ref[0:TRUNK, pl.ds(column, WIN)],
            ref[pl.ds(pl.multiple_of(TRUNK + SEG * b, SEG), SEG), pl.ds(column, WIN)],
            ref[pl.ds(pl.multiple_of(320 + 64 * b + SEG * c, SEG), SEG), pl.ds(column, WIN)],
        ]
    return jnp.concatenate(parts, axis=0)


def fam_rows(b, c):
    base = TRUNK + FAM * b
    return (pl.ds(pl.multiple_of(base, 32), 64), 64) if c == 0 else (pl.ds(pl.multiple_of(base + 64, 32), SEG), SEG)


def group_norm(ho, m0, m1):
    def stat(v):
        s0 = jnp.sum(jnp.where(m0, v, 0.0), axis=-1, keepdims=True) * (1.0 / HD)
        s1 = jnp.sum(jnp.where(m1, v, 0.0), axis=-1, keepdims=True) * (1.0 / HD)
        return jnp.where(m0, s0, s1)

    centered = jnp.where(m0 | m1, ho - stat(ho), 0.0)
    inv = lax.rsqrt(stat(centered * centered) + 1e-05)
    return centered * inv, inv, stat


def fwd_kernel(mix_ref, qkv_ref, t_ref, gn_ref, jj_ref, nh_ref, att_ref, pre_ref, qs_ref, ho_ref, dist_ref, qx_ref, mx_ref):
    g = pl.program_id(1)
    w0 = pl.multiple_of(g * 128, 128)
    m0, m1, from_first = head_masks(g)
    m0f, m1f = m0.astype(F32), m1.astype(F32)
    fill_distance(jj_ref, dist_ref)
    qx_ref[0:8] = jnp.zeros((8, WIN), F32)
    for token, size, _, ext, parent in SEGS:
        if parent >= 0:
            low = qkv_ref[parent - 8 : parent + 8, pl.ds(w0, WIN)].astype(F32)
            qx_ref[ext : ext + 8] = low[8:16]
        qx_ref[ext + 8 : ext + 8 + size] = qkv_ref[token : token + size, pl.ds(w0, WIN)].astype(F32)
    for a in range(CQ):
        for _, size, row, ext, _ in SEGS:
            part = qx_ref[ext + 8 - a : ext + 8 - a + size]
            qs_ref[0, a, row : row + size] = (part * m0f).astype(BF16)
            qs_ref[1, a, row : row + size] = (part * m1f).astype(BF16)
    k0, v0 = w0 + 384, w0 + 768
    k_trunk = path_rows(qkv_ref, None, 0, k0)

    def trunk_scores(a, carry):
        scores = nt(qs_ref[:, a, 0:TRUNK].reshape(2 * TRUNK, WIN), k_trunk).reshape(2, TRUNK, WIN)
        kept = dist_ref[0:TRUNK] >= a
        for e in range(2):
            pre_ref[e, 0:TRUNK, pl.ds(pl.multiple_of(a * WIN, WIN), WIN)] = jnp.where(kept, scores[e], 0.0).astype(BF16)
        return carry

    lax.fori_loop(0, CQ, trunk_scores, 0)

    def fam_scores(b, carry):
        for c in range(2):
            rows, size = fam_rows(b, c)
            keys = path_rows(qkv_ref, b, c, k0)
            scores = nt(qs_ref[:, :, rows].reshape(2 * CQ * size, WIN), keys).reshape(2, CQ, size, WIN)
            dist = dist_ref[rows]
            for a in range(CQ):
                kept = dist >= a
                for e in range(2):
                    pre_ref[e, rows, a * WIN : (a + 1) * WIN] = jnp.where(kept, scores[e, a], 0.0).astype(BF16)
        return carry

    lax.fori_loop(0, 4, fam_scores, 0)
    for e in range(2):
        conv = nn(pre_ref[e], t_ref[e])
        logits = jnp.where(dist_ref[...] >= 0, conv, -1e30)
        shifted = jnp.exp(logits - jnp.max(logits, axis=-1, keepdims=True))
        att_ref[e] = shifted / jnp.sum(shifted, axis=-1, keepdims=True)
    for c in range(2):
        mx_ref[c] = (mix_ref[4 * g + 2 * c] * att_ref[0] + mix_ref[4 * g + 2 * c + 1] * att_ref[1]).astype(BF16)

    def put_out(rows, size, values):
        out = nn(mx_ref[:, rows].reshape(2 * size, WIN), values).reshape(2, size, WIN)
        ho_ref[rows] = jnp.where(m0, out[0], jnp.where(m1, out[1], 0.0))

    put_out(pl.ds(0, TRUNK), TRUNK, path_rows(qkv_ref, None, 0, v0))

    def fam_out(b, carry):
        for c in range(2):
            rows, size = fam_rows(b, c)
            put_out(rows, size, path_rows(qkv_ref, b, c, v0))
        return carry

    lax.fori_loop(0, 4, fam_out, 0)
    gain = gn_ref[0:1, pl.ds(w0, WIN)]
    for token, size, row, _, _ in SEGS:
        unit, _, _ = group_norm(ho_ref[row : row + size], m0, m1)
        old = nh_ref[token : token + size, pl.ds(w0, WIN)].astype(F32)
        nh_ref[token : token + size, pl.ds(w0, WIN)] = jnp.where(from_first, unit * gain, old).astype(BF16)


def bwd_kernel(
    mix_ref, qkv_ref, t_ref, gn_ref, jj_ref, dn_ref, att_ref, pre_ref, qs_ref, ho_ref,
    dqkv_ref, ggn_ref, gmix_ref, gconv_ref,
    dist_ref, dh_ref, mx_ref, dm_ref, dc_ref, es_ref, dqx_ref, dk_ref, dv_ref,
):
    t, g = pl.program_id(0), pl.program_id(1)
    w0 = pl.multiple_of(g * 128, 128)
    m0, m1, from_first = head_masks(g)
    both = m0 | m1
    fill_distance(jj_ref, dist_ref)
    gain = gn_ref[0:1, pl.ds(w0, WIN)]
    gn_sum = jnp.zeros((1, WIN), F32)
    for token, size, row, _, _ in SEGS:
        unit, inv, stat = group_norm(ho_ref[row : row + size], m0, m1)
        dn = jnp.where(both, dn_ref[token : token + size, pl.ds(w0, WIN)].astype(F32), 0.0)
        gn_sum = gn_sum + jnp.sum(dn * unit, axis=0, keepdims=True)
        scaled = dn * gain
        d_head = inv * (scaled - stat(scaled) - unit * stat(scaled * unit))
        dh_ref[0, row : row + size] = jnp.where(m0, d_head, 0.0).astype(BF16)
        dh_ref[1, row : row + size] = jnp.where(m1, d_head, 0.0).astype(BF16)

    @pl.when((t == 0) & (g == 0))
    def _():
        ggn_ref[...] = jnp.zeros_like(ggn_ref)

    ggn_ref[0:1, pl.ds(w0, WIN)] += gn_sum
    k0, v0 = w0 + 384, w0 + 768
    for c in range(2):
        mx_ref[c] = (mix_ref[4 * g + 2 * c] * att_ref[0] + mix_ref[4 * g + 2 * c + 1] * att_ref[1]).astype(BF16)

    def add_keys(acc_ref, b, c, grads):
        acc_ref[0:TRUNK] += grads[0:TRUNK]
        branch = pl.ds(pl.multiple_of(TRUNK + SEG * b, SEG), SEG)
        if c == 0:
            acc_ref[branch] = grads[TRUNK : TRUNK + SEG]
        else:
            acc_ref[branch] += grads[TRUNK : TRUNK + SEG]
        acc_ref[pl.ds(pl.multiple_of(320 + 64 * b + SEG * c, SEG), SEG)] = grads[TRUNK + SEG :]

    def value_part(rows, size, values):
        heads = dh_ref[:, rows].reshape(2 * size, WIN)
        dm_ref[:, rows] = nt(heads, values).reshape(2, size, WIN)
        return tn(mx_ref[:, rows].reshape(2 * size, WIN), heads)

    dv_ref[0:TRUNK] = value_part(pl.ds(0, TRUNK), TRUNK, path_rows(qkv_ref, None, 0, v0))[0:TRUNK]

    def fam_values(b, carry):
        for c in range(2):
            rows, size = fam_rows(b, c)
            add_keys(dv_ref, b, c, value_part(rows, size, path_rows(qkv_ref, b, c, v0)))
        return carry

    lax.fori_loop(0, 4, fam_values, 0)

    def soft_part(block, sums):
        rows = pl.ds(pl.multiple_of(block * FAM, 32), FAM)
        dm = [dm_ref[c, rows] for c in range(2)]
        att = [att_ref[e, rows] for e in range(2)]
        out = []
        for e in range(2):
            d_att = mix_ref[4 * g + e] * dm[0] + mix_ref[4 * g + 2 + e] * dm[1]
            d_conv = att[e] * (d_att - jnp.sum(d_att * att[e], axis=-1, keepdims=True))
            dc_ref[e, rows] = d_conv.astype(BF16)
        for c in range(2):
            for e in range(2):
                out.append(sums[2 * c + e] + jnp.sum(dm[c] * att[e], axis=0, keepdims=True))
        return tuple(out)

    mix_sums = lax.fori_loop(0, 6, soft_part, tuple(jnp.zeros((1, WIN), F32) for _ in range(4)))
    gmix_ref[...] = jnp.zeros_like(gmix_ref)
    gconv_ref[...] = jnp.zeros_like(gconv_ref)
    for index in range(4):
        gmix_ref[index : index + 1] = mix_sums[index]
    mirror = lax.broadcasted_iota(jnp.int32, (WIN, WIN), 0) + lax.broadcasted_iota(jnp.int32, (WIN, WIN), 1) - (WIN - 1)
    band = jnp.abs(mirror) <= CK // 2
    flip = jnp.where(mirror == 0, 1.0, 0.0).astype(BF16)
    for e in range(2):
        flipped = nn(dc_ref[e], flip).astype(BF16)
        for a in range(CQ):
            cols = slice(a * WIN, (a + 1) * WIN)
            products = jnp.where(band, tn(flipped, pre_ref[e, :, cols]), 0.0)
            rolled = pltpu.roll(products, 24, 1, stride=1, stride_axis=0)
            gconv_ref[e, a : a + 1] = jnp.sum(rolled, axis=0, keepdims=True)
            grads = nt(dc_ref[e], t_ref[e, cols, :])
            es_ref[e, a] = jnp.where(dist_ref[...] >= a, grads, 0.0).astype(BF16)

    def score_part(rows, size, keys):
        grads = es_ref[:, :, rows].reshape(2 * CQ * size, WIN)
        back = nn(grads, keys).reshape(2, CQ, size, WIN)
        d_query = [jnp.where(m0, back[0, a], jnp.where(m1, back[1, a], 0.0)) for a in range(CQ)]
        return d_query, tn(grads, qs_ref[:, :, rows].reshape(2 * CQ * size, WIN))

    def shifted_sum(parts, start, size):
        zeros = jnp.zeros((8, WIN), F32)
        total = None
        for a in range(CQ):
            padded = jnp.concatenate([zeros, parts[a][start : start + size]], axis=0)
            if a:
                padded = pltpu.roll(padded, size + 8 - a, 0)
            total = padded if total is None else total + padded
        return total

    d_query, d_keys = score_part(pl.ds(0, TRUNK), TRUNK, path_rows(qkv_ref, None, 0, k0))
    dqx_ref[0:200] = shifted_sum(d_query, 0, TRUNK)
    dk_ref[0:TRUNK] = d_keys[0:TRUNK]

    def fam_scores(b, carry):
        ext = 200 + 120 * b
        for c in range(2):
            rows, size = fam_rows(b, c)
            d_query, d_keys = score_part(rows, size, path_rows(qkv_ref, b, c, k0))
            add_keys(dk_ref, b, c, d_keys)
            if c == 0:
                dqx_ref[pl.ds(pl.multiple_of(ext, 8), 40)] = shifted_sum(d_query, 0, SEG)
                dqx_ref[pl.ds(pl.multiple_of(ext + 40, 8), 40)] = shifted_sum(d_query, SEG, SEG)
            else:
                dqx_ref[pl.ds(pl.multiple_of(ext + 80, 8), 40)] = shifted_sum(d_query, 0, SEG)
        return carry

    lax.fori_loop(0, 4, fam_scores, 0)
    for b in range(4):
        ext = 200 + 120 * b
        dqx_ref[192:200] += dqx_ref[ext : ext + 8]
        dqx_ref[ext + 32 : ext + 40] += dqx_ref[ext + 40 : ext + 48] + dqx_ref[ext + 80 : ext + 88]

    def put(token, size, column, value):
        old = dqkv_ref[token : token + size, pl.ds(column, WIN)].astype(F32)
        dqkv_ref[token : token + size, pl.ds(column, WIN)] = jnp.where(from_first, value, old).astype(BF16)

    for token, size, _, ext, _ in SEGS:
        put(token, size, w0, dqx_ref[ext + 8 : ext + 8 + size])
        put(token, size, k0, dk_ref[token : token + size])
        put(token, size, v0, dv_ref[token : token + size])


def by_tree(shape, last):
    return pl.BlockSpec(shape, lambda t, g: (t,) + (0,) * last)


def by_group(shape):
    tail = (0,) * (len(shape) - 2)
    return pl.BlockSpec((None, None) + shape[2:], lambda t, g: (t, g) + tail)


def common_specs():
    return [
        pl.BlockSpec(memory_space=pltpu.SMEM),
        pl.BlockSpec((TREE, 1152), lambda t, g: (t, 0)),
        pl.BlockSpec((None, 2, CQ * WIN, WIN), lambda t, g: (g, 0, 0, 0)),
        pl.BlockSpec((8, 384), lambda t, g: (0, 0)),
        pl.BlockSpec((None, 16, WIN), lambda t, g: (t, 0, 0)),
    ]


PARAMS = dict(vmem_limit_bytes=60 * 1024 * 1024, dimension_semantics=("arbitrary", "arbitrary"))


def saved_shapes(trees):
    return [(trees, 2, 2, TREE, WIN), (trees, 2, 2, TREE, CQ * WIN), (trees, 2, 2, CQ, TREE, WIN), (trees, 2, TREE, WIN)]


def attention_forward(mix, qkv, toeplitz, gains, jj):
    trees = qkv.shape[0] // TREE
    shapes = saved_shapes(trees)
    kinds = (F32, BF16, BF16, F32)
    return pl.pallas_call(
        fwd_kernel,
        grid=(trees, 2),
        in_specs=common_specs(),
        out_specs=[pl.BlockSpec((TREE, 384), lambda t, g: (t, 0))] + [by_group(s) for s in shapes],
        out_shape=[jax.ShapeDtypeStruct((trees * TREE, 384), BF16)] + [jax.ShapeDtypeStruct(s, k) for s, k in zip(shapes, kinds)],
        scratch_shapes=[pltpu.VMEM((TREE, WIN), jnp.int32), pltpu.VMEM((EXT, WIN), F32), pltpu.VMEM((2, TREE, WIN), BF16)],
        compiler_params=pltpu.CompilerParams(**PARAMS),
        cost_estimate=pl.CostEstimate(flops=40_000_000_000, bytes_accessed=60_000_000, transcendentals=0),
    )(mix, qkv, toeplitz, gains, jj)


def attention_backward(mix, qkv, toeplitz, gains, jj, d_normed, saved):
    trees = qkv.shape[0] // TREE
    shapes = saved_shapes(trees)
    return pl.pallas_call(
        bwd_kernel,
        grid=(trees, 2),
        in_specs=common_specs() + [pl.BlockSpec((TREE, 384), lambda t, g: (t, 0))] + [by_group(s) for s in shapes],
        out_specs=[
            pl.BlockSpec((TREE, 1152), lambda t, g: (t, 0)),
            pl.BlockSpec((8, 384), lambda t, g: (0, 0)),
            by_group((trees, 2, 8, WIN)),
            by_group((trees, 2, 2, 8, WIN)),
        ],
        out_shape=[
            jax.ShapeDtypeStruct((trees * TREE, 1152), BF16),
            jax.ShapeDtypeStruct((8, 384), F32),
            jax.ShapeDtypeStruct((trees, 2, 8, WIN), F32),
            jax.ShapeDtypeStruct((trees, 2, 2, 8, WIN), F32),
        ],
        scratch_shapes=[
            pltpu.VMEM((TREE, WIN), jnp.int32),
            pltpu.VMEM((2, TREE, WIN), BF16),
            pltpu.VMEM((2, TREE, WIN), BF16),
            pltpu.VMEM((2, TREE, WIN), F32),
            pltpu.VMEM((2, TREE, WIN), BF16),
            pltpu.VMEM((2, CQ, TREE, WIN), BF16),
            pltpu.VMEM((EXT, WIN), F32),
            pltpu.VMEM((TREE, WIN), F32),
            pltpu.VMEM((TREE, WIN), F32),
        ],
        compiler_params=pltpu.CompilerParams(**PARAMS),
        cost_estimate=pl.CostEstimate(flops=80_000_000_000, bytes_accessed=60_000_000, transcendentals=0),
    )(mix, qkv, toeplitz, gains, jj, d_normed, *saved)


def toeplitz_of(conv_w):
    heads = conv_w.shape[0]
    offset = lax.broadcasted_iota(jnp.int32, (WIN, WIN), 1) - lax.broadcasted_iota(jnp.int32, (WIN, WIN), 0) + CK // 2
    total = jnp.zeros((heads, CQ, WIN, WIN), F32)
    for b in range(CK):
        total = total + jnp.where(offset == b, 1.0, 0.0) * (conv_w[:, :, b] * (1.0 / math.sqrt(HD)))[:, :, None, None]
    return total.astype(BF16).reshape(heads // 2, 2, CQ * WIN, WIN)


def key_positions(valid):
    trees = valid.shape[0] // TREE
    valid = valid.reshape(trees, TREE)
    far = jnp.int32(1 << 20)

    def places(part, start):
        return jnp.where(part > 0, lax.broadcasted_iota(jnp.int32, part.shape, 1) + start, far)

    trunk = places(valid[:, :TRUNK], 0)
    empty = jnp.full((trees, SEG), far, jnp.int32)
    rows = [jnp.concatenate([trunk, empty, empty], axis=1)]
    for b in range(4):
        branch = places(valid[:, TRUNK + SEG * b : TRUNK + SEG * (b + 1)], TRUNK)
        rows.append(jnp.concatenate([trunk, branch, empty], axis=1))
        for c in range(2):
            first = 320 + 64 * b + SEG * c
            leaf = places(valid[:, first : first + SEG], TRUNK + SEG)
            rows.append(jnp.concatenate([trunk, branch, leaf], axis=1))
    rows += [jnp.zeros((trees, WIN), jnp.int32)] * 3
    return jnp.stack(rows, axis=1)


def conv_grads(gconv):
    lanes = gconv[..., :CQ, 18:29][..., ::-1] * (1.0 / math.sqrt(HD))
    return jnp.sum(lanes, axis=0).reshape(-1, CQ, CK)


def mix_grads(gmix):
    return jnp.sum(gmix[:, :, :4], axis=(0, 3)).reshape(-1, 2, 2)


MESH = pl.DeviceIdType.MESH

GATHERS = ((0, 0, 0), (1, 0, 1), (2, 0, 2), (3, 1, 0), (4, 2, 0), (5, 2, 1), (6, 3, 0))


def greet(peers):
    sem = pltpu.get_barrier_semaphore()
    for peer in peers:
        pl.semaphore_signal(sem, inc=1, device_id=peer, device_id_type=MESH)
    pl.semaphore_wait(sem, len(peers))


class Gather:
    def __init__(self, items, weights, firsts, seconds, send, recv, local, held):
        self.held = held
        self.items, self.weights, self.firsts, self.seconds = items, weights, firsts, seconds
        self.send, self.recv, self.local = send, recv, local
        q, c, z = lax.axis_index("plane"), lax.axis_index("core"), lax.axis_index("tensor")
        self.home = (z // 2) == c
        self.q = q
        self.far = (q, 1 - c, (z + 2) % 4)
        self.near = (q, c, (z // 2) * 2 + (1 - z % 2))
        self.by_x = ((q // 2) * 2 + (1 - q % 2), c, z)
        self.by_y = ((q + 2) % 4, c, z)

    def barrier(self):
        greet((self.near, self.far, self.by_x, self.by_y))

    def whole(self, item, side):
        _, out, part = self.items[item]
        ref = (self.firsts, self.seconds)[side][out]
        width = self.weights[item].shape[1]
        return ref, pl.ds(part * width, width)

    def z_copy(self, item, side, relay=False):
        rows = self.weights[item].shape[0] // 4
        mine = pl.ds(pl.multiple_of(self.q * rows, 128), rows)
        ref, cols = self.whole(item, side)
        source = self.whole(item, 0)[0].at[mine, cols] if relay else self.weights[item].at[mine]
        return pltpu.make_async_remote_copy(
            src_ref=source, dst_ref=ref.at[mine, cols], send_sem=self.send.at[item, side],
            recv_sem=self.recv.at[item, side], device_id=(self.far, self.near)[side], device_id_type=MESH)

    def plane_copy(self, item, side, step, receiving=False):
        ref, cols = self.whole(item, side)
        rows = ref.shape[0] // 4
        if step < 2:
            owner, first, size = self.q, 0, rows
        elif step == 2:
            owner, first, size = self.by_x[0], 0, rows // 2
        else:
            owner, first, size = self.by_y[0], rows // 2, rows // 2
        span = pl.ds(pl.multiple_of(owner * rows + first, 64), size)
        slot = 2 + 4 * side + step
        return pltpu.make_async_remote_copy(
            src_ref=ref.at[span, cols], dst_ref=ref.at[span, cols], send_sem=self.send.at[item, slot], recv_sem=self.recv.at[item, slot],
            device_id=(self.by_x, self.by_y, self.by_y, self.by_x)[step], device_id_type=MESH)

    def own_load(self, item):
        return pltpu.make_async_copy(self.weights[item], self.held[item], self.local.at[item, 0])

    def own_store(self, item):
        ref, cols = self.whole(item, 0)
        return pltpu.make_async_copy(self.held[item], ref.at[:, cols], self.local.at[item, 1])

    def each(self, action):
        action(1)

        @pl.when(jnp.logical_not(self.home))
        def _():
            action(0)

    def start_z(self, item):
        @pl.when(self.home)
        def _():
            self.z_copy(item, 1).start()

        @pl.when(jnp.logical_not(self.home))
        def _():
            self.z_copy(item, 0).start()

    def relay_z(self, item):
        @pl.when(jnp.logical_not(self.home))
        def _():
            self.z_copy(item, 0).wait_recv()
            self.z_copy(item, 1, True).start()
            self.plane_copy(item, 0, 0).start()
            self.plane_copy(item, 0, 1).start()

    def own(self, item):
        @pl.when(self.home)
        def _():
            self.own_load(item).start()

    def pass_own(self, item):
        @pl.when(self.home)
        def _():
            self.own_load(item).wait()
            self.own_store(item).start()

    def wait_own(self, item):
        @pl.when(self.home)
        def _():
            self.own_store(item).wait()

    def start_plane(self, item):
        self.z_copy(item, 1).wait_recv()
        self.plane_copy(item, 1, 0).start()
        self.plane_copy(item, 1, 1).start()

    def forward(self, item):
        def act(side):
            self.plane_copy(item, side, 0).wait_recv()
            self.plane_copy(item, side, 2).start()
            self.plane_copy(item, side, 1).wait_recv()
            self.plane_copy(item, side, 3).start()

        self.each(act)

    def finish(self, item):
        def act(side):
            self.plane_copy(item, side, 2).wait_recv()
            self.plane_copy(item, side, 3).wait_recv()
            self.z_copy(item, side).wait_send()
            for step in range(4):
                self.plane_copy(item, side, step).wait_send()

        self.each(act)
        self.wait_own(item)


def gather_kernel(items, weights, outs, send, recv, local, *held, ahead=3):
    count = len(items)
    half = len(outs) // 2
    work = Gather(items, weights, outs[:half], outs[half:], send, recv, local, held)
    for item in range(count):
        work.own(item)
    work.barrier()
    for item in range(min(ahead, count)):
        work.start_z(item)
    for step in range(count + 1):
        if step < count:
            work.relay_z(step)
            if step + ahead < count:
                work.start_z(step + ahead)
            work.start_plane(step)
            work.pass_own(step)
        if step >= 1:
            work.forward(step - 1)
    for item in range(count):
        work.finish(item)


def gather_weights(weights, items, widths, collective_id):
    depth = weights[0].shape[0]
    count = len(items)

    def kernel(*refs):
        gather_kernel(items, refs[:count], refs[count : count + 2 * len(widths)], *refs[count + 2 * len(widths) :])

    shapes = [jax.ShapeDtypeStruct((depth, w), BF16) for w in widths] * 2
    outs = pl.pallas_call(
        kernel,
        in_specs=[pl.BlockSpec(memory_space=pl.ANY)] * count,
        out_specs=[pl.BlockSpec(memory_space=pl.ANY)] * len(shapes),
        out_shape=shapes,
        scratch_shapes=[pltpu.SemaphoreType.DMA((count, 10)), pltpu.SemaphoreType.DMA((count, 10)), pltpu.SemaphoreType.DMA((count, 2))]
        + [pltpu.VMEM(w.shape, BF16) for w in weights],
        compiler_params=pltpu.CompilerParams(collective_id=collective_id, has_side_effects=True, vmem_limit_bytes=60 * 1024 * 1024),
    )(*weights)
    return [(outs[i], outs[len(widths) + i]) for i in range(len(widths))]


class Finish:
    def __init__(self, plan, parts, raw, outs, small, bufs):
        q, c, z = lax.axis_index("plane"), lax.axis_index("core"), lax.axis_index("tensor")
        self.q, self.c = q, c
        self.home = (z // 2) == c
        self.by_x = ((q // 2) * 2 + (1 - q % 2), c, z)
        self.by_y = ((q + 2) % 4, c, z)
        self.core = (q, 1 - c, z)
        self.near = (q, c, (z // 2) * 2 + (1 - z % 2))
        self.far = (q, 1 - c, (z + 2) % 4)
        self.across = (q, c, (z + 2) % 4)
        self.plan, self.parts, self.raw, self.outs, self.small = plan, parts, raw, outs, small
        (self.near_buf, self.far_buf, self.core_buf, self.here_buf, self.total_buf, self.raw_part, self.raw_own, self.raw_first,
         self.raw_second, self.small_buf, self.small_in, self.send, self.recv, self.raw_send, self.raw_recv, self.small_send,
         self.small_recv, self.local) = bufs

    def remote(self, src, dst, sems, index, peer):
        return pltpu.make_async_remote_copy(
            src_ref=src, dst_ref=dst, send_sem=sems[0].at[index], recv_sem=sems[1].at[index], device_id=peer, device_id_type=MESH)

    def columns(self, item):
        _, first_a, first_b, size, _, _, at = self.plan[item]
        return pl.ds(first_a, size), pl.ds(first_b, size), pl.ds(at, size)

    def part(self, item):
        source = self.plan[item][0]
        return self.raw_part if source < 0 else self.parts[source]

    def away(self, action):
        pl.when(jnp.logical_not(self.home))(action)

    def raw_copies(self, item):
        cols_a, cols_b, _ = self.columns(item)
        sems = (self.raw_send, self.raw_recv)

        def rows(owner):
            return pl.ds(pl.multiple_of(owner * 384, 128), 384)

        across = 3 - self.q
        x, y = self.by_x[0], self.by_y[0]
        return [
            self.remote(self.raw.at[rows(x), cols_a], self.raw_first.at[0, :, cols_a], sems, (item, 0), self.by_x),
            self.remote(self.raw.at[rows(across), cols_a], self.raw_first.at[1, :, cols_a], sems, (item, 1), self.by_x),
            self.remote(self.raw.at[rows(y), cols_b], self.raw_first.at[0, :, cols_b], sems, (item, 2), self.by_y),
            self.remote(self.raw.at[rows(across), cols_b], self.raw_first.at[1, :, cols_b], sems, (item, 3), self.by_y),
        ], [
            pltpu.make_async_copy(self.raw.at[rows(self.q), cols_a], self.raw_own.at[0, :, cols_a], self.local.at[item, 0]),
            pltpu.make_async_copy(self.raw.at[rows(y), cols_a], self.raw_own.at[1, :, cols_a], self.local.at[item, 1]),
            pltpu.make_async_copy(self.raw.at[rows(self.q), cols_b], self.raw_own.at[0, :, cols_b], self.local.at[item, 2]),
            pltpu.make_async_copy(self.raw.at[rows(x), cols_b], self.raw_own.at[1, :, cols_b], self.local.at[item, 3]),
        ]

    def raw_second_copies(self, item):
        cols_a, cols_b, _ = self.columns(item)
        sems = (self.raw_send, self.raw_recv)
        return [
            self.remote(self.raw_own.at[1, :, cols_a], self.raw_second.at[:, cols_a], sems, (item, 4), self.by_y),
            self.remote(self.raw_own.at[1, :, cols_b], self.raw_second.at[:, cols_b], sems, (item, 5), self.by_x),
        ]

    def r1(self, item):
        for group in self.raw_copies(item):
            for copy in group:
                copy.start()

    def r2(self, item):
        remote, own = self.raw_copies(item)
        for copy in own:
            copy.wait()
        for side, cols in enumerate(self.columns(item)[:2]):
            remote[2 * side + 1].wait_recv()
            self.raw_own[1, :, cols] = added(self.raw_own[1, :, cols], self.raw_first[1, :, cols])
            self.raw_second_copies(item)[side].start()

    def r3(self, item):
        remote, _ = self.raw_copies(item)
        for side, cols in enumerate(self.columns(item)[:2]):
            remote[2 * side].wait_recv()
            self.raw_second_copies(item)[side].wait_recv()
            total = self.raw_own[0, :, cols].astype(F32) + self.raw_first[0, :, cols].astype(F32) + self.raw_second[:, cols].astype(F32)
            self.raw_part[:, cols] = total.astype(BF16)

    def near_copy(self, item):
        _, cols_b, at = self.columns(item)
        return self.remote(self.part(item).at[:, cols_b], self.near_buf.at[:, self.spot(item)], (self.send, self.recv), (item, 0), self.near)

    def spot(self, item):
        return pl.ds(self.plan[item][5], self.plan[item][3])

    def far_copy(self, item):
        spot = self.spot(item)
        return self.remote(self.here_buf.at[:, spot], self.far_buf.at[:, spot], (self.send, self.recv), (item, 1), self.far)

    def core_copy(self, item, relayed):
        spot = self.spot(item)
        source = self.far_buf if relayed else self.here_buf
        return self.remote(source.at[:, spot], self.core_buf.at[:, spot], (self.send, self.recv), (item, 2), self.core)

    def s1(self, item):
        self.near_copy(item).start()

    def s2(self, item):
        spot, cols_a = self.spot(item), self.columns(item)[0]
        self.near_copy(item).wait_recv()
        self.here_buf[:, spot] = added(self.part(item)[:, cols_a], self.near_buf[:, spot])

        @pl.when(self.home)
        def _():
            self.core_copy(item, False).start()

        @self.away
        def _():
            self.far_copy(item).start()

    def s3(self, item):
        @self.away
        def _():
            self.far_copy(item).wait_recv()
            self.core_copy(item, True).start()

    def plane_copies(self, item):
        out = self.outs[self.plan[item][4]]
        at, spot = self.columns(item)[2], self.spot(item)
        sems = (self.send, self.recv)
        half = self.c * 192

        def rows(owner, first, size):
            return pl.ds(pl.multiple_of(owner * 384 + half + first, 32), size)

        mine = self.total_buf.at[pl.ds(pl.multiple_of(half, 32), 192), spot]
        x, y, across = self.by_x[0], self.by_y[0], 3 - self.q
        own = out.at[rows(self.q, 0, 192), at]
        top, low = out.at[rows(x, 0, 96), at], out.at[rows(y, 96, 96), at]
        return [
            self.remote(mine, own, sems, (item, 3), self.by_x),
            self.remote(mine, own, sems, (item, 4), self.by_y),
            self.remote(top, top, sems, (item, 5), self.by_y),
            self.remote(low, low, sems, (item, 6), self.by_x),
        ] + [
            self.remote(out.at[rows(o, 0, 192), at], out.at[rows(o, 0, 192), at], sems, (item, 7 + i), self.core)
            for i, o in enumerate((x, y, across))
        ]

    def own_copy(self, item):
        out = self.outs[self.plan[item][4]]
        rows = pl.ds(pl.multiple_of(self.q * 384, 128), 384)
        return pltpu.make_async_copy(self.total_buf.at[:, self.spot(item)], out.at[rows, self.columns(item)[2]], self.local.at[item, 4])

    def s4(self, item):
        spot = self.spot(item)

        @pl.when(self.home)
        def _():
            self.core_copy(item, False).wait_recv()
            self.total_buf[:, spot] = added(self.here_buf[:, spot], self.core_buf[:, spot])

        @self.away
        def _():
            self.core_copy(item, True).wait_recv()
            self.total_buf[:, spot] = added(self.far_buf[:, spot], self.core_buf[:, spot])

        self.own_copy(item).start()
        copies = self.plane_copies(item)
        copies[0].start()
        copies[1].start()

    def s5(self, item):
        copies = self.plane_copies(item)
        copies[0].wait_recv()
        copies[2].start()
        copies[4].start()
        copies[1].wait_recv()
        copies[3].start()
        copies[5].start()

    def s6(self, item):
        copies = self.plane_copies(item)
        copies[2].wait_recv()
        copies[3].wait_recv()
        copies[6].start()

    def s7(self, item):
        copies = self.plane_copies(item)
        self.own_copy(item).wait()
        for copy in copies[4:]:
            copy.wait_recv()
        for copy in copies:
            copy.wait_send()
        self.near_copy(item).wait_send()

        @pl.when(self.home)
        def _():
            self.core_copy(item, False).wait_send()

        @self.away
        def _():
            self.core_copy(item, True).wait_send()
            self.far_copy(item).wait_send()

        if self.plan[item][0] < 0:
            for copy in self.raw_copies(item)[0] + self.raw_second_copies(item):
                copy.wait_send()

    def small_copy(self, turn):
        peer = (self.core, self.by_x, self.by_y, self.near, self.across)[turn]
        return self.remote(self.small_buf.at[turn], self.small_in.at[turn], (self.small_send, self.small_recv), turn, peer)

    def small_start(self):
        self.small_buf[0] = self.small[...]
        self.small_copy(0).start()

    def small_next(self, turn):
        self.small_copy(turn).wait_recv()
        self.small_buf[turn + 1] = self.small_buf[turn] + self.small_in[turn]
        if turn < 4:
            self.small_copy(turn + 1).start()

    def small_done(self, out):
        for turn in range(5):
            self.small_copy(turn).wait_send()
        out[...] = self.small_buf[5]


def added(left, right):
    return (left.astype(F32) + right.astype(F32)).astype(BF16)


FINISH = (
    (0, 0, 1024, 1024, 0, 0, 0),
    (1, 0, 2048, 1024, 1, 1024, 0),
    (1, 1024, 3072, 1024, 1, 2048, 1024),
    (2, 0, 384, 384, 2, 3072, 0),
    (-1, 0, 1152, 384, 3, 3456, 0),
    (-1, 384, 1536, 384, 3, 3840, 384),
    (-1, 768, 1920, 384, 3, 4224, 768),
)


def finish_kernel(small, down, gu, out, raw, small_out, o_down, o_gu, o_out, o_qkv, *bufs):
    work = Finish(FINISH, (down, gu, out), raw, (o_down, o_gu, o_out, o_qkv), small, bufs)
    greet((work.near, work.far, work.by_x, work.by_y, work.core, work.across))
    for item in (4, 5, 6):
        work.r1(item)
    work.s1(0)
    work.s1(1)
    work.small_start()
    script = (
        ("s2", 0), ("s1", 2), ("r2", 4), ("s3", 0), ("m", 0),
        ("s2", 1), ("s1", 3), ("r2", 5), ("s4", 0), ("s3", 1), ("m", 1),
        ("r2", 6), ("s2", 2), ("r3", 4), ("s1", 4), ("s5", 0), ("s4", 1), ("s3", 2), ("m", 2),
        ("r3", 5), ("s1", 5), ("s2", 3), ("r3", 6), ("s1", 6), ("s6", 0), ("s5", 1), ("s4", 2), ("s3", 3), ("m", 3),
        ("s2", 4), ("s6", 1), ("s5", 2), ("s4", 3), ("s3", 4), ("m", 4),
        ("s2", 5), ("s6", 2), ("s5", 3), ("s4", 4), ("s3", 5),
        ("s2", 6), ("s6", 3), ("s5", 4), ("s4", 5), ("s3", 6),
        ("s6", 4), ("s5", 5), ("s4", 6), ("s6", 5), ("s5", 6), ("s6", 6),
    )
    for name, item in script:
        (work.small_next if name == "m" else getattr(work, name))(item)
    for item in range(len(FINISH)):
        work.s7(item)
    work.small_done(small_out)


def finish_gradients(small, down, gu, out, raw, collective_id):
    vmem = pl.BlockSpec(memory_space=pltpu.VMEM)
    anywhere = pl.BlockSpec(memory_space=pl.ANY)
    rows, width, count = 384, 4608, len(FINISH)
    wide = (rows, width)
    return pl.pallas_call(
        finish_kernel,
        in_specs=[vmem] * 4 + [anywhere],
        out_specs=[vmem] + [anywhere] * 4,
        out_shape=[jax.ShapeDtypeStruct(small.shape, F32)] + [jax.ShapeDtypeStruct((1536, n), BF16) for n in (1024, 2048, 384, 1152)],
        scratch_shapes=[pltpu.VMEM(wide, BF16)] * 5
        + [pltpu.VMEM((rows, 2304), BF16)]
        + [pltpu.VMEM((2, rows, 2304), BF16)] * 2
        + [pltpu.VMEM((rows, 2304), BF16)]
        + [pltpu.VMEM((6,) + small.shape, F32), pltpu.VMEM((5,) + small.shape, F32)]
        + [pltpu.SemaphoreType.DMA((count, 10))] * 2
        + [pltpu.SemaphoreType.DMA((count, 6))] * 2
        + [pltpu.SemaphoreType.DMA((5,))] * 2
        + [pltpu.SemaphoreType.DMA((count, 5))],
        compiler_params=pltpu.CompilerParams(collective_id=collective_id, has_side_effects=True, vmem_limit_bytes=60 * 1024 * 1024),
    )(small, down, gu, out, raw)


def rows_dot(lhs, rhs):
    return tn(lhs, rhs).astype(BF16)


def make_local(planes, tensors):
    every = ("plane", "core", "tensor")
    sides = [(c, z) for c in range(2) for z in range(tensors)]

    def spot(q, c, z):
        return (q * 2 + c) * tensors + z

    def is_home(c, z):
        return z // 2 == c

    far_pairs = [(spot(q, c, z), spot(q, 1 - c, z ^ 2)) for q in range(planes) for c, z in sides if not is_home(c, z)]
    near_pairs = [
        (spot(q, c, z), spot(q, c, z ^ 1) if is_home(c, z) else spot(q, 1 - c, z ^ 3)) for q in range(planes) for c, z in sides
    ]

    def over_core(value):
        return lax.ppermute(value, "core", [(0, 1), (1, 0)])

    def first_from(value):
        return lax.ppermute(value, every, far_pairs)

    def second_from(value):
        return lax.ppermute(value, every, near_pairs)

    square = planes == 4

    def local(
        tokens, teacher, valid_mask, norm1_gain, w_query, w_key, w_value, conv_weight, head_mix, gn_gain, w_out, norm2_gain,
        w_gate, w_up, w_down,
    ):
        q, c, z = lax.axis_index("plane"), lax.axis_index("core"), lax.axis_index("tensor")
        own_rows, width = tokens.shape
        home = (z // 2) == c
        heads = conv_weight.shape[0]
        wide = w_query.shape[1]

        def collect_all(weights):
            groups = ((0, 1, 2), (3,), (4, 5), (6,))
            if square and tensors == 4:
                widths = [sum(weights[i].shape[1] for i in group) for group in groups]
                return gather_weights(weights, GATHERS, widths, 1)
            pairs = []
            for group in groups:
                whole = jnp.concatenate([weights[i] for i in group], axis=1)
                pairs.append((jnp.where(home, whole, first_from(whole)), second_from(whole)))
            return pairs

        fused = square and tensors == 4

        def plane_sum(grads):
            return lax.psum_scatter(grads, "plane", scatter_dimension=0, tiled=True)

        def reduce(part):
            count = part.shape[1] // 2
            first, second = part[:, :count], part[:, count:]
            here = added(first, lax.ppermute(second, "tensor", [(i, i ^ 1) for i in range(tensors)]))
            here = jnp.where(home, here, first_from(here))
            total = added(here, over_core(here))
            return lax.all_gather(total, "plane", axis=0, tiled=True)

        small = jnp.concatenate([conv_weight.reshape(-1), head_mix.reshape(-1), gn_gain.reshape(-1)])
        small_first = jnp.where(home, small, first_from(small))
        small_second = second_from(small)
        conv_size, mix_size = conv_weight.size, head_mix.size

        gain_one, gain_two = norm1_gain, norm2_gain
        own_valid = lax.dynamic_slice_in_dim(valid_mask, z * own_rows, own_rows, 0)
        jj = key_positions(jnp.concatenate([own_valid, over_core(own_valid)]))

        qkv_weights, out_weights, gu_weights, down_weights = collect_all([w_query, w_key, w_value, w_out, w_gate, w_up, w_down])

        def with_partner(value):
            return jnp.concatenate([value, over_core(value)], axis=0)

        def summed(lefts, rights):
            def half(rows):
                total = nt(lefts[0][rows], rights[0])
                return total + nt(lefts[1][rows], rights[1])

            sent = over_core(half(slice(own_rows, None)).astype(BF16))
            return half(slice(0, own_rows)) + sent.astype(F32)

        inputs = tokens.astype(F32)
        inv_one = lax.rsqrt(jnp.mean(inputs * inputs, axis=-1, keepdims=True) + 1e-06)
        normed_one = with_partner((inputs * inv_one * gain_one).astype(BF16))
        sides_small = []
        for vec in (small_first, small_second):
            conv = vec[:conv_size].reshape(conv_weight.shape)
            mix = vec[conv_size : conv_size + mix_size]
            gains = jnp.broadcast_to(vec[conv_size + mix_size :][None], (8, wide))
            sides_small.append((mix, toeplitz_of(conv), gains))
        qkv, heads_out, saved = [], [], []
        for (mix, toep, gains), weight in zip(sides_small, qkv_weights):
            projected = nn(normed_one, weight).astype(BF16)
            result = attention_forward(mix, projected, toep, gains, jj)
            qkv.append(projected)
            heads_out.append(result[0])
            saved.append(result[1:])
        hidden_in = inputs + summed(heads_out, out_weights)
        inv_two = lax.rsqrt(jnp.mean(hidden_in * hidden_in, axis=-1, keepdims=True) + 1e-06)
        normed_two = with_partner((hidden_in * inv_two * gain_two).astype(BF16))
        units = w_gate.shape[1]
        gates, ups, hiddens = [], [], []
        for weight in gu_weights:
            both = nn(normed_two, weight)
            gate, up = both[:, :units], both[:, units:]
            gates.append(gate.astype(BF16))
            ups.append(up.astype(BF16))
            hiddens.append((jax.nn.silu(gate) * up).astype(BF16))
        final_rows = hidden_in + summed(hiddens, down_weights)
        output = final_rows.astype(BF16)
        own_mask = own_valid.astype(F32)
        error = own_mask[:, None] * (final_rows - teacher.astype(F32))
        squared_sum = jnp.sum(error * error)
        count_sum = jnp.sum(own_mask)

        d_all = with_partner(error.astype(BF16))
        down_grads = rows_dot(d_all, jnp.concatenate(hiddens, axis=1))
        down_grads, d_all = lax.optimization_barrier((down_grads, d_all))
        down_part = plane_sum(down_grads)
        d_gus = []
        for index, weight in enumerate(down_weights):
            d_hidden = nn(d_all, weight)
            gate, up = gates[index].astype(F32), ups[index].astype(F32)
            s = jax.nn.sigmoid(gate)
            d_gate = (d_hidden * up * s * (1.0 + gate * (1.0 - s))).astype(BF16)
            d_up = (d_hidden * gate * s).astype(BF16)
            d_gus.append(jnp.concatenate([d_gate, d_up], axis=1))
        gu_grads = rows_dot(normed_two, jnp.concatenate(d_gus, axis=1))
        gu_grads, d_gus = lax.optimization_barrier((gu_grads, d_gus))
        gu_part = plane_sum(gu_grads)
        d_normed_two = summed(d_gus, gu_weights)
        scaled_two = d_normed_two * gain_two
        grad_gain_two = jnp.sum(d_normed_two * hidden_in * inv_two, axis=0)
        d_hidden_in = (
            error + inv_two * scaled_two - hidden_in * inv_two**3 * jnp.mean(scaled_two * hidden_in, axis=-1, keepdims=True)
        )
        d_attn = with_partner(d_hidden_in.astype(BF16))
        out_grads = rows_dot(d_attn, jnp.concatenate(heads_out, axis=1))
        out_grads, d_attn = lax.optimization_barrier((out_grads, d_attn))
        out_part = plane_sum(out_grads)
        d_qkv, small_grads = [], []
        for index, (mix, toep, gains) in enumerate(sides_small):
            d_normed = nn(d_attn, out_weights[index])
            if index == 0:
                d_normed, down_part = lax.optimization_barrier((d_normed, down_part))
            else:
                d_normed, gu_part = lax.optimization_barrier((d_normed, gu_part))
            dqkv, ggn, gmix, gconv = attention_backward(mix, qkv[index], toep, gains, jj, d_normed, saved[index])
            d_qkv.append(dqkv)
            small_grads.append(jnp.concatenate([conv_grads(gconv).reshape(-1), mix_grads(gmix).reshape(-1), ggn[0]]))
        qkv_grads = rows_dot(normed_one, jnp.concatenate(d_qkv, axis=1))
        d_normed_one = summed(d_qkv, qkv_weights)
        scaled_one = d_normed_one * gain_one
        grad_gain_one = jnp.sum(d_normed_one * inputs * inv_one, axis=0)
        grad_input = (
            d_hidden_in + inv_one * scaled_one - inputs * inv_one**3 * jnp.mean(scaled_one * inputs, axis=-1, keepdims=True)
        )

        table = jnp.zeros((tensors, small.size), F32)
        table = lax.dynamic_update_slice(table, small_grads[0][None], (2 * c + z % 2, 0))
        table = lax.dynamic_update_slice(table, small_grads[1][None], (2 * c + 1 - z % 2, 0))
        packed = jnp.concatenate(
            [table.reshape(-1), grad_gain_one, grad_gain_two, squared_sum[None], count_sum[None]]
        )
        if fused:
            length = packed.size
            lines = -(-length // 1024) * 8
            packed = jnp.pad(packed, (0, lines * 128 - length)).reshape(lines, 128)
            packed, *sums = finish_gradients(packed, down_part, gu_part, out_part, qkv_grads, 2)
            packed = packed.reshape(-1)[:length]
        else:
            packed = lax.psum(packed, every)
            sums = [reduce(part) for part in (down_part, gu_part, out_part, plane_sum(qkv_grads))]
        grad_down, grad_gu, grad_out, grad_qkv = [value.astype(F32) for value in sums]
        table_size = tensors * small.size
        small_sum = lax.dynamic_slice_in_dim(packed, z * small.size, small.size, 0)
        gain_slice = width // tensors
        gain_one_out = lax.dynamic_slice_in_dim(packed, table_size + z * gain_slice, gain_slice, 0)
        gain_two_out = lax.dynamic_slice_in_dim(packed, table_size + width + z * gain_slice, gain_slice, 0)
        loss = packed[-2] / (packed[-1] * width)
        return (
            output,
            loss,
            grad_input,
            gain_one_out,
            grad_qkv[:, :wide],
            grad_qkv[:, wide : 2 * wide],
            grad_qkv[:, 2 * wide :],
            small_sum[:conv_size].reshape(conv_weight.shape),
            small_sum[conv_size : conv_size + mix_size].reshape(head_mix.shape),
            small_sum[conv_size + mix_size :].reshape(gn_gain.shape),
            grad_out,
            gain_two_out,
            grad_gu[:, :units],
            grad_gu[:, units:],
            grad_down,
        )

    return local


def solution(mesh):
    tensors = mesh.shape["tensor"]
    planes = mesh.shape["dp"] // 2
    inner = jax.sharding.Mesh(mesh.devices.reshape(planes, 2, tensors), ("plane", "core", "tensor"))
    rows = P(("plane", "core", "tensor"), None)
    columns = P(None, "tensor")
    cube = P("tensor", None, None)
    return jax.shard_map(
        make_local(planes, tensors),
        mesh=inner,
        in_specs=(
            rows, rows, P(("plane", "core")), P(), columns, columns, columns, cube, cube, P("tensor", None), columns, P(),
            columns, columns, columns,
        ),
        out_specs=(
            rows, P(), rows, P("tensor"), columns, columns, columns, cube, cube, P("tensor", None), columns, P("tensor"),
            columns, columns, columns,
        ),
        check_vma=False,
    )
```

```python
import math
import jax
import jax.numpy as jnp
from jax import lax
from jax.experimental import pallas as pl
from jax.experimental.pallas import tpu as pltpu
from jax.sharding import PartitionSpec as P

HD = 96
CQ = 6
CK = 11
TRUNK = 192
SEG = 32
TREE = 576
WIN = 256
FAM = 96
EXT = 680
F32 = jnp.float32
BF16 = jnp.bfloat16


def segments():
    rows = [(0, TRUNK, 0, 0, -1)]
    for b in range(4):
        base, ext = TRUNK + FAM * b, 200 + 120 * b
        rows.append((TRUNK + SEG * b, SEG, base, ext, TRUNK - 8))
        for c in range(2):
            rows.append((320 + 64 * b + SEG * c, SEG, base + SEG * (c + 1), ext + 40 * (c + 1), TRUNK + SEG * b + SEG - 8))
    return rows


SEGS = segments()


def nn(a, b):
    return lax.dot_general(a, b, (((1,), (0,)), ((), ())), preferred_element_type=F32)


def nt(a, b):
    return lax.dot_general(a, b, (((1,), (1,)), ((), ())), preferred_element_type=F32)


def tn(a, b):
    return lax.dot_general(a, b, (((0,), (0,)), ((), ())), preferred_element_type=F32)


def head_masks(g):
    lane = lax.broadcasted_iota(jnp.int32, (1, WIN), 1)
    first = 64 * g
    m0 = (lane >= first) & (lane < first + HD)
    m1 = (lane >= first + HD) & (lane < first + 2 * HD)
    return m0, m1, lane >= first


def fill_distance(jj_ref, dist_ref):
    for index, (_, size, row, _, _) in enumerate(SEGS):
        start = 0 if index == 0 else (TRUNK if (index - 1) % 3 == 0 else TRUNK + SEG)
        pos = lax.broadcasted_iota(jnp.int32, (size, WIN), 0) + start
        dist_ref[row : row + size] = pos - jj_ref[index : index + 1, :]


def path_rows(ref, b, c, column):
    if b is None:
        parts = [ref[0:TRUNK, pl.ds(column, WIN)], ref[TRUNK : TRUNK + SEG, pl.ds(column, WIN)], ref[320 : 320 + SEG, pl.ds(column, WIN)]]
    else:
        parts = [
            ref[0:TRUNK, pl.ds(column, WIN)],
            ref[pl.ds(pl.multiple_of(TRUNK + SEG * b, SEG), SEG), pl.ds(column, WIN)],
            ref[pl.ds(pl.multiple_of(320 + 64 * b + SEG * c, SEG), SEG), pl.ds(column, WIN)],
        ]
    return jnp.concatenate(parts, axis=0)


def fam_rows(b, c):
    base = TRUNK + FAM * b
    return (pl.ds(pl.multiple_of(base, 32), 64), 64) if c == 0 else (pl.ds(pl.multiple_of(base + 64, 32), SEG), SEG)


def group_norm(ho, m0, m1):
    def stat(v):
        s0 = jnp.sum(jnp.where(m0, v, 0.0), axis=-1, keepdims=True) * (1.0 / HD)
        s1 = jnp.sum(jnp.where(m1, v, 0.0), axis=-1, keepdims=True) * (1.0 / HD)
        return jnp.where(m0, s0, s1)

    centered = jnp.where(m0 | m1, ho - stat(ho), 0.0)
    inv = lax.rsqrt(stat(centered * centered) + 1e-05)
    return centered * inv, inv, stat


def fwd_kernel(hook, mix_ref, qkv_ref, t_ref, gn_ref, jj_ref, nh_ref, att_ref, pre_ref, qs_ref, ho_ref, dist_ref, qx_ref, mx_ref):
    side, t, g = pl.program_id(0), pl.program_id(1), pl.program_id(2)
    step = (side * 2 + t) * 2 + g
    mix0 = 8 * side + 4 * g
    hook(step, 0)
    w0 = pl.multiple_of(g * 128, 128)
    m0, m1, from_first = head_masks(g)
    m0f, m1f = m0.astype(F32), m1.astype(F32)
    fill_distance(jj_ref, dist_ref)
    qx_ref[0:8] = jnp.zeros((8, WIN), F32)
    for token, size, _, ext, parent in SEGS:
        if parent >= 0:
            low = qkv_ref[parent - 8 : parent + 8, pl.ds(w0, WIN)].astype(F32)
            qx_ref[ext : ext + 8] = low[8:16]
        qx_ref[ext + 8 : ext + 8 + size] = qkv_ref[token : token + size, pl.ds(w0, WIN)].astype(F32)
    for a in range(CQ):
        for _, size, row, ext, _ in SEGS:
            part = qx_ref[ext + 8 - a : ext + 8 - a + size]
            qs_ref[0, a, row : row + size] = (part * m0f).astype(BF16)
            qs_ref[1, a, row : row + size] = (part * m1f).astype(BF16)
    k0, v0 = w0 + 384, w0 + 768
    k_trunk = path_rows(qkv_ref, None, 0, k0)

    def trunk_scores(a, carry):
        scores = nt(qs_ref[:, a, 0:TRUNK].reshape(2 * TRUNK, WIN), k_trunk).reshape(2, TRUNK, WIN)
        kept = dist_ref[0:TRUNK] >= a
        for e in range(2):
            pre_ref[e, 0:TRUNK, pl.ds(pl.multiple_of(a * WIN, WIN), WIN)] = jnp.where(kept, scores[e], 0.0).astype(BF16)
        return carry

    lax.fori_loop(0, CQ, trunk_scores, 0)

    def fam_scores(b, carry):
        for c in range(2):
            rows, size = fam_rows(b, c)
            keys = path_rows(qkv_ref, b, c, k0)
            scores = nt(qs_ref[:, :, rows].reshape(2 * CQ * size, WIN), keys).reshape(2, CQ, size, WIN)
            dist = dist_ref[rows]
            for a in range(CQ):
                kept = dist >= a
                for e in range(2):
                    pre_ref[e, rows, a * WIN : (a + 1) * WIN] = jnp.where(kept, scores[e, a], 0.0).astype(BF16)
        return carry

    lax.fori_loop(0, 4, fam_scores, 0)
    hook(step, 1)
    for e in range(2):
        conv = nn(pre_ref[e], t_ref[e])
        logits = jnp.where(dist_ref[...] >= 0, conv, -1e30)
        shifted = jnp.exp(logits - jnp.max(logits, axis=-1, keepdims=True))
        att_ref[e] = shifted / jnp.sum(shifted, axis=-1, keepdims=True)
    for c in range(2):
        mx_ref[c] = (mix_ref[mix0 + 2 * c] * att_ref[0] + mix_ref[mix0 + 2 * c + 1] * att_ref[1]).astype(BF16)

    def put_out(rows, size, values):
        out = nn(mx_ref[:, rows].reshape(2 * size, WIN), values).reshape(2, size, WIN)
        ho_ref[rows] = jnp.where(m0, out[0], jnp.where(m1, out[1], 0.0))

    put_out(pl.ds(0, TRUNK), TRUNK, path_rows(qkv_ref, None, 0, v0))

    def fam_out(b, carry):
        for c in range(2):
            rows, size = fam_rows(b, c)
            put_out(rows, size, path_rows(qkv_ref, b, c, v0))
        return carry

    lax.fori_loop(0, 4, fam_out, 0)
    gain = gn_ref[0:1, pl.ds(w0, WIN)]
    for token, size, row, _, _ in SEGS:
        unit, _, _ = group_norm(ho_ref[row : row + size], m0, m1)
        old = nh_ref[token : token + size, pl.ds(w0, WIN)].astype(F32)
        nh_ref[token : token + size, pl.ds(w0, WIN)] = jnp.where(from_first, unit * gain, old).astype(BF16)
    hook(step, 2)


def bwd_kernel(
    mix_ref, qkv_ref, t_ref, gn_ref, jj_ref, dn_ref, att_ref, pre_ref, qs_ref, ho_ref,
    dqkv_ref, ggn_ref, gmix_ref, gconv_ref,
    dist_ref, dh_ref, mx_ref, dm_ref, dc_ref, es_ref, dqx_ref, dk_ref, dv_ref,
):
    side, t, g = pl.program_id(0), pl.program_id(1), pl.program_id(2)
    mix0 = 8 * side + 4 * g
    w0 = pl.multiple_of(g * 128, 128)
    m0, m1, from_first = head_masks(g)
    both = m0 | m1
    fill_distance(jj_ref, dist_ref)
    gain = gn_ref[0:1, pl.ds(w0, WIN)]
    gn_sum = jnp.zeros((1, WIN), F32)
    for token, size, row, _, _ in SEGS:
        unit, inv, stat = group_norm(ho_ref[row : row + size], m0, m1)
        dn = jnp.where(both, dn_ref[token : token + size, pl.ds(w0, WIN)].astype(F32), 0.0)
        gn_sum = gn_sum + jnp.sum(dn * unit, axis=0, keepdims=True)
        scaled = dn * gain
        d_head = inv * (scaled - stat(scaled) - unit * stat(scaled * unit))
        dh_ref[0, row : row + size] = jnp.where(m0, d_head, 0.0).astype(BF16)
        dh_ref[1, row : row + size] = jnp.where(m1, d_head, 0.0).astype(BF16)

    @pl.when((t == 0) & (g == 0))
    def _():
        ggn_ref[...] = jnp.zeros_like(ggn_ref)

    ggn_ref[0:1, pl.ds(w0, WIN)] += gn_sum
    k0, v0 = w0 + 384, w0 + 768
    for c in range(2):
        mx_ref[c] = (mix_ref[mix0 + 2 * c] * att_ref[0] + mix_ref[mix0 + 2 * c + 1] * att_ref[1]).astype(BF16)

    def add_keys(acc_ref, b, c, grads):
        acc_ref[0:TRUNK] += grads[0:TRUNK]
        branch = pl.ds(pl.multiple_of(TRUNK + SEG * b, SEG), SEG)
        if c == 0:
            acc_ref[branch] = grads[TRUNK : TRUNK + SEG]
        else:
            acc_ref[branch] += grads[TRUNK : TRUNK + SEG]
        acc_ref[pl.ds(pl.multiple_of(320 + 64 * b + SEG * c, SEG), SEG)] = grads[TRUNK + SEG :]

    def value_part(rows, size, values):
        heads = dh_ref[:, rows].reshape(2 * size, WIN)
        dm_ref[:, rows] = nt(heads, values).reshape(2, size, WIN)
        return tn(mx_ref[:, rows].reshape(2 * size, WIN), heads)

    dv_ref[0:TRUNK] = value_part(pl.ds(0, TRUNK), TRUNK, path_rows(qkv_ref, None, 0, v0))[0:TRUNK]

    def fam_values(b, carry):
        for c in range(2):
            rows, size = fam_rows(b, c)
            add_keys(dv_ref, b, c, value_part(rows, size, path_rows(qkv_ref, b, c, v0)))
        return carry

    lax.fori_loop(0, 4, fam_values, 0)

    def soft_part(block, sums):
        rows = pl.ds(pl.multiple_of(block * FAM, 32), FAM)
        dm = [dm_ref[c, rows] for c in range(2)]
        att = [att_ref[e, rows] for e in range(2)]
        out = []
        for e in range(2):
            d_att = mix_ref[mix0 + e] * dm[0] + mix_ref[mix0 + 2 + e] * dm[1]
            d_conv = att[e] * (d_att - jnp.sum(d_att * att[e], axis=-1, keepdims=True))
            dc_ref[e, rows] = d_conv.astype(BF16)
        for c in range(2):
            for e in range(2):
                out.append(sums[2 * c + e] + jnp.sum(dm[c] * att[e], axis=0, keepdims=True))
        return tuple(out)

    mix_sums = lax.fori_loop(0, 6, soft_part, tuple(jnp.zeros((1, WIN), F32) for _ in range(4)))
    gmix_ref[...] = jnp.zeros_like(gmix_ref)
    gconv_ref[...] = jnp.zeros_like(gconv_ref)
    for index in range(4):
        gmix_ref[index : index + 1] = mix_sums[index]
    mirror = lax.broadcasted_iota(jnp.int32, (WIN, WIN), 0) + lax.broadcasted_iota(jnp.int32, (WIN, WIN), 1) - (WIN - 1)
    band = jnp.abs(mirror) <= CK // 2
    flip = jnp.where(mirror == 0, 1.0, 0.0).astype(BF16)
    for e in range(2):
        flipped = nn(dc_ref[e], flip).astype(BF16)
        for a in range(CQ):
            cols = slice(a * WIN, (a + 1) * WIN)
            products = jnp.where(band, tn(flipped, pre_ref[e, :, cols]), 0.0)
            rolled = pltpu.roll(products, 24, 1, stride=1, stride_axis=0)
            gconv_ref[e, a : a + 1] = jnp.sum(rolled, axis=0, keepdims=True)
            grads = nt(dc_ref[e], t_ref[e, cols, :])
            es_ref[e, a] = jnp.where(dist_ref[...] >= a, grads, 0.0).astype(BF16)

    def score_part(rows, size, keys):
        grads = es_ref[:, :, rows].reshape(2 * CQ * size, WIN)
        back = nn(grads, keys).reshape(2, CQ, size, WIN)
        d_query = [jnp.where(m0, back[0, a], jnp.where(m1, back[1, a], 0.0)) for a in range(CQ)]
        return d_query, tn(grads, qs_ref[:, :, rows].reshape(2 * CQ * size, WIN))

    def shifted_sum(parts, start, size):
        zeros = jnp.zeros((8, WIN), F32)
        total = None
        for a in range(CQ):
            padded = jnp.concatenate([zeros, parts[a][start : start + size]], axis=0)
            if a:
                padded = pltpu.roll(padded, size + 8 - a, 0)
            total = padded if total is None else total + padded
        return total

    d_query, d_keys = score_part(pl.ds(0, TRUNK), TRUNK, path_rows(qkv_ref, None, 0, k0))
    dqx_ref[0:200] = shifted_sum(d_query, 0, TRUNK)
    dk_ref[0:TRUNK] = d_keys[0:TRUNK]

    def fam_scores(b, carry):
        ext = 200 + 120 * b
        for c in range(2):
            rows, size = fam_rows(b, c)
            d_query, d_keys = score_part(rows, size, path_rows(qkv_ref, b, c, k0))
            add_keys(dk_ref, b, c, d_keys)
            if c == 0:
                dqx_ref[pl.ds(pl.multiple_of(ext, 8), 40)] = shifted_sum(d_query, 0, SEG)
                dqx_ref[pl.ds(pl.multiple_of(ext + 40, 8), 40)] = shifted_sum(d_query, SEG, SEG)
            else:
                dqx_ref[pl.ds(pl.multiple_of(ext + 80, 8), 40)] = shifted_sum(d_query, 0, SEG)
        return carry

    lax.fori_loop(0, 4, fam_scores, 0)
    for b in range(4):
        ext = 200 + 120 * b
        dqx_ref[192:200] += dqx_ref[ext : ext + 8]
        dqx_ref[ext + 32 : ext + 40] += dqx_ref[ext + 40 : ext + 48] + dqx_ref[ext + 80 : ext + 88]

    def put(token, size, column, value):
        old = dqkv_ref[token : token + size, pl.ds(column, WIN)].astype(F32)
        dqkv_ref[token : token + size, pl.ds(column, WIN)] = jnp.where(from_first, value, old).astype(BF16)

    for token, size, _, ext, _ in SEGS:
        put(token, size, w0, dqx_ref[ext + 8 : ext + 8 + size])
        put(token, size, k0, dk_ref[token : token + size])
        put(token, size, v0, dv_ref[token : token + size])


def by_group(shape):
    tail = (0,) * (len(shape) - 3)
    return pl.BlockSpec((None, None, None) + shape[3:], lambda s, t, g: (s, t, g) + tail)


def by_side(shape):
    return pl.BlockSpec((None,) + shape, lambda s, t, g: (s, 0, 0))


def common_specs():
    return [
        pl.BlockSpec(memory_space=pltpu.SMEM),
        pl.BlockSpec((TREE, 1152), lambda s, t, g: (t, s)),
        pl.BlockSpec((None, None, 2, CQ * WIN, WIN), lambda s, t, g: (s, g, 0, 0, 0)),
        by_side((8, 384)),
        pl.BlockSpec((None, 16, WIN), lambda s, t, g: (t, 0, 0)),
    ]


PARAMS = dict(vmem_limit_bytes=60 * 1024 * 1024, dimension_semantics=("arbitrary",) * 3)


def saved_shapes(trees):
    lead = (2, trees, 2)
    return [lead + (2, TREE, WIN), lead + (2, TREE, CQ * WIN), lead + (2, CQ, TREE, WIN), lead + (TREE, WIN)]


def attention_forward(mix, qkv, toeplitz, gains, jj, gather=None):
    trees = qkv.shape[0] // TREE
    shapes = saved_shapes(trees)
    kinds = (F32, BF16, BF16, F32)
    weights, wide, count, collective = gather if gather else ((), (), 0, {})
    many, held = len(weights), len(wide)

    def kernel(*refs):
        inputs, loads, refs = refs[:5], refs[5 : 5 + many], refs[5 + many :]
        outs, full, refs = refs[:5], refs[5 : 5 + held], refs[5 + held :]
        work = Gather(LATER, loads, full, *refs[3:]) if gather else None

        def hook(step, place):
            if work:
                background(work, step, place)

        fwd_kernel(hook, *inputs, *outs, *refs[:3])

    anywhere = pl.BlockSpec(memory_space=pl.ANY)
    result = pl.pallas_call(
        kernel,
        grid=(2, trees, 2),
        in_specs=common_specs() + [anywhere] * many,
        out_specs=[pl.BlockSpec((TREE, 384), lambda s, t, g: (t, s))] + [by_group(s) for s in shapes] + [anywhere] * held,
        out_shape=[jax.ShapeDtypeStruct((trees * TREE, 768), BF16)]
        + [jax.ShapeDtypeStruct(s, k) for s, k in zip(shapes, kinds)]
        + [jax.ShapeDtypeStruct((1536, w), BF16) for w in wide],
        scratch_shapes=[pltpu.VMEM((TREE, WIN), jnp.int32), pltpu.VMEM((EXT, WIN), F32), pltpu.VMEM((2, TREE, WIN), BF16)]
        + gather_scratch(weights, count),
        compiler_params=pltpu.CompilerParams(**PARAMS, **collective),
        cost_estimate=pl.CostEstimate(flops=80_000_000_000, bytes_accessed=120_000_000, transcendentals=0),
    )(mix, qkv, toeplitz, gains, jj, *weights)
    return result[0], result[1:5], result[5:]


def attention_backward(mix, qkv, toeplitz, gains, jj, d_normed, saved):
    trees = qkv.shape[0] // TREE
    shapes = saved_shapes(trees)
    return pl.pallas_call(
        bwd_kernel,
        grid=(2, trees, 2),
        in_specs=common_specs() + [pl.BlockSpec((TREE, 384), lambda s, t, g: (t, s))] + [by_group(s) for s in shapes],
        out_specs=[
            pl.BlockSpec((TREE, 1152), lambda s, t, g: (t, s)),
            by_side((8, 384)),
            by_group((2, trees, 2, 8, WIN)),
            by_group((2, trees, 2, 2, 8, WIN)),
        ],
        out_shape=[
            jax.ShapeDtypeStruct((trees * TREE, 2304), BF16),
            jax.ShapeDtypeStruct((2, 8, 384), F32),
            jax.ShapeDtypeStruct((2, trees, 2, 8, WIN), F32),
            jax.ShapeDtypeStruct((2, trees, 2, 2, 8, WIN), F32),
        ],
        scratch_shapes=[
            pltpu.VMEM((TREE, WIN), jnp.int32),
            pltpu.VMEM((2, TREE, WIN), BF16),
            pltpu.VMEM((2, TREE, WIN), BF16),
            pltpu.VMEM((2, TREE, WIN), F32),
            pltpu.VMEM((2, TREE, WIN), BF16),
            pltpu.VMEM((2, CQ, TREE, WIN), BF16),
            pltpu.VMEM((EXT, WIN), F32),
            pltpu.VMEM((TREE, WIN), F32),
            pltpu.VMEM((TREE, WIN), F32),
        ],
        compiler_params=pltpu.CompilerParams(**PARAMS),
        cost_estimate=pl.CostEstimate(flops=160_000_000_000, bytes_accessed=120_000_000, transcendentals=0),
    )(mix, qkv, toeplitz, gains, jj, d_normed, *saved)


def band_rows(conv_w):
    rows = conv_w.reshape(-1, CK) * (1.0 / math.sqrt(HD))
    middle = jnp.zeros((rows.shape[0], WIN - CK), F32)
    return jnp.concatenate([rows[:, CK // 2 :], middle, rows[:, : CK // 2]], axis=1)


def fill_toeplitz(rows_ref, side, out_ref):
    offset = lax.broadcasted_iota(jnp.int32, (WIN, WIN), 1) - lax.broadcasted_iota(jnp.int32, (WIN, WIN), 0)
    band = jnp.abs(offset) <= CK // 2
    for head in range(4):
        for a in range(CQ):
            row = rows_ref[side, head * CQ + a : head * CQ + a + 1, :]
            rolled = pltpu.roll(jnp.broadcast_to(row, (WIN, WIN)), 0, 1, stride=1, stride_axis=0)
            out_ref[side, head // 2, head % 2, a * WIN : (a + 1) * WIN, :] = jnp.where(band, rolled, 0.0).astype(BF16)


def key_positions(valid):
    trees = valid.shape[0] // TREE
    valid = valid.reshape(trees, TREE)
    far = jnp.int32(1 << 20)

    def places(part, start):
        return jnp.where(part > 0, lax.broadcasted_iota(jnp.int32, part.shape, 1) + start, far)

    trunk = places(valid[:, :TRUNK], 0)
    empty = jnp.full((trees, SEG), far, jnp.int32)
    rows = [jnp.concatenate([trunk, empty, empty], axis=1)]
    for b in range(4):
        branch = places(valid[:, TRUNK + SEG * b : TRUNK + SEG * (b + 1)], TRUNK)
        rows.append(jnp.concatenate([trunk, branch, empty], axis=1))
        for c in range(2):
            first = 320 + 64 * b + SEG * c
            leaf = places(valid[:, first : first + SEG], TRUNK + SEG)
            rows.append(jnp.concatenate([trunk, branch, leaf], axis=1))
    rows += [jnp.zeros((trees, WIN), jnp.int32)] * 3
    return jnp.stack(rows, axis=1)


def conv_grads(gconv):
    lanes = gconv[..., :CQ, 18:29][..., ::-1] * (1.0 / math.sqrt(HD))
    return jnp.sum(lanes, axis=1).reshape(2, -1)


def mix_grads(gmix):
    return jnp.sum(gmix[:, :, :, :4], axis=(1, 4)).reshape(2, -1)


MESH = pl.DeviceIdType.MESH

FIRST = ((0, 0, 0, 0, 1152, 384), (1, 0, 0, 384, 1536, 384), (2, 0, 0, 768, 1920, 384))
LATER = (
    (0, 0, 0, 0, 384, 384),
    (1, 1, 0, 0, 1024, 512),
    (1, 1, 512, 512, 1536, 512),
    (2, 1, 0, 2048, 3072, 512),
    (2, 1, 512, 2560, 3584, 512),
    (3, 2, 0, 0, 1024, 512),
    (3, 2, 512, 512, 1536, 512),
)


def greet(peers):
    sem = pltpu.get_barrier_semaphore()
    for peer in peers:
        pl.semaphore_signal(sem, inc=1, device_id=peer, device_id_type=MESH)
    pl.semaphore_wait(sem, len(peers))


class Gather:
    def __init__(self, items, weights, fulls, send, recv, local, *held):
        self.items, self.weights, self.fulls, self.held = items, weights, fulls, held
        self.send, self.recv, self.local = send, recv, local
        q, c, z = lax.axis_index("plane"), lax.axis_index("core"), lax.axis_index("tensor")
        self.home = (z // 2) == c
        self.q = q
        self.core = (q, 1 - c, z)
        self.far = (q, 1 - c, (z + 2) % 4)
        self.near = (q, c, (z // 2) * 2 + (1 - z % 2))
        self.by_x = ((q // 2) * 2 + (1 - q % 2), c, z)
        self.by_y = ((q + 2) % 4, c, z)

    def away(self, action):
        pl.when(jnp.logical_not(self.home))(action)

    def whole(self, item, side):
        _, out, _, first, second, size = self.items[item]
        return self.fulls[out], pl.ds((first, second)[side], size)

    def z_copy(self, item, side, relay=False):
        weight, _, source_col, _, _, size = self.items[item]
        mine = pl.ds(pl.multiple_of(self.q * 384, 128), 384)
        ref, cols = self.whole(item, side)
        source = ref.at[mine, self.whole(item, 0)[1]] if relay else self.weights[weight].at[mine, pl.ds(source_col, size)]
        return pltpu.make_async_remote_copy(
            src_ref=source, dst_ref=ref.at[mine, cols], send_sem=self.send.at[item, side],
            recv_sem=self.recv.at[item, side], device_id=(self.far, self.near)[side], device_id_type=MESH)

    def plane_copy(self, item, side, step):
        ref, cols = self.whole(item, side)
        if step < 2:
            owner, first, size = self.q, 0, 384
        elif step == 2:
            owner, first, size = self.by_x[0], 0, 192
        else:
            owner, first, size = self.by_y[0], 192, 192
        span = pl.ds(pl.multiple_of(owner * 384 + first, 64), size)
        slot = 2 + 4 * side + step
        return pltpu.make_async_remote_copy(
            src_ref=ref.at[span, cols], dst_ref=ref.at[span, cols], send_sem=self.send.at[item, slot], recv_sem=self.recv.at[item, slot],
            device_id=(self.by_x, self.by_y, self.by_y, self.by_x)[step], device_id_type=MESH)

    def own_load(self, weight):
        return pltpu.make_async_copy(self.weights[weight], self.held[weight], self.local.at[weight, 0])

    def own_stores(self, weight):
        copies = []
        for number, (index, out, source_col, first, _, size) in enumerate(self.items):
            if index == weight:
                source = self.held[weight].at[:, pl.ds(source_col, size)]
                copies.append(pltpu.make_async_copy(source, self.fulls[out].at[:, pl.ds(first, size)], self.local.at[number, 1]))
        return copies

    def own(self):
        @pl.when(self.home)
        def _():
            for weight in range(len(self.weights)):
                self.own_load(weight).start()

    def pass_own(self, weight):
        @pl.when(self.home)
        def _():
            self.own_load(weight).wait()
            for copy in self.own_stores(weight):
                copy.start()

    def wait_own(self):
        @pl.when(self.home)
        def _():
            for weight in range(len(self.weights)):
                for copy in self.own_stores(weight):
                    copy.wait()

    def each(self, action):
        action(1)

        @self.away
        def _():
            action(0)

    def start_z(self, item):
        @pl.when(self.home)
        def _():
            self.z_copy(item, 1).start()

        @self.away
        def _():
            self.z_copy(item, 0).start()

    def relay_z(self, item):
        @self.away
        def _():
            self.z_copy(item, 0).wait_recv()
            self.z_copy(item, 1, True).start()
            self.plane_copy(item, 0, 0).start()
            self.plane_copy(item, 0, 1).start()

    def start_plane(self, item):
        self.z_copy(item, 1).wait_recv()
        self.plane_copy(item, 1, 0).start()
        self.plane_copy(item, 1, 1).start()

    def forward(self, item):
        def act(side):
            self.plane_copy(item, side, 0).wait_recv()
            self.plane_copy(item, side, 2).start()
            self.plane_copy(item, side, 1).wait_recv()
            self.plane_copy(item, side, 3).start()

        self.each(act)

    def finish(self, item):
        def act(side):
            self.plane_copy(item, side, 2).wait_recv()
            self.plane_copy(item, side, 3).wait_recv()
            self.z_copy(item, side).wait_send()
            for step in range(4):
                self.plane_copy(item, side, step).wait_send()

        self.each(act)


def gather_scratch(weights, count):
    if not weights:
        return []
    return [pltpu.SemaphoreType.DMA((count, 10)), pltpu.SemaphoreType.DMA((count, 10)), pltpu.SemaphoreType.DMA((max(count, len(weights)), 2))] + [
        pltpu.VMEM(w.shape, BF16) for w in weights
    ]


AHEAD = 3


def background(work, step, place):
    count = len(work.items)
    if place == 2:

        @pl.when(step == 7)
        def _():
            work.forward(count - 1)
            for item in range(count):
                work.finish(item)
            work.wait_own()

        return

    for turn in range(8):
        slot = 2 * turn + place

        @pl.when(step == turn)
        def _(slot=slot):
            if slot == 0:
                work.own()
                greet((work.near, work.far, work.by_x, work.by_y))
                for item in range(AHEAD):
                    work.start_z(item)
            elif slot <= 2 * count:
                item = (slot - 1) // 2
                if slot % 2:
                    work.relay_z(item)
                    if item + AHEAD < count:
                        work.start_z(item + AHEAD)
                    if item < len(work.weights):
                        work.pass_own(item)
                else:
                    work.start_plane(item)
                    if item >= 1:
                        work.forward(item - 1)


def opening_kernel(tokens_ref, gain_ref, small_ref, wq_ref, wk_ref, wv_ref, full_ref, normed_ref, toep_ref, both_ref, send, recv, local, held0, held1, held2, extra_send, extra_recv):
    work = Gather(FIRST, (wq_ref, wk_ref, wv_ref), (full_ref,), send, recv, local, held0, held1, held2)
    rows = tokens_ref.shape[0]

    def extra(source, target, index, peer):
        return pltpu.make_async_remote_copy(
            src_ref=source, dst_ref=target, send_sem=extra_send.at[index], recv_sem=extra_recv.at[index], device_id=peer, device_id_type=MESH)

    far_small = extra(small_ref, both_ref.at[0], 0, work.far)
    near_small = extra(both_ref.at[0], both_ref.at[1], 1, work.near)
    normed_out = extra(normed_ref.at[0:rows], normed_ref.at[rows : 2 * rows], 2, work.core)
    work.own()
    greet((work.near, work.far, work.by_x, work.by_y, work.core))

    @work.away
    def _():
        far_small.start()

    @pl.when(work.home)
    def _():
        both_ref[0] = small_ref[...]
        near_small.start()

    for item in range(3):
        work.start_z(item)
    for start in range(0, rows, 96):
        x = tokens_ref[start : start + 96].astype(F32)
        inv = lax.rsqrt(jnp.mean(x * x, axis=-1, keepdims=True) + 1e-06)
        normed_ref[start : start + 96] = (x * inv * gain_ref[...]).astype(BF16)
    normed_out.start()

    @work.away
    def _():
        far_small.wait_recv()
        near_small.start()

    work.relay_z(0)
    work.start_plane(0)
    fill_toeplitz(both_ref, 0, toep_ref)
    work.relay_z(1)
    work.start_plane(1)
    work.forward(0)
    for weight in range(3):
        work.pass_own(weight)
    near_small.wait_recv()
    work.relay_z(2)
    work.start_plane(2)
    work.forward(1)
    fill_toeplitz(both_ref, 1, toep_ref)
    work.forward(2)
    for item in range(3):
        work.finish(item)
    work.wait_own()
    near_small.wait_send()

    @work.away
    def _():
        far_small.wait_send()

    normed_out.wait()


def opening(tokens, gain, small, weights, collective_id):
    vmem = pl.BlockSpec(memory_space=pltpu.VMEM)
    anywhere = pl.BlockSpec(memory_space=pl.ANY)
    rows, width = tokens.shape
    return pl.pallas_call(
        opening_kernel,
        in_specs=[vmem] * 3 + [anywhere] * 3,
        out_specs=[anywhere] + [vmem] * 3,
        out_shape=[
            jax.ShapeDtypeStruct((width, 2304), BF16),
            jax.ShapeDtypeStruct((2 * rows, width), BF16),
            jax.ShapeDtypeStruct((2, 2, 2, CQ * WIN, WIN), BF16),
            jax.ShapeDtypeStruct((2,) + small.shape, F32),
        ],
        scratch_shapes=gather_scratch(weights, 3) + [pltpu.SemaphoreType.DMA((3,)), pltpu.SemaphoreType.DMA((3,))],
        compiler_params=pltpu.CompilerParams(collective_id=collective_id, has_side_effects=True, vmem_limit_bytes=60 * 1024 * 1024),
    )(tokens, gain, small, *weights)


class Finish:
    def __init__(self, plan, parts, raw, outs, small, bufs):
        q, c, z = lax.axis_index("plane"), lax.axis_index("core"), lax.axis_index("tensor")
        self.q, self.c = q, c
        self.home = (z // 2) == c
        self.by_x = ((q // 2) * 2 + (1 - q % 2), c, z)
        self.by_y = ((q + 2) % 4, c, z)
        self.core = (q, 1 - c, z)
        self.near = (q, c, (z // 2) * 2 + (1 - z % 2))
        self.far = (q, 1 - c, (z + 2) % 4)
        self.across = (q, c, (z + 2) % 4)
        self.plan, self.parts, self.raw, self.outs, self.small = plan, parts, raw, outs, small
        (self.near_buf, self.far_buf, self.core_buf, self.here_buf, self.total_buf, self.raw_part, self.raw_own, self.raw_first,
         self.raw_second, self.small_buf, self.small_in, self.send, self.recv, self.raw_send, self.raw_recv, self.small_send,
         self.small_recv, self.local) = bufs

    def remote(self, src, dst, sems, index, peer):
        return pltpu.make_async_remote_copy(
            src_ref=src, dst_ref=dst, send_sem=sems[0].at[index], recv_sem=sems[1].at[index], device_id=peer, device_id_type=MESH)

    def columns(self, item):
        _, first_a, first_b, size, _, _, at = self.plan[item]
        return pl.ds(first_a, size), pl.ds(first_b, size), pl.ds(at, size)

    def part(self, item):
        source = self.plan[item][0]
        return self.raw_part if source < 0 else self.parts[source]

    def away(self, action):
        pl.when(jnp.logical_not(self.home))(action)

    def raw_copies(self, item):
        cols_a, cols_b, _ = self.columns(item)
        sems = (self.raw_send, self.raw_recv)

        def rows(owner):
            return pl.ds(pl.multiple_of(owner * 384, 128), 384)

        across = 3 - self.q
        x, y = self.by_x[0], self.by_y[0]
        return [
            self.remote(self.raw.at[rows(x), cols_a], self.raw_first.at[0, :, cols_a], sems, (item, 0), self.by_x),
            self.remote(self.raw.at[rows(across), cols_a], self.raw_first.at[1, :, cols_a], sems, (item, 1), self.by_x),
            self.remote(self.raw.at[rows(y), cols_b], self.raw_first.at[0, :, cols_b], sems, (item, 2), self.by_y),
            self.remote(self.raw.at[rows(across), cols_b], self.raw_first.at[1, :, cols_b], sems, (item, 3), self.by_y),
        ], [
            pltpu.make_async_copy(self.raw.at[rows(self.q), cols_a], self.raw_own.at[0, :, cols_a], self.local.at[item, 0]),
            pltpu.make_async_copy(self.raw.at[rows(y), cols_a], self.raw_own.at[1, :, cols_a], self.local.at[item, 1]),
            pltpu.make_async_copy(self.raw.at[rows(self.q), cols_b], self.raw_own.at[0, :, cols_b], self.local.at[item, 2]),
            pltpu.make_async_copy(self.raw.at[rows(x), cols_b], self.raw_own.at[1, :, cols_b], self.local.at[item, 3]),
        ]

    def raw_second_copies(self, item):
        cols_a, cols_b, _ = self.columns(item)
        sems = (self.raw_send, self.raw_recv)
        return [
            self.remote(self.raw_own.at[1, :, cols_a], self.raw_second.at[:, cols_a], sems, (item, 4), self.by_y),
            self.remote(self.raw_own.at[1, :, cols_b], self.raw_second.at[:, cols_b], sems, (item, 5), self.by_x),
        ]

    def r1(self, item):
        for group in self.raw_copies(item):
            for copy in group:
                copy.start()

    def r2(self, item):
        remote, own = self.raw_copies(item)
        for copy in own:
            copy.wait()
        for side, cols in enumerate(self.columns(item)[:2]):
            remote[2 * side + 1].wait_recv()
            self.raw_own[1, :, cols] = added(self.raw_own[1, :, cols], self.raw_first[1, :, cols])
            self.raw_second_copies(item)[side].start()

    def r3(self, item):
        remote, _ = self.raw_copies(item)
        for side, cols in enumerate(self.columns(item)[:2]):
            remote[2 * side].wait_recv()
            self.raw_second_copies(item)[side].wait_recv()
            total = self.raw_own[0, :, cols].astype(F32) + self.raw_first[0, :, cols].astype(F32) + self.raw_second[:, cols].astype(F32)
            self.raw_part[:, cols] = total.astype(BF16)

    def near_copy(self, item):
        _, cols_b, at = self.columns(item)
        return self.remote(self.part(item).at[:, cols_b], self.near_buf.at[:, self.spot(item)], (self.send, self.recv), (item, 0), self.near)

    def spot(self, item):
        return pl.ds(self.plan[item][5], self.plan[item][3])

    def far_copy(self, item):
        spot = self.spot(item)
        return self.remote(self.here_buf.at[:, spot], self.far_buf.at[:, spot], (self.send, self.recv), (item, 1), self.far)

    def core_copy(self, item, relayed):
        spot = self.spot(item)
        source = self.far_buf if relayed else self.here_buf
        return self.remote(source.at[:, spot], self.core_buf.at[:, spot], (self.send, self.recv), (item, 2), self.core)

    def s1(self, item):
        self.near_copy(item).start()

    def s2(self, item):
        spot, cols_a = self.spot(item), self.columns(item)[0]
        self.near_copy(item).wait_recv()
        self.here_buf[:, spot] = added(self.part(item)[:, cols_a], self.near_buf[:, spot])

        @pl.when(self.home)
        def _():
            self.core_copy(item, False).start()

        @self.away
        def _():
            self.far_copy(item).start()

    def s3(self, item):
        @self.away
        def _():
            self.far_copy(item).wait_recv()
            self.core_copy(item, True).start()

    def plane_copies(self, item):
        out = self.outs[self.plan[item][4]]
        at, spot = self.columns(item)[2], self.spot(item)
        sems = (self.send, self.recv)
        half = self.c * 192

        def rows(owner, first, size):
            return pl.ds(pl.multiple_of(owner * 384 + half + first, 32), size)

        mine = self.total_buf.at[pl.ds(pl.multiple_of(half, 32), 192), spot]
        x, y, across = self.by_x[0], self.by_y[0], 3 - self.q
        own = out.at[rows(self.q, 0, 192), at]
        top, low = out.at[rows(x, 0, 96), at], out.at[rows(y, 96, 96), at]
        return [
            self.remote(mine, own, sems, (item, 3), self.by_x),
            self.remote(mine, own, sems, (item, 4), self.by_y),
            self.remote(top, top, sems, (item, 5), self.by_y),
            self.remote(low, low, sems, (item, 6), self.by_x),
        ] + [
            self.remote(out.at[rows(o, 0, 192), at], out.at[rows(o, 0, 192), at], sems, (item, 7 + i), self.core)
            for i, o in enumerate((x, y, across))
        ]

    def own_copy(self, item):
        out = self.outs[self.plan[item][4]]
        rows = pl.ds(pl.multiple_of(self.q * 384, 128), 384)
        return pltpu.make_async_copy(self.total_buf.at[:, self.spot(item)], out.at[rows, self.columns(item)[2]], self.local.at[item, 4])

    def s4(self, item):
        spot = self.spot(item)

        @pl.when(self.home)
        def _():
            self.core_copy(item, False).wait_recv()
            self.total_buf[:, spot] = added(self.here_buf[:, spot], self.core_buf[:, spot])

        @self.away
        def _():
            self.core_copy(item, True).wait_recv()
            self.total_buf[:, spot] = added(self.far_buf[:, spot], self.core_buf[:, spot])

        self.own_copy(item).start()
        copies = self.plane_copies(item)
        copies[0].start()
        copies[1].start()

    def s5(self, item):
        copies = self.plane_copies(item)
        copies[0].wait_recv()
        copies[2].start()
        copies[4].start()
        copies[1].wait_recv()
        copies[3].start()
        copies[5].start()

    def s6(self, item):
        copies = self.plane_copies(item)
        copies[2].wait_recv()
        copies[3].wait_recv()
        copies[6].start()

    def s7(self, item):
        copies = self.plane_copies(item)
        self.own_copy(item).wait()
        for copy in copies[4:]:
            copy.wait_recv()
        for copy in copies:
            copy.wait_send()
        self.near_copy(item).wait_send()

        @pl.when(self.home)
        def _():
            self.core_copy(item, False).wait_send()

        @self.away
        def _():
            self.core_copy(item, True).wait_send()
            self.far_copy(item).wait_send()

        if self.plan[item][0] < 0:
            for copy in self.raw_copies(item)[0] + self.raw_second_copies(item):
                copy.wait_send()

    def small_copy(self, turn):
        peer = (self.core, self.by_x, self.by_y, self.near, self.across)[turn]
        return self.remote(self.small_buf.at[turn], self.small_in.at[turn], (self.small_send, self.small_recv), turn, peer)

    def small_start(self):
        self.small_buf[0] = self.small[...]
        self.small_copy(0).start()

    def small_next(self, turn):
        self.small_copy(turn).wait_recv()
        self.small_buf[turn + 1] = self.small_buf[turn] + self.small_in[turn]
        if turn < 4:
            self.small_copy(turn + 1).start()

    def small_done(self, out):
        for turn in range(5):
            self.small_copy(turn).wait_send()
        out[...] = self.small_buf[5]


def added(left, right):
    return (left.astype(F32) + right.astype(F32)).astype(BF16)


FINISH = (
    (0, 0, 1024, 1024, 0, 0, 0),
    (1, 0, 1024, 1024, 1, 1024, 0),
    (1, 2048, 3072, 1024, 1, 2048, 1024),
    (2, 0, 384, 384, 2, 3072, 0),
    (-1, 0, 1152, 384, 3, 3456, 0),
    (-1, 384, 1536, 384, 3, 3840, 384),
    (-1, 768, 1920, 384, 3, 4224, 768),
)


def finish_kernel(small, down, gu, out, raw, small_out, o_down, o_gu, o_out, o_qkv, *bufs):
    work = Finish(FINISH, (down, gu, out), raw, (o_down, o_gu, o_out, o_qkv), small, bufs)
    greet((work.near, work.far, work.by_x, work.by_y, work.core, work.across))
    for item in (4, 5, 6):
        work.r1(item)
    work.s1(0)
    work.s1(1)
    work.small_start()
    script = (
        ("s2", 0), ("s1", 2), ("r2", 4), ("s3", 0), ("m", 0),
        ("s2", 1), ("s1", 3), ("r2", 5), ("s4", 0), ("s3", 1), ("m", 1),
        ("r2", 6), ("s2", 2), ("r3", 4), ("s1", 4), ("s5", 0), ("s4", 1), ("s3", 2), ("m", 2),
        ("r3", 5), ("s1", 5), ("s2", 3), ("r3", 6), ("s1", 6), ("s6", 0), ("s5", 1), ("s4", 2), ("s3", 3), ("m", 3),
        ("s2", 4), ("s6", 1), ("s5", 2), ("s4", 3), ("s3", 4), ("m", 4),
        ("s2", 5), ("s6", 2), ("s5", 3), ("s4", 4), ("s3", 5),
        ("s2", 6), ("s6", 3), ("s5", 4), ("s4", 5), ("s3", 6),
        ("s6", 4), ("s5", 5), ("s4", 6), ("s6", 5), ("s5", 6), ("s6", 6),
    )
    for name, item in script:
        (work.small_next if name == "m" else getattr(work, name))(item)
    for item in range(len(FINISH)):
        work.s7(item)
    work.small_done(small_out)


def finish_gradients(small, down, gu, out, raw, collective_id):
    vmem = pl.BlockSpec(memory_space=pltpu.VMEM)
    anywhere = pl.BlockSpec(memory_space=pl.ANY)
    rows, width, count = 384, 4608, len(FINISH)
    wide = (rows, width)
    return pl.pallas_call(
        finish_kernel,
        in_specs=[vmem] * 4 + [anywhere],
        out_specs=[vmem] + [anywhere] * 4,
        out_shape=[jax.ShapeDtypeStruct(small.shape, F32)] + [jax.ShapeDtypeStruct((1536, n), BF16) for n in (1024, 2048, 384, 1152)],
        scratch_shapes=[pltpu.VMEM(wide, BF16)] * 5
        + [pltpu.VMEM((rows, 2304), BF16)]
        + [pltpu.VMEM((2, rows, 2304), BF16)] * 2
        + [pltpu.VMEM((rows, 2304), BF16)]
        + [pltpu.VMEM((6,) + small.shape, F32), pltpu.VMEM((5,) + small.shape, F32)]
        + [pltpu.SemaphoreType.DMA((count, 10))] * 2
        + [pltpu.SemaphoreType.DMA((count, 6))] * 2
        + [pltpu.SemaphoreType.DMA((5,))] * 2
        + [pltpu.SemaphoreType.DMA((count, 5))],
        compiler_params=pltpu.CompilerParams(collective_id=collective_id, has_side_effects=True, vmem_limit_bytes=60 * 1024 * 1024),
    )(small, down, gu, out, raw)


def rows_dot(lhs, rhs):
    return tn(lhs, rhs).astype(BF16)


def toeplitz_alone(both):
    def kernel(rows_ref, out_ref):
        fill_toeplitz(rows_ref, 0, out_ref)
        fill_toeplitz(rows_ref, 1, out_ref)

    return pl.pallas_call(
        kernel,
        out_shape=jax.ShapeDtypeStruct((2, 2, 2, CQ * WIN, WIN), BF16),
        compiler_params=pltpu.CompilerParams(vmem_limit_bytes=60 * 1024 * 1024),
    )(both)


def make_local(planes, tensors):
    every = ("plane", "core", "tensor")
    sides = [(c, z) for c in range(2) for z in range(tensors)]

    def spot(q, c, z):
        return (q * 2 + c) * tensors + z

    def is_home(c, z):
        return z // 2 == c

    far_pairs = [(spot(q, c, z), spot(q, 1 - c, z ^ 2)) for q in range(planes) for c, z in sides if not is_home(c, z)]
    near_pairs = [
        (spot(q, c, z), spot(q, c, z ^ 1) if is_home(c, z) else spot(q, 1 - c, z ^ 3)) for q in range(planes) for c, z in sides
    ]

    def over_core(value):
        return lax.ppermute(value, "core", [(0, 1), (1, 0)])

    def first_from(value):
        return lax.ppermute(value, every, far_pairs)

    def second_from(value):
        return lax.ppermute(value, every, near_pairs)

    square = planes == 4

    def local(
        tokens, teacher, valid_mask, norm1_gain, w_query, w_key, w_value, conv_weight, head_mix, gn_gain, w_out, norm2_gain,
        w_gate, w_up, w_down,
    ):
        q, c, z = lax.axis_index("plane"), lax.axis_index("core"), lax.axis_index("tensor")
        own_rows, width = tokens.shape
        home = (z // 2) == c
        wide = w_query.shape[1]

        def collect(weights):
            pairs = []
            for weight in weights:
                pairs.append(jnp.where(home, weight, first_from(weight)))
                pairs.append(second_from(weight))
            return pairs

        fused = square and tensors == 4

        def plane_sum(grads):
            return lax.psum_scatter(grads, "plane", scatter_dimension=0, tiled=True)

        def reduce(first, second):
            here = added(first, lax.ppermute(second, "tensor", [(i, i ^ 1) for i in range(tensors)]))
            here = jnp.where(home, here, first_from(here))
            total = added(here, over_core(here))
            return lax.all_gather(total, "plane", axis=0, tiled=True)

        small = jnp.concatenate(
            [
                band_rows(conv_weight),
                jnp.pad(head_mix.reshape(1, -1), ((0, 0), (0, WIN - head_mix.size))),
                jnp.pad(gn_gain.reshape(1, -1), ((0, 0), (0, 2 * WIN - wide))).reshape(2, WIN),
                jnp.zeros((5, WIN), F32),
            ]
        )
        conv_size, mix_size = conv_weight.size, head_mix.size
        small_size = conv_size + mix_size + wide
        gain_one, gain_two = norm1_gain, norm2_gain
        own_valid = lax.dynamic_slice_in_dim(valid_mask, z * own_rows, own_rows, 0)
        jj = key_positions(jnp.concatenate([own_valid, over_core(own_valid)]))

        def with_partner(value):
            return jnp.concatenate([value, over_core(value)], axis=0)

        def summed(left, right):
            sent = over_core(nt(left[own_rows:], right).astype(BF16))
            return nt(left[:own_rows], right) + sent.astype(F32)

        inputs = tokens.astype(F32)
        inv_one = lax.rsqrt(jnp.mean(inputs * inputs, axis=-1, keepdims=True) + 1e-06)
        if fused:
            qkv_weight, normed_one, toep, both_small = opening(tokens, gain_one[None], small, [w_query, w_key, w_value], 1)
            gather = ([w_out, w_gate, w_up, w_down], (768, 4096, 2048), len(LATER), dict(collective_id=3, has_side_effects=True))
        else:
            both_small = jnp.stack([jnp.where(home, small, first_from(small)), second_from(small)])
            toep = toeplitz_alone(both_small)
            normed_one = with_partner((inputs * inv_one * gain_one).astype(BF16))
            parts = collect([w_query, w_key, w_value])
            qkv_weight = jnp.concatenate(parts[0::2] + parts[1::2], axis=1)
            gather = None
        mix = both_small[:, 24, :mix_size].reshape(-1)
        gains = jnp.broadcast_to(both_small[:, 25:27].reshape(2, 1, 2 * WIN)[:, :, :wide], (2, 8, wide))
        qkv = nn(normed_one, qkv_weight).astype(BF16)
        heads_out, saved, later = attention_forward(mix, qkv, toep, gains, jj, gather)
        if fused:
            out_weight, gu_weight, down_weight = later
        else:
            out_weight = jnp.concatenate(collect([w_out]), axis=1)
            gu_weight = jnp.concatenate(collect([w_gate, w_up]), axis=1)
            down_weight = jnp.concatenate(collect([w_down]), axis=1)
        hidden_in = inputs + summed(heads_out, out_weight)
        inv_two = lax.rsqrt(jnp.mean(hidden_in * hidden_in, axis=-1, keepdims=True) + 1e-06)
        normed_two = with_partner((hidden_in * inv_two * gain_two).astype(BF16))
        units = w_gate.shape[1]
        both = nn(normed_two, gu_weight)
        gate, up = both[:, : 2 * units], both[:, 2 * units :]
        hidden = (jax.nn.silu(gate) * up).astype(BF16)
        gate, up = gate.astype(BF16), up.astype(BF16)
        final_rows = hidden_in + summed(hidden, down_weight)
        output = final_rows.astype(BF16)
        own_mask = own_valid.astype(F32)
        error = own_mask[:, None] * (final_rows - teacher.astype(F32))
        squared_sum = jnp.sum(error * error)
        count_sum = jnp.sum(own_mask)

        d_all = with_partner(error.astype(BF16))
        down_grads = rows_dot(d_all, hidden)
        down_grads, d_all = lax.optimization_barrier((down_grads, d_all))
        down_part = plane_sum(down_grads)
        d_hidden = nn(d_all, down_weight)
        gate, up = gate.astype(F32), up.astype(F32)
        s = jax.nn.sigmoid(gate)
        d_gate = (d_hidden * up * s * (1.0 + gate * (1.0 - s))).astype(BF16)
        d_up = (d_hidden * gate * s).astype(BF16)
        d_gu = jnp.concatenate([d_gate, d_up], axis=1)
        gu_grads = rows_dot(normed_two, d_gu)
        gu_grads, d_gu = lax.optimization_barrier((gu_grads, d_gu))
        gu_part = plane_sum(gu_grads)
        d_normed_two = summed(d_gu, gu_weight)
        scaled_two = d_normed_two * gain_two
        grad_gain_two = jnp.sum(d_normed_two * hidden_in * inv_two, axis=0)
        d_hidden_in = (
            error + inv_two * scaled_two - hidden_in * inv_two**3 * jnp.mean(scaled_two * hidden_in, axis=-1, keepdims=True)
        )
        d_attn = with_partner(d_hidden_in.astype(BF16))
        out_grads = rows_dot(d_attn, heads_out)
        out_grads, d_attn = lax.optimization_barrier((out_grads, d_attn))
        out_part = plane_sum(out_grads)
        d_normed = nn(d_attn, out_weight)
        d_normed, down_part = lax.optimization_barrier((d_normed, down_part))
        d_qkv, ggn, gmix, gconv = attention_backward(mix, qkv, toep, gains, jj, d_normed, saved)
        small_grads = jnp.concatenate([conv_grads(gconv), mix_grads(gmix), ggn[:, 0]], axis=1)
        qkv_grads = rows_dot(normed_one, d_qkv)
        d_normed_one = summed(d_qkv, qkv_weight)
        scaled_one = d_normed_one * gain_one
        grad_gain_one = jnp.sum(d_normed_one * inputs * inv_one, axis=0)
        grad_input = (
            d_hidden_in + inv_one * scaled_one - inputs * inv_one**3 * jnp.mean(scaled_one * inputs, axis=-1, keepdims=True)
        )

        table = jnp.zeros((tensors, small_size), F32)
        table = lax.dynamic_update_slice(table, small_grads[:1], (2 * c + z % 2, 0))
        table = lax.dynamic_update_slice(table, small_grads[1:], (2 * c + 1 - z % 2, 0))
        packed = jnp.concatenate(
            [table.reshape(-1), grad_gain_one, grad_gain_two, squared_sum[None], count_sum[None]]
        )
        if fused:
            length = packed.size
            lines = -(-length // 1024) * 8
            packed = jnp.pad(packed, (0, lines * 128 - length)).reshape(lines, 128)
            packed, *sums = finish_gradients(packed, down_part, gu_part, out_part, qkv_grads, 2)
            packed = packed.reshape(-1)[:length]
        else:
            packed = lax.psum(packed, every)
            qkv_part = plane_sum(qkv_grads)
            sums = [reduce(part[:, : part.shape[1] // 2], part[:, part.shape[1] // 2 :]) for part in (down_part, out_part, qkv_part)]
            places = [slice(i * units, (i + 1) * units) for i in range(4)]
            first, second = [jnp.concatenate([gu_part[:, places[i]], gu_part[:, places[i + 2]]], axis=1) for i in range(2)]
            sums.insert(1, reduce(first, second))
        grad_down, grad_gu, grad_out, grad_qkv = [value.astype(F32) for value in sums]
        table_size = tensors * small_size
        small_sum = lax.dynamic_slice_in_dim(packed, z * small_size, small_size, 0)
        gain_slice = width // tensors
        gain_one_out = lax.dynamic_slice_in_dim(packed, table_size + z * gain_slice, gain_slice, 0)
        gain_two_out = lax.dynamic_slice_in_dim(packed, table_size + width + z * gain_slice, gain_slice, 0)
        loss = packed[-2] / (packed[-1] * width)
        return (
            output,
            loss,
            grad_input,
            gain_one_out,
            grad_qkv[:, :wide],
            grad_qkv[:, wide : 2 * wide],
            grad_qkv[:, 2 * wide :],
            small_sum[:conv_size].reshape(conv_weight.shape),
            small_sum[conv_size : conv_size + mix_size].reshape(head_mix.shape),
            small_sum[conv_size + mix_size :].reshape(gn_gain.shape),
            grad_out,
            gain_two_out,
            grad_gu[:, :units],
            grad_gu[:, units:],
            grad_down,
        )

    return local


def solution(mesh):
    tensors = mesh.shape["tensor"]
    planes = mesh.shape["dp"] // 2
    inner = jax.sharding.Mesh(mesh.devices.reshape(planes, 2, tensors), ("plane", "core", "tensor"))
    rows = P(("plane", "core", "tensor"), None)
    columns = P(None, "tensor")
    cube = P("tensor", None, None)
    return jax.shard_map(
        make_local(planes, tensors),
        mesh=inner,
        in_specs=(
            rows, rows, P(("plane", "core")), P(), columns, columns, columns, cube, cube, P("tensor", None), columns, P(),
            columns, columns, columns,
        ),
        out_specs=(
            rows, P(), rows, P("tensor"), columns, columns, columns, cube, cube, P("tensor", None), columns, P("tensor"),
            columns, columns, columns,
        ),
        check_vma=False,
    )
```

```python
import math
import jax
import jax.numpy as jnp
from jax import lax
from jax.experimental import pallas as pl
from jax.experimental.pallas import tpu as pltpu
from jax.sharding import PartitionSpec as P

HD = 96
CQ = 6
CK = 11
TRUNK = 192
SEG = 32
TREE = 576
WIN = 256
FAM = 96
EXT = 680
F32 = jnp.float32
BF16 = jnp.bfloat16


def segments():
    rows = [(0, TRUNK, 0, 0, -1)]
    for b in range(4):
        base, ext = TRUNK + FAM * b, 200 + 120 * b
        rows.append((TRUNK + SEG * b, SEG, base, ext, TRUNK - 8))
        for c in range(2):
            rows.append((320 + 64 * b + SEG * c, SEG, base + SEG * (c + 1), ext + 40 * (c + 1), TRUNK + SEG * b + SEG - 8))
    return rows


SEGS = segments()


def nn(a, b):
    return lax.dot_general(a, b, (((1,), (0,)), ((), ())), preferred_element_type=F32)


def nt(a, b):
    return lax.dot_general(a, b, (((1,), (1,)), ((), ())), preferred_element_type=F32)


def tn(a, b):
    return lax.dot_general(a, b, (((0,), (0,)), ((), ())), preferred_element_type=F32)


def head_masks(g):
    lane = lax.broadcasted_iota(jnp.int32, (1, WIN), 1)
    first = 64 * g
    m0 = (lane >= first) & (lane < first + HD)
    m1 = (lane >= first + HD) & (lane < first + 2 * HD)
    return m0, m1, lane >= first


def fill_distance(jj_ref, dist_ref):
    for index, (_, size, row, _, _) in enumerate(SEGS):
        start = 0 if index == 0 else (TRUNK if (index - 1) % 3 == 0 else TRUNK + SEG)
        pos = lax.broadcasted_iota(jnp.int32, (size, WIN), 0) + start
        dist_ref[row : row + size] = pos - jj_ref[index : index + 1, :]


def path_rows(ref, b, c, column):
    if b is None:
        parts = [ref[0:TRUNK, pl.ds(column, WIN)], ref[TRUNK : TRUNK + SEG, pl.ds(column, WIN)], ref[320 : 320 + SEG, pl.ds(column, WIN)]]
    else:
        parts = [
            ref[0:TRUNK, pl.ds(column, WIN)],
            ref[pl.ds(pl.multiple_of(TRUNK + SEG * b, SEG), SEG), pl.ds(column, WIN)],
            ref[pl.ds(pl.multiple_of(320 + 64 * b + SEG * c, SEG), SEG), pl.ds(column, WIN)],
        ]
    return jnp.concatenate(parts, axis=0)


def fam_rows(b, c):
    base = TRUNK + FAM * b
    return (pl.ds(pl.multiple_of(base, 32), 64), 64) if c == 0 else (pl.ds(pl.multiple_of(base + 64, 32), SEG), SEG)


def group_norm(ho, m0, m1):
    def stat(v):
        s0 = jnp.sum(jnp.where(m0, v, 0.0), axis=-1, keepdims=True) * (1.0 / HD)
        s1 = jnp.sum(jnp.where(m1, v, 0.0), axis=-1, keepdims=True) * (1.0 / HD)
        return jnp.where(m0, s0, s1)

    centered = jnp.where(m0 | m1, ho - stat(ho), 0.0)
    inv = lax.rsqrt(stat(centered * centered) + 1e-05)
    return centered * inv, inv, stat


def fwd_kernel(hook, mix_ref, qkv_ref, t_ref, gn_ref, jj_ref, nh_ref, att_ref, pre_ref, qs_ref, ho_ref, dist_ref, qx_ref, mx_ref):
    side, t, g = pl.program_id(0), pl.program_id(1), pl.program_id(2)
    step = (side * 2 + t) * 2 + g
    mix0 = 8 * side + 4 * g
    hook(step, 0)
    w0 = pl.multiple_of(g * 128, 128)
    m0, m1, from_first = head_masks(g)
    m0f, m1f = m0.astype(F32), m1.astype(F32)
    fill_distance(jj_ref, dist_ref)
    qx_ref[0:8] = jnp.zeros((8, WIN), F32)
    for token, size, _, ext, parent in SEGS:
        if parent >= 0:
            low = qkv_ref[parent - 8 : parent + 8, pl.ds(w0, WIN)].astype(F32)
            qx_ref[ext : ext + 8] = low[8:16]
        qx_ref[ext + 8 : ext + 8 + size] = qkv_ref[token : token + size, pl.ds(w0, WIN)].astype(F32)
    for a in range(CQ):
        for _, size, row, ext, _ in SEGS:
            part = qx_ref[ext + 8 - a : ext + 8 - a + size]
            qs_ref[0, a, row : row + size] = (part * m0f).astype(BF16)
            qs_ref[1, a, row : row + size] = (part * m1f).astype(BF16)
    k0, v0 = w0 + 384, w0 + 768
    k_trunk = path_rows(qkv_ref, None, 0, k0)

    def trunk_scores(a, carry):
        scores = nt(qs_ref[:, a, 0:TRUNK].reshape(2 * TRUNK, WIN), k_trunk).reshape(2, TRUNK, WIN)
        kept = dist_ref[0:TRUNK] >= a
        for e in range(2):
            pre_ref[e, 0:TRUNK, pl.ds(pl.multiple_of(a * WIN, WIN), WIN)] = jnp.where(kept, scores[e], 0.0).astype(BF16)
        return carry

    lax.fori_loop(0, CQ, trunk_scores, 0)

    def fam_scores(b, carry):
        for c in range(2):
            rows, size = fam_rows(b, c)
            keys = path_rows(qkv_ref, b, c, k0)
            scores = nt(qs_ref[:, :, rows].reshape(2 * CQ * size, WIN), keys).reshape(2, CQ, size, WIN)
            dist = dist_ref[rows]
            for a in range(CQ):
                kept = dist >= a
                for e in range(2):
                    pre_ref[e, rows, a * WIN : (a + 1) * WIN] = jnp.where(kept, scores[e, a], 0.0).astype(BF16)
        return carry

    lax.fori_loop(0, 4, fam_scores, 0)
    hook(step, 1)
    for e in range(2):
        conv = nn(pre_ref[e], t_ref[e])
        logits = jnp.where(dist_ref[...] >= 0, conv, -1e30)
        shifted = jnp.exp(logits - jnp.max(logits, axis=-1, keepdims=True))
        att_ref[e] = shifted / jnp.sum(shifted, axis=-1, keepdims=True)
    for c in range(2):
        mx_ref[c] = (mix_ref[mix0 + 2 * c] * att_ref[0] + mix_ref[mix0 + 2 * c + 1] * att_ref[1]).astype(BF16)

    def put_out(rows, size, values):
        out = nn(mx_ref[:, rows].reshape(2 * size, WIN), values).reshape(2, size, WIN)
        ho_ref[rows] = jnp.where(m0, out[0], jnp.where(m1, out[1], 0.0))

    put_out(pl.ds(0, TRUNK), TRUNK, path_rows(qkv_ref, None, 0, v0))

    def fam_out(b, carry):
        for c in range(2):
            rows, size = fam_rows(b, c)
            put_out(rows, size, path_rows(qkv_ref, b, c, v0))
        return carry

    lax.fori_loop(0, 4, fam_out, 0)
    gain = gn_ref[0:1, pl.ds(w0, WIN)]
    for token, size, row, _, _ in SEGS:
        unit, _, _ = group_norm(ho_ref[row : row + size], m0, m1)
        old = nh_ref[token : token + size, pl.ds(w0, WIN)].astype(F32)
        nh_ref[token : token + size, pl.ds(w0, WIN)] = jnp.where(from_first, unit * gain, old).astype(BF16)
    hook(step, 2)


def bwd_kernel(
    hook, mix_ref, qkv_ref, t_ref, gn_ref, jj_ref, dn_ref, att_ref, pre_ref, qs_ref, ho_ref,
    dqkv_ref, ggn_ref, gmix_ref, gconv_ref,
    dist_ref, dh_ref, mx_ref, dm_ref, dc_ref, es_ref, dqx_ref, dk_ref, dv_ref,
):
    side, t, g = pl.program_id(0), pl.program_id(1), pl.program_id(2)
    mix0 = 8 * side + 4 * g
    step = (side * 2 + t) * 2 + g
    hook(step, 0)
    w0 = pl.multiple_of(g * 128, 128)
    m0, m1, from_first = head_masks(g)
    both = m0 | m1
    fill_distance(jj_ref, dist_ref)
    gain = gn_ref[0:1, pl.ds(w0, WIN)]
    gn_sum = jnp.zeros((1, WIN), F32)
    for token, size, row, _, _ in SEGS:
        unit, inv, stat = group_norm(ho_ref[row : row + size], m0, m1)
        dn = jnp.where(both, dn_ref[token : token + size, pl.ds(w0, WIN)].astype(F32), 0.0)
        gn_sum = gn_sum + jnp.sum(dn * unit, axis=0, keepdims=True)
        scaled = dn * gain
        d_head = inv * (scaled - stat(scaled) - unit * stat(scaled * unit))
        dh_ref[0, row : row + size] = jnp.where(m0, d_head, 0.0).astype(BF16)
        dh_ref[1, row : row + size] = jnp.where(m1, d_head, 0.0).astype(BF16)

    @pl.when((t == 0) & (g == 0))
    def _():
        ggn_ref[...] = jnp.zeros_like(ggn_ref)

    ggn_ref[0:1, pl.ds(w0, WIN)] += gn_sum
    k0, v0 = w0 + 384, w0 + 768
    for c in range(2):
        mx_ref[c] = (mix_ref[mix0 + 2 * c] * att_ref[0] + mix_ref[mix0 + 2 * c + 1] * att_ref[1]).astype(BF16)

    def add_keys(acc_ref, b, c, grads):
        acc_ref[0:TRUNK] += grads[0:TRUNK]
        branch = pl.ds(pl.multiple_of(TRUNK + SEG * b, SEG), SEG)
        if c == 0:
            acc_ref[branch] = grads[TRUNK : TRUNK + SEG]
        else:
            acc_ref[branch] += grads[TRUNK : TRUNK + SEG]
        acc_ref[pl.ds(pl.multiple_of(320 + 64 * b + SEG * c, SEG), SEG)] = grads[TRUNK + SEG :]

    def value_part(rows, size, values):
        heads = dh_ref[:, rows].reshape(2 * size, WIN)
        dm_ref[:, rows] = nt(heads, values).reshape(2, size, WIN)
        return tn(mx_ref[:, rows].reshape(2 * size, WIN), heads)

    dv_ref[0:TRUNK] = value_part(pl.ds(0, TRUNK), TRUNK, path_rows(qkv_ref, None, 0, v0))[0:TRUNK]

    def fam_values(b, carry):
        for c in range(2):
            rows, size = fam_rows(b, c)
            add_keys(dv_ref, b, c, value_part(rows, size, path_rows(qkv_ref, b, c, v0)))
        return carry

    lax.fori_loop(0, 4, fam_values, 0)

    def soft_part(block, sums):
        rows = pl.ds(pl.multiple_of(block * FAM, 32), FAM)
        dm = [dm_ref[c, rows] for c in range(2)]
        att = [att_ref[e, rows] for e in range(2)]
        out = []
        for e in range(2):
            d_att = mix_ref[mix0 + e] * dm[0] + mix_ref[mix0 + 2 + e] * dm[1]
            d_conv = att[e] * (d_att - jnp.sum(d_att * att[e], axis=-1, keepdims=True))
            dc_ref[e, rows] = d_conv.astype(BF16)
        for c in range(2):
            for e in range(2):
                out.append(sums[2 * c + e] + jnp.sum(dm[c] * att[e], axis=0, keepdims=True))
        return tuple(out)

    mix_sums = lax.fori_loop(0, 6, soft_part, tuple(jnp.zeros((1, WIN), F32) for _ in range(4)))
    gmix_ref[...] = jnp.zeros_like(gmix_ref)
    gconv_ref[...] = jnp.zeros_like(gconv_ref)
    for index in range(4):
        gmix_ref[index : index + 1] = mix_sums[index]
    mirror = lax.broadcasted_iota(jnp.int32, (WIN, WIN), 0) + lax.broadcasted_iota(jnp.int32, (WIN, WIN), 1) - (WIN - 1)
    band = jnp.abs(mirror) <= CK // 2
    hook(step, 1)
    flip = jnp.where(mirror == 0, 1.0, 0.0).astype(BF16)
    for e in range(2):
        flipped = nn(dc_ref[e], flip).astype(BF16)
        for a in range(CQ):
            cols = slice(a * WIN, (a + 1) * WIN)
            products = jnp.where(band, tn(flipped, pre_ref[e, :, cols]), 0.0)
            rolled = pltpu.roll(products, 24, 1, stride=1, stride_axis=0)
            gconv_ref[e, a : a + 1] = jnp.sum(rolled, axis=0, keepdims=True)
            grads = nt(dc_ref[e], t_ref[e, cols, :])
            es_ref[e, a] = jnp.where(dist_ref[...] >= a, grads, 0.0).astype(BF16)

    def score_part(rows, size, keys):
        grads = es_ref[:, :, rows].reshape(2 * CQ * size, WIN)
        back = nn(grads, keys).reshape(2, CQ, size, WIN)
        d_query = [jnp.where(m0, back[0, a], jnp.where(m1, back[1, a], 0.0)) for a in range(CQ)]
        return d_query, tn(grads, qs_ref[:, :, rows].reshape(2 * CQ * size, WIN))

    def shifted_sum(parts, start, size):
        zeros = jnp.zeros((8, WIN), F32)
        total = None
        for a in range(CQ):
            padded = jnp.concatenate([zeros, parts[a][start : start + size]], axis=0)
            if a:
                padded = pltpu.roll(padded, size + 8 - a, 0)
            total = padded if total is None else total + padded
        return total

    d_query, d_keys = score_part(pl.ds(0, TRUNK), TRUNK, path_rows(qkv_ref, None, 0, k0))
    dqx_ref[0:200] = shifted_sum(d_query, 0, TRUNK)
    dk_ref[0:TRUNK] = d_keys[0:TRUNK]

    def fam_scores(b, carry):
        ext = 200 + 120 * b
        for c in range(2):
            rows, size = fam_rows(b, c)
            d_query, d_keys = score_part(rows, size, path_rows(qkv_ref, b, c, k0))
            add_keys(dk_ref, b, c, d_keys)
            if c == 0:
                dqx_ref[pl.ds(pl.multiple_of(ext, 8), 40)] = shifted_sum(d_query, 0, SEG)
                dqx_ref[pl.ds(pl.multiple_of(ext + 40, 8), 40)] = shifted_sum(d_query, SEG, SEG)
            else:
                dqx_ref[pl.ds(pl.multiple_of(ext + 80, 8), 40)] = shifted_sum(d_query, 0, SEG)
        return carry

    lax.fori_loop(0, 4, fam_scores, 0)
    for b in range(4):
        ext = 200 + 120 * b
        dqx_ref[192:200] += dqx_ref[ext : ext + 8]
        dqx_ref[ext + 32 : ext + 40] += dqx_ref[ext + 40 : ext + 48] + dqx_ref[ext + 80 : ext + 88]

    def put(token, size, column, value):
        old = dqkv_ref[token : token + size, pl.ds(column, WIN)].astype(F32)
        dqkv_ref[token : token + size, pl.ds(column, WIN)] = jnp.where(from_first, value, old).astype(BF16)

    for token, size, _, ext, _ in SEGS:
        put(token, size, w0, dqx_ref[ext + 8 : ext + 8 + size])
        put(token, size, k0, dk_ref[token : token + size])
        put(token, size, v0, dv_ref[token : token + size])
    hook(step, 2)


def by_group(shape):
    tail = (0,) * (len(shape) - 3)
    return pl.BlockSpec((None, None, None) + shape[3:], lambda s, t, g: (s, t, g) + tail)


def by_side(shape):
    return pl.BlockSpec((None,) + shape, lambda s, t, g: (s, 0, 0))


def common_specs():
    return [
        pl.BlockSpec(memory_space=pltpu.SMEM),
        pl.BlockSpec((TREE, 1152), lambda s, t, g: (t, s)),
        pl.BlockSpec((None, None, 2, CQ * WIN, WIN), lambda s, t, g: (s, g, 0, 0, 0)),
        by_side((8, 384)),
        pl.BlockSpec((None, 16, WIN), lambda s, t, g: (t, 0, 0)),
    ]


PARAMS = dict(vmem_limit_bytes=60 * 1024 * 1024, dimension_semantics=("arbitrary",) * 3)


def saved_shapes(trees):
    lead = (2, trees, 2)
    return [lead + (2, TREE, WIN), lead + (2, TREE, CQ * WIN), lead + (2, CQ, TREE, WIN), lead + (TREE, WIN)]


def attention_forward(mix, qkv, toeplitz, gains, jj, gather=None):
    trees = qkv.shape[0] // TREE
    shapes = saved_shapes(trees)
    kinds = (F32, BF16, BF16, F32)
    weights, wide, count, collective = gather if gather else ((), (), 0, {})
    many, held = len(weights), len(wide)

    def kernel(*refs):
        inputs, loads, refs = refs[:5], refs[5 : 5 + many], refs[5 + many :]
        outs, full, refs = refs[:5], refs[5 : 5 + held], refs[5 + held :]
        work = Gather(LATER, loads, full, *refs[3:]) if gather else None

        def hook(step, place):
            if work:
                background(work, step, place)

        fwd_kernel(hook, *inputs, *outs, *refs[:3])

    anywhere = pl.BlockSpec(memory_space=pl.ANY)
    result = pl.pallas_call(
        kernel,
        grid=(2, trees, 2),
        in_specs=common_specs() + [anywhere] * many,
        out_specs=[pl.BlockSpec((TREE, 384), lambda s, t, g: (t, s))] + [by_group(s) for s in shapes] + [anywhere] * held,
        out_shape=[jax.ShapeDtypeStruct((trees * TREE, 768), BF16)]
        + [jax.ShapeDtypeStruct(s, k) for s, k in zip(shapes, kinds)]
        + [jax.ShapeDtypeStruct((1536, w), BF16) for w in wide],
        scratch_shapes=[pltpu.VMEM((TREE, WIN), jnp.int32), pltpu.VMEM((EXT, WIN), F32), pltpu.VMEM((2, TREE, WIN), BF16)]
        + gather_scratch(weights, count),
        compiler_params=pltpu.CompilerParams(**PARAMS, **collective),
        cost_estimate=pl.CostEstimate(flops=80_000_000_000, bytes_accessed=120_000_000, transcendentals=0),
    )(mix, qkv, toeplitz, gains, jj, *weights)
    return result[0], result[1:5], result[5:]


def attention_backward(mix, qkv, toeplitz, gains, jj, d_normed, saved, sums=None):
    trees = qkv.shape[0] // TREE
    shapes = saved_shapes(trees)
    collective = dict(collective_id=4, has_side_effects=True) if sums else {}
    many = len(sums or ())

    def kernel(*refs):
        inputs, extra, refs = refs[:10], refs[10 : 10 + many], refs[10 + many :]
        outs, full, refs = refs[:4], refs[4 : 4 + many], refs[4 + many :]
        work = Finish(BESIDE, extra, None, full, None, refs[9:]) if sums else None

        def hook(step, place):
            if work:
                beside(work, step, place)

        bwd_kernel(hook, *inputs, *outs, *refs[:9])

    anywhere = pl.BlockSpec(memory_space=pl.ANY)
    extra_in = [pl.BlockSpec((384, 2048), lambda s, t, g: (0, 0))] if sums else []
    result = pl.pallas_call(
        kernel,
        grid=(2, trees, 2),
        in_specs=common_specs() + [pl.BlockSpec((TREE, 384), lambda s, t, g: (t, s))] + [by_group(s) for s in shapes] + extra_in,
        out_specs=[
            pl.BlockSpec((TREE, 1152), lambda s, t, g: (t, s)),
            by_side((8, 384)),
            by_group((2, trees, 2, 8, WIN)),
            by_group((2, trees, 2, 2, 8, WIN)),
        ]
        + [anywhere] * many,
        out_shape=[
            jax.ShapeDtypeStruct((trees * TREE, 2304), BF16),
            jax.ShapeDtypeStruct((2, 8, 384), F32),
            jax.ShapeDtypeStruct((2, trees, 2, 8, WIN), F32),
            jax.ShapeDtypeStruct((2, trees, 2, 2, 8, WIN), F32),
        ]
        + [jax.ShapeDtypeStruct((1536, n), BF16) for n in (1024,)[:many]],
        scratch_shapes=[
            pltpu.VMEM((TREE, WIN), jnp.int32),
            pltpu.VMEM((2, TREE, WIN), BF16),
            pltpu.VMEM((2, TREE, WIN), BF16),
            pltpu.VMEM((2, TREE, WIN), F32),
            pltpu.VMEM((2, TREE, WIN), BF16),
            pltpu.VMEM((2, CQ, TREE, WIN), BF16),
            pltpu.VMEM((EXT, WIN), F32),
            pltpu.VMEM((TREE, WIN), F32),
            pltpu.VMEM((TREE, WIN), F32),
        ]
        + (finish_scratch(BESIDE, 128) if sums else []),
        compiler_params=pltpu.CompilerParams(**PARAMS, **collective),
        cost_estimate=pl.CostEstimate(flops=1_000_000_000, bytes_accessed=1_000_000, transcendentals=0),
    )(mix, qkv, toeplitz, gains, jj, d_normed, *saved, *(sums or ()))
    return result[:4], result[4:]


def band_rows(conv_w):
    rows = conv_w.reshape(-1, CK) * (1.0 / math.sqrt(HD))
    middle = jnp.zeros((rows.shape[0], WIN - CK), F32)
    return jnp.concatenate([rows[:, CK // 2 :], middle, rows[:, : CK // 2]], axis=1)


def fill_toeplitz(rows_ref, side, out_ref):
    offset = lax.broadcasted_iota(jnp.int32, (WIN, WIN), 1) - lax.broadcasted_iota(jnp.int32, (WIN, WIN), 0)
    band = jnp.abs(offset) <= CK // 2
    for head in range(4):
        for a in range(CQ):
            row = rows_ref[side, head * CQ + a : head * CQ + a + 1, :]
            rolled = pltpu.roll(jnp.broadcast_to(row, (WIN, WIN)), 0, 1, stride=1, stride_axis=0)
            out_ref[side, head // 2, head % 2, a * WIN : (a + 1) * WIN, :] = jnp.where(band, rolled, 0.0).astype(BF16)


def key_positions(valid):
    trees = valid.shape[0] // TREE
    valid = valid.reshape(trees, TREE)
    far = jnp.int32(1 << 20)

    def places(part, start):
        return jnp.where(part > 0, lax.broadcasted_iota(jnp.int32, part.shape, 1) + start, far)

    trunk = places(valid[:, :TRUNK], 0)
    empty = jnp.full((trees, SEG), far, jnp.int32)
    rows = [jnp.concatenate([trunk, empty, empty], axis=1)]
    for b in range(4):
        branch = places(valid[:, TRUNK + SEG * b : TRUNK + SEG * (b + 1)], TRUNK)
        rows.append(jnp.concatenate([trunk, branch, empty], axis=1))
        for c in range(2):
            first = 320 + 64 * b + SEG * c
            leaf = places(valid[:, first : first + SEG], TRUNK + SEG)
            rows.append(jnp.concatenate([trunk, branch, leaf], axis=1))
    rows += [jnp.zeros((trees, WIN), jnp.int32)] * 3
    return jnp.stack(rows, axis=1)


def conv_grads(gconv):
    lanes = gconv[..., :CQ, 18:29][..., ::-1] * (1.0 / math.sqrt(HD))
    return jnp.sum(lanes, axis=1).reshape(2, -1)


def mix_grads(gmix):
    return jnp.sum(gmix[:, :, :, :4], axis=(1, 4)).reshape(2, -1)


MESH = pl.DeviceIdType.MESH

FIRST = ((0, 0, 0, 0, 1152, 384), (1, 0, 0, 384, 1536, 384), (2, 0, 0, 768, 1920, 384))
LATER = (
    (0, 0, 0, 0, 384, 384),
    (1, 1, 0, 0, 1024, 512),
    (1, 1, 512, 512, 1536, 512),
    (2, 1, 0, 2048, 3072, 512),
    (2, 1, 512, 2560, 3584, 512),
    (3, 2, 0, 0, 1024, 512),
    (3, 2, 512, 512, 1536, 512),
)


def greet(peers):
    sem = pltpu.get_barrier_semaphore()
    for peer in peers:
        pl.semaphore_signal(sem, inc=1, device_id=peer, device_id_type=MESH)
    pl.semaphore_wait(sem, len(peers))


class Gather:
    def __init__(self, items, weights, fulls, send, recv, local, *held):
        self.items, self.weights, self.fulls, self.held = items, weights, fulls, held
        self.send, self.recv, self.local = send, recv, local
        q, c, z = lax.axis_index("plane"), lax.axis_index("core"), lax.axis_index("tensor")
        self.home = (z // 2) == c
        self.q = q
        self.core = (q, 1 - c, z)
        self.far = (q, 1 - c, (z + 2) % 4)
        self.near = (q, c, (z // 2) * 2 + (1 - z % 2))
        self.by_x = ((q // 2) * 2 + (1 - q % 2), c, z)
        self.by_y = ((q + 2) % 4, c, z)

    def away(self, action):
        pl.when(jnp.logical_not(self.home))(action)

    def whole(self, item, side):
        _, out, _, first, second, size = self.items[item]
        return self.fulls[out], pl.ds((first, second)[side], size)

    def z_copy(self, item, side, relay=False):
        weight, _, source_col, _, _, size = self.items[item]
        mine = pl.ds(pl.multiple_of(self.q * 384, 128), 384)
        ref, cols = self.whole(item, side)
        source = ref.at[mine, self.whole(item, 0)[1]] if relay else self.weights[weight].at[mine, pl.ds(source_col, size)]
        return pltpu.make_async_remote_copy(
            src_ref=source, dst_ref=ref.at[mine, cols], send_sem=self.send.at[item, side],
            recv_sem=self.recv.at[item, side], device_id=(self.far, self.near)[side], device_id_type=MESH)

    def plane_copy(self, item, side, step):
        ref, cols = self.whole(item, side)
        if step < 2:
            owner, first, size = self.q, 0, 384
        elif step == 2:
            owner, first, size = self.by_x[0], 0, 192
        else:
            owner, first, size = self.by_y[0], 192, 192
        span = pl.ds(pl.multiple_of(owner * 384 + first, 64), size)
        slot = 2 + 4 * side + step
        return pltpu.make_async_remote_copy(
            src_ref=ref.at[span, cols], dst_ref=ref.at[span, cols], send_sem=self.send.at[item, slot], recv_sem=self.recv.at[item, slot],
            device_id=(self.by_x, self.by_y, self.by_y, self.by_x)[step], device_id_type=MESH)

    def own_load(self, weight):
        return pltpu.make_async_copy(self.weights[weight], self.held[weight], self.local.at[weight, 0])

    def own_stores(self, weight):
        copies = []
        for number, (index, out, source_col, first, _, size) in enumerate(self.items):
            if index == weight:
                source = self.held[weight].at[:, pl.ds(source_col, size)]
                copies.append(pltpu.make_async_copy(source, self.fulls[out].at[:, pl.ds(first, size)], self.local.at[number, 1]))
        return copies

    def own(self):
        @pl.when(self.home)
        def _():
            for weight in range(len(self.weights)):
                self.own_load(weight).start()

    def pass_own(self, weight):
        @pl.when(self.home)
        def _():
            self.own_load(weight).wait()
            for copy in self.own_stores(weight):
                copy.start()

    def wait_own(self):
        @pl.when(self.home)
        def _():
            for weight in range(len(self.weights)):
                for copy in self.own_stores(weight):
                    copy.wait()

    def each(self, action):
        action(1)

        @self.away
        def _():
            action(0)

    def start_z(self, item):
        @pl.when(self.home)
        def _():
            self.z_copy(item, 1).start()

        @self.away
        def _():
            self.z_copy(item, 0).start()

    def relay_z(self, item):
        @self.away
        def _():
            self.z_copy(item, 0).wait_recv()
            self.z_copy(item, 1, True).start()
            self.plane_copy(item, 0, 0).start()
            self.plane_copy(item, 0, 1).start()

    def start_plane(self, item):
        self.z_copy(item, 1).wait_recv()
        self.plane_copy(item, 1, 0).start()
        self.plane_copy(item, 1, 1).start()

    def forward(self, item):
        def act(side):
            self.plane_copy(item, side, 0).wait_recv()
            self.plane_copy(item, side, 2).start()
            self.plane_copy(item, side, 1).wait_recv()
            self.plane_copy(item, side, 3).start()

        self.each(act)

    def finish(self, item):
        def act(side):
            self.plane_copy(item, side, 2).wait_recv()
            self.plane_copy(item, side, 3).wait_recv()
            self.z_copy(item, side).wait_send()
            for step in range(4):
                self.plane_copy(item, side, step).wait_send()

        self.each(act)


def gather_scratch(weights, count):
    if not weights:
        return []
    return [pltpu.SemaphoreType.DMA((count, 10)), pltpu.SemaphoreType.DMA((count, 10)), pltpu.SemaphoreType.DMA((max(count, len(weights)), 2))] + [
        pltpu.VMEM(w.shape, BF16) for w in weights
    ]


AHEAD = 3


def background(work, step, place):
    count = len(work.items)
    if place == 2:

        @pl.when(step == 7)
        def _():
            work.forward(count - 1)
            for item in range(count):
                work.finish(item)
            work.wait_own()

        return

    for turn in range(8):
        slot = 2 * turn + place

        @pl.when(step == turn)
        def _(slot=slot):
            if slot == 0:
                work.own()
                greet((work.near, work.far, work.by_x, work.by_y))
                for item in range(AHEAD):
                    work.start_z(item)
            elif slot <= 2 * count:
                item = (slot - 1) // 2
                if slot % 2:
                    work.relay_z(item)
                    if item + AHEAD < count:
                        work.start_z(item + AHEAD)
                    if item < len(work.weights):
                        work.pass_own(item)
                else:
                    work.start_plane(item)
                    if item >= 1:
                        work.forward(item - 1)


def opening_kernel(tokens_ref, gain_ref, small_ref, wq_ref, wk_ref, wv_ref, full_ref, normed_ref, toep_ref, both_ref, send, recv, local, held0, held1, held2, extra_send, extra_recv):
    work = Gather(FIRST, (wq_ref, wk_ref, wv_ref), (full_ref,), send, recv, local, held0, held1, held2)
    rows = tokens_ref.shape[0]

    def extra(source, target, index, peer):
        return pltpu.make_async_remote_copy(
            src_ref=source, dst_ref=target, send_sem=extra_send.at[index], recv_sem=extra_recv.at[index], device_id=peer, device_id_type=MESH)

    far_small = extra(small_ref, both_ref.at[0], 0, work.far)
    near_small = extra(both_ref.at[0], both_ref.at[1], 1, work.near)
    normed_out = extra(normed_ref.at[0:rows], normed_ref.at[rows : 2 * rows], 2, work.core)
    work.own()
    greet((work.near, work.far, work.by_x, work.by_y, work.core))

    @work.away
    def _():
        far_small.start()

    @pl.when(work.home)
    def _():
        both_ref[0] = small_ref[...]
        near_small.start()

    for item in range(3):
        work.start_z(item)
    for start in range(0, rows, 96):
        x = tokens_ref[start : start + 96].astype(F32)
        inv = lax.rsqrt(jnp.mean(x * x, axis=-1, keepdims=True) + 1e-06)
        normed_ref[start : start + 96] = (x * inv * gain_ref[...]).astype(BF16)
    normed_out.start()

    @work.away
    def _():
        far_small.wait_recv()
        near_small.start()

    work.relay_z(0)
    work.start_plane(0)
    fill_toeplitz(both_ref, 0, toep_ref)
    work.relay_z(1)
    work.start_plane(1)
    work.forward(0)
    for weight in range(3):
        work.pass_own(weight)
    near_small.wait_recv()
    work.relay_z(2)
    work.start_plane(2)
    work.forward(1)
    fill_toeplitz(both_ref, 1, toep_ref)
    work.forward(2)
    for item in range(3):
        work.finish(item)
    work.wait_own()
    near_small.wait_send()

    @work.away
    def _():
        far_small.wait_send()

    normed_out.wait()


def opening(tokens, gain, small, weights, collective_id):
    vmem = pl.BlockSpec(memory_space=pltpu.VMEM)
    anywhere = pl.BlockSpec(memory_space=pl.ANY)
    rows, width = tokens.shape
    return pl.pallas_call(
        opening_kernel,
        in_specs=[vmem] * 3 + [anywhere] * 3,
        out_specs=[anywhere] + [vmem] * 3,
        out_shape=[
            jax.ShapeDtypeStruct((width, 2304), BF16),
            jax.ShapeDtypeStruct((2 * rows, width), BF16),
            jax.ShapeDtypeStruct((2, 2, 2, CQ * WIN, WIN), BF16),
            jax.ShapeDtypeStruct((2,) + small.shape, F32),
        ],
        scratch_shapes=gather_scratch(weights, 3) + [pltpu.SemaphoreType.DMA((3,)), pltpu.SemaphoreType.DMA((3,))],
        compiler_params=pltpu.CompilerParams(collective_id=collective_id, has_side_effects=True, vmem_limit_bytes=60 * 1024 * 1024),
    )(tokens, gain, small, *weights)


class Finish:
    def __init__(self, plan, parts, raw, outs, small, bufs, made=False):
        self.made = made
        q, c, z = lax.axis_index("plane"), lax.axis_index("core"), lax.axis_index("tensor")
        self.q, self.c = q, c
        self.home = (z // 2) == c
        self.by_x = ((q // 2) * 2 + (1 - q % 2), c, z)
        self.by_y = ((q + 2) % 4, c, z)
        self.core = (q, 1 - c, z)
        self.near = (q, c, (z // 2) * 2 + (1 - z % 2))
        self.far = (q, 1 - c, (z + 2) % 4)
        self.across = (q, c, (z + 2) % 4)
        self.plan, self.parts, self.raw, self.outs, self.small = plan, parts, raw, outs, small
        (self.near_buf, self.far_buf, self.core_buf, self.here_buf, self.raw_part, self.raw_own, self.raw_first,
         self.raw_second, self.send, self.recv, self.raw_send, self.raw_recv, self.local) = bufs[:13]
        if small is not None:
            self.small_buf, self.small_in, self.small_send, self.small_recv = bufs[13:]

    def remote(self, src, dst, sems, index, peer):
        return pltpu.make_async_remote_copy(
            src_ref=src, dst_ref=dst, send_sem=sems[0].at[index], recv_sem=sems[1].at[index], device_id=peer, device_id_type=MESH)

    def columns(self, item):
        _, first_a, first_b, size, _, _, at = self.plan[item]
        return pl.ds(first_a, size), pl.ds(first_b, size), pl.ds(at, size)

    def part(self, item):
        source = self.plan[item][0]
        if source >= 0:
            return self.parts[source]
        return self.raw.at[self.rows(self.q)] if self.made else self.raw_part

    def away(self, action):
        pl.when(jnp.logical_not(self.home))(action)

    def rows(self, owner):
        return pl.ds(pl.multiple_of(owner * 384, 128), 384)

    def raw_copies(self, item):
        cols_a, cols_b, _ = self.columns(item)
        sems = (self.raw_send, self.raw_recv)
        across = 3 - self.q
        x, y = self.by_x[0], self.by_y[0]
        remote = [
            self.remote(self.raw.at[self.rows(x), cols_a], self.raw_first.at[0, :, cols_a], sems, (item, 0), self.by_x),
            self.remote(self.raw.at[self.rows(across), cols_a], self.raw_first.at[1, :, cols_a], sems, (item, 1), self.by_x),
            self.remote(self.raw.at[self.rows(y), cols_b], self.raw_first.at[0, :, cols_b], sems, (item, 2), self.by_y),
            self.remote(self.raw.at[self.rows(across), cols_b], self.raw_first.at[1, :, cols_b], sems, (item, 3), self.by_y),
        ]
        if self.made:
            return remote, []
        return remote, [
            pltpu.make_async_copy(self.raw.at[self.rows(self.q), cols_a], self.raw_own.at[0, :, cols_a], self.local.at[item, 0]),
            pltpu.make_async_copy(self.raw.at[self.rows(y), cols_a], self.raw_own.at[1, :, cols_a], self.local.at[item, 1]),
            pltpu.make_async_copy(self.raw.at[self.rows(self.q), cols_b], self.raw_own.at[0, :, cols_b], self.local.at[item, 2]),
            pltpu.make_async_copy(self.raw.at[self.rows(x), cols_b], self.raw_own.at[1, :, cols_b], self.local.at[item, 3]),
        ]

    def raw_place(self, which, side, cols):
        if self.made:
            owner = self.q if which == 0 else (self.by_y[0], self.by_x[0])[side]
            return self.raw, (self.rows(owner), cols)
        return self.raw_own, (which, slice(None), cols)

    def raw_second_copies(self, item):
        sems = (self.raw_send, self.raw_recv)
        copies = []
        for side, cols in enumerate(self.columns(item)[:2]):
            ref, place = self.raw_place(1, side, cols)
            copies.append(self.remote(ref.at[place], self.raw_second.at[:, cols], sems, (item, 4 + side), (self.by_y, self.by_x)[side]))
        return copies

    def r1_side(self, item, side):
        for copy in self.raw_copies(item)[0][2 * side : 2 * side + 2]:
            copy.start()

    def r1(self, item):
        for group in self.raw_copies(item):
            for copy in group:
                copy.start()

    def r2(self, item):
        remote, own = self.raw_copies(item)
        for copy in own:
            copy.wait()
        for side, cols in enumerate(self.columns(item)[:2]):
            remote[2 * side + 1].wait_recv()
            ref, place = self.raw_place(1, side, cols)
            ref[place] = added(ref[place], self.raw_first[1, :, cols])
            self.raw_second_copies(item)[side].start()

    def r3(self, item):
        remote, _ = self.raw_copies(item)
        for side, cols in enumerate(self.columns(item)[:2]):
            remote[2 * side].wait_recv()
            self.raw_second_copies(item)[side].wait_recv()
            ref, place = self.raw_place(0, side, cols)
            total = ref[place].astype(F32) + self.raw_first[0, :, cols].astype(F32) + self.raw_second[:, cols].astype(F32)
            self.part(item)[:, cols] = total.astype(BF16)

    def near_copy(self, item):
        _, cols_b, at = self.columns(item)
        return self.remote(self.part(item).at[:, cols_b], self.near_buf.at[:, self.spot(item)], (self.send, self.recv), (item, 0), self.near)

    def spot(self, item):
        return pl.ds(self.plan[item][5], self.plan[item][3])

    def far_copy(self, item):
        spot = self.spot(item)
        return self.remote(self.here_buf.at[:, spot], self.far_buf.at[:, spot], (self.send, self.recv), (item, 1), self.far)

    def core_copy(self, item, relayed):
        spot = self.spot(item)
        source = self.far_buf if relayed else self.here_buf
        return self.remote(source.at[:, spot], self.core_buf.at[:, spot], (self.send, self.recv), (item, 2), self.core)

    def s1(self, item):
        self.near_copy(item).start()

    def s2(self, item):
        spot, cols_a = self.spot(item), self.columns(item)[0]
        self.near_copy(item).wait_recv()
        self.here_buf[:, spot] = added(self.part(item)[:, cols_a], self.near_buf[:, spot])

        @pl.when(self.home)
        def _():
            self.core_copy(item, False).start()

        @self.away
        def _():
            self.far_copy(item).start()

    def s3(self, item):
        @self.away
        def _():
            self.far_copy(item).wait_recv()
            self.core_copy(item, True).start()

    def plane_copies(self, item):
        out = self.outs[self.plan[item][4]]
        at, spot = self.columns(item)[2], self.spot(item)
        sems = (self.send, self.recv)
        half = self.c * 192

        def rows(owner, first, size):
            return pl.ds(pl.multiple_of(owner * 384 + half + first, 32), size)

        mine = self.core_buf.at[pl.ds(pl.multiple_of(half, 32), 192), spot]
        x, y, across = self.by_x[0], self.by_y[0], 3 - self.q
        own = out.at[rows(self.q, 0, 192), at]
        top, low = out.at[rows(x, 0, 96), at], out.at[rows(y, 96, 96), at]
        return [
            self.remote(mine, own, sems, (item, 3), self.by_x),
            self.remote(mine, own, sems, (item, 4), self.by_y),
            self.remote(top, top, sems, (item, 5), self.by_y),
            self.remote(low, low, sems, (item, 6), self.by_x),
        ] + [
            self.remote(out.at[rows(o, 0, 192), at], out.at[rows(o, 0, 192), at], sems, (item, 7 + i), self.core)
            for i, o in enumerate((x, y, across))
        ]

    def own_copy(self, item):
        out = self.outs[self.plan[item][4]]
        rows = pl.ds(pl.multiple_of(self.q * 384, 128), 384)
        return pltpu.make_async_copy(self.core_buf.at[:, self.spot(item)], out.at[rows, self.columns(item)[2]], self.local.at[item, 4])

    def s4(self, item):
        spot = self.spot(item)

        @pl.when(self.home)
        def _():
            self.core_copy(item, False).wait_recv()
            self.core_buf[:, spot] = added(self.here_buf[:, spot], self.core_buf[:, spot])

        @self.away
        def _():
            self.core_copy(item, True).wait_recv()
            self.core_buf[:, spot] = added(self.far_buf[:, spot], self.core_buf[:, spot])

        self.own_copy(item).start()
        copies = self.plane_copies(item)
        copies[0].start()
        copies[1].start()

    def s5(self, item):
        copies = self.plane_copies(item)
        copies[0].wait_recv()
        copies[2].start()
        copies[4].start()
        copies[1].wait_recv()
        copies[3].start()
        copies[5].start()

    def s6(self, item):
        copies = self.plane_copies(item)
        copies[2].wait_recv()
        copies[3].wait_recv()
        copies[6].start()

    def s7(self, item):
        copies = self.plane_copies(item)
        self.own_copy(item).wait()
        for copy in copies[4:]:
            copy.wait_recv()
        for copy in copies:
            copy.wait_send()
        self.near_copy(item).wait_send()

        @pl.when(self.home)
        def _():
            self.core_copy(item, False).wait_send()

        @self.away
        def _():
            self.core_copy(item, True).wait_send()
            self.far_copy(item).wait_send()

        if self.plan[item][0] < 0:
            for copy in self.raw_copies(item)[0] + self.raw_second_copies(item):
                copy.wait_send()

    def small_copy(self, turn):
        peer = (self.core, self.by_x, self.by_y, self.near, self.across)[turn]
        return self.remote(self.small_buf.at[turn], self.small_in.at[turn], (self.small_send, self.small_recv), turn, peer)

    def small_start(self):
        self.small_copy(0).start()

    def small_next(self, turn):
        self.small_copy(turn).wait_recv()
        self.small_buf[turn + 1] = self.small_buf[turn] + self.small_in[turn]
        if turn < 4:
            self.small_copy(turn + 1).start()

    def small_done(self, out):
        for turn in range(5):
            self.small_copy(turn).wait_send()
        out[...] = self.small_buf[5]


def added(left, right):
    return (left.astype(F32) + right.astype(F32)).astype(BF16)


FINISH = (
    (0, 0, 1024, 1024, 0, 0, 0),
    (0, 2048, 3072, 1024, 0, 1024, 1024),
    (-1, 0, 1152, 384, 1, 2048, 0),
    (-1, 384, 1536, 384, 1, 2432, 384),
    (-1, 768, 1920, 384, 1, 2816, 768),
)
LONE = ((-1, 0, 384, 384, 0, 0, 0),)
BESIDE = (
    (0, 0, 1024, 512, 0, 0, 0),
    (0, 512, 1536, 512, 0, 512, 512),
)
BESIDE_STEPS = (
    (("greet", 0), ("s1", 0), ("s1", 1)),
    (),
    (("s2", 0),),
    (("s2", 1),),
    (("s3", 0),),
    (("s3", 1),),
    (("s4", 0),),
    (("s4", 1),),
    (),
    (),
    (("s5", 0),),
    (("s5", 1),),
    (),
    (("s6", 0),),
    (("s6", 1),),
)


def finish_scratch(plan, raw_width, made=False):
    count, width = len(plan), sum(item[3] for item in plan)
    return (
        [pltpu.VMEM((384, width), BF16)] * 4
        + [pltpu.VMEM((384, 128 if made else raw_width), BF16)]
        + [pltpu.VMEM((2, 384, 128 if made else raw_width), BF16), pltpu.VMEM((2, 384, raw_width), BF16)]
        + [pltpu.VMEM((384, raw_width), BF16)]
        + [pltpu.SemaphoreType.DMA((count, 10))] * 2
        + [pltpu.SemaphoreType.DMA((count, 6))] * 2
        + [pltpu.SemaphoreType.DMA((count, 5))]
    )


def beside(work, step, place):
    if place == 2:

        @pl.when(step == 7)
        def _():
            for item in range(len(work.plan)):
                work.s7(item)

        return

    for slot, names in enumerate(BESIDE_STEPS):
        if slot % 2 == place:

            @pl.when(step == slot // 2)
            def _(names=names):
                for name, item in names:
                    if name == "greet":
                        greet((work.near, work.far, work.by_x, work.by_y, work.core))
                    else:
                        getattr(work, name)(item)


def finish_kernel(
    small, gu, out, normed_t, d_qkv, weight, tokens, gain, d_hidden, small_out, d_input, o_gu, o_qkv, o_out,
    made, partner, arrived, loaded, load_sem, hidden_buf, tokens_buf, hidden_sem, core_send, core_recv, *bufs,
):
    lone = Finish(LONE, (), out, (o_out,), None, bufs[-13:])
    work = Finish(FINISH, (gu,), made, (o_gu, o_qkv), small, bufs[:-13], True)
    rows = tokens.shape[0]

    def load(part):
        return pltpu.make_async_copy(weight.at[384 * part : 384 * (part + 1)], loaded.at[part % 2], load_sem.at[part % 2])

    def exchange(part):
        cols = pl.ds(384 * part, 384)
        return work.remote(partner.at[:, cols], arrived.at[:, cols], (core_send, core_recv), part, work.core)

    def load_hidden(part):
        span = pl.ds(64 * part, 64)
        return (
            pltpu.make_async_copy(d_hidden.at[span], hidden_buf.at[part % 2], hidden_sem.at[0, part % 2]),
            pltpu.make_async_copy(tokens.at[span], tokens_buf.at[part % 2], hidden_sem.at[1, part % 2]),
        )

    load(0).start()
    load(1).start()
    for copy in load_hidden(0):
        copy.start()
    greet((work.near, work.far, work.by_x, work.by_y, work.core, work.across))
    lone.r1(0)
    work.s1(0)

    def make(side, owner):
        cols = slice(1152 * side, 1152 * (side + 1))
        made[work.rows(owner), cols] = nn(normed_t[work.rows(owner), :], d_qkv[:, cols]).astype(BF16)

    across = 3 - work.q
    for side, owners in enumerate(((across, work.by_x[0]), (across, work.by_y[0]))):
        for owner in owners:
            make(side, owner)
        for item in (2, 3, 4):
            work.r1_side(item, side)
    work.s2(0)
    work.s1(1)
    lone.r2(0)
    make(0, work.by_y[0])
    make(1, work.by_x[0])
    work.s3(0)
    make(0, work.q)
    make(1, work.q)
    work.r2(2)
    lone.r3(0)
    lone.s1(0)
    work.s4(0)

    def back(part):
        cols = slice(384 * part, 384 * (part + 1))
        load(part).wait()
        both = nt(d_qkv[...], loaded[part % 2])
        d_input[:, cols] = both[:rows]
        partner[:, cols] = both[rows:].astype(BF16)
        if part < 2:
            load(part + 2).start()
        exchange(part).start()

    back(0)
    work.r2(3)
    work.s2(1)
    back(1)
    work.r2(4)
    work.r3(2)
    work.s1(2)
    back(2)
    work.s3(1)
    lone.s2(0)
    work.r3(3)
    work.s1(3)
    work.s5(0)
    back(3)
    work.s2(2)
    work.r3(4)
    work.s1(4)
    work.s4(1)
    for part in range(4):
        exchange(part).wait_recv()
    gain_sum = jnp.zeros((1, tokens.shape[1]), F32)
    for part in range(rows // 64):
        span = slice(64 * part, 64 * (part + 1))
        if part + 1 < rows // 64:
            for copy in load_hidden(part + 1):
                copy.start()
        for copy in load_hidden(part):
            copy.wait()
        x = tokens_buf[part % 2].astype(F32)
        inv = lax.rsqrt(jnp.mean(x * x, axis=-1, keepdims=True) + 1e-06)
        d_normed = d_input[span] + arrived[span].astype(F32)
        scaled = d_normed * gain[...]
        gain_sum = gain_sum + jnp.sum(d_normed * x * inv, axis=0, keepdims=True)
        d_input[span] = hidden_buf[part % 2] + inv * scaled - x * inv**3 * jnp.mean(scaled * x, axis=-1, keepdims=True)
    work.small_buf[0] = small[...]
    work.small_buf[0, 0:1] = gain_sum
    work.small_start()
    script = (
        ("s3", 2), ("s2", 3), ("s3", 5), ("s6", 0), ("m", 0),
        ("s5", 1), ("s4", 2), ("s3", 3), ("s2", 4), ("s4", 5), ("m", 1),
        ("s6", 1), ("s5", 2), ("s4", 3), ("s3", 4), ("s5", 5), ("m", 2),
        ("s6", 2), ("s5", 3), ("s4", 4), ("s6", 5), ("m", 3), ("s6", 3), ("s5", 4), ("m", 4), ("s6", 4),
    )
    for name, item in script:
        if name == "m":
            work.small_next(item)
        elif item == 5:
            getattr(lone, name)(0)
        else:
            getattr(work, name)(item)
    for item in range(len(FINISH)):
        work.s7(item)
    lone.s7(0)
    for part in range(4):
        exchange(part).wait_send()
    work.small_done(small_out)


def finish_gradients(small, gu, out, normed_t, d_qkv, weight, tokens, gain, d_hidden, collective_id):
    vmem = pl.BlockSpec(memory_space=pltpu.VMEM)
    anywhere = pl.BlockSpec(memory_space=pl.ANY)
    rows, width = tokens.shape
    return pl.pallas_call(
        finish_kernel,
        in_specs=[vmem] * 2 + [anywhere] + [vmem] * 2 + [anywhere] * 2 + [vmem] + [anywhere],
        out_specs=[vmem] * 2 + [anywhere] * 3,
        out_shape=[jax.ShapeDtypeStruct(small.shape, F32), jax.ShapeDtypeStruct((rows, width), F32)]
        + [jax.ShapeDtypeStruct((1536, n), BF16) for n in (2048, 1152, 384)],
        scratch_shapes=[
            pltpu.VMEM((1536, 2304), BF16),
            pltpu.VMEM((rows, width), BF16),
            pltpu.VMEM((rows, width), BF16),
            pltpu.VMEM((2, 384, 2304), BF16),
            pltpu.SemaphoreType.DMA((2,)),
            pltpu.VMEM((2, 64, width), F32),
            pltpu.VMEM((2, 64, width), BF16),
            pltpu.SemaphoreType.DMA((2, 2)),
            pltpu.SemaphoreType.DMA((4,)),
            pltpu.SemaphoreType.DMA((4,)),
        ]
        + finish_scratch(FINISH, 2304, True)
        + [pltpu.VMEM((6,) + small.shape, F32), pltpu.VMEM((5,) + small.shape, F32)]
        + [pltpu.SemaphoreType.DMA((5,))] * 2
        + finish_scratch(LONE, 768),
        compiler_params=pltpu.CompilerParams(collective_id=collective_id, has_side_effects=True, vmem_limit_bytes=60 * 1024 * 1024),
    )(small, gu, out, normed_t, d_qkv, weight, tokens, gain, d_hidden)


def rows_dot(lhs, rhs):
    return tn(lhs, rhs).astype(BF16)


def toeplitz_alone(both):
    def kernel(rows_ref, out_ref):
        fill_toeplitz(rows_ref, 0, out_ref)
        fill_toeplitz(rows_ref, 1, out_ref)

    return pl.pallas_call(
        kernel,
        out_shape=jax.ShapeDtypeStruct((2, 2, 2, CQ * WIN, WIN), BF16),
        compiler_params=pltpu.CompilerParams(vmem_limit_bytes=60 * 1024 * 1024),
    )(both)


def make_local(planes, tensors):
    every = ("plane", "core", "tensor")
    sides = [(c, z) for c in range(2) for z in range(tensors)]

    def spot(q, c, z):
        return (q * 2 + c) * tensors + z

    def is_home(c, z):
        return z // 2 == c

    far_pairs = [(spot(q, c, z), spot(q, 1 - c, z ^ 2)) for q in range(planes) for c, z in sides if not is_home(c, z)]
    near_pairs = [
        (spot(q, c, z), spot(q, c, z ^ 1) if is_home(c, z) else spot(q, 1 - c, z ^ 3)) for q in range(planes) for c, z in sides
    ]

    def over_core(value):
        return lax.ppermute(value, "core", [(0, 1), (1, 0)])

    def first_from(value):
        return lax.ppermute(value, every, far_pairs)

    def second_from(value):
        return lax.ppermute(value, every, near_pairs)

    square = planes == 4

    def local(
        tokens, teacher, valid_mask, norm1_gain, w_query, w_key, w_value, conv_weight, head_mix, gn_gain, w_out, norm2_gain,
        w_gate, w_up, w_down,
    ):
        q, c, z = lax.axis_index("plane"), lax.axis_index("core"), lax.axis_index("tensor")
        own_rows, width = tokens.shape
        home = (z // 2) == c
        wide = w_query.shape[1]

        def collect(weights):
            pairs = []
            for weight in weights:
                pairs.append(jnp.where(home, weight, first_from(weight)))
                pairs.append(second_from(weight))
            return pairs

        fused = square and tensors == 4

        def plane_sum(grads):
            return lax.psum_scatter(grads, "plane", scatter_dimension=0, tiled=True)

        def reduce(first, second):
            here = added(first, lax.ppermute(second, "tensor", [(i, i ^ 1) for i in range(tensors)]))
            here = jnp.where(home, here, first_from(here))
            total = added(here, over_core(here))
            return lax.all_gather(total, "plane", axis=0, tiled=True)

        small = jnp.concatenate(
            [
                band_rows(conv_weight),
                jnp.pad(head_mix.reshape(1, -1), ((0, 0), (0, WIN - head_mix.size))),
                jnp.pad(gn_gain.reshape(1, -1), ((0, 0), (0, 2 * WIN - wide))).reshape(2, WIN),
                jnp.zeros((5, WIN), F32),
            ]
        )
        conv_size, mix_size = conv_weight.size, head_mix.size
        small_size = conv_size + mix_size + wide
        gain_one, gain_two = norm1_gain, norm2_gain
        own_valid = lax.dynamic_slice_in_dim(valid_mask, z * own_rows, own_rows, 0)
        jj = key_positions(jnp.concatenate([own_valid, over_core(own_valid)]))

        def with_partner(value):
            return jnp.concatenate([value, over_core(value)], axis=0)

        def summed(left, right):
            sent = over_core(nt(left[own_rows:], right).astype(BF16))
            return nt(left[:own_rows], right) + sent.astype(F32)

        inputs = tokens.astype(F32)
        inv_one = lax.rsqrt(jnp.mean(inputs * inputs, axis=-1, keepdims=True) + 1e-06)
        if fused:
            qkv_weight, normed_one, toep, both_small = opening(tokens, gain_one[None], small, [w_query, w_key, w_value], 1)
            gather = ([w_out, w_gate, w_up, w_down], (768, 4096, 2048), len(LATER), dict(collective_id=3, has_side_effects=True))
        else:
            both_small = jnp.stack([jnp.where(home, small, first_from(small)), second_from(small)])
            toep = toeplitz_alone(both_small)
            normed_one = with_partner((inputs * inv_one * gain_one).astype(BF16))
            parts = collect([w_query, w_key, w_value])
            qkv_weight = jnp.concatenate(parts[0::2] + parts[1::2], axis=1)
            gather = None
        mix = both_small[:, 24, :mix_size].reshape(-1)
        gains = jnp.broadcast_to(both_small[:, 25:27].reshape(2, 1, 2 * WIN)[:, :, :wide], (2, 8, wide))
        qkv = nn(normed_one, qkv_weight).astype(BF16)
        heads_out, saved, later = attention_forward(mix, qkv, toep, gains, jj, gather)
        if fused:
            out_weight, gu_weight, down_weight = later
        else:
            out_weight = jnp.concatenate(collect([w_out]), axis=1)
            gu_weight = jnp.concatenate(collect([w_gate, w_up]), axis=1)
            down_weight = jnp.concatenate(collect([w_down]), axis=1)
        hidden_in = inputs + summed(heads_out, out_weight)
        inv_two = lax.rsqrt(jnp.mean(hidden_in * hidden_in, axis=-1, keepdims=True) + 1e-06)
        normed_two = with_partner((hidden_in * inv_two * gain_two).astype(BF16))
        units = w_gate.shape[1]
        both = nn(normed_two, gu_weight)
        gate, up = both[:, : 2 * units], both[:, 2 * units :]
        hidden = (jax.nn.silu(gate) * up).astype(BF16)
        gate, up = gate.astype(BF16), up.astype(BF16)
        final_rows = hidden_in + summed(hidden, down_weight)
        output = final_rows.astype(BF16)
        own_mask = own_valid.astype(F32)
        error = own_mask[:, None] * (final_rows - teacher.astype(F32))
        squared_sum = jnp.sum(error * error)
        count_sum = jnp.sum(own_mask)

        d_all = with_partner(error.astype(BF16))
        down_grads = rows_dot(d_all, hidden)
        down_grads, d_all = lax.optimization_barrier((down_grads, d_all))
        down_part = plane_sum(down_grads)
        d_hidden = nn(d_all, down_weight)
        gate, up = gate.astype(F32), up.astype(F32)
        s = jax.nn.sigmoid(gate)
        d_gate = (d_hidden * up * s * (1.0 + gate * (1.0 - s))).astype(BF16)
        d_up = (d_hidden * gate * s).astype(BF16)
        d_gu = jnp.concatenate([d_gate, d_up], axis=1)
        gu_grads = rows_dot(normed_two, d_gu)
        gu_grads, d_gu = lax.optimization_barrier((gu_grads, d_gu))
        gu_part = plane_sum(gu_grads)
        d_normed_two = summed(d_gu, gu_weight)
        scaled_two = d_normed_two * gain_two
        grad_gain_two = jnp.sum(d_normed_two * hidden_in * inv_two, axis=0)
        d_hidden_in = (
            error + inv_two * scaled_two - hidden_in * inv_two**3 * jnp.mean(scaled_two * hidden_in, axis=-1, keepdims=True)
        )
        d_attn = with_partner(d_hidden_in.astype(BF16))
        out_grads = rows_dot(d_attn, heads_out)
        out_grads, d_attn = lax.optimization_barrier((out_grads, d_attn))
        d_normed = nn(d_attn, out_weight)
        d_normed, down_part = lax.optimization_barrier((d_normed, down_part))
        (d_qkv, ggn, gmix, gconv), done = attention_backward(
            mix, qkv, toep, gains, jj, d_normed, saved, (down_part,) if fused else None
        )
        small_grads = jnp.concatenate([conv_grads(gconv), mix_grads(gmix), ggn[:, 0]], axis=1)
        table = jnp.zeros((tensors, small_size), F32)
        table = lax.dynamic_update_slice(table, small_grads[:1], (2 * c + z % 2, 0))
        table = lax.dynamic_update_slice(table, small_grads[1:], (2 * c + 1 - z % 2, 0))
        table = jnp.pad(table.reshape(-1), (0, 4 * width - table.size)).reshape(4, width)
        last = jnp.pad(jnp.stack([squared_sum, count_sum]), (0, 2 * width - 2)).reshape(2, width)
        packed = jnp.concatenate([jnp.zeros((1, width), F32), grad_gain_two[None], table, last])
        if fused:
            packed, grad_input, sum_gu, sum_qkv, sum_out = finish_gradients(
                packed, gu_part, out_grads, normed_one.T, d_qkv, qkv_weight, tokens, gain_one[None], d_hidden_in, 2
            )
            sums = [done[0], sum_gu, sum_out, sum_qkv]
        else:
            qkv_grads = rows_dot(normed_one, d_qkv)
            d_normed_one = summed(d_qkv, qkv_weight)
            scaled_one = d_normed_one * gain_one
            packed = packed.at[0].set(jnp.sum(d_normed_one * inputs * inv_one, axis=0))
            grad_input = (
                d_hidden_in + inv_one * scaled_one - inputs * inv_one**3 * jnp.mean(scaled_one * inputs, axis=-1, keepdims=True)
            )
            packed = lax.psum(packed, every)
            out_part, qkv_part = plane_sum(out_grads), plane_sum(qkv_grads)
            sums = [reduce(part[:, : part.shape[1] // 2], part[:, part.shape[1] // 2 :]) for part in (down_part, out_part, qkv_part)]
            places = [slice(i * units, (i + 1) * units) for i in range(4)]
            first, second = [jnp.concatenate([gu_part[:, places[i]], gu_part[:, places[i + 2]]], axis=1) for i in range(2)]
            sums.insert(1, reduce(first, second))
        grad_down, grad_gu, grad_out, grad_qkv = [value.astype(F32) for value in sums]
        small_sum = lax.dynamic_slice_in_dim(packed[2:6].reshape(-1), z * small_size, small_size, 0)
        gain_slice = width // tensors
        gain_one_out = lax.dynamic_slice_in_dim(packed[0], z * gain_slice, gain_slice, 0)
        gain_two_out = lax.dynamic_slice_in_dim(packed[1], z * gain_slice, gain_slice, 0)
        loss = packed[6, 0] / (packed[6, 1] * width)
        return (
            output,
            loss,
            grad_input,
            gain_one_out,
            grad_qkv[:, :wide],
            grad_qkv[:, wide : 2 * wide],
            grad_qkv[:, 2 * wide :],
            small_sum[:conv_size].reshape(conv_weight.shape),
            small_sum[conv_size : conv_size + mix_size].reshape(head_mix.shape),
            small_sum[conv_size + mix_size :].reshape(gn_gain.shape),
            grad_out,
            gain_two_out,
            grad_gu[:, :units],
            grad_gu[:, units:],
            grad_down,
        )

    return local


def solution(mesh):
    tensors = mesh.shape["tensor"]
    planes = mesh.shape["dp"] // 2
    inner = jax.sharding.Mesh(mesh.devices.reshape(planes, 2, tensors), ("plane", "core", "tensor"))
    rows = P(("plane", "core", "tensor"), None)
    columns = P(None, "tensor")
    cube = P("tensor", None, None)
    return jax.shard_map(
        make_local(planes, tensors),
        mesh=inner,
        in_specs=(
            rows, rows, P(("plane", "core")), P(), columns, columns, columns, cube, cube, P("tensor", None), columns, P(),
            columns, columns, columns,
        ),
        out_specs=(
            rows, P(), rows, P("tensor"), columns, columns, columns, cube, cube, P("tensor", None), columns, P("tensor"),
            columns, columns, columns,
        ),
        check_vma=False,
    )
```

```python
import math
import jax
import jax.numpy as jnp
from jax import lax
from jax.experimental import pallas as pl
from jax.experimental.pallas import tpu as pltpu
from jax.sharding import PartitionSpec as P

HD = 96
CQ = 6
CK = 11
TRUNK = 192
SEG = 32
TREE = 576
WIN = 256
FAM = 96
EXT = 680
F32 = jnp.float32
BF16 = jnp.bfloat16


def segments():
    rows = [(0, TRUNK, 0, 0, -1)]
    for b in range(4):
        base, ext = TRUNK + FAM * b, 200 + 120 * b
        rows.append((TRUNK + SEG * b, SEG, base, ext, TRUNK - 8))
        for c in range(2):
            rows.append((320 + 64 * b + SEG * c, SEG, base + SEG * (c + 1), ext + 40 * (c + 1), TRUNK + SEG * b + SEG - 8))
    return rows


SEGS = segments()


def nn(a, b):
    return lax.dot_general(a, b, (((1,), (0,)), ((), ())), preferred_element_type=F32)


def nt(a, b):
    return lax.dot_general(a, b, (((1,), (1,)), ((), ())), preferred_element_type=F32)


def tn(a, b):
    return lax.dot_general(a, b, (((0,), (0,)), ((), ())), preferred_element_type=F32)


def head_masks(g):
    lane = lax.broadcasted_iota(jnp.int32, (1, WIN), 1)
    first = 64 * g
    m0 = (lane >= first) & (lane < first + HD)
    m1 = (lane >= first + HD) & (lane < first + 2 * HD)
    return m0, m1, lane >= first


def fill_distance(jj_ref, dist_ref):
    for index, (_, size, row, _, _) in enumerate(SEGS):
        start = 0 if index == 0 else (TRUNK if (index - 1) % 3 == 0 else TRUNK + SEG)
        pos = lax.broadcasted_iota(jnp.int32, (size, WIN), 0) + start
        dist_ref[row : row + size] = pos - jj_ref[index : index + 1, :]


def path_rows(ref, b, c, column):
    if b is None:
        parts = [ref[0:TRUNK, pl.ds(column, WIN)], ref[TRUNK : TRUNK + SEG, pl.ds(column, WIN)], ref[320 : 320 + SEG, pl.ds(column, WIN)]]
    else:
        parts = [
            ref[0:TRUNK, pl.ds(column, WIN)],
            ref[pl.ds(pl.multiple_of(TRUNK + SEG * b, SEG), SEG), pl.ds(column, WIN)],
            ref[pl.ds(pl.multiple_of(320 + 64 * b + SEG * c, SEG), SEG), pl.ds(column, WIN)],
        ]
    return jnp.concatenate(parts, axis=0)


def fam_rows(b, c):
    base = TRUNK + FAM * b
    return (pl.ds(pl.multiple_of(base, 32), 64), 64) if c == 0 else (pl.ds(pl.multiple_of(base + 64, 32), SEG), SEG)


def group_norm(ho, m0, m1):
    def stat(v):
        s0 = jnp.sum(jnp.where(m0, v, 0.0), axis=-1, keepdims=True) * (1.0 / HD)
        s1 = jnp.sum(jnp.where(m1, v, 0.0), axis=-1, keepdims=True) * (1.0 / HD)
        return jnp.where(m0, s0, s1)

    centered = jnp.where(m0 | m1, ho - stat(ho), 0.0)
    inv = lax.rsqrt(stat(centered * centered) + 1e-05)
    return centered * inv, inv, stat


def fwd_kernel(hook, mix_ref, qkv_ref, t_ref, gn_ref, jj_ref, nh_ref, att_ref, pre_ref, qs_ref, ho_ref, dist_ref, qx_ref, mx_ref):
    side, t, g = pl.program_id(0), pl.program_id(1), pl.program_id(2)
    step = (side * 2 + t) * 2 + g
    mix0 = 8 * side + 4 * g
    hook(step, 0)
    w0 = pl.multiple_of(g * 128, 128)
    m0, m1, from_first = head_masks(g)
    m0f, m1f = m0.astype(F32), m1.astype(F32)
    fill_distance(jj_ref, dist_ref)
    qx_ref[0:8] = jnp.zeros((8, WIN), F32)
    for token, size, _, ext, parent in SEGS:
        if parent >= 0:
            low = qkv_ref[parent - 8 : parent + 8, pl.ds(w0, WIN)].astype(F32)
            qx_ref[ext : ext + 8] = low[8:16]
        qx_ref[ext + 8 : ext + 8 + size] = qkv_ref[token : token + size, pl.ds(w0, WIN)].astype(F32)
    for a in range(CQ):
        for _, size, row, ext, _ in SEGS:
            part = qx_ref[ext + 8 - a : ext + 8 - a + size]
            qs_ref[0, a, row : row + size] = (part * m0f).astype(BF16)
            qs_ref[1, a, row : row + size] = (part * m1f).astype(BF16)
    k0, v0 = w0 + 384, w0 + 768
    k_trunk = path_rows(qkv_ref, None, 0, k0)

    def trunk_scores(a, carry):
        scores = nt(qs_ref[:, a, 0:TRUNK].reshape(2 * TRUNK, WIN), k_trunk).reshape(2, TRUNK, WIN)
        kept = dist_ref[0:TRUNK] >= a
        for e in range(2):
            pre_ref[e, 0:TRUNK, pl.ds(pl.multiple_of(a * WIN, WIN), WIN)] = jnp.where(kept, scores[e], 0.0).astype(BF16)
        return carry

    lax.fori_loop(0, CQ, trunk_scores, 0)

    def fam_scores(b, carry):
        for c in range(2):
            rows, size = fam_rows(b, c)
            keys = path_rows(qkv_ref, b, c, k0)
            scores = nt(qs_ref[:, :, rows].reshape(2 * CQ * size, WIN), keys).reshape(2, CQ, size, WIN)
            dist = dist_ref[rows]
            for a in range(CQ):
                kept = dist >= a
                for e in range(2):
                    pre_ref[e, rows, a * WIN : (a + 1) * WIN] = jnp.where(kept, scores[e, a], 0.0).astype(BF16)
        return carry

    lax.fori_loop(0, 4, fam_scores, 0)
    hook(step, 1)
    for e in range(2):
        conv = nn(pre_ref[e], t_ref[e])
        logits = jnp.where(dist_ref[...] >= 0, conv, -1e30)
        shifted = jnp.exp(logits - jnp.max(logits, axis=-1, keepdims=True))
        att_ref[e] = shifted / jnp.sum(shifted, axis=-1, keepdims=True)
    for c in range(2):
        mx_ref[c] = (mix_ref[mix0 + 2 * c] * att_ref[0] + mix_ref[mix0 + 2 * c + 1] * att_ref[1]).astype(BF16)

    def put_out(rows, size, values):
        out = nn(mx_ref[:, rows].reshape(2 * size, WIN), values).reshape(2, size, WIN)
        ho_ref[rows] = jnp.where(m0, out[0], jnp.where(m1, out[1], 0.0))

    put_out(pl.ds(0, TRUNK), TRUNK, path_rows(qkv_ref, None, 0, v0))

    def fam_out(b, carry):
        for c in range(2):
            rows, size = fam_rows(b, c)
            put_out(rows, size, path_rows(qkv_ref, b, c, v0))
        return carry

    lax.fori_loop(0, 4, fam_out, 0)
    gain = gn_ref[0:1, pl.ds(w0, WIN)]
    for token, size, row, _, _ in SEGS:
        unit, _, _ = group_norm(ho_ref[row : row + size], m0, m1)
        old = nh_ref[token : token + size, pl.ds(w0, WIN)].astype(F32)
        nh_ref[token : token + size, pl.ds(w0, WIN)] = jnp.where(from_first, unit * gain, old).astype(BF16)
    hook(step, 2)


def bwd_kernel(
    hook, mix_ref, qkv_ref, t_ref, gn_ref, jj_ref, dn_ref, att_ref, pre_ref, qs_ref, ho_ref,
    dqkv_ref, ggn_ref, gmix_ref, gconv_ref,
    dist_ref, dh_ref, mx_ref, dm_ref, dc_ref, es_ref, dqx_ref, dk_ref, dv_ref,
):
    side, t, g = pl.program_id(0), pl.program_id(1), pl.program_id(2)
    mix0 = 8 * side + 4 * g
    step = (side * 2 + t) * 2 + g
    hook(step, 0)
    w0 = pl.multiple_of(g * 128, 128)
    m0, m1, from_first = head_masks(g)
    both = m0 | m1
    fill_distance(jj_ref, dist_ref)
    gain = gn_ref[0:1, pl.ds(w0, WIN)]
    gn_sum = jnp.zeros((1, WIN), F32)
    for token, size, row, _, _ in SEGS:
        unit, inv, stat = group_norm(ho_ref[row : row + size], m0, m1)
        dn = jnp.where(both, dn_ref[token : token + size, pl.ds(w0, WIN)].astype(F32), 0.0)
        gn_sum = gn_sum + jnp.sum(dn * unit, axis=0, keepdims=True)
        scaled = dn * gain
        d_head = inv * (scaled - stat(scaled) - unit * stat(scaled * unit))
        dh_ref[0, row : row + size] = jnp.where(m0, d_head, 0.0).astype(BF16)
        dh_ref[1, row : row + size] = jnp.where(m1, d_head, 0.0).astype(BF16)

    @pl.when((t == 0) & (g == 0))
    def _():
        ggn_ref[...] = jnp.zeros_like(ggn_ref)

    ggn_ref[0:1, pl.ds(w0, WIN)] += gn_sum
    k0, v0 = w0 + 384, w0 + 768
    for c in range(2):
        mx_ref[c] = (mix_ref[mix0 + 2 * c] * att_ref[0] + mix_ref[mix0 + 2 * c + 1] * att_ref[1]).astype(BF16)

    def add_keys(acc_ref, b, c, grads):
        acc_ref[0:TRUNK] += grads[0:TRUNK]
        branch = pl.ds(pl.multiple_of(TRUNK + SEG * b, SEG), SEG)
        if c == 0:
            acc_ref[branch] = grads[TRUNK : TRUNK + SEG]
        else:
            acc_ref[branch] += grads[TRUNK : TRUNK + SEG]
        acc_ref[pl.ds(pl.multiple_of(320 + 64 * b + SEG * c, SEG), SEG)] = grads[TRUNK + SEG :]

    def value_part(rows, size, values):
        heads = dh_ref[:, rows].reshape(2 * size, WIN)
        dm_ref[:, rows] = nt(heads, values).reshape(2, size, WIN)
        return tn(mx_ref[:, rows].reshape(2 * size, WIN), heads)

    dv_ref[0:TRUNK] = value_part(pl.ds(0, TRUNK), TRUNK, path_rows(qkv_ref, None, 0, v0))[0:TRUNK]

    def fam_values(b, carry):
        for c in range(2):
            rows, size = fam_rows(b, c)
            add_keys(dv_ref, b, c, value_part(rows, size, path_rows(qkv_ref, b, c, v0)))
        return carry

    lax.fori_loop(0, 4, fam_values, 0)

    def soft_part(block, sums):
        rows = pl.ds(pl.multiple_of(block * FAM, 32), FAM)
        dm = [dm_ref[c, rows] for c in range(2)]
        att = [att_ref[e, rows] for e in range(2)]
        out = []
        for e in range(2):
            d_att = mix_ref[mix0 + e] * dm[0] + mix_ref[mix0 + 2 + e] * dm[1]
            d_conv = att[e] * (d_att - jnp.sum(d_att * att[e], axis=-1, keepdims=True))
            dc_ref[e, rows] = d_conv.astype(BF16)
        for c in range(2):
            for e in range(2):
                out.append(sums[2 * c + e] + jnp.sum(dm[c] * att[e], axis=0, keepdims=True))
        return tuple(out)

    mix_sums = lax.fori_loop(0, 6, soft_part, tuple(jnp.zeros((1, WIN), F32) for _ in range(4)))
    gmix_ref[...] = jnp.zeros_like(gmix_ref)
    gconv_ref[...] = jnp.zeros_like(gconv_ref)
    for index in range(4):
        gmix_ref[index : index + 1] = mix_sums[index]
    mirror = lax.broadcasted_iota(jnp.int32, (WIN, WIN), 0) + lax.broadcasted_iota(jnp.int32, (WIN, WIN), 1) - (WIN - 1)
    band = jnp.abs(mirror) <= CK // 2
    hook(step, 1)
    flip = jnp.where(mirror == 0, 1.0, 0.0).astype(BF16)
    for e in range(2):
        flipped = nn(dc_ref[e], flip).astype(BF16)
        for a in range(CQ):
            cols = slice(a * WIN, (a + 1) * WIN)
            products = jnp.where(band, tn(flipped, pre_ref[e, :, cols]), 0.0)
            rolled = pltpu.roll(products, 24, 1, stride=1, stride_axis=0)
            gconv_ref[e, a : a + 1] = jnp.sum(rolled, axis=0, keepdims=True)
            grads = nt(dc_ref[e], t_ref[e, cols, :])
            es_ref[e, a] = jnp.where(dist_ref[...] >= a, grads, 0.0).astype(BF16)

    def score_part(rows, size, keys):
        grads = es_ref[:, :, rows].reshape(2 * CQ * size, WIN)
        back = nn(grads, keys).reshape(2, CQ, size, WIN)
        d_query = [jnp.where(m0, back[0, a], jnp.where(m1, back[1, a], 0.0)) for a in range(CQ)]
        return d_query, tn(grads, qs_ref[:, :, rows].reshape(2 * CQ * size, WIN))

    def shifted_sum(parts, start, size):
        zeros = jnp.zeros((8, WIN), F32)
        total = None
        for a in range(CQ):
            padded = jnp.concatenate([zeros, parts[a][start : start + size]], axis=0)
            if a:
                padded = pltpu.roll(padded, size + 8 - a, 0)
            total = padded if total is None else total + padded
        return total

    d_query, d_keys = score_part(pl.ds(0, TRUNK), TRUNK, path_rows(qkv_ref, None, 0, k0))
    dqx_ref[0:200] = shifted_sum(d_query, 0, TRUNK)
    dk_ref[0:TRUNK] = d_keys[0:TRUNK]

    def fam_scores(b, carry):
        ext = 200 + 120 * b
        for c in range(2):
            rows, size = fam_rows(b, c)
            d_query, d_keys = score_part(rows, size, path_rows(qkv_ref, b, c, k0))
            add_keys(dk_ref, b, c, d_keys)
            if c == 0:
                dqx_ref[pl.ds(pl.multiple_of(ext, 8), 40)] = shifted_sum(d_query, 0, SEG)
                dqx_ref[pl.ds(pl.multiple_of(ext + 40, 8), 40)] = shifted_sum(d_query, SEG, SEG)
            else:
                dqx_ref[pl.ds(pl.multiple_of(ext + 80, 8), 40)] = shifted_sum(d_query, 0, SEG)
        return carry

    lax.fori_loop(0, 4, fam_scores, 0)
    for b in range(4):
        ext = 200 + 120 * b
        dqx_ref[192:200] += dqx_ref[ext : ext + 8]
        dqx_ref[ext + 32 : ext + 40] += dqx_ref[ext + 40 : ext + 48] + dqx_ref[ext + 80 : ext + 88]

    def put(token, size, column, value):
        old = dqkv_ref[token : token + size, pl.ds(column, WIN)].astype(F32)
        dqkv_ref[token : token + size, pl.ds(column, WIN)] = jnp.where(from_first, value, old).astype(BF16)

    for token, size, _, ext, _ in SEGS:
        put(token, size, w0, dqx_ref[ext + 8 : ext + 8 + size])
        put(token, size, k0, dk_ref[token : token + size])
        put(token, size, v0, dv_ref[token : token + size])
    hook(step, 2)


def by_group(shape):
    tail = (0,) * (len(shape) - 3)
    return pl.BlockSpec((None, None, None) + shape[3:], lambda s, t, g: (s, t, g) + tail)


def by_side(shape):
    return pl.BlockSpec((None,) + shape, lambda s, t, g: (s, 0, 0))


def common_specs():
    return [
        pl.BlockSpec(memory_space=pltpu.SMEM),
        pl.BlockSpec((TREE, 1152), lambda s, t, g: (t, s)),
        pl.BlockSpec((None, None, 2, CQ * WIN, WIN), lambda s, t, g: (s, g, 0, 0, 0)),
        by_side((8, 384)),
        pl.BlockSpec((None, 16, WIN), lambda s, t, g: (t, 0, 0)),
    ]


PARAMS = dict(vmem_limit_bytes=60 * 1024 * 1024, dimension_semantics=("arbitrary",) * 3)


def saved_shapes(trees):
    lead = (2, trees, 2)
    return [lead + (2, TREE, WIN), lead + (2, TREE, CQ * WIN), lead + (2, CQ, TREE, WIN), lead + (TREE, WIN)]


def attention_forward(mix, qkv, toeplitz, gains, jj, gather=None):
    trees = qkv.shape[0] // TREE
    shapes = saved_shapes(trees)
    kinds = (F32, BF16, BF16, F32)
    weights, wide, count, collective = gather if gather else ((), (), 0, {})
    many, held = len(weights), len(wide)

    def kernel(*refs):
        inputs, loads, refs = refs[:5], refs[5 : 5 + many], refs[5 + many :]
        outs, full, refs = refs[:5], refs[5 : 5 + held], refs[5 + held :]
        work = Gather(DIRECT, LATER, loads, full, *refs[3:]) if gather else None

        def hook(step, place):
            if work:
                background(work, step, place)

        fwd_kernel(hook, *inputs, *outs, *refs[:3])

    anywhere = pl.BlockSpec(memory_space=pl.ANY)
    result = pl.pallas_call(
        kernel,
        grid=(2, trees, 2),
        in_specs=common_specs() + [anywhere] * many,
        out_specs=[pl.BlockSpec((TREE, 384), lambda s, t, g: (t, s))] + [by_group(s) for s in shapes] + [anywhere] * held,
        out_shape=[jax.ShapeDtypeStruct((trees * TREE, 768), BF16)]
        + [jax.ShapeDtypeStruct(s, k) for s, k in zip(shapes, kinds)]
        + [jax.ShapeDtypeStruct((1536, w), BF16) for w in wide],
        scratch_shapes=[pltpu.VMEM((TREE, WIN), jnp.int32), pltpu.VMEM((EXT, WIN), F32), pltpu.VMEM((2, TREE, WIN), BF16)]
        + gather_scratch(weights, count),
        compiler_params=pltpu.CompilerParams(**PARAMS, **collective),
        cost_estimate=pl.CostEstimate(flops=80_000_000_000, bytes_accessed=120_000_000, transcendentals=0),
    )(mix, qkv, toeplitz, gains, jj, *weights)
    return result[0], result[1:5], result[5:]


def attention_backward(mix, qkv, toeplitz, gains, jj, d_normed, saved, sums=None):
    trees = qkv.shape[0] // TREE
    shapes = saved_shapes(trees)
    collective = dict(collective_id=4, has_side_effects=True) if sums else {}
    many = len(sums or ())

    def kernel(*refs):
        inputs, extra, refs = refs[:10], refs[10 : 10 + many], refs[10 + many :]
        outs, full, refs = refs[:4], refs[4 : 4 + many], refs[4 + many :]
        work = Finish(BESIDE, extra, None, full, None, refs[9:]) if sums else None

        def hook(step, place):
            if work:
                beside(work, step, place)

        bwd_kernel(hook, *inputs, *outs, *refs[:9])

    anywhere = pl.BlockSpec(memory_space=pl.ANY)
    extra_in = [pl.BlockSpec((384, 2048), lambda s, t, g: (0, 0))] if sums else []
    result = pl.pallas_call(
        kernel,
        grid=(2, trees, 2),
        in_specs=common_specs() + [pl.BlockSpec((TREE, 384), lambda s, t, g: (t, s))] + [by_group(s) for s in shapes] + extra_in,
        out_specs=[
            pl.BlockSpec((TREE, 1152), lambda s, t, g: (t, s)),
            by_side((8, 384)),
            by_group((2, trees, 2, 8, WIN)),
            by_group((2, trees, 2, 2, 8, WIN)),
        ]
        + [anywhere] * many,
        out_shape=[
            jax.ShapeDtypeStruct((trees * TREE, 2304), BF16),
            jax.ShapeDtypeStruct((2, 8, 384), F32),
            jax.ShapeDtypeStruct((2, trees, 2, 8, WIN), F32),
            jax.ShapeDtypeStruct((2, trees, 2, 2, 8, WIN), F32),
        ]
        + [jax.ShapeDtypeStruct((1536, n), BF16) for n in (1024,)[:many]],
        scratch_shapes=[
            pltpu.VMEM((TREE, WIN), jnp.int32),
            pltpu.VMEM((2, TREE, WIN), BF16),
            pltpu.VMEM((2, TREE, WIN), BF16),
            pltpu.VMEM((2, TREE, WIN), F32),
            pltpu.VMEM((2, TREE, WIN), BF16),
            pltpu.VMEM((2, CQ, TREE, WIN), BF16),
            pltpu.VMEM((EXT, WIN), F32),
            pltpu.VMEM((TREE, WIN), F32),
            pltpu.VMEM((TREE, WIN), F32),
        ]
        + (finish_scratch(BESIDE, 128) if sums else []),
        compiler_params=pltpu.CompilerParams(**PARAMS, **collective),
        cost_estimate=pl.CostEstimate(flops=1_000_000_000, bytes_accessed=1_000_000, transcendentals=0),
    )(mix, qkv, toeplitz, gains, jj, d_normed, *saved, *(sums or ()))
    return result[:4], result[4:]


def band_rows(conv_w):
    rows = conv_w.reshape(-1, CK) * (1.0 / math.sqrt(HD))
    middle = jnp.zeros((rows.shape[0], WIN - CK), F32)
    return jnp.concatenate([rows[:, CK // 2 :], middle, rows[:, : CK // 2]], axis=1)


def fill_toeplitz(rows_ref, side, out_ref):
    offset = lax.broadcasted_iota(jnp.int32, (WIN, WIN), 1) - lax.broadcasted_iota(jnp.int32, (WIN, WIN), 0)
    band = jnp.abs(offset) <= CK // 2
    for head in range(4):
        for a in range(CQ):
            row = rows_ref[side, head * CQ + a : head * CQ + a + 1, :]
            rolled = pltpu.roll(jnp.broadcast_to(row, (WIN, WIN)), 0, 1, stride=1, stride_axis=0)
            out_ref[side, head // 2, head % 2, a * WIN : (a + 1) * WIN, :] = jnp.where(band, rolled, 0.0).astype(BF16)


def key_positions(valid):
    trees = valid.shape[0] // TREE
    valid = valid.reshape(trees, TREE)
    far = jnp.int32(1 << 20)

    def places(part, start):
        return jnp.where(part > 0, lax.broadcasted_iota(jnp.int32, part.shape, 1) + start, far)

    trunk = places(valid[:, :TRUNK], 0)
    empty = jnp.full((trees, SEG), far, jnp.int32)
    rows = [jnp.concatenate([trunk, empty, empty], axis=1)]
    for b in range(4):
        branch = places(valid[:, TRUNK + SEG * b : TRUNK + SEG * (b + 1)], TRUNK)
        rows.append(jnp.concatenate([trunk, branch, empty], axis=1))
        for c in range(2):
            first = 320 + 64 * b + SEG * c
            leaf = places(valid[:, first : first + SEG], TRUNK + SEG)
            rows.append(jnp.concatenate([trunk, branch, leaf], axis=1))
    rows += [jnp.zeros((trees, WIN), jnp.int32)] * 3
    return jnp.stack(rows, axis=1)


def conv_grads(gconv):
    lanes = gconv[..., :CQ, 18:29][..., ::-1] * (1.0 / math.sqrt(HD))
    return jnp.sum(lanes, axis=1).reshape(2, -1)


def mix_grads(gmix):
    return jnp.sum(gmix[:, :, :, :4], axis=(1, 4)).reshape(2, -1)


MESH = pl.DeviceIdType.MESH

FIRST = ((0, 0, 0, 0, 1152, 384), (1, 0, 0, 384, 1536, 384), (2, 0, 0, 768, 1920, 384))
LATER = (
    (0, 0, 0, 0, 384, 384),
    (1, 1, 0, 0, 2048, 512),
    (2, 1, 0, 512, 2560, 512),
    (1, 1, 512, 1024, 3072, 512),
    (2, 1, 512, 1536, 3584, 512),
    (3, 2, 0, 0, 1024, 512),
    (3, 2, 512, 512, 1536, 512),
)
WHOLE = 5
DIRECT = 0
LAST = ((0, 0, 0, 0, 1024, 512), (0, 0, 512, 512, 1536, 512))


def greet(peers):
    sem = pltpu.get_barrier_semaphore()
    for peer in peers:
        pl.semaphore_signal(sem, inc=1, device_id=peer, device_id_type=MESH)
    pl.semaphore_wait(sem, len(peers))


class Gather:
    def __init__(self, direct, items, weights, fulls, send, recv, local, *held):
        self.direct = direct
        self.items, self.weights, self.fulls, self.held = items, weights, fulls, held
        self.send, self.recv, self.local = send, recv, local
        q, c, z = lax.axis_index("plane"), lax.axis_index("core"), lax.axis_index("tensor")
        self.home = (z // 2) == c
        self.q = q
        self.core = (q, 1 - c, z)
        self.far = (q, 1 - c, (z + 2) % 4)
        self.near = (q, c, (z // 2) * 2 + (1 - z % 2))
        self.by_x = ((q // 2) * 2 + (1 - q % 2), c, z)
        self.by_y = ((q + 2) % 4, c, z)

    def away(self, action):
        pl.when(jnp.logical_not(self.home))(action)

    def whole(self, item, side):
        _, out, _, first, second, size = self.items[item]
        return self.fulls[out], pl.ds((first, second)[side], size)

    def z_copy(self, item, side, relay=False):
        weight, _, source_col, _, _, size = self.items[item]
        mine = pl.ds(pl.multiple_of(self.q * 384, 128), 384)
        ref, cols = self.whole(item, side)
        source = ref.at[mine, self.whole(item, 0)[1]] if relay else self.weights[weight].at[mine, pl.ds(source_col, size)]
        return pltpu.make_async_remote_copy(
            src_ref=source, dst_ref=ref.at[mine, cols], send_sem=self.send.at[item, side],
            recv_sem=self.recv.at[item, side], device_id=(self.far, self.near)[side], device_id_type=MESH)

    def plane_copy(self, item, side, step):
        ref, cols = self.whole(item, side)
        if step < 2:
            owner, first, size = self.q, 0, 384
        elif step == 2:
            owner, first, size = self.by_x[0], 0, 192
        else:
            owner, first, size = self.by_y[0], 192, 192
        span = pl.ds(pl.multiple_of(owner * 384 + first, 64), size)
        slot = 2 + 4 * side + step
        return pltpu.make_async_remote_copy(
            src_ref=ref.at[span, cols], dst_ref=ref.at[span, cols], send_sem=self.send.at[item, slot], recv_sem=self.recv.at[item, slot],
            device_id=(self.by_x, self.by_y, self.by_y, self.by_x)[step], device_id_type=MESH)

    def own_load(self, weight):
        return pltpu.make_async_copy(self.weights[weight], self.held[weight], self.local.at[weight, 0])

    def own_stores(self, weight):
        copies = []
        for number, (index, out, source_col, first, _, size) in enumerate(self.items):
            if index == weight:
                source = self.held[weight].at[:, pl.ds(source_col, size)]
                copies.append(pltpu.make_async_copy(source, self.fulls[out].at[:, pl.ds(first, size)], self.local.at[number, 1]))
        return copies

    def own(self):
        @pl.when(self.home)
        def _():
            for weight in range(len(self.weights)):
                self.own_load(weight).start()

    def pass_own(self, weight):
        @pl.when(self.home)
        def _():
            self.own_load(weight).wait()
            for copy in self.own_stores(weight):
                copy.start()

    def wait_own(self):
        @pl.when(self.home)
        def _():
            for weight in range(len(self.weights)):
                for copy in self.own_stores(weight):
                    copy.wait()

    def each(self, action):
        action(1)

        @self.away
        def _():
            action(0)

    def across_copy(self, item):
        weight, _, source_col, _, _, size = self.items[item]
        span = pl.ds(pl.multiple_of((3 - self.q) * 384, 128), 384)
        ref, cols = self.whole(item, 1)
        return pltpu.make_async_remote_copy(
            src_ref=self.weights[weight].at[span, pl.ds(source_col, size)], dst_ref=ref.at[span, cols], send_sem=self.send.at[item, 8],
            recv_sem=self.recv.at[item, 8], device_id=self.near, device_id_type=MESH)

    def start_z(self, item):
        @pl.when(self.home)
        def _():
            self.z_copy(item, 1).start()
            if item < self.direct:
                self.across_copy(item).start()

        @self.away
        def _():
            self.z_copy(item, 0).start()

    def relay_z(self, item):
        @self.away
        def _():
            self.z_copy(item, 0).wait_recv()
            self.z_copy(item, 1, True).start()
            self.plane_copy(item, 0, 0).start()
            self.plane_copy(item, 0, 1).start()

    def relay_only(self, item):
        @self.away
        def _():
            self.z_copy(item, 0).wait_recv()
            self.z_copy(item, 1, True).start()

    def finish_z(self, item):
        self.z_copy(item, 1).wait_recv()
        self.each(lambda side: self.z_copy(item, side).wait_send())

    def start_both(self, item):
        def act(side):
            self.plane_copy(item, side, 0).start()
            self.plane_copy(item, side, 1).start()

        self.each(act)

    def start_plane(self, item):
        self.z_copy(item, 1).wait_recv()
        self.plane_copy(item, 1, 0).start()
        self.plane_copy(item, 1, 1).start()

    def forward(self, item):
        def act(side):
            self.plane_copy(item, side, 0).wait_recv()
            self.plane_copy(item, side, 2).start()
            self.plane_copy(item, side, 1).wait_recv()
            self.plane_copy(item, side, 3).start()

        if item < self.direct:

            @self.away
            def _():
                act(1)
                act(0)

        else:
            self.each(act)

    def finish(self, item):
        def act(side):
            self.plane_copy(item, side, 2).wait_recv()
            self.plane_copy(item, side, 3).wait_recv()
            if self.weights:
                self.z_copy(item, side).wait_send()
            for step in range(4):
                self.plane_copy(item, side, step).wait_send()

        if item >= self.direct:
            self.each(act)
            return

        @self.away
        def _():
            act(1)
            act(0)

        @pl.when(self.home)
        def _():
            self.z_copy(item, 1).wait_send()
            self.across_copy(item).wait()
            for step in range(2):
                self.plane_copy(item, 1, step).wait()


def gather_scratch(weights, count):
    if not weights:
        return []
    return [pltpu.SemaphoreType.DMA((count, 10)), pltpu.SemaphoreType.DMA((count, 10)), pltpu.SemaphoreType.DMA((max(count, len(weights)), 2))] + [
        pltpu.VMEM(w.shape, BF16) for w in weights
    ]


AHEAD = 3


def background(work, step, place):
    if place == 2:

        @pl.when(step == 7)
        def _():
            work.forward(WHOLE - 1)
            for item in range(len(work.items)):
                if item < WHOLE:
                    work.finish(item)
                else:
                    work.finish_z(item)
            work.wait_own()

        return

    for turn in range(8):
        slot = 2 * turn + place

        @pl.when(step == turn)
        def _(slot=slot):
            if slot == 0:
                work.own()
                greet((work.near, work.far, work.by_x, work.by_y))
                for item in range(AHEAD):
                    work.start_z(item)
            elif slot <= 2 * WHOLE:
                item = (slot - 1) // 2
                if slot % 2:
                    work.relay_z(item)
                    if item + AHEAD < len(work.items):
                        work.start_z(item + AHEAD)
                    if item < len(work.weights):
                        work.pass_own(item)
                else:
                    work.start_plane(item)
                    if item >= 1:
                        work.forward(item - 1)
            elif slot <= 2 * WHOLE + 2:
                work.relay_only(slot - 2 * WHOLE - 1 + WHOLE)


TILE = 512


def beside_gate(work, step):
    script = (("start_both", 0), ("start_both", 1)), (), (("forward", 0),), (("forward", 1),)
    for turn, names in enumerate(script):
        if names:

            @pl.when(step == turn)
            def _(names=names, turn=turn):
                if turn == 0:
                    greet((work.by_x, work.by_y))
                for name, item in names:
                    getattr(work, name)(item)


def gated_forward(normed, weight, part=None):
    rows, width = normed.shape
    units = weight.shape[1] // 2
    many = 0 if part is None else 1
    count = len(LAST)

    def kernel(x_ref, w_ref, *refs):
        hidden_ref, gate_ref, up_ref, refs = refs[many], refs[many + 1], refs[many + 2], refs[many + 3 :]
        step = pl.program_id(0)
        work = Gather(0, LAST, (), refs[:1], refs[1], refs[2], None) if many else None
        if work:
            beside_gate(work, step)
        gate = nn(x_ref[...], w_ref[:, :TILE])
        gate_ref[...] = gate.astype(BF16)
        up = nn(x_ref[...], w_ref[:, TILE:])
        up_ref[...] = up.astype(BF16)
        hidden_ref[...] = (gate * jax.nn.sigmoid(gate) * up).astype(BF16)
        if work:

            @pl.when(step == units // TILE - 1)
            def _():
                for item in range(count):
                    work.finish(item)

    anywhere = pl.BlockSpec(memory_space=pl.ANY)
    tile = pl.BlockSpec((rows, TILE), lambda j: (0, j))
    collective = dict(collective_id=5, has_side_effects=True) if many else {}
    extra = [] if part is None else [part]
    result = pl.pallas_call(
        kernel,
        grid=(units // TILE,),
        in_specs=[pl.BlockSpec((rows, width), lambda j: (0, 0)), pl.BlockSpec((width, 2 * TILE), lambda j: (0, j))] + [anywhere] * many,
        out_specs=[tile] * 3 + [anywhere] * many,
        out_shape=[jax.ShapeDtypeStruct((rows, units), BF16)] * 3 + [jax.ShapeDtypeStruct(p.shape, BF16) for p in extra],
        scratch_shapes=[pltpu.SemaphoreType.DMA((count, 10))] * 2 * many,
        input_output_aliases={2: 3} if many else {},
        compiler_params=pltpu.CompilerParams(vmem_limit_bytes=60 * 1024 * 1024, **collective),
    )(normed, weight, *extra)
    return result[:3], result[3:]


def gated_backward(d_out, down, gate, up, normed):
    rows, width = d_out.shape
    units = gate.shape[1]

    def kernel(d_ref, down_ref, gate_ref, up_ref, x_ref, d_gu_ref, grads_ref):
        d_hidden = nn(d_ref[...], down_ref[...])
        gate_value, up_value = gate_ref[...].astype(F32), up_ref[...].astype(F32)
        s = jax.nn.sigmoid(gate_value)
        d_gu_ref[:, :TILE] = (d_hidden * up_value * s * (1.0 + gate_value * (1.0 - s))).astype(BF16)
        d_gu_ref[:, TILE:] = (d_hidden * gate_value * s).astype(BF16)
        grads_ref[...] = tn(x_ref[...], d_gu_ref[...]).astype(BF16)

    whole = pl.BlockSpec((rows, width), lambda j: (0, 0))
    tile = pl.BlockSpec((rows, TILE), lambda j: (0, j))
    return pl.pallas_call(
        kernel,
        grid=(units // TILE,),
        in_specs=[whole, pl.BlockSpec((width, TILE), lambda j: (0, j)), tile, tile, whole],
        out_specs=[pl.BlockSpec((rows, 2 * TILE), lambda j: (0, j)), pl.BlockSpec((width, 2 * TILE), lambda j: (0, j))],
        out_shape=[jax.ShapeDtypeStruct((rows, 2 * units), BF16), jax.ShapeDtypeStruct((width, 2 * units), BF16)],
        compiler_params=pltpu.CompilerParams(vmem_limit_bytes=60 * 1024 * 1024),
        cost_estimate=pl.CostEstimate(flops=22_000_000_000, bytes_accessed=40_000_000, transcendentals=0),
    )(d_out, down, gate, up, normed)


def opening_kernel(tokens_ref, gain_ref, small_ref, wq_ref, wk_ref, wv_ref, full_ref, normed_ref, toep_ref, both_ref, send, recv, local, held0, held1, held2, extra_send, extra_recv):
    work = Gather(3, FIRST, (wq_ref, wk_ref, wv_ref), (full_ref,), send, recv, local, held0, held1, held2)
    rows = tokens_ref.shape[0]

    def extra(source, target, index, peer):
        return pltpu.make_async_remote_copy(
            src_ref=source, dst_ref=target, send_sem=extra_send.at[index], recv_sem=extra_recv.at[index], device_id=peer, device_id_type=MESH)

    far_small = extra(small_ref, both_ref.at[0], 0, work.far)
    near_small = extra(both_ref.at[0], both_ref.at[1], 1, work.near)
    normed_out = extra(normed_ref.at[0:rows], normed_ref.at[rows : 2 * rows], 2, work.core)
    work.own()
    greet((work.near, work.far, work.by_x, work.by_y, work.core))

    @work.away
    def _():
        far_small.start()

    @pl.when(work.home)
    def _():
        both_ref[0] = small_ref[...]
        near_small.start()

    for item in range(3):
        work.start_z(item)
    for start in range(0, rows, 96):
        x = tokens_ref[start : start + 96].astype(F32)
        inv = lax.rsqrt(jnp.mean(x * x, axis=-1, keepdims=True) + 1e-06)
        normed_ref[start : start + 96] = (x * inv * gain_ref[...]).astype(BF16)
    normed_out.start()

    @work.away
    def _():
        far_small.wait_recv()
        near_small.start()

    work.relay_z(0)
    work.start_plane(0)
    fill_toeplitz(both_ref, 0, toep_ref)
    work.relay_z(1)
    work.start_plane(1)
    work.forward(0)
    for weight in range(3):
        work.pass_own(weight)
    near_small.wait_recv()
    work.relay_z(2)
    work.start_plane(2)
    work.forward(1)
    fill_toeplitz(both_ref, 1, toep_ref)
    work.forward(2)
    for item in range(3):
        work.finish(item)
    work.wait_own()
    near_small.wait_send()

    @work.away
    def _():
        far_small.wait_send()

    normed_out.wait()


def opening(tokens, gain, small, weights, collective_id):
    vmem = pl.BlockSpec(memory_space=pltpu.VMEM)
    anywhere = pl.BlockSpec(memory_space=pl.ANY)
    rows, width = tokens.shape
    return pl.pallas_call(
        opening_kernel,
        in_specs=[vmem] * 3 + [anywhere] * 3,
        out_specs=[anywhere] + [vmem] * 3,
        out_shape=[
            jax.ShapeDtypeStruct((width, 2304), BF16),
            jax.ShapeDtypeStruct((2 * rows, width), BF16),
            jax.ShapeDtypeStruct((2, 2, 2, CQ * WIN, WIN), BF16),
            jax.ShapeDtypeStruct((2,) + small.shape, F32),
        ],
        scratch_shapes=gather_scratch(weights, 3) + [pltpu.SemaphoreType.DMA((3,)), pltpu.SemaphoreType.DMA((3,))],
        compiler_params=pltpu.CompilerParams(collective_id=collective_id, has_side_effects=True, vmem_limit_bytes=60 * 1024 * 1024),
    )(tokens, gain, small, *weights)


class Finish:
    def __init__(self, plan, parts, raw, outs, small, bufs, made=False):
        self.made = made
        q, c, z = lax.axis_index("plane"), lax.axis_index("core"), lax.axis_index("tensor")
        self.q, self.c = q, c
        self.home = (z // 2) == c
        self.by_x = ((q // 2) * 2 + (1 - q % 2), c, z)
        self.by_y = ((q + 2) % 4, c, z)
        self.core = (q, 1 - c, z)
        self.near = (q, c, (z // 2) * 2 + (1 - z % 2))
        self.far = (q, 1 - c, (z + 2) % 4)
        self.across = (q, c, (z + 2) % 4)
        self.plan, self.parts, self.raw, self.outs, self.small = plan, parts, raw, outs, small
        (self.near_buf, self.far_buf, self.core_buf, self.here_buf, self.raw_part, self.raw_own, self.raw_first,
         self.raw_second, self.send, self.recv, self.raw_send, self.raw_recv, self.local) = bufs[:13]
        if small is not None:
            self.small_buf, self.small_in, self.small_send, self.small_recv = bufs[13:]

    def remote(self, src, dst, sems, index, peer):
        return pltpu.make_async_remote_copy(
            src_ref=src, dst_ref=dst, send_sem=sems[0].at[index], recv_sem=sems[1].at[index], device_id=peer, device_id_type=MESH)

    def columns(self, item):
        _, first_a, first_b, size, _, _, at = self.plan[item]
        return pl.ds(first_a, size), pl.ds(first_b, size), pl.ds(at, size)

    def part(self, item):
        source = self.plan[item][0]
        if source >= 0:
            return self.parts[source]
        return self.raw.at[self.rows(self.q)] if self.made else self.raw_part

    def away(self, action):
        pl.when(jnp.logical_not(self.home))(action)

    def rows(self, owner):
        return pl.ds(pl.multiple_of(owner * 384, 128), 384)

    def raw_copies(self, item):
        cols_a, cols_b, _ = self.columns(item)
        sems = (self.raw_send, self.raw_recv)
        across = 3 - self.q
        x, y = self.by_x[0], self.by_y[0]
        remote = [
            self.remote(self.raw.at[self.rows(x), cols_a], self.raw_first.at[0, :, cols_a], sems, (item, 0), self.by_x),
            self.remote(self.raw.at[self.rows(across), cols_a], self.raw_first.at[1, :, cols_a], sems, (item, 1), self.by_x),
            self.remote(self.raw.at[self.rows(y), cols_b], self.raw_first.at[0, :, cols_b], sems, (item, 2), self.by_y),
            self.remote(self.raw.at[self.rows(across), cols_b], self.raw_first.at[1, :, cols_b], sems, (item, 3), self.by_y),
        ]
        if self.made:
            return remote, []
        return remote, [
            pltpu.make_async_copy(self.raw.at[self.rows(self.q), cols_a], self.raw_own.at[0, :, cols_a], self.local.at[item, 0]),
            pltpu.make_async_copy(self.raw.at[self.rows(y), cols_a], self.raw_own.at[1, :, cols_a], self.local.at[item, 1]),
            pltpu.make_async_copy(self.raw.at[self.rows(self.q), cols_b], self.raw_own.at[0, :, cols_b], self.local.at[item, 2]),
            pltpu.make_async_copy(self.raw.at[self.rows(x), cols_b], self.raw_own.at[1, :, cols_b], self.local.at[item, 3]),
        ]

    def raw_place(self, which, side, cols):
        if self.made:
            owner = self.q if which == 0 else (self.by_y[0], self.by_x[0])[side]
            return self.raw, (self.rows(owner), cols)
        return self.raw_own, (which, slice(None), cols)

    def raw_second_copies(self, item):
        sems = (self.raw_send, self.raw_recv)
        copies = []
        for side, cols in enumerate(self.columns(item)[:2]):
            ref, place = self.raw_place(1, side, cols)
            copies.append(self.remote(ref.at[place], self.raw_second.at[:, cols], sems, (item, 4 + side), (self.by_y, self.by_x)[side]))
        return copies

    def r1_side(self, item, side):
        for copy in self.raw_copies(item)[0][2 * side : 2 * side + 2]:
            copy.start()

    def r1(self, item):
        for group in self.raw_copies(item):
            for copy in group:
                copy.start()

    def r2(self, item):
        remote, own = self.raw_copies(item)
        for copy in own:
            copy.wait()
        for side, cols in enumerate(self.columns(item)[:2]):
            remote[2 * side + 1].wait_recv()
            ref, place = self.raw_place(1, side, cols)
            ref[place] = added(ref[place], self.raw_first[1, :, cols])
            self.raw_second_copies(item)[side].start()

    def r3(self, item):
        remote, _ = self.raw_copies(item)
        for side, cols in enumerate(self.columns(item)[:2]):
            remote[2 * side].wait_recv()
            self.raw_second_copies(item)[side].wait_recv()
            ref, place = self.raw_place(0, side, cols)
            total = ref[place].astype(F32) + self.raw_first[0, :, cols].astype(F32) + self.raw_second[:, cols].astype(F32)
            self.part(item)[:, cols] = total.astype(BF16)

    def near_copy(self, item):
        _, cols_b, at = self.columns(item)
        return self.remote(self.part(item).at[:, cols_b], self.near_buf.at[:, self.spot(item)], (self.send, self.recv), (item, 0), self.near)

    def spot(self, item):
        return pl.ds(self.plan[item][5], self.plan[item][3])

    def far_copy(self, item):
        spot = self.spot(item)
        return self.remote(self.here_buf.at[:, spot], self.far_buf.at[:, spot], (self.send, self.recv), (item, 1), self.far)

    def core_copy(self, item, relayed):
        spot = self.spot(item)
        source = self.far_buf if relayed else self.here_buf
        return self.remote(source.at[:, spot], self.core_buf.at[:, spot], (self.send, self.recv), (item, 2), self.core)

    def s1(self, item):
        self.near_copy(item).start()

    def s2(self, item):
        spot, cols_a = self.spot(item), self.columns(item)[0]
        self.near_copy(item).wait_recv()
        self.here_buf[:, spot] = added(self.part(item)[:, cols_a], self.near_buf[:, spot])

        @pl.when(self.home)
        def _():
            self.core_copy(item, False).start()

        @self.away
        def _():
            self.far_copy(item).start()

    def s3(self, item):
        @self.away
        def _():
            self.far_copy(item).wait_recv()
            self.core_copy(item, True).start()

    def plane_copies(self, item):
        out = self.outs[self.plan[item][4]]
        at, spot = self.columns(item)[2], self.spot(item)
        sems = (self.send, self.recv)
        half = self.c * 192

        def rows(owner, first, size):
            return pl.ds(pl.multiple_of(owner * 384 + half + first, 32), size)

        mine = self.core_buf.at[pl.ds(pl.multiple_of(half, 32), 192), spot]
        x, y, across = self.by_x[0], self.by_y[0], 3 - self.q
        own = out.at[rows(self.q, 0, 192), at]
        top, low = out.at[rows(x, 0, 96), at], out.at[rows(y, 96, 96), at]
        return [
            self.remote(mine, own, sems, (item, 3), self.by_x),
            self.remote(mine, own, sems, (item, 4), self.by_y),
            self.remote(top, top, sems, (item, 5), self.by_y),
            self.remote(low, low, sems, (item, 6), self.by_x),
        ] + [
            self.remote(out.at[rows(o, 0, 192), at], out.at[rows(o, 0, 192), at], sems, (item, 7 + i), self.core)
            for i, o in enumerate((x, y, across))
        ]

    def own_copy(self, item):
        out = self.outs[self.plan[item][4]]
        rows = pl.ds(pl.multiple_of(self.q * 384, 128), 384)
        return pltpu.make_async_copy(self.core_buf.at[:, self.spot(item)], out.at[rows, self.columns(item)[2]], self.local.at[item, 4])

    def s4(self, item):
        spot = self.spot(item)

        @pl.when(self.home)
        def _():
            self.core_copy(item, False).wait_recv()
            self.core_buf[:, spot] = added(self.here_buf[:, spot], self.core_buf[:, spot])

        @self.away
        def _():
            self.core_copy(item, True).wait_recv()
            self.core_buf[:, spot] = added(self.far_buf[:, spot], self.core_buf[:, spot])

        self.own_copy(item).start()
        copies = self.plane_copies(item)
        copies[0].start()
        copies[1].start()

    def s5(self, item):
        copies = self.plane_copies(item)
        copies[0].wait_recv()
        copies[2].start()
        copies[4].start()
        copies[1].wait_recv()
        copies[3].start()
        copies[5].start()

    def s6(self, item):
        copies = self.plane_copies(item)
        copies[2].wait_recv()
        copies[3].wait_recv()
        copies[6].start()

    def s7(self, item):
        copies = self.plane_copies(item)
        self.own_copy(item).wait()
        for copy in copies[4:]:
            copy.wait_recv()
        for copy in copies:
            copy.wait_send()
        self.near_copy(item).wait_send()

        @pl.when(self.home)
        def _():
            self.core_copy(item, False).wait_send()

        @self.away
        def _():
            self.core_copy(item, True).wait_send()
            self.far_copy(item).wait_send()

        if self.plan[item][0] < 0:
            for copy in self.raw_copies(item)[0] + self.raw_second_copies(item):
                copy.wait_send()

    def small_copy(self, turn):
        peer = (self.core, self.by_x, self.by_y, self.near, self.across)[turn]
        return self.remote(self.small_buf.at[turn], self.small_in.at[turn], (self.small_send, self.small_recv), turn, peer)

    def small_start(self):
        self.small_copy(0).start()

    def small_next(self, turn):
        self.small_copy(turn).wait_recv()
        self.small_buf[turn + 1] = self.small_buf[turn] + self.small_in[turn]
        if turn < 4:
            self.small_copy(turn + 1).start()

    def small_done(self, out):
        for turn in range(5):
            self.small_copy(turn).wait_send()
        out[...] = self.small_buf[5]


def added(left, right):
    return (left.astype(F32) + right.astype(F32)).astype(BF16)


FINISH = (
    (0, 0, 2048, 512, 0, 0, 0),
    (0, 512, 2560, 512, 1, 512, 0),
    (0, 1024, 3072, 512, 0, 1024, 512),
    (0, 1536, 3584, 512, 1, 1536, 512),
    (-1, 0, 1152, 384, 2, 2048, 0),
    (-1, 384, 1536, 384, 2, 2432, 384),
    (-1, 768, 1920, 384, 2, 2816, 768),
)
LONE = ((-1, 0, 384, 384, 0, 0, 0),)
BESIDE = (
    (0, 0, 1024, 512, 0, 0, 0),
    (0, 512, 1536, 512, 0, 512, 512),
)
BESIDE_STEPS = (
    (("greet", 0), ("s1", 0), ("s1", 1)),
    (),
    (("s2", 0),),
    (("s2", 1),),
    (("s3", 0),),
    (("s3", 1),),
    (("s4", 0),),
    (("s4", 1),),
    (),
    (),
    (("s5", 0),),
    (("s5", 1),),
    (),
    (("s6", 0),),
    (("s6", 1),),
)


def finish_scratch(plan, raw_width, made=False):
    count, width = len(plan), sum(item[3] for item in plan)
    return (
        [pltpu.VMEM((384, width), BF16)] * 4
        + [pltpu.VMEM((384, 128 if made else raw_width), BF16)]
        + [pltpu.VMEM((2, 384, 128 if made else raw_width), BF16), pltpu.VMEM((2, 384, raw_width), BF16)]
        + [pltpu.VMEM((384, raw_width), BF16)]
        + [pltpu.SemaphoreType.DMA((count, 10))] * 2
        + [pltpu.SemaphoreType.DMA((count, 6))] * 2
        + [pltpu.SemaphoreType.DMA((count, 5))]
    )


def beside(work, step, place):
    if place == 2:

        @pl.when(step == 7)
        def _():
            for item in range(len(work.plan)):
                work.s7(item)

        return

    for slot, names in enumerate(BESIDE_STEPS):
        if slot % 2 == place:

            @pl.when(step == slot // 2)
            def _(names=names):
                for name, item in names:
                    if name == "greet":
                        greet((work.near, work.far, work.by_x, work.by_y, work.core))
                    else:
                        getattr(work, name)(item)


def finish_kernel(
    small, gu, out, normed, d_qkv, weight, tokens, gain, d_hidden, small_out, d_input, o_gate, o_up, o_qkv, o_out,
    made, partner, arrived, loaded, load_sem, hidden_buf, tokens_buf, hidden_sem, core_send, core_recv, *bufs,
):
    lone = Finish(LONE, (), out, (o_out,), None, bufs[-13:])
    work = Finish(FINISH, (gu,), made, (o_gate, o_up, o_qkv), small, bufs[:-13], True)
    rows = tokens.shape[0]

    def load(part):
        return pltpu.make_async_copy(weight.at[384 * part : 384 * (part + 1)], loaded.at[part % 2], load_sem.at[part % 2])

    def exchange(part):
        cols = pl.ds(384 * part, 384)
        return work.remote(partner.at[:, cols], arrived.at[:, cols], (core_send, core_recv), part, work.core)

    def load_hidden(part):
        span = pl.ds(64 * part, 64)
        return (
            pltpu.make_async_copy(d_hidden.at[span], hidden_buf.at[part % 2], hidden_sem.at[0, part % 2]),
            pltpu.make_async_copy(tokens.at[span], tokens_buf.at[part % 2], hidden_sem.at[1, part % 2]),
        )

    load(0).start()
    load(1).start()
    for copy in load_hidden(0):
        copy.start()
    greet((work.near, work.far, work.by_x, work.by_y, work.core, work.across))
    lone.r1(0)
    work.s1(0)
    work.s1(1)

    def make(side, owner):
        cols = slice(1152 * side, 1152 * (side + 1))
        made[work.rows(owner), cols] = tn(normed[:, work.rows(owner)], d_qkv[:, cols]).astype(BF16)

    across = 3 - work.q
    for side, owners in enumerate(((across, work.by_x[0]), (across, work.by_y[0]))):
        for owner in owners:
            make(side, owner)
        for item in (4, 5, 6):
            work.r1_side(item, side)
    work.s2(0)
    work.s1(2)
    lone.r2(0)
    make(0, work.by_y[0])
    work.s2(1)
    work.s1(3)
    make(1, work.by_x[0])
    work.s3(0)
    make(0, work.q)
    work.s2(2)
    work.s3(1)
    make(1, work.q)
    work.r2(4)
    lone.r3(0)
    lone.s1(0)
    work.s4(0)

    def back(part):
        cols = slice(384 * part, 384 * (part + 1))
        load(part).wait()
        both = nt(d_qkv[...], loaded[part % 2])
        d_input[:, cols] = both[:rows]
        partner[:, cols] = both[rows:].astype(BF16)
        if part < 2:
            load(part + 2).start()
        exchange(part).start()

    back(0)
    work.r2(5)
    work.s2(3)
    work.s4(1)
    back(1)
    work.r2(6)
    work.r3(4)
    work.s1(4)
    work.s3(2)
    work.s5(0)
    back(2)
    lone.s2(0)
    work.r3(5)
    work.s1(5)
    work.s3(3)
    work.s4(2)
    work.s5(1)
    back(3)
    work.s2(4)
    work.r3(6)
    work.s1(6)
    work.s4(3)
    work.s6(0)
    for part in range(4):
        exchange(part).wait_recv()
    gain_sum = jnp.zeros((1, tokens.shape[1]), F32)
    for part in range(rows // 64):
        span = slice(64 * part, 64 * (part + 1))
        if part + 1 < rows // 64:
            for copy in load_hidden(part + 1):
                copy.start()
        for copy in load_hidden(part):
            copy.wait()
        x = tokens_buf[part % 2].astype(F32)
        inv = lax.rsqrt(jnp.mean(x * x, axis=-1, keepdims=True) + 1e-06)
        d_normed = d_input[span] + arrived[span].astype(F32)
        scaled = d_normed * gain[...]
        gain_sum = gain_sum + jnp.sum(d_normed * x * inv, axis=0, keepdims=True)
        d_input[span] = hidden_buf[part % 2] + inv * scaled - x * inv**3 * jnp.mean(scaled * x, axis=-1, keepdims=True)
    work.small_buf[0] = small[...]
    work.small_buf[0, 0:1] = gain_sum
    work.small_start()
    script = (
        ("s3", 4), ("s2", 5), ("s3", 7), ("s6", 1), ("s5", 2), ("m", 0),
        ("s4", 4), ("s3", 5), ("s2", 6), ("s4", 7), ("s5", 3), ("s6", 2), ("m", 1),
        ("s5", 4), ("s4", 5), ("s3", 6), ("s5", 7), ("s6", 3), ("m", 2),
        ("s6", 4), ("s5", 5), ("s4", 6), ("s6", 7), ("m", 3), ("s6", 5), ("s5", 6), ("m", 4), ("s6", 6),
    )
    for name, item in script:
        if name == "m":
            work.small_next(item)
        elif item == 7:
            getattr(lone, name)(0)
        else:
            getattr(work, name)(item)
    for item in range(len(FINISH)):
        work.s7(item)
    lone.s7(0)
    for part in range(4):
        exchange(part).wait_send()
    work.small_done(small_out)


def finish_gradients(small, gu, out, normed, d_qkv, weight, tokens, gain, d_hidden, collective_id):
    vmem = pl.BlockSpec(memory_space=pltpu.VMEM)
    anywhere = pl.BlockSpec(memory_space=pl.ANY)
    rows, width = tokens.shape
    return pl.pallas_call(
        finish_kernel,
        in_specs=[vmem] * 2 + [anywhere] + [vmem] * 2 + [anywhere] * 2 + [vmem] + [anywhere],
        out_specs=[vmem] * 2 + [anywhere] * 4,
        out_shape=[jax.ShapeDtypeStruct(small.shape, F32), jax.ShapeDtypeStruct((rows, width), F32)]
        + [jax.ShapeDtypeStruct((1536, n), BF16) for n in (1024, 1024, 1152, 384)],
        scratch_shapes=[
            pltpu.VMEM((1536, 2304), BF16),
            pltpu.VMEM((rows, width), BF16),
            pltpu.VMEM((rows, width), BF16),
            pltpu.VMEM((2, 384, 2304), BF16),
            pltpu.SemaphoreType.DMA((2,)),
            pltpu.VMEM((2, 64, width), F32),
            pltpu.VMEM((2, 64, width), BF16),
            pltpu.SemaphoreType.DMA((2, 2)),
            pltpu.SemaphoreType.DMA((4,)),
            pltpu.SemaphoreType.DMA((4,)),
        ]
        + finish_scratch(FINISH, 2304, True)
        + [pltpu.VMEM((6,) + small.shape, F32), pltpu.VMEM((5,) + small.shape, F32)]
        + [pltpu.SemaphoreType.DMA((5,))] * 2
        + finish_scratch(LONE, 768),
        compiler_params=pltpu.CompilerParams(collective_id=collective_id, has_side_effects=True, vmem_limit_bytes=60 * 1024 * 1024),
    )(small, gu, out, normed, d_qkv, weight, tokens, gain, d_hidden)


def rows_dot(lhs, rhs):
    return tn(lhs, rhs).astype(BF16)


def toeplitz_alone(both):
    def kernel(rows_ref, out_ref):
        fill_toeplitz(rows_ref, 0, out_ref)
        fill_toeplitz(rows_ref, 1, out_ref)

    return pl.pallas_call(
        kernel,
        out_shape=jax.ShapeDtypeStruct((2, 2, 2, CQ * WIN, WIN), BF16),
        compiler_params=pltpu.CompilerParams(vmem_limit_bytes=60 * 1024 * 1024),
    )(both)


def make_local(planes, tensors):
    every = ("plane", "core", "tensor")
    sides = [(c, z) for c in range(2) for z in range(tensors)]

    def spot(q, c, z):
        return (q * 2 + c) * tensors + z

    def is_home(c, z):
        return z // 2 == c

    far_pairs = [(spot(q, c, z), spot(q, 1 - c, z ^ 2)) for q in range(planes) for c, z in sides if not is_home(c, z)]
    near_pairs = [
        (spot(q, c, z), spot(q, c, z ^ 1) if is_home(c, z) else spot(q, 1 - c, z ^ 3)) for q in range(planes) for c, z in sides
    ]

    def over_core(value):
        return lax.ppermute(value, "core", [(0, 1), (1, 0)])

    def first_from(value):
        return lax.ppermute(value, every, far_pairs)

    def second_from(value):
        return lax.ppermute(value, every, near_pairs)

    square = planes == 4

    def local(
        tokens, teacher, valid_mask, norm1_gain, w_query, w_key, w_value, conv_weight, head_mix, gn_gain, w_out, norm2_gain,
        w_gate, w_up, w_down,
    ):
        q, c, z = lax.axis_index("plane"), lax.axis_index("core"), lax.axis_index("tensor")
        own_rows, width = tokens.shape
        home = (z // 2) == c
        wide = w_query.shape[1]

        def collect(weights):
            pairs = []
            for weight in weights:
                pairs.append(jnp.where(home, weight, first_from(weight)))
                pairs.append(second_from(weight))
            return pairs

        fused = square and tensors == 4
        units = w_gate.shape[1]

        def plane_sum(grads):
            return lax.psum_scatter(grads, "plane", scatter_dimension=0, tiled=True)

        def reduce(first, second):
            here = added(first, lax.ppermute(second, "tensor", [(i, i ^ 1) for i in range(tensors)]))
            here = jnp.where(home, here, first_from(here))
            total = added(here, over_core(here))
            return lax.all_gather(total, "plane", axis=0, tiled=True)

        small = jnp.concatenate(
            [
                band_rows(conv_weight),
                jnp.pad(head_mix.reshape(1, -1), ((0, 0), (0, WIN - head_mix.size))),
                jnp.pad(gn_gain.reshape(1, -1), ((0, 0), (0, 2 * WIN - wide))).reshape(2, WIN),
                jnp.zeros((5, WIN), F32),
            ]
        )
        conv_size, mix_size = conv_weight.size, head_mix.size
        small_size = conv_size + mix_size + wide
        gain_one, gain_two = norm1_gain, norm2_gain
        own_valid = lax.dynamic_slice_in_dim(valid_mask, z * own_rows, own_rows, 0)
        jj = key_positions(jnp.concatenate([own_valid, over_core(own_valid)]))

        def with_partner(value):
            return jnp.concatenate([value, over_core(value)], axis=0)

        def summed(left, right):
            sent = over_core(nt(left[own_rows:], right).astype(BF16))
            return nt(left[:own_rows], right) + sent.astype(F32)

        inputs = tokens.astype(F32)
        inv_one = lax.rsqrt(jnp.mean(inputs * inputs, axis=-1, keepdims=True) + 1e-06)
        if fused:
            qkv_weight, normed_one, toep, both_small = opening(tokens, gain_one[None], small, [w_query, w_key, w_value], 1)
            gather = ([w_out, w_gate, w_up, w_down], (768, 4096, 2048), len(LATER), dict(collective_id=3, has_side_effects=True))
        else:
            both_small = jnp.stack([jnp.where(home, small, first_from(small)), second_from(small)])
            toep = toeplitz_alone(both_small)
            normed_one = with_partner((inputs * inv_one * gain_one).astype(BF16))
            parts = collect([w_query, w_key, w_value])
            qkv_weight = jnp.concatenate(parts[0::2] + parts[1::2], axis=1)
            gather = None
        mix = both_small[:, 24, :mix_size].reshape(-1)
        gains = jnp.broadcast_to(both_small[:, 25:27].reshape(2, 1, 2 * WIN)[:, :, :wide], (2, 8, wide))
        qkv = nn(normed_one, qkv_weight).astype(BF16)
        heads_out, saved, later = attention_forward(mix, qkv, toep, gains, jj, gather)
        if fused:
            out_weight, gu_weight, down_weight = later
        else:
            out_weight = jnp.concatenate(collect([w_out]), axis=1)
            pieces = collect([w_gate, w_up])
            pieces = [pieces[2 * kind + side][:, start : start + TILE] for side in range(2) for start in range(0, units, TILE) for kind in range(2)]
            gu_weight = jnp.concatenate(pieces, axis=1)
        hidden_in = inputs + summed(heads_out, out_weight)
        inv_two = lax.rsqrt(jnp.mean(hidden_in * hidden_in, axis=-1, keepdims=True) + 1e-06)
        normed_two = with_partner((hidden_in * inv_two * gain_two).astype(BF16))
        (hidden, gate, up), last = gated_forward(normed_two, gu_weight, down_weight if fused else None)
        down_weight = last[0] if fused else jnp.concatenate(collect([w_down]), axis=1)
        final_rows = hidden_in + summed(hidden, down_weight)
        output = final_rows.astype(BF16)
        own_mask = own_valid.astype(F32)
        error = own_mask[:, None] * (final_rows - teacher.astype(F32))
        squared_sum = jnp.sum(error * error)
        count_sum = jnp.sum(own_mask)

        d_all = with_partner(error.astype(BF16))
        down_grads = rows_dot(d_all, hidden)
        down_grads, d_all = lax.optimization_barrier((down_grads, d_all))
        down_part = plane_sum(down_grads)
        d_gu, gu_grads = gated_backward(d_all, down_weight, gate, up, normed_two)
        gu_grads, d_gu = lax.optimization_barrier((gu_grads, d_gu))
        gu_part = plane_sum(gu_grads)
        d_normed_two = summed(d_gu, gu_weight)
        scaled_two = d_normed_two * gain_two
        grad_gain_two = jnp.sum(d_normed_two * hidden_in * inv_two, axis=0)
        d_hidden_in = (
            error + inv_two * scaled_two - hidden_in * inv_two**3 * jnp.mean(scaled_two * hidden_in, axis=-1, keepdims=True)
        )
        d_attn = with_partner(d_hidden_in.astype(BF16))
        out_grads = rows_dot(d_attn, heads_out)
        out_grads, d_attn = lax.optimization_barrier((out_grads, d_attn))
        d_normed = nn(d_attn, out_weight)
        d_normed, down_part = lax.optimization_barrier((d_normed, down_part))
        (d_qkv, ggn, gmix, gconv), done = attention_backward(
            mix, qkv, toep, gains, jj, d_normed, saved, (down_part,) if fused else None
        )
        small_grads = jnp.concatenate([conv_grads(gconv), mix_grads(gmix), ggn[:, 0]], axis=1)
        table = jnp.zeros((tensors, small_size), F32)
        table = lax.dynamic_update_slice(table, small_grads[:1], (2 * c + z % 2, 0))
        table = lax.dynamic_update_slice(table, small_grads[1:], (2 * c + 1 - z % 2, 0))
        table = jnp.pad(table.reshape(-1), (0, 4 * width - table.size)).reshape(4, width)
        last = jnp.pad(jnp.stack([squared_sum, count_sum]), (0, 2 * width - 2)).reshape(2, width)
        packed = jnp.concatenate([jnp.zeros((1, width), F32), grad_gain_two[None], table, last])
        if fused:
            packed, grad_input, sum_gate, sum_up, sum_qkv, sum_out = finish_gradients(
                packed, gu_part, out_grads, normed_one, d_qkv, qkv_weight, tokens, gain_one[None], d_hidden_in, 2
            )
            sums = [done[0], sum_gate, sum_up, sum_out, sum_qkv]
        else:
            qkv_grads = rows_dot(normed_one, d_qkv)
            d_normed_one = summed(d_qkv, qkv_weight)
            scaled_one = d_normed_one * gain_one
            packed = packed.at[0].set(jnp.sum(d_normed_one * inputs * inv_one, axis=0))
            grad_input = (
                d_hidden_in + inv_one * scaled_one - inputs * inv_one**3 * jnp.mean(scaled_one * inputs, axis=-1, keepdims=True)
            )
            packed = lax.psum(packed, every)
            out_part, qkv_part = plane_sum(out_grads), plane_sum(qkv_grads)
            sums = [reduce(part[:, : part.shape[1] // 2], part[:, part.shape[1] // 2 :]) for part in (down_part, out_part, qkv_part)]
            sum_gu = reduce(gu_part[:, : 2 * units], gu_part[:, 2 * units :])
            for kind in range(2):
                places = range(kind * TILE, 2 * units, 2 * TILE)
                sums.insert(1 + kind, jnp.concatenate([sum_gu[:, i : i + TILE] for i in places], axis=1))
        grad_down, grad_gate, grad_up, grad_out, grad_qkv = [value.astype(F32) for value in sums]
        small_sum = lax.dynamic_slice_in_dim(packed[2:6].reshape(-1), z * small_size, small_size, 0)
        gain_slice = width // tensors
        gain_one_out = lax.dynamic_slice_in_dim(packed[0], z * gain_slice, gain_slice, 0)
        gain_two_out = lax.dynamic_slice_in_dim(packed[1], z * gain_slice, gain_slice, 0)
        loss = packed[6, 0] / (packed[6, 1] * width)
        return (
            output,
            loss,
            grad_input,
            gain_one_out,
            grad_qkv[:, :wide],
            grad_qkv[:, wide : 2 * wide],
            grad_qkv[:, 2 * wide :],
            small_sum[:conv_size].reshape(conv_weight.shape),
            small_sum[conv_size : conv_size + mix_size].reshape(head_mix.shape),
            small_sum[conv_size + mix_size :].reshape(gn_gain.shape),
            grad_out,
            gain_two_out,
            grad_gate,
            grad_up,
            grad_down,
        )

    return local


def solution(mesh):
    tensors = mesh.shape["tensor"]
    planes = mesh.shape["dp"] // 2
    inner = jax.sharding.Mesh(mesh.devices.reshape(planes, 2, tensors), ("plane", "core", "tensor"))
    rows = P(("plane", "core", "tensor"), None)
    columns = P(None, "tensor")
    cube = P("tensor", None, None)
    return jax.shard_map(
        make_local(planes, tensors),
        mesh=inner,
        in_specs=(
            rows, rows, P(("plane", "core")), P(), columns, columns, columns, cube, cube, P("tensor", None), columns, P(),
            columns, columns, columns,
        ),
        out_specs=(
            rows, P(), rows, P("tensor"), columns, columns, columns, cube, cube, P("tensor", None), columns, P("tensor"),
            columns, columns, columns,
        ),
        check_vma=False,
    )
```

```python
import math
import jax
import jax.numpy as jnp
from jax import lax
from jax.experimental import pallas as pl
from jax.experimental.pallas import tpu as pltpu
from jax.sharding import PartitionSpec as P

HD = 96
CQ = 6
CK = 11
TRUNK = 192
SEG = 32
TREE = 576
WIN = 256
FAM = 96
EXT = 680
F32 = jnp.float32
BF16 = jnp.bfloat16


def segments():
    rows = [(0, TRUNK, 0, 0, -1)]
    for b in range(4):
        base, ext = TRUNK + FAM * b, 200 + 120 * b
        rows.append((TRUNK + SEG * b, SEG, base, ext, TRUNK - 8))
        for c in range(2):
            rows.append((320 + 64 * b + SEG * c, SEG, base + SEG * (c + 1), ext + 40 * (c + 1), TRUNK + SEG * b + SEG - 8))
    return rows


SEGS = segments()


def nn(a, b):
    return lax.dot_general(a, b, (((1,), (0,)), ((), ())), preferred_element_type=F32)


def nt(a, b):
    return lax.dot_general(a, b, (((1,), (1,)), ((), ())), preferred_element_type=F32)


def tn(a, b):
    return lax.dot_general(a, b, (((0,), (0,)), ((), ())), preferred_element_type=F32)


def head_masks(g):
    lane = lax.broadcasted_iota(jnp.int32, (1, WIN), 1)
    first = 64 * g
    m0 = (lane >= first) & (lane < first + HD)
    m1 = (lane >= first + HD) & (lane < first + 2 * HD)
    return m0, m1, lane >= first


def fill_distance(jj_ref, dist_ref):
    for index, (_, size, row, _, _) in enumerate(SEGS):
        start = 0 if index == 0 else (TRUNK if (index - 1) % 3 == 0 else TRUNK + SEG)
        pos = lax.broadcasted_iota(jnp.int32, (size, WIN), 0) + start
        dist_ref[row : row + size] = pos - jj_ref[index : index + 1, :]


def path_rows(ref, b, c, column):
    if b is None:
        parts = [ref[0:TRUNK, pl.ds(column, WIN)], ref[TRUNK : TRUNK + SEG, pl.ds(column, WIN)], ref[320 : 320 + SEG, pl.ds(column, WIN)]]
    else:
        parts = [
            ref[0:TRUNK, pl.ds(column, WIN)],
            ref[pl.ds(pl.multiple_of(TRUNK + SEG * b, SEG), SEG), pl.ds(column, WIN)],
            ref[pl.ds(pl.multiple_of(320 + 64 * b + SEG * c, SEG), SEG), pl.ds(column, WIN)],
        ]
    return jnp.concatenate(parts, axis=0)


def fam_rows(b, c):
    base = TRUNK + FAM * b
    return (pl.ds(pl.multiple_of(base, 32), 64), 64) if c == 0 else (pl.ds(pl.multiple_of(base + 64, 32), SEG), SEG)


def group_norm(ho, m0, m1):
    def stat(v):
        s0 = jnp.sum(jnp.where(m0, v, 0.0), axis=-1, keepdims=True) * (1.0 / HD)
        s1 = jnp.sum(jnp.where(m1, v, 0.0), axis=-1, keepdims=True) * (1.0 / HD)
        return jnp.where(m0, s0, s1)

    centered = jnp.where(m0 | m1, ho - stat(ho), 0.0)
    inv = lax.rsqrt(stat(centered * centered) + 1e-05)
    return centered * inv, inv, stat


def fwd_kernel(
    hook, mix_ref, normed_ref, weight_ref, t_ref, gn_ref, jj_ref, nh_ref, att_ref, pre_ref, qs_ref, ho_ref, qkv_ref, dist_ref, qx_ref, mx_ref
):
    side, t, g = pl.program_id(0), pl.program_id(1), pl.program_id(2)
    step = (side * 2 + t) * 2 + g
    mix0 = 8 * side + 4 * g
    hook(step, 0)

    @pl.when(g == 0)
    def _():
        for part in range(3):
            cols = slice(384 * part, 384 * (part + 1))
            qkv_ref[:, cols] = nn(normed_ref[...], weight_ref[:, cols]).astype(BF16)

    w0 = pl.multiple_of(g * 128, 128)
    m0, m1, from_first = head_masks(g)
    m0f, m1f = m0.astype(F32), m1.astype(F32)
    fill_distance(jj_ref, dist_ref)
    qx_ref[0:8] = jnp.zeros((8, WIN), F32)
    for token, size, _, ext, parent in SEGS:
        if parent >= 0:
            low = qkv_ref[parent - 8 : parent + 8, pl.ds(w0, WIN)].astype(F32)
            qx_ref[ext : ext + 8] = low[8:16]
        qx_ref[ext + 8 : ext + 8 + size] = qkv_ref[token : token + size, pl.ds(w0, WIN)].astype(F32)
    for a in range(CQ):
        for _, size, row, ext, _ in SEGS:
            part = qx_ref[ext + 8 - a : ext + 8 - a + size]
            qs_ref[0, a, row : row + size] = (part * m0f).astype(BF16)
            qs_ref[1, a, row : row + size] = (part * m1f).astype(BF16)
    k0, v0 = w0 + 384, w0 + 768
    k_trunk = path_rows(qkv_ref, None, 0, k0)

    def trunk_scores(a, carry):
        scores = nt(qs_ref[:, a, 0:TRUNK].reshape(2 * TRUNK, WIN), k_trunk).reshape(2, TRUNK, WIN)
        kept = dist_ref[0:TRUNK] >= a
        for e in range(2):
            pre_ref[e, 0:TRUNK, pl.ds(pl.multiple_of(a * WIN, WIN), WIN)] = jnp.where(kept, scores[e], 0.0).astype(BF16)
        return carry

    lax.fori_loop(0, CQ, trunk_scores, 0)

    def fam_scores(b, carry):
        for c in range(2):
            rows, size = fam_rows(b, c)
            keys = path_rows(qkv_ref, b, c, k0)
            scores = nt(qs_ref[:, :, rows].reshape(2 * CQ * size, WIN), keys).reshape(2, CQ, size, WIN)
            dist = dist_ref[rows]
            for a in range(CQ):
                kept = dist >= a
                for e in range(2):
                    pre_ref[e, rows, a * WIN : (a + 1) * WIN] = jnp.where(kept, scores[e, a], 0.0).astype(BF16)
        return carry

    lax.fori_loop(0, 4, fam_scores, 0)
    hook(step, 1)
    for e in range(2):
        conv = nn(pre_ref[e], t_ref[e])
        logits = jnp.where(dist_ref[...] >= 0, conv, -1e30)
        shifted = jnp.exp(logits - jnp.max(logits, axis=-1, keepdims=True))
        att_ref[e] = shifted / jnp.sum(shifted, axis=-1, keepdims=True)
    for c in range(2):
        mx_ref[c] = (mix_ref[mix0 + 2 * c] * att_ref[0] + mix_ref[mix0 + 2 * c + 1] * att_ref[1]).astype(BF16)

    def put_out(rows, size, values):
        out = nn(mx_ref[:, rows].reshape(2 * size, WIN), values).reshape(2, size, WIN)
        ho_ref[rows] = jnp.where(m0, out[0], jnp.where(m1, out[1], 0.0))

    put_out(pl.ds(0, TRUNK), TRUNK, path_rows(qkv_ref, None, 0, v0))

    def fam_out(b, carry):
        for c in range(2):
            rows, size = fam_rows(b, c)
            put_out(rows, size, path_rows(qkv_ref, b, c, v0))
        return carry

    lax.fori_loop(0, 4, fam_out, 0)
    gain = gn_ref[0:1, pl.ds(w0, WIN)]
    for token, size, row, _, _ in SEGS:
        unit, _, _ = group_norm(ho_ref[row : row + size], m0, m1)
        old = nh_ref[token : token + size, pl.ds(w0, WIN)].astype(F32)
        nh_ref[token : token + size, pl.ds(w0, WIN)] = jnp.where(from_first, unit * gain, old).astype(BF16)
    hook(step, 2)


def bwd_kernel(
    hook, mix_ref, qkv_ref, t_ref, gn_ref, jj_ref, dn_ref, att_ref, pre_ref, qs_ref, ho_ref,
    dqkv_ref, ggn_ref, gmix_ref, gconv_ref,
    dist_ref, dh_ref, mx_ref, dm_ref, dc_ref, es_ref, dqx_ref, dk_ref, dv_ref,
):
    side, t, g = pl.program_id(0), pl.program_id(1), pl.program_id(2)
    mix0 = 8 * side + 4 * g
    step = (side * 2 + t) * 2 + g
    hook(step, 0)
    w0 = pl.multiple_of(g * 128, 128)
    m0, m1, from_first = head_masks(g)
    both = m0 | m1
    fill_distance(jj_ref, dist_ref)
    gain = gn_ref[0:1, pl.ds(w0, WIN)]
    gn_sum = jnp.zeros((1, WIN), F32)
    for token, size, row, _, _ in SEGS:
        unit, inv, stat = group_norm(ho_ref[row : row + size], m0, m1)
        dn = jnp.where(both, dn_ref[token : token + size, pl.ds(w0, WIN)].astype(F32), 0.0)
        gn_sum = gn_sum + jnp.sum(dn * unit, axis=0, keepdims=True)
        scaled = dn * gain
        d_head = inv * (scaled - stat(scaled) - unit * stat(scaled * unit))
        dh_ref[0, row : row + size] = jnp.where(m0, d_head, 0.0).astype(BF16)
        dh_ref[1, row : row + size] = jnp.where(m1, d_head, 0.0).astype(BF16)

    @pl.when((t == 0) & (g == 0))
    def _():
        ggn_ref[...] = jnp.zeros_like(ggn_ref)

    ggn_ref[0:1, pl.ds(w0, WIN)] += gn_sum
    k0, v0 = w0 + 384, w0 + 768
    for c in range(2):
        mx_ref[c] = (mix_ref[mix0 + 2 * c] * att_ref[0] + mix_ref[mix0 + 2 * c + 1] * att_ref[1]).astype(BF16)

    def add_keys(acc_ref, b, c, grads):
        acc_ref[0:TRUNK] += grads[0:TRUNK]
        branch = pl.ds(pl.multiple_of(TRUNK + SEG * b, SEG), SEG)
        if c == 0:
            acc_ref[branch] = grads[TRUNK : TRUNK + SEG]
        else:
            acc_ref[branch] += grads[TRUNK : TRUNK + SEG]
        acc_ref[pl.ds(pl.multiple_of(320 + 64 * b + SEG * c, SEG), SEG)] = grads[TRUNK + SEG :]

    def value_part(rows, size, values):
        heads = dh_ref[:, rows].reshape(2 * size, WIN)
        dm_ref[:, rows] = nt(heads, values).reshape(2, size, WIN)
        return tn(mx_ref[:, rows].reshape(2 * size, WIN), heads)

    dv_ref[0:TRUNK] = value_part(pl.ds(0, TRUNK), TRUNK, path_rows(qkv_ref, None, 0, v0))[0:TRUNK]

    def fam_values(b, carry):
        for c in range(2):
            rows, size = fam_rows(b, c)
            add_keys(dv_ref, b, c, value_part(rows, size, path_rows(qkv_ref, b, c, v0)))
        return carry

    lax.fori_loop(0, 4, fam_values, 0)

    def soft_part(block, sums):
        rows = pl.ds(pl.multiple_of(block * FAM, 32), FAM)
        dm = [dm_ref[c, rows] for c in range(2)]
        att = [att_ref[e, rows] for e in range(2)]
        out = []
        for e in range(2):
            d_att = mix_ref[mix0 + e] * dm[0] + mix_ref[mix0 + 2 + e] * dm[1]
            d_conv = att[e] * (d_att - jnp.sum(d_att * att[e], axis=-1, keepdims=True))
            dc_ref[e, rows] = d_conv.astype(BF16)
        for c in range(2):
            for e in range(2):
                out.append(sums[2 * c + e] + jnp.sum(dm[c] * att[e], axis=0, keepdims=True))
        return tuple(out)

    mix_sums = lax.fori_loop(0, 6, soft_part, tuple(jnp.zeros((1, WIN), F32) for _ in range(4)))
    gmix_ref[...] = jnp.zeros_like(gmix_ref)
    gconv_ref[...] = jnp.zeros_like(gconv_ref)
    for index in range(4):
        gmix_ref[index : index + 1] = mix_sums[index]
    mirror = lax.broadcasted_iota(jnp.int32, (WIN, WIN), 0) + lax.broadcasted_iota(jnp.int32, (WIN, WIN), 1) - (WIN - 1)
    band = jnp.abs(mirror) <= CK // 2
    hook(step, 1)
    flip = jnp.where(mirror == 0, 1.0, 0.0).astype(BF16)
    for e in range(2):
        flipped = nn(dc_ref[e], flip).astype(BF16)
        for a in range(CQ):
            cols = slice(a * WIN, (a + 1) * WIN)
            products = jnp.where(band, tn(flipped, pre_ref[e, :, cols]), 0.0)
            rolled = pltpu.roll(products, 24, 1, stride=1, stride_axis=0)
            gconv_ref[e, a : a + 1] = jnp.sum(rolled, axis=0, keepdims=True)
            grads = nt(dc_ref[e], t_ref[e, cols, :])
            es_ref[e, a] = jnp.where(dist_ref[...] >= a, grads, 0.0).astype(BF16)

    def score_part(rows, size, keys):
        grads = es_ref[:, :, rows].reshape(2 * CQ * size, WIN)
        back = nn(grads, keys).reshape(2, CQ, size, WIN)
        d_query = [jnp.where(m0, back[0, a], jnp.where(m1, back[1, a], 0.0)) for a in range(CQ)]
        return d_query, tn(grads, qs_ref[:, :, rows].reshape(2 * CQ * size, WIN))

    def shifted_sum(parts, start, size):
        zeros = jnp.zeros((8, WIN), F32)
        total = None
        for a in range(CQ):
            padded = jnp.concatenate([zeros, parts[a][start : start + size]], axis=0)
            if a:
                padded = pltpu.roll(padded, size + 8 - a, 0)
            total = padded if total is None else total + padded
        return total

    d_query, d_keys = score_part(pl.ds(0, TRUNK), TRUNK, path_rows(qkv_ref, None, 0, k0))
    dqx_ref[0:200] = shifted_sum(d_query, 0, TRUNK)
    dk_ref[0:TRUNK] = d_keys[0:TRUNK]

    def fam_scores(b, carry):
        ext = 200 + 120 * b
        for c in range(2):
            rows, size = fam_rows(b, c)
            d_query, d_keys = score_part(rows, size, path_rows(qkv_ref, b, c, k0))
            add_keys(dk_ref, b, c, d_keys)
            if c == 0:
                dqx_ref[pl.ds(pl.multiple_of(ext, 8), 40)] = shifted_sum(d_query, 0, SEG)
                dqx_ref[pl.ds(pl.multiple_of(ext + 40, 8), 40)] = shifted_sum(d_query, SEG, SEG)
            else:
                dqx_ref[pl.ds(pl.multiple_of(ext + 80, 8), 40)] = shifted_sum(d_query, 0, SEG)
        return carry

    lax.fori_loop(0, 4, fam_scores, 0)
    for b in range(4):
        ext = 200 + 120 * b
        dqx_ref[192:200] += dqx_ref[ext : ext + 8]
        dqx_ref[ext + 32 : ext + 40] += dqx_ref[ext + 40 : ext + 48] + dqx_ref[ext + 80 : ext + 88]

    def put(token, size, column, value):
        old = dqkv_ref[token : token + size, pl.ds(column, WIN)].astype(F32)
        dqkv_ref[token : token + size, pl.ds(column, WIN)] = jnp.where(from_first, value, old).astype(BF16)

    for token, size, _, ext, _ in SEGS:
        put(token, size, w0, dqx_ref[ext + 8 : ext + 8 + size])
        put(token, size, k0, dk_ref[token : token + size])
        put(token, size, v0, dv_ref[token : token + size])
    hook(step, 2)


def by_group(shape):
    tail = (0,) * (len(shape) - 3)
    return pl.BlockSpec((None, None, None) + shape[3:], lambda s, t, g: (s, t, g) + tail)


def by_side(shape):
    return pl.BlockSpec((None,) + shape, lambda s, t, g: (s, 0, 0))


def common_specs(first=None):
    return [
        pl.BlockSpec(memory_space=pltpu.SMEM),
        *(first or [pl.BlockSpec((TREE, 1152), lambda s, t, g: (t, s))]),
        pl.BlockSpec((None, None, 2, CQ * WIN, WIN), lambda s, t, g: (s, g, 0, 0, 0)),
        by_side((8, 384)),
        pl.BlockSpec((None, 16, WIN), lambda s, t, g: (t, 0, 0)),
    ]


PARAMS = dict(vmem_limit_bytes=60 * 1024 * 1024, dimension_semantics=("arbitrary",) * 3)


def saved_shapes(trees):
    lead = (2, trees, 2)
    return [lead + (2, TREE, WIN), lead + (2, TREE, CQ * WIN), lead + (2, CQ, TREE, WIN), lead + (TREE, WIN)]


def attention_forward(mix, normed, weight, toeplitz, gains, jj, gather=None):
    trees, width = normed.shape[0] // TREE, normed.shape[1]
    shapes = saved_shapes(trees)
    kinds = (F32, BF16, BF16, F32)
    weights, wide, count, collective = gather if gather else ((), (), 0, {})
    many, held = len(weights), len(wide)

    def kernel(*refs):
        inputs, loads, refs = refs[:6], refs[6 : 6 + many], refs[6 + many :]
        outs, full, refs = refs[:6], refs[6 : 6 + held], refs[6 + held :]
        work = Gather(DIRECT, LATER, loads, full, *refs[3:]) if gather else None

        def hook(step, place):
            if work:
                background(work, step, place)

        fwd_kernel(hook, *inputs, *outs, *refs[:3])

    anywhere = pl.BlockSpec(memory_space=pl.ANY)
    first = [pl.BlockSpec((TREE, width), lambda s, t, g: (t, 0)), pl.BlockSpec((width, 1152), lambda s, t, g: (0, s))]
    result = pl.pallas_call(
        kernel,
        grid=(2, trees, 2),
        in_specs=common_specs(first) + [anywhere] * many,
        out_specs=[pl.BlockSpec((TREE, 384), lambda s, t, g: (t, s))]
        + [by_group(s) for s in shapes]
        + [pl.BlockSpec((TREE, 1152), lambda s, t, g: (t, s))]
        + [anywhere] * held,
        out_shape=[jax.ShapeDtypeStruct((trees * TREE, 768), BF16)]
        + [jax.ShapeDtypeStruct(s, k) for s, k in zip(shapes, kinds)]
        + [jax.ShapeDtypeStruct((trees * TREE, 2304), BF16)]
        + [jax.ShapeDtypeStruct((width, w), BF16) for w in wide],
        scratch_shapes=[pltpu.VMEM((TREE, WIN), jnp.int32), pltpu.VMEM((EXT, WIN), F32), pltpu.VMEM((2, TREE, WIN), BF16)]
        + gather_scratch(weights, count),
        compiler_params=pltpu.CompilerParams(**PARAMS, **collective),
        cost_estimate=pl.CostEstimate(flops=90_000_000_000, bytes_accessed=120_000_000, transcendentals=0),
    )(mix, normed, weight, toeplitz, gains, jj, *weights)
    return result[0], result[1:5], result[5], result[6:]


def attention_backward(mix, qkv, toeplitz, gains, jj, d_normed, saved, sums=None):
    trees = qkv.shape[0] // TREE
    shapes = saved_shapes(trees)
    collective = dict(collective_id=4, has_side_effects=True) if sums else {}
    many = len(sums or ())

    def kernel(*refs):
        inputs, extra, refs = refs[:10], refs[10 : 10 + many], refs[10 + many :]
        outs, full, refs = refs[:4], refs[4 : 4 + many], refs[4 + many :]
        work = Finish(BESIDE, extra, None, full, None, refs[9:]) if sums else None

        def hook(step, place):
            if work:
                beside(work, step, place)

        bwd_kernel(hook, *inputs, *outs, *refs[:9])

    anywhere = pl.BlockSpec(memory_space=pl.ANY)
    extra_in = [pl.BlockSpec((384, 2048), lambda s, t, g: (0, 0))] if sums else []
    result = pl.pallas_call(
        kernel,
        grid=(2, trees, 2),
        in_specs=common_specs() + [pl.BlockSpec((TREE, 384), lambda s, t, g: (t, s))] + [by_group(s) for s in shapes] + extra_in,
        out_specs=[
            pl.BlockSpec((TREE, 1152), lambda s, t, g: (t, s)),
            by_side((8, 384)),
            by_group((2, trees, 2, 8, WIN)),
            by_group((2, trees, 2, 2, 8, WIN)),
        ]
        + [anywhere] * many,
        out_shape=[
            jax.ShapeDtypeStruct((trees * TREE, 2304), BF16),
            jax.ShapeDtypeStruct((2, 8, 384), F32),
            jax.ShapeDtypeStruct((2, trees, 2, 8, WIN), F32),
            jax.ShapeDtypeStruct((2, trees, 2, 2, 8, WIN), F32),
        ]
        + [jax.ShapeDtypeStruct((1536, n), BF16) for n in (1024,)[:many]],
        scratch_shapes=[
            pltpu.VMEM((TREE, WIN), jnp.int32),
            pltpu.VMEM((2, TREE, WIN), BF16),
            pltpu.VMEM((2, TREE, WIN), BF16),
            pltpu.VMEM((2, TREE, WIN), F32),
            pltpu.VMEM((2, TREE, WIN), BF16),
            pltpu.VMEM((2, CQ, TREE, WIN), BF16),
            pltpu.VMEM((EXT, WIN), F32),
            pltpu.VMEM((TREE, WIN), F32),
            pltpu.VMEM((TREE, WIN), F32),
        ]
        + (finish_scratch(BESIDE, 128) if sums else []),
        compiler_params=pltpu.CompilerParams(**PARAMS, **collective),
        cost_estimate=pl.CostEstimate(flops=1_000_000_000, bytes_accessed=1_000_000, transcendentals=0),
    )(mix, qkv, toeplitz, gains, jj, d_normed, *saved, *(sums or ()))
    return result[:4], result[4:]


def band_rows(conv_w):
    rows = conv_w.reshape(-1, CK) * (1.0 / math.sqrt(HD))
    middle = jnp.zeros((rows.shape[0], WIN - CK), F32)
    return jnp.concatenate([rows[:, CK // 2 :], middle, rows[:, : CK // 2]], axis=1)


def fill_toeplitz(rows_ref, side, out_ref):
    offset = lax.broadcasted_iota(jnp.int32, (WIN, WIN), 1) - lax.broadcasted_iota(jnp.int32, (WIN, WIN), 0)
    band = jnp.abs(offset) <= CK // 2
    for head in range(4):
        for a in range(CQ):
            row = rows_ref[side, head * CQ + a : head * CQ + a + 1, :]
            rolled = pltpu.roll(jnp.broadcast_to(row, (WIN, WIN)), 0, 1, stride=1, stride_axis=0)
            out_ref[side, head // 2, head % 2, a * WIN : (a + 1) * WIN, :] = jnp.where(band, rolled, 0.0).astype(BF16)


def key_positions(valid):
    trees = valid.shape[0] // TREE
    valid = valid.reshape(trees, TREE)
    far = jnp.int32(1 << 20)

    def places(part, start):
        return jnp.where(part > 0, lax.broadcasted_iota(jnp.int32, part.shape, 1) + start, far)

    trunk = places(valid[:, :TRUNK], 0)
    empty = jnp.full((trees, SEG), far, jnp.int32)
    rows = [jnp.concatenate([trunk, empty, empty], axis=1)]
    for b in range(4):
        branch = places(valid[:, TRUNK + SEG * b : TRUNK + SEG * (b + 1)], TRUNK)
        rows.append(jnp.concatenate([trunk, branch, empty], axis=1))
        for c in range(2):
            first = 320 + 64 * b + SEG * c
            leaf = places(valid[:, first : first + SEG], TRUNK + SEG)
            rows.append(jnp.concatenate([trunk, branch, leaf], axis=1))
    rows += [jnp.zeros((trees, WIN), jnp.int32)] * 3
    return jnp.stack(rows, axis=1)


def conv_grads(gconv):
    lanes = gconv[..., :CQ, 18:29][..., ::-1] * (1.0 / math.sqrt(HD))
    return jnp.sum(lanes, axis=1).reshape(2, -1)


def mix_grads(gmix):
    return jnp.sum(gmix[:, :, :, :4], axis=(1, 4)).reshape(2, -1)


MESH = pl.DeviceIdType.MESH

FIRST = ((0, 0, 0, 0, 1152, 384), (1, 0, 0, 384, 1536, 384), (2, 0, 0, 768, 1920, 384))
LATER = (
    (0, 0, 0, 0, 384, 384),
    (1, 1, 0, 0, 2048, 512),
    (2, 1, 0, 512, 2560, 512),
    (1, 1, 512, 1024, 3072, 512),
    (2, 1, 512, 1536, 3584, 512),
    (3, 2, 0, 0, 1024, 512),
    (3, 2, 512, 512, 1536, 512),
)
WHOLE = 5
DIRECT = 0
LAST = ((0, 0, 0, 0, 1024, 512), (0, 0, 512, 512, 1536, 512))


def greet(peers):
    sem = pltpu.get_barrier_semaphore()
    for peer in peers:
        pl.semaphore_signal(sem, inc=1, device_id=peer, device_id_type=MESH)
    pl.semaphore_wait(sem, len(peers))


class Gather:
    def __init__(self, direct, items, weights, fulls, send, recv, local, *held):
        self.direct = direct
        self.items, self.weights, self.fulls, self.held = items, weights, fulls, held
        self.send, self.recv, self.local = send, recv, local
        q, c, z = lax.axis_index("plane"), lax.axis_index("core"), lax.axis_index("tensor")
        self.home = (z // 2) == c
        self.q = q
        self.core = (q, 1 - c, z)
        self.far = (q, 1 - c, (z + 2) % 4)
        self.near = (q, c, (z // 2) * 2 + (1 - z % 2))
        self.by_x = ((q // 2) * 2 + (1 - q % 2), c, z)
        self.by_y = ((q + 2) % 4, c, z)

    def away(self, action):
        pl.when(jnp.logical_not(self.home))(action)

    def whole(self, item, side):
        _, out, _, first, second, size = self.items[item]
        return self.fulls[out], pl.ds((first, second)[side], size)

    def z_copy(self, item, side, relay=False):
        weight, _, source_col, _, _, size = self.items[item]
        mine = pl.ds(pl.multiple_of(self.q * 384, 128), 384)
        ref, cols = self.whole(item, side)
        source = ref.at[mine, self.whole(item, 0)[1]] if relay else self.weights[weight].at[mine, pl.ds(source_col, size)]
        return pltpu.make_async_remote_copy(
            src_ref=source, dst_ref=ref.at[mine, cols], send_sem=self.send.at[item, side],
            recv_sem=self.recv.at[item, side], device_id=(self.far, self.near)[side], device_id_type=MESH)

    def plane_copy(self, item, side, step):
        ref, cols = self.whole(item, side)
        if step < 2:
            owner, first, size = self.q, 0, 384
        elif step == 2:
            owner, first, size = self.by_x[0], 0, 192
        else:
            owner, first, size = self.by_y[0], 192, 192
        span = pl.ds(pl.multiple_of(owner * 384 + first, 64), size)
        slot = 2 + 4 * side + step
        return pltpu.make_async_remote_copy(
            src_ref=ref.at[span, cols], dst_ref=ref.at[span, cols], send_sem=self.send.at[item, slot], recv_sem=self.recv.at[item, slot],
            device_id=(self.by_x, self.by_y, self.by_y, self.by_x)[step], device_id_type=MESH)

    def own_load(self, weight):
        return pltpu.make_async_copy(self.weights[weight], self.held[weight], self.local.at[weight, 0])

    def own_stores(self, weight):
        copies = []
        for number, (index, out, source_col, first, _, size) in enumerate(self.items):
            if index == weight:
                source = self.held[weight].at[:, pl.ds(source_col, size)]
                copies.append(pltpu.make_async_copy(source, self.fulls[out].at[:, pl.ds(first, size)], self.local.at[number, 1]))
        return copies

    def own(self):
        @pl.when(self.home)
        def _():
            for weight in range(len(self.weights)):
                self.own_load(weight).start()

    def pass_own(self, weight):
        @pl.when(self.home)
        def _():
            self.own_load(weight).wait()
            for copy in self.own_stores(weight):
                copy.start()

    def wait_own(self):
        @pl.when(self.home)
        def _():
            for weight in range(len(self.weights)):
                for copy in self.own_stores(weight):
                    copy.wait()

    def each(self, action):
        action(1)

        @self.away
        def _():
            action(0)

    def across_copy(self, item):
        weight, _, source_col, _, _, size = self.items[item]
        span = pl.ds(pl.multiple_of((3 - self.q) * 384, 128), 384)
        ref, cols = self.whole(item, 1)
        return pltpu.make_async_remote_copy(
            src_ref=self.weights[weight].at[span, pl.ds(source_col, size)], dst_ref=ref.at[span, cols], send_sem=self.send.at[item, 8],
            recv_sem=self.recv.at[item, 8], device_id=self.near, device_id_type=MESH)

    def start_z(self, item):
        @pl.when(self.home)
        def _():
            self.z_copy(item, 1).start()
            if item < self.direct:
                self.across_copy(item).start()

        @self.away
        def _():
            self.z_copy(item, 0).start()

    def relay_z(self, item):
        @self.away
        def _():
            self.z_copy(item, 0).wait_recv()
            self.z_copy(item, 1, True).start()
            self.plane_copy(item, 0, 0).start()
            self.plane_copy(item, 0, 1).start()

    def relay_only(self, item):
        @self.away
        def _():
            self.z_copy(item, 0).wait_recv()
            self.z_copy(item, 1, True).start()

    def finish_z(self, item):
        self.z_copy(item, 1).wait_recv()
        self.each(lambda side: self.z_copy(item, side).wait_send())

    def start_both(self, item):
        def act(side):
            self.plane_copy(item, side, 0).start()
            self.plane_copy(item, side, 1).start()

        self.each(act)

    def start_plane(self, item):
        self.z_copy(item, 1).wait_recv()
        self.plane_copy(item, 1, 0).start()
        self.plane_copy(item, 1, 1).start()

    def forward(self, item):
        def act(side):
            self.plane_copy(item, side, 0).wait_recv()
            self.plane_copy(item, side, 2).start()
            self.plane_copy(item, side, 1).wait_recv()
            self.plane_copy(item, side, 3).start()

        if item < self.direct:

            @self.away
            def _():
                act(1)
                act(0)

        else:
            self.each(act)

    def finish(self, item):
        def act(side):
            self.plane_copy(item, side, 2).wait_recv()
            self.plane_copy(item, side, 3).wait_recv()
            if self.weights:
                self.z_copy(item, side).wait_send()
            for step in range(4):
                self.plane_copy(item, side, step).wait_send()

        if item >= self.direct:
            self.each(act)
            return

        @self.away
        def _():
            act(1)
            act(0)

        @pl.when(self.home)
        def _():
            self.z_copy(item, 1).wait_send()
            self.across_copy(item).wait()
            for step in range(2):
                self.plane_copy(item, 1, step).wait()


def gather_scratch(weights, count):
    if not weights:
        return []
    return [pltpu.SemaphoreType.DMA((count, 10)), pltpu.SemaphoreType.DMA((count, 10)), pltpu.SemaphoreType.DMA((max(count, len(weights)), 2))] + [
        pltpu.VMEM(w.shape, BF16) for w in weights
    ]


SLOTS = {
    1: (("relay_z", 0), ("start_z", 2), ("pass_own", 0)),
    2: (("start_plane", 0),),
    3: (("relay_z", 1), ("start_z", 3), ("pass_own", 1)),
    4: (("start_plane", 1), ("forward", 0)),
    5: (("relay_z", 2), ("start_z", 4), ("pass_own", 2)),
    6: (("start_plane", 2), ("forward", 1)),
    7: (("relay_z", 3), ("pass_own", 3)),
    8: (("start_plane", 3), ("forward", 2), ("start_z", 5)),
    9: (("relay_z", 4), ("start_z", 6)),
    10: (("start_plane", 4), ("forward", 3)),
    11: (("relay_only", 5),),
    12: (("forward", 4),),
    13: (("relay_only", 6),),
}


def background(work, step, place):
    if place == 2:

        @pl.when(step == 7)
        def _():
            for item in range(len(work.items)):
                if item < WHOLE:
                    work.finish(item)
                else:
                    work.finish_z(item)
            work.wait_own()

        return

    for turn in range(8):
        slot = 2 * turn + place

        @pl.when(step == turn)
        def _(slot=slot):
            if slot == 0:
                work.own()
                greet((work.near, work.far, work.by_x, work.by_y))
                for item in range(2):
                    work.start_z(item)
            for name, item in SLOTS.get(slot, ()):
                getattr(work, name)(item)


TILE = 512


def beside_gate(work, step, place):
    script = {(0, 0): (("start_both", 0), ("start_both", 1)), (1, 1): (("forward", 0),), (3, 0): (("forward", 1),)}
    for (turn, where), names in script.items():
        if where == place:

            @pl.when(step == turn)
            def _(names=names, turn=turn):
                if turn == 0:
                    greet((work.by_x, work.by_y))
                for name, item in names:
                    getattr(work, name)(item)


def gated_forward(normed, weight, part=None):
    rows, width = normed.shape
    units = weight.shape[1] // 2
    many = 0 if part is None else 1
    count = len(LAST)

    def kernel(x_ref, w_ref, *refs):
        hidden_ref, gate_ref, up_ref, refs = refs[many], refs[many + 1], refs[many + 2], refs[many + 3 :]
        step = pl.program_id(0)
        work = Gather(0, LAST, (), refs[:1], refs[1], refs[2], None) if many else None
        if work:
            beside_gate(work, step, 0)
        gate = nn(x_ref[...], w_ref[:, :TILE])
        gate_ref[...] = gate.astype(BF16)
        if work:
            beside_gate(work, step, 1)
        up = nn(x_ref[...], w_ref[:, TILE:])
        up_ref[...] = up.astype(BF16)
        hidden_ref[...] = (gate * jax.nn.sigmoid(gate) * up).astype(BF16)
        if work:

            @pl.when(step == units // TILE - 1)
            def _():
                for item in range(count):
                    work.finish(item)

    anywhere = pl.BlockSpec(memory_space=pl.ANY)
    tile = pl.BlockSpec((rows, TILE), lambda j: (0, j))
    collective = dict(collective_id=5, has_side_effects=True) if many else {}
    extra = [] if part is None else [part]
    result = pl.pallas_call(
        kernel,
        grid=(units // TILE,),
        in_specs=[pl.BlockSpec((rows, width), lambda j: (0, 0)), pl.BlockSpec((width, 2 * TILE), lambda j: (0, j))] + [anywhere] * many,
        out_specs=[tile] * 3 + [anywhere] * many,
        out_shape=[jax.ShapeDtypeStruct((rows, units), BF16)] * 3 + [jax.ShapeDtypeStruct(p.shape, BF16) for p in extra],
        scratch_shapes=[pltpu.SemaphoreType.DMA((count, 10))] * 2 * many,
        input_output_aliases={2: 3} if many else {},
        compiler_params=pltpu.CompilerParams(vmem_limit_bytes=60 * 1024 * 1024, **collective),
    )(normed, weight, *extra)
    return result[:3], result[3:]


def gated_backward(d_out, down, gate, up, normed):
    rows, width = d_out.shape
    units = gate.shape[1]

    def kernel(d_ref, down_ref, gate_ref, up_ref, x_ref, d_gu_ref, grads_ref):
        d_hidden = nn(d_ref[...], down_ref[...])
        gate_value, up_value = gate_ref[...].astype(F32), up_ref[...].astype(F32)
        s = jax.nn.sigmoid(gate_value)
        d_gu_ref[:, :TILE] = (d_hidden * up_value * s * (1.0 + gate_value * (1.0 - s))).astype(BF16)
        d_gu_ref[:, TILE:] = (d_hidden * gate_value * s).astype(BF16)
        grads_ref[...] = tn(x_ref[...], d_gu_ref[...]).astype(BF16)

    whole = pl.BlockSpec((rows, width), lambda j: (0, 0))
    tile = pl.BlockSpec((rows, TILE), lambda j: (0, j))
    return pl.pallas_call(
        kernel,
        grid=(units // TILE,),
        in_specs=[whole, pl.BlockSpec((width, TILE), lambda j: (0, j)), tile, tile, whole],
        out_specs=[pl.BlockSpec((rows, 2 * TILE), lambda j: (0, j)), pl.BlockSpec((width, 2 * TILE), lambda j: (0, j))],
        out_shape=[jax.ShapeDtypeStruct((rows, 2 * units), BF16), jax.ShapeDtypeStruct((width, 2 * units), BF16)],
        compiler_params=pltpu.CompilerParams(vmem_limit_bytes=60 * 1024 * 1024),
        cost_estimate=pl.CostEstimate(flops=22_000_000_000, bytes_accessed=40_000_000, transcendentals=0),
    )(d_out, down, gate, up, normed)


def opening_kernel(tokens_ref, gain_ref, small_ref, wq_ref, wk_ref, wv_ref, full_ref, normed_ref, toep_ref, both_ref, send, recv, local, held0, held1, held2, extra_send, extra_recv):
    work = Gather(3, FIRST, (wq_ref, wk_ref, wv_ref), (full_ref,), send, recv, local, held0, held1, held2)
    rows = tokens_ref.shape[0]

    def extra(source, target, index, peer):
        return pltpu.make_async_remote_copy(
            src_ref=source, dst_ref=target, send_sem=extra_send.at[index], recv_sem=extra_recv.at[index], device_id=peer, device_id_type=MESH)

    far_small = extra(small_ref, both_ref.at[0], 0, work.far)
    near_small = extra(both_ref.at[0], both_ref.at[1], 1, work.near)
    normed_out = extra(normed_ref.at[0:rows], normed_ref.at[rows : 2 * rows], 2, work.core)
    work.own()
    greet((work.near, work.far, work.by_x, work.by_y, work.core))

    @work.away
    def _():
        far_small.start()

    @pl.when(work.home)
    def _():
        both_ref[0] = small_ref[...]
        near_small.start()

    for item in range(3):
        work.start_z(item)
    for start in range(0, rows, 96):
        x = tokens_ref[start : start + 96].astype(F32)
        inv = lax.rsqrt(jnp.mean(x * x, axis=-1, keepdims=True) + 1e-06)
        normed_ref[start : start + 96] = (x * inv * gain_ref[...]).astype(BF16)
    normed_out.start()

    @work.away
    def _():
        far_small.wait_recv()
        near_small.start()

    work.relay_z(0)
    work.start_plane(0)
    fill_toeplitz(both_ref, 0, toep_ref)
    work.relay_z(1)
    work.start_plane(1)
    work.forward(0)
    for weight in range(3):
        work.pass_own(weight)
    near_small.wait_recv()
    work.relay_z(2)
    work.start_plane(2)
    work.forward(1)
    fill_toeplitz(both_ref, 1, toep_ref)
    work.forward(2)
    for item in range(3):
        work.finish(item)
    work.wait_own()
    near_small.wait_send()

    @work.away
    def _():
        far_small.wait_send()

    normed_out.wait()


def opening(tokens, gain, small, weights, collective_id):
    vmem = pl.BlockSpec(memory_space=pltpu.VMEM)
    anywhere = pl.BlockSpec(memory_space=pl.ANY)
    rows, width = tokens.shape
    return pl.pallas_call(
        opening_kernel,
        in_specs=[vmem] * 3 + [anywhere] * 3,
        out_specs=[anywhere] + [vmem] * 3,
        out_shape=[
            jax.ShapeDtypeStruct((width, 2304), BF16),
            jax.ShapeDtypeStruct((2 * rows, width), BF16),
            jax.ShapeDtypeStruct((2, 2, 2, CQ * WIN, WIN), BF16),
            jax.ShapeDtypeStruct((2,) + small.shape, F32),
        ],
        scratch_shapes=gather_scratch(weights, 3) + [pltpu.SemaphoreType.DMA((3,)), pltpu.SemaphoreType.DMA((3,))],
        compiler_params=pltpu.CompilerParams(collective_id=collective_id, has_side_effects=True, vmem_limit_bytes=60 * 1024 * 1024),
    )(tokens, gain, small, *weights)


class Finish:
    def __init__(self, plan, parts, raw, outs, small, bufs, made=False):
        self.made = made
        q, c, z = lax.axis_index("plane"), lax.axis_index("core"), lax.axis_index("tensor")
        self.q, self.c = q, c
        self.home = (z // 2) == c
        self.by_x = ((q // 2) * 2 + (1 - q % 2), c, z)
        self.by_y = ((q + 2) % 4, c, z)
        self.core = (q, 1 - c, z)
        self.near = (q, c, (z // 2) * 2 + (1 - z % 2))
        self.far = (q, 1 - c, (z + 2) % 4)
        self.across = (q, c, (z + 2) % 4)
        self.plan, self.parts, self.raw, self.outs, self.small = plan, parts, raw, outs, small
        (self.near_buf, self.far_buf, self.core_buf, self.here_buf, self.raw_part, self.raw_own, self.raw_first,
         self.raw_second, self.send, self.recv, self.raw_send, self.raw_recv, self.local) = bufs[:13]
        if small is not None:
            self.small_buf, self.small_in, self.small_send, self.small_recv = bufs[13:]

    def remote(self, src, dst, sems, index, peer):
        return pltpu.make_async_remote_copy(
            src_ref=src, dst_ref=dst, send_sem=sems[0].at[index], recv_sem=sems[1].at[index], device_id=peer, device_id_type=MESH)

    def columns(self, item):
        _, first_a, first_b, size, _, _, at = self.plan[item]
        return pl.ds(first_a, size), pl.ds(first_b, size), pl.ds(at, size)

    def part(self, item):
        source = self.plan[item][0]
        if source >= 0:
            return self.parts[source]
        return self.raw.at[self.rows(self.q)] if self.made else self.raw_part

    def away(self, action):
        pl.when(jnp.logical_not(self.home))(action)

    def rows(self, owner):
        return pl.ds(pl.multiple_of(owner * 384, 128), 384)

    def raw_copies(self, item):
        cols_a, cols_b, _ = self.columns(item)
        sems = (self.raw_send, self.raw_recv)
        across = 3 - self.q
        x, y = self.by_x[0], self.by_y[0]
        remote = [
            self.remote(self.raw.at[self.rows(x), cols_a], self.raw_first.at[0, :, cols_a], sems, (item, 0), self.by_x),
            self.remote(self.raw.at[self.rows(across), cols_a], self.raw_first.at[1, :, cols_a], sems, (item, 1), self.by_x),
            self.remote(self.raw.at[self.rows(y), cols_b], self.raw_first.at[0, :, cols_b], sems, (item, 2), self.by_y),
            self.remote(self.raw.at[self.rows(across), cols_b], self.raw_first.at[1, :, cols_b], sems, (item, 3), self.by_y),
        ]
        if self.made:
            return remote, []
        return remote, [
            pltpu.make_async_copy(self.raw.at[self.rows(self.q), cols_a], self.raw_own.at[0, :, cols_a], self.local.at[item, 0]),
            pltpu.make_async_copy(self.raw.at[self.rows(y), cols_a], self.raw_own.at[1, :, cols_a], self.local.at[item, 1]),
            pltpu.make_async_copy(self.raw.at[self.rows(self.q), cols_b], self.raw_own.at[0, :, cols_b], self.local.at[item, 2]),
            pltpu.make_async_copy(self.raw.at[self.rows(x), cols_b], self.raw_own.at[1, :, cols_b], self.local.at[item, 3]),
        ]

    def raw_place(self, which, side, cols):
        if self.made:
            owner = self.q if which == 0 else (self.by_y[0], self.by_x[0])[side]
            return self.raw, (self.rows(owner), cols)
        return self.raw_own, (which, slice(None), cols)

    def raw_second_copies(self, item):
        sems = (self.raw_send, self.raw_recv)
        copies = []
        for side, cols in enumerate(self.columns(item)[:2]):
            ref, place = self.raw_place(1, side, cols)
            copies.append(self.remote(ref.at[place], self.raw_second.at[:, cols], sems, (item, 4 + side), (self.by_y, self.by_x)[side]))
        return copies

    def r1_side(self, item, side):
        for copy in self.raw_copies(item)[0][2 * side : 2 * side + 2]:
            copy.start()

    def r1(self, item):
        for group in self.raw_copies(item):
            for copy in group:
                copy.start()

    def r2(self, item):
        remote, own = self.raw_copies(item)
        for copy in own:
            copy.wait()
        for side, cols in enumerate(self.columns(item)[:2]):
            remote[2 * side + 1].wait_recv()
            ref, place = self.raw_place(1, side, cols)
            ref[place] = added(ref[place], self.raw_first[1, :, cols])
            self.raw_second_copies(item)[side].start()

    def r3(self, item):
        remote, _ = self.raw_copies(item)
        for side, cols in enumerate(self.columns(item)[:2]):
            remote[2 * side].wait_recv()
            self.raw_second_copies(item)[side].wait_recv()
            ref, place = self.raw_place(0, side, cols)
            total = ref[place].astype(F32) + self.raw_first[0, :, cols].astype(F32) + self.raw_second[:, cols].astype(F32)
            self.part(item)[:, cols] = total.astype(BF16)

    def near_copy(self, item):
        _, cols_b, at = self.columns(item)
        return self.remote(self.part(item).at[:, cols_b], self.near_buf.at[:, self.spot(item)], (self.send, self.recv), (item, 0), self.near)

    def spot(self, item):
        return pl.ds(self.plan[item][5], self.plan[item][3])

    def far_copy(self, item):
        spot = self.spot(item)
        return self.remote(self.here_buf.at[:, spot], self.far_buf.at[:, spot], (self.send, self.recv), (item, 1), self.far)

    def core_copy(self, item, relayed):
        spot = self.spot(item)
        source = self.far_buf if relayed else self.here_buf
        return self.remote(source.at[:, spot], self.core_buf.at[:, spot], (self.send, self.recv), (item, 2), self.core)

    def s1(self, item):
        self.near_copy(item).start()

    def s2(self, item):
        spot, cols_a = self.spot(item), self.columns(item)[0]
        self.near_copy(item).wait_recv()
        self.here_buf[:, spot] = added(self.part(item)[:, cols_a], self.near_buf[:, spot])

        @pl.when(self.home)
        def _():
            self.core_copy(item, False).start()

        @self.away
        def _():
            self.far_copy(item).start()

    def s3(self, item):
        @self.away
        def _():
            self.far_copy(item).wait_recv()
            self.core_copy(item, True).start()

    def plane_copies(self, item):
        out = self.outs[self.plan[item][4]]
        at, spot = self.columns(item)[2], self.spot(item)
        sems = (self.send, self.recv)
        half = self.c * 192

        def rows(owner, first, size):
            return pl.ds(pl.multiple_of(owner * 384 + half + first, 32), size)

        mine = self.core_buf.at[pl.ds(pl.multiple_of(half, 32), 192), spot]
        x, y, across = self.by_x[0], self.by_y[0], 3 - self.q
        own = out.at[rows(self.q, 0, 192), at]
        top, low = out.at[rows(x, 0, 96), at], out.at[rows(y, 96, 96), at]
        return [
            self.remote(mine, own, sems, (item, 3), self.by_x),
            self.remote(mine, own, sems, (item, 4), self.by_y),
            self.remote(top, top, sems, (item, 5), self.by_y),
            self.remote(low, low, sems, (item, 6), self.by_x),
        ] + [
            self.remote(out.at[rows(o, 0, 192), at], out.at[rows(o, 0, 192), at], sems, (item, 7 + i), self.core)
            for i, o in enumerate((x, y, across))
        ]

    def own_copy(self, item):
        out = self.outs[self.plan[item][4]]
        rows = pl.ds(pl.multiple_of(self.q * 384, 128), 384)
        return pltpu.make_async_copy(self.core_buf.at[:, self.spot(item)], out.at[rows, self.columns(item)[2]], self.local.at[item, 4])

    def s4(self, item):
        spot = self.spot(item)

        @pl.when(self.home)
        def _():
            self.core_copy(item, False).wait_recv()
            self.core_buf[:, spot] = added(self.here_buf[:, spot], self.core_buf[:, spot])

        @self.away
        def _():
            self.core_copy(item, True).wait_recv()
            self.core_buf[:, spot] = added(self.far_buf[:, spot], self.core_buf[:, spot])

        self.own_copy(item).start()
        copies = self.plane_copies(item)
        copies[0].start()
        copies[1].start()

    def s5(self, item):
        copies = self.plane_copies(item)
        copies[0].wait_recv()
        copies[2].start()
        copies[4].start()
        copies[1].wait_recv()
        copies[3].start()
        copies[5].start()

    def s6(self, item):
        copies = self.plane_copies(item)
        copies[2].wait_recv()
        copies[3].wait_recv()
        copies[6].start()

    def s7(self, item):
        copies = self.plane_copies(item)
        self.own_copy(item).wait()
        for copy in copies[4:]:
            copy.wait_recv()
        for copy in copies:
            copy.wait_send()
        self.near_copy(item).wait_send()

        @pl.when(self.home)
        def _():
            self.core_copy(item, False).wait_send()

        @self.away
        def _():
            self.core_copy(item, True).wait_send()
            self.far_copy(item).wait_send()

        if self.plan[item][0] < 0:
            for copy in self.raw_copies(item)[0] + self.raw_second_copies(item):
                copy.wait_send()

    def small_copy(self, turn):
        peer = (self.core, self.by_x, self.by_y, self.near, self.across)[turn]
        return self.remote(self.small_buf.at[turn], self.small_in.at[turn], (self.small_send, self.small_recv), turn, peer)

    def small_start(self):
        self.small_copy(0).start()

    def small_next(self, turn):
        self.small_copy(turn).wait_recv()
        self.small_buf[turn + 1] = self.small_buf[turn] + self.small_in[turn]
        if turn < 4:
            self.small_copy(turn + 1).start()

    def small_done(self, out):
        for turn in range(5):
            self.small_copy(turn).wait_send()
        out[...] = self.small_buf[5]


def added(left, right):
    return (left.astype(F32) + right.astype(F32)).astype(BF16)


FINISH = (
    (0, 0, 2048, 512, 0, 0, 0),
    (0, 512, 2560, 512, 1, 512, 0),
    (0, 1024, 3072, 512, 0, 1024, 512),
    (0, 1536, 3584, 512, 1, 1536, 512),
    (-1, 0, 1152, 384, 2, 2048, 0),
    (-1, 384, 1536, 384, 2, 2432, 384),
    (-1, 768, 1920, 384, 2, 2816, 768),
)
LONE = ((-1, 0, 384, 384, 0, 0, 0),)
BESIDE = (
    (0, 0, 1024, 512, 0, 0, 0),
    (0, 512, 1536, 512, 0, 512, 512),
)
BESIDE_STEPS = (
    (("greet", 0), ("s1", 0), ("s1", 1)),
    (),
    (("s2", 0),),
    (("s2", 1),),
    (("s3", 0),),
    (("s3", 1),),
    (("s4", 0),),
    (("s4", 1),),
    (),
    (),
    (("s5", 0),),
    (("s5", 1),),
    (),
    (("s6", 0),),
    (("s6", 1),),
)


def finish_scratch(plan, raw_width, made=False):
    count, width = len(plan), sum(item[3] for item in plan)
    return (
        [pltpu.VMEM((384, width), BF16)] * 4
        + [pltpu.VMEM((384, 128 if made else raw_width), BF16)]
        + [pltpu.VMEM((2, 384, 128 if made else raw_width), BF16), pltpu.VMEM((2, 384, raw_width), BF16)]
        + [pltpu.VMEM((384, raw_width), BF16)]
        + [pltpu.SemaphoreType.DMA((count, 10))] * 2
        + [pltpu.SemaphoreType.DMA((count, 6))] * 2
        + [pltpu.SemaphoreType.DMA((count, 5))]
    )


def beside(work, step, place):
    if place == 2:

        @pl.when(step == 7)
        def _():
            for item in range(len(work.plan)):
                work.s7(item)

        return

    for slot, names in enumerate(BESIDE_STEPS):
        if slot % 2 == place:

            @pl.when(step == slot // 2)
            def _(names=names):
                for name, item in names:
                    if name == "greet":
                        greet((work.near, work.far, work.by_x, work.by_y, work.core))
                    else:
                        getattr(work, name)(item)


def finish_kernel(
    small, gu, out, normed, d_qkv, weight, tokens, gain, d_hidden, small_out, d_input, o_gate, o_up, o_qkv, o_out,
    made, partner, arrived, loaded, load_sem, hidden_buf, tokens_buf, hidden_sem, core_send, core_recv, *bufs,
):
    lone = Finish(LONE, (), out, (o_out,), None, bufs[-13:])
    work = Finish(FINISH, (gu,), made, (o_gate, o_up, o_qkv), small, bufs[:-13], True)
    rows = tokens.shape[0]

    def load(part):
        return pltpu.make_async_copy(weight.at[384 * part : 384 * (part + 1)], loaded.at[part % 2], load_sem.at[part % 2])

    def exchange(part):
        cols = pl.ds(384 * part, 384)
        return work.remote(partner.at[:, cols], arrived.at[:, cols], (core_send, core_recv), part, work.core)

    def load_hidden(part):
        span = pl.ds(64 * part, 64)
        return (
            pltpu.make_async_copy(d_hidden.at[span], hidden_buf.at[part % 2], hidden_sem.at[0, part % 2]),
            pltpu.make_async_copy(tokens.at[span], tokens_buf.at[part % 2], hidden_sem.at[1, part % 2]),
        )

    load(0).start()
    load(1).start()
    for copy in load_hidden(0):
        copy.start()
    greet((work.near, work.far, work.by_x, work.by_y, work.core, work.across))
    lone.r1(0)
    work.s1(0)
    work.s1(1)

    def make(side, owner):
        cols = slice(1152 * side, 1152 * (side + 1))
        made[work.rows(owner), cols] = tn(normed[:, work.rows(owner)], d_qkv[:, cols]).astype(BF16)

    across = 3 - work.q
    for side, owners in enumerate(((across, work.by_x[0]), (across, work.by_y[0]))):
        for owner in owners:
            make(side, owner)
        for item in (4, 5, 6):
            work.r1_side(item, side)
    work.s2(0)
    work.s1(2)
    lone.r2(0)
    make(0, work.by_y[0])
    work.s2(1)
    work.s1(3)
    make(1, work.by_x[0])
    work.s3(0)
    make(0, work.q)
    work.s2(2)
    work.s3(1)
    make(1, work.q)
    work.r2(4)
    lone.r3(0)
    lone.s1(0)
    work.s4(0)

    def back(part):
        cols = slice(384 * part, 384 * (part + 1))
        load(part).wait()
        both = nt(d_qkv[...], loaded[part % 2])
        d_input[:, cols] = both[:rows]
        partner[:, cols] = both[rows:].astype(BF16)
        if part < 2:
            load(part + 2).start()
        exchange(part).start()

    back(0)
    work.r2(5)
    work.s2(3)
    work.s4(1)
    back(1)
    work.r2(6)
    work.r3(4)
    work.s1(4)
    work.s3(2)
    work.s5(0)
    back(2)
    lone.s2(0)
    work.r3(5)
    work.s1(5)
    work.s3(3)
    work.s4(2)
    work.s5(1)
    back(3)
    work.s2(4)
    work.r3(6)
    work.s1(6)
    work.s4(3)
    work.s6(0)
    for part in range(4):
        exchange(part).wait_recv()
    gain_sum = jnp.zeros((1, tokens.shape[1]), F32)
    for part in range(rows // 64):
        span = slice(64 * part, 64 * (part + 1))
        if part + 1 < rows // 64:
            for copy in load_hidden(part + 1):
                copy.start()
        for copy in load_hidden(part):
            copy.wait()
        x = tokens_buf[part % 2].astype(F32)
        inv = lax.rsqrt(jnp.mean(x * x, axis=-1, keepdims=True) + 1e-06)
        d_normed = d_input[span] + arrived[span].astype(F32)
        scaled = d_normed * gain[...]
        gain_sum = gain_sum + jnp.sum(d_normed * x * inv, axis=0, keepdims=True)
        d_input[span] = hidden_buf[part % 2] + inv * scaled - x * inv**3 * jnp.mean(scaled * x, axis=-1, keepdims=True)
    work.small_buf[0] = small[...]
    work.small_buf[0, 0:1] = gain_sum
    work.small_start()
    script = (
        ("s3", 4), ("s2", 5), ("s3", 7), ("s6", 1), ("s5", 2), ("m", 0),
        ("s4", 4), ("s3", 5), ("s2", 6), ("s4", 7), ("s5", 3), ("s6", 2), ("m", 1),
        ("s5", 4), ("s4", 5), ("s3", 6), ("s5", 7), ("s6", 3), ("m", 2),
        ("s6", 4), ("s5", 5), ("s4", 6), ("s6", 7), ("m", 3), ("s6", 5), ("s5", 6), ("m", 4), ("s6", 6),
    )
    for name, item in script:
        if name == "m":
            work.small_next(item)
        elif item == 7:
            getattr(lone, name)(0)
        else:
            getattr(work, name)(item)
    for item in range(len(FINISH)):
        work.s7(item)
    lone.s7(0)
    for part in range(4):
        exchange(part).wait_send()
    work.small_done(small_out)


def finish_gradients(small, gu, out, normed, d_qkv, weight, tokens, gain, d_hidden, collective_id):
    vmem = pl.BlockSpec(memory_space=pltpu.VMEM)
    anywhere = pl.BlockSpec(memory_space=pl.ANY)
    rows, width = tokens.shape
    return pl.pallas_call(
        finish_kernel,
        in_specs=[vmem] * 2 + [anywhere] + [vmem] * 2 + [anywhere] * 2 + [vmem] + [anywhere],
        out_specs=[vmem] * 2 + [anywhere] * 4,
        out_shape=[jax.ShapeDtypeStruct(small.shape, F32), jax.ShapeDtypeStruct((rows, width), F32)]
        + [jax.ShapeDtypeStruct((1536, n), BF16) for n in (1024, 1024, 1152, 384)],
        scratch_shapes=[
            pltpu.VMEM((1536, 2304), BF16),
            pltpu.VMEM((rows, width), BF16),
            pltpu.VMEM((rows, width), BF16),
            pltpu.VMEM((2, 384, 2304), BF16),
            pltpu.SemaphoreType.DMA((2,)),
            pltpu.VMEM((2, 64, width), F32),
            pltpu.VMEM((2, 64, width), BF16),
            pltpu.SemaphoreType.DMA((2, 2)),
            pltpu.SemaphoreType.DMA((4,)),
            pltpu.SemaphoreType.DMA((4,)),
        ]
        + finish_scratch(FINISH, 2304, True)
        + [pltpu.VMEM((6,) + small.shape, F32), pltpu.VMEM((5,) + small.shape, F32)]
        + [pltpu.SemaphoreType.DMA((5,))] * 2
        + finish_scratch(LONE, 768),
        compiler_params=pltpu.CompilerParams(collective_id=collective_id, has_side_effects=True, vmem_limit_bytes=60 * 1024 * 1024),
    )(small, gu, out, normed, d_qkv, weight, tokens, gain, d_hidden)


def rows_dot(lhs, rhs):
    return tn(lhs, rhs).astype(BF16)


def toeplitz_alone(both):
    def kernel(rows_ref, out_ref):
        fill_toeplitz(rows_ref, 0, out_ref)
        fill_toeplitz(rows_ref, 1, out_ref)

    return pl.pallas_call(
        kernel,
        out_shape=jax.ShapeDtypeStruct((2, 2, 2, CQ * WIN, WIN), BF16),
        compiler_params=pltpu.CompilerParams(vmem_limit_bytes=60 * 1024 * 1024),
    )(both)


def make_local(planes, tensors):
    every = ("plane", "core", "tensor")
    sides = [(c, z) for c in range(2) for z in range(tensors)]

    def spot(q, c, z):
        return (q * 2 + c) * tensors + z

    def is_home(c, z):
        return z // 2 == c

    far_pairs = [(spot(q, c, z), spot(q, 1 - c, z ^ 2)) for q in range(planes) for c, z in sides if not is_home(c, z)]
    near_pairs = [
        (spot(q, c, z), spot(q, c, z ^ 1) if is_home(c, z) else spot(q, 1 - c, z ^ 3)) for q in range(planes) for c, z in sides
    ]

    def over_core(value):
        return lax.ppermute(value, "core", [(0, 1), (1, 0)])

    def first_from(value):
        return lax.ppermute(value, every, far_pairs)

    def second_from(value):
        return lax.ppermute(value, every, near_pairs)

    square = planes == 4

    def local(
        tokens, teacher, valid_mask, norm1_gain, w_query, w_key, w_value, conv_weight, head_mix, gn_gain, w_out, norm2_gain,
        w_gate, w_up, w_down,
    ):
        q, c, z = lax.axis_index("plane"), lax.axis_index("core"), lax.axis_index("tensor")
        own_rows, width = tokens.shape
        home = (z // 2) == c
        wide = w_query.shape[1]

        def collect(weights):
            pairs = []
            for weight in weights:
                pairs.append(jnp.where(home, weight, first_from(weight)))
                pairs.append(second_from(weight))
            return pairs

        fused = square and tensors == 4
        units = w_gate.shape[1]

        def plane_sum(grads):
            return lax.psum_scatter(grads, "plane", scatter_dimension=0, tiled=True)

        def reduce(first, second):
            here = added(first, lax.ppermute(second, "tensor", [(i, i ^ 1) for i in range(tensors)]))
            here = jnp.where(home, here, first_from(here))
            total = added(here, over_core(here))
            return lax.all_gather(total, "plane", axis=0, tiled=True)

        small = jnp.concatenate(
            [
                band_rows(conv_weight),
                jnp.pad(head_mix.reshape(1, -1), ((0, 0), (0, WIN - head_mix.size))),
                jnp.pad(gn_gain.reshape(1, -1), ((0, 0), (0, 2 * WIN - wide))).reshape(2, WIN),
                jnp.zeros((5, WIN), F32),
            ]
        )
        conv_size, mix_size = conv_weight.size, head_mix.size
        small_size = conv_size + mix_size + wide
        gain_one, gain_two = norm1_gain, norm2_gain
        own_valid = lax.dynamic_slice_in_dim(valid_mask, z * own_rows, own_rows, 0)
        jj = key_positions(jnp.concatenate([own_valid, over_core(own_valid)]))

        def with_partner(value):
            return jnp.concatenate([value, over_core(value)], axis=0)

        def summed(left, right):
            sent = over_core(nt(left[own_rows:], right).astype(BF16))
            return nt(left[:own_rows], right) + sent.astype(F32)

        inputs = tokens.astype(F32)
        inv_one = lax.rsqrt(jnp.mean(inputs * inputs, axis=-1, keepdims=True) + 1e-06)
        if fused:
            qkv_weight, normed_one, toep, both_small = opening(tokens, gain_one[None], small, [w_query, w_key, w_value], 1)
            gather = ([w_out, w_gate, w_up, w_down], (768, 4096, 2048), len(LATER), dict(collective_id=3, has_side_effects=True))
        else:
            both_small = jnp.stack([jnp.where(home, small, first_from(small)), second_from(small)])
            toep = toeplitz_alone(both_small)
            normed_one = with_partner((inputs * inv_one * gain_one).astype(BF16))
            parts = collect([w_query, w_key, w_value])
            qkv_weight = jnp.concatenate(parts[0::2] + parts[1::2], axis=1)
            gather = None
        mix = both_small[:, 24, :mix_size].reshape(-1)
        gains = jnp.broadcast_to(both_small[:, 25:27].reshape(2, 1, 2 * WIN)[:, :, :wide], (2, 8, wide))
        heads_out, saved, qkv, later = attention_forward(mix, normed_one, qkv_weight, toep, gains, jj, gather)
        if fused:
            out_weight, gu_weight, down_weight = later
        else:
            out_weight = jnp.concatenate(collect([w_out]), axis=1)
            pieces = collect([w_gate, w_up])
            pieces = [pieces[2 * kind + side][:, start : start + TILE] for side in range(2) for start in range(0, units, TILE) for kind in range(2)]
            gu_weight = jnp.concatenate(pieces, axis=1)
        hidden_in = inputs + summed(heads_out, out_weight)
        inv_two = lax.rsqrt(jnp.mean(hidden_in * hidden_in, axis=-1, keepdims=True) + 1e-06)
        normed_two = with_partner((hidden_in * inv_two * gain_two).astype(BF16))
        (hidden, gate, up), last = gated_forward(normed_two, gu_weight, down_weight if fused else None)
        down_weight = last[0] if fused else jnp.concatenate(collect([w_down]), axis=1)
        final_rows = hidden_in + summed(hidden, down_weight)
        output = final_rows.astype(BF16)
        own_mask = own_valid.astype(F32)
        error = own_mask[:, None] * (final_rows - teacher.astype(F32))
        squared_sum = jnp.sum(error * error)
        count_sum = jnp.sum(own_mask)

        d_all = with_partner(error.astype(BF16))
        down_grads = rows_dot(d_all, hidden)
        down_grads, d_all = lax.optimization_barrier((down_grads, d_all))
        down_part = plane_sum(down_grads)
        d_gu, gu_grads = gated_backward(d_all, down_weight, gate, up, normed_two)
        gu_grads, d_gu = lax.optimization_barrier((gu_grads, d_gu))
        gu_part = plane_sum(gu_grads)
        d_normed_two = summed(d_gu, gu_weight)
        scaled_two = d_normed_two * gain_two
        grad_gain_two = jnp.sum(d_normed_two * hidden_in * inv_two, axis=0)
        d_hidden_in = (
            error + inv_two * scaled_two - hidden_in * inv_two**3 * jnp.mean(scaled_two * hidden_in, axis=-1, keepdims=True)
        )
        d_attn = with_partner(d_hidden_in.astype(BF16))
        out_grads = rows_dot(d_attn, heads_out)
        out_grads, d_attn = lax.optimization_barrier((out_grads, d_attn))
        d_normed = nn(d_attn, out_weight)
        d_normed, down_part = lax.optimization_barrier((d_normed, down_part))
        (d_qkv, ggn, gmix, gconv), done = attention_backward(
            mix, qkv, toep, gains, jj, d_normed, saved, (down_part,) if fused else None
        )
        small_grads = jnp.concatenate([conv_grads(gconv), mix_grads(gmix), ggn[:, 0]], axis=1)
        table = jnp.zeros((tensors, small_size), F32)
        table = lax.dynamic_update_slice(table, small_grads[:1], (2 * c + z % 2, 0))
        table = lax.dynamic_update_slice(table, small_grads[1:], (2 * c + 1 - z % 2, 0))
        table = jnp.pad(table.reshape(-1), (0, 4 * width - table.size)).reshape(4, width)
        last = jnp.pad(jnp.stack([squared_sum, count_sum]), (0, 2 * width - 2)).reshape(2, width)
        packed = jnp.concatenate([jnp.zeros((1, width), F32), grad_gain_two[None], table, last])
        if fused:
            packed, grad_input, sum_gate, sum_up, sum_qkv, sum_out = finish_gradients(
                packed, gu_part, out_grads, normed_one, d_qkv, qkv_weight, tokens, gain_one[None], d_hidden_in, 2
            )
            sums = [done[0], sum_gate, sum_up, sum_out, sum_qkv]
        else:
            qkv_grads = rows_dot(normed_one, d_qkv)
            d_normed_one = summed(d_qkv, qkv_weight)
            scaled_one = d_normed_one * gain_one
            packed = packed.at[0].set(jnp.sum(d_normed_one * inputs * inv_one, axis=0))
            grad_input = (
                d_hidden_in + inv_one * scaled_one - inputs * inv_one**3 * jnp.mean(scaled_one * inputs, axis=-1, keepdims=True)
            )
            packed = lax.psum(packed, every)
            out_part, qkv_part = plane_sum(out_grads), plane_sum(qkv_grads)
            sums = [reduce(part[:, : part.shape[1] // 2], part[:, part.shape[1] // 2 :]) for part in (down_part, out_part, qkv_part)]
            sum_gu = reduce(gu_part[:, : 2 * units], gu_part[:, 2 * units :])
            for kind in range(2):
                places = range(kind * TILE, 2 * units, 2 * TILE)
                sums.insert(1 + kind, jnp.concatenate([sum_gu[:, i : i + TILE] for i in places], axis=1))
        grad_down, grad_gate, grad_up, grad_out, grad_qkv = [value.astype(F32) for value in sums]
        small_sum = lax.dynamic_slice_in_dim(packed[2:6].reshape(-1), z * small_size, small_size, 0)
        gain_slice = width // tensors
        gain_one_out = lax.dynamic_slice_in_dim(packed[0], z * gain_slice, gain_slice, 0)
        gain_two_out = lax.dynamic_slice_in_dim(packed[1], z * gain_slice, gain_slice, 0)
        loss = packed[6, 0] / (packed[6, 1] * width)
        return (
            output,
            loss,
            grad_input,
            gain_one_out,
            grad_qkv[:, :wide],
            grad_qkv[:, wide : 2 * wide],
            grad_qkv[:, 2 * wide :],
            small_sum[:conv_size].reshape(conv_weight.shape),
            small_sum[conv_size : conv_size + mix_size].reshape(head_mix.shape),
            small_sum[conv_size + mix_size :].reshape(gn_gain.shape),
            grad_out,
            gain_two_out,
            grad_gate,
            grad_up,
            grad_down,
        )

    return local


def solution(mesh):
    tensors = mesh.shape["tensor"]
    planes = mesh.shape["dp"] // 2
    inner = jax.sharding.Mesh(mesh.devices.reshape(planes, 2, tensors), ("plane", "core", "tensor"))
    rows = P(("plane", "core", "tensor"), None)
    columns = P(None, "tensor")
    cube = P("tensor", None, None)
    return jax.shard_map(
        make_local(planes, tensors),
        mesh=inner,
        in_specs=(
            rows, rows, P(("plane", "core")), P(), columns, columns, columns, cube, cube, P("tensor", None), columns, P(),
            columns, columns, columns,
        ),
        out_specs=(
            rows, P(), rows, P("tensor"), columns, columns, columns, cube, cube, P("tensor", None), columns, P("tensor"),
            columns, columns, columns,
        ),
        check_vma=False,
    )
```

```python
import math
import jax
import jax.numpy as jnp
from jax import lax
from jax.experimental import pallas as pl
from jax.experimental.pallas import tpu as pltpu
from jax.sharding import PartitionSpec as P

HD = 96
CQ = 6
CK = 11
TRUNK = 192
SEG = 32
TREE = 576
WIN = 256
FAM = 96
EXT = 680
F32 = jnp.float32
BF16 = jnp.bfloat16


def segments():
    rows = [(0, TRUNK, 0, 0, -1)]
    for b in range(4):
        base, ext = TRUNK + FAM * b, 200 + 120 * b
        rows.append((TRUNK + SEG * b, SEG, base, ext, TRUNK - 8))
        for c in range(2):
            rows.append((320 + 64 * b + SEG * c, SEG, base + SEG * (c + 1), ext + 40 * (c + 1), TRUNK + SEG * b + SEG - 8))
    return rows


SEGS = segments()


def nn(a, b):
    return lax.dot_general(a, b, (((1,), (0,)), ((), ())), preferred_element_type=F32)


def nt(a, b):
    return lax.dot_general(a, b, (((1,), (1,)), ((), ())), preferred_element_type=F32)


def tn(a, b):
    return lax.dot_general(a, b, (((0,), (0,)), ((), ())), preferred_element_type=F32)


def head_masks(g):
    lane = lax.broadcasted_iota(jnp.int32, (1, WIN), 1)
    first = 64 * g
    m0 = (lane >= first) & (lane < first + HD)
    m1 = (lane >= first + HD) & (lane < first + 2 * HD)
    return m0, m1, lane >= first


def fill_distance(jj_ref, dist_ref):
    for index, (_, size, row, _, _) in enumerate(SEGS):
        start = 0 if index == 0 else (TRUNK if (index - 1) % 3 == 0 else TRUNK + SEG)
        pos = lax.broadcasted_iota(jnp.int32, (size, WIN), 0) + start
        dist_ref[row : row + size] = pos - jj_ref[index : index + 1, :]


def path_rows(ref, b, c, column):
    if b is None:
        parts = [ref[0:TRUNK, pl.ds(column, WIN)], ref[TRUNK : TRUNK + SEG, pl.ds(column, WIN)], ref[320 : 320 + SEG, pl.ds(column, WIN)]]
    else:
        parts = [
            ref[0:TRUNK, pl.ds(column, WIN)],
            ref[pl.ds(pl.multiple_of(TRUNK + SEG * b, SEG), SEG), pl.ds(column, WIN)],
            ref[pl.ds(pl.multiple_of(320 + 64 * b + SEG * c, SEG), SEG), pl.ds(column, WIN)],
        ]
    return jnp.concatenate(parts, axis=0)


def fam_rows(b, c):
    base = TRUNK + FAM * b
    return (pl.ds(pl.multiple_of(base, 32), 64), 64) if c == 0 else (pl.ds(pl.multiple_of(base + 64, 32), SEG), SEG)


def group_norm(ho, m0, m1):
    def stat(v):
        s0 = jnp.sum(jnp.where(m0, v, 0.0), axis=-1, keepdims=True) * (1.0 / HD)
        s1 = jnp.sum(jnp.where(m1, v, 0.0), axis=-1, keepdims=True) * (1.0 / HD)
        return jnp.where(m0, s0, s1)

    centered = jnp.where(m0 | m1, ho - stat(ho), 0.0)
    inv = lax.rsqrt(stat(centered * centered) + 1e-05)
    return centered * inv, inv, stat


def fwd_kernel(
    hook, mix_ref, normed_ref, weight_ref, t_ref, gn_ref, jj_ref, nh_ref, att_ref, pre_ref, qs_ref, ho_ref, qkv_ref, dist_ref, qx_ref, mx_ref
):
    side, t, g = pl.program_id(0), pl.program_id(1), pl.program_id(2)
    step = (side * 2 + t) * 2 + g
    mix0 = 8 * side + 4 * g
    hook(step, 0)

    @pl.when(g == 0)
    def _():
        for part in range(3):
            cols = slice(384 * part, 384 * (part + 1))
            qkv_ref[:, cols] = nn(normed_ref[...], weight_ref[:, cols]).astype(BF16)

    w0 = pl.multiple_of(g * 128, 128)
    m0, m1, from_first = head_masks(g)
    m0f, m1f = m0.astype(F32), m1.astype(F32)
    fill_distance(jj_ref, dist_ref)
    qx_ref[0:8] = jnp.zeros((8, WIN), F32)
    for token, size, _, ext, parent in SEGS:
        if parent >= 0:
            low = qkv_ref[parent - 8 : parent + 8, pl.ds(w0, WIN)].astype(F32)
            qx_ref[ext : ext + 8] = low[8:16]
        qx_ref[ext + 8 : ext + 8 + size] = qkv_ref[token : token + size, pl.ds(w0, WIN)].astype(F32)
    for a in range(CQ):
        for _, size, row, ext, _ in SEGS:
            part = qx_ref[ext + 8 - a : ext + 8 - a + size]
            qs_ref[0, a, row : row + size] = (part * m0f).astype(BF16)
            qs_ref[1, a, row : row + size] = (part * m1f).astype(BF16)
    k0, v0 = w0 + 384, w0 + 768
    k_trunk = path_rows(qkv_ref, None, 0, k0)

    def trunk_scores(a, carry):
        scores = nt(qs_ref[:, a, 0:TRUNK].reshape(2 * TRUNK, WIN), k_trunk).reshape(2, TRUNK, WIN)
        kept = dist_ref[0:TRUNK] >= a
        for e in range(2):
            pre_ref[e, 0:TRUNK, pl.ds(pl.multiple_of(a * WIN, WIN), WIN)] = jnp.where(kept, scores[e], 0.0).astype(BF16)
        return carry

    lax.fori_loop(0, CQ, trunk_scores, 0)

    def fam_scores(b, carry):
        for c in range(2):
            rows, size = fam_rows(b, c)
            keys = path_rows(qkv_ref, b, c, k0)
            scores = nt(qs_ref[:, :, rows].reshape(2 * CQ * size, WIN), keys).reshape(2, CQ, size, WIN)
            dist = dist_ref[rows]
            for a in range(CQ):
                kept = dist >= a
                for e in range(2):
                    pre_ref[e, rows, a * WIN : (a + 1) * WIN] = jnp.where(kept, scores[e, a], 0.0).astype(BF16)
        return carry

    lax.fori_loop(0, 4, fam_scores, 0)
    hook(step, 1)
    for e in range(2):
        conv = nn(pre_ref[e], t_ref[e])
        logits = jnp.where(dist_ref[...] >= 0, conv, -1e30)
        shifted = jnp.exp(logits - jnp.max(logits, axis=-1, keepdims=True))
        att_ref[e] = shifted / jnp.sum(shifted, axis=-1, keepdims=True)
    for c in range(2):
        mx_ref[c] = (mix_ref[mix0 + 2 * c] * att_ref[0] + mix_ref[mix0 + 2 * c + 1] * att_ref[1]).astype(BF16)

    def put_out(rows, size, values):
        out = nn(mx_ref[:, rows].reshape(2 * size, WIN), values).reshape(2, size, WIN)
        ho_ref[rows] = jnp.where(m0, out[0], jnp.where(m1, out[1], 0.0))

    put_out(pl.ds(0, TRUNK), TRUNK, path_rows(qkv_ref, None, 0, v0))

    def fam_out(b, carry):
        for c in range(2):
            rows, size = fam_rows(b, c)
            put_out(rows, size, path_rows(qkv_ref, b, c, v0))
        return carry

    lax.fori_loop(0, 4, fam_out, 0)
    gain = gn_ref[0:1, pl.ds(w0, WIN)]
    for token, size, row, _, _ in SEGS:
        unit, _, _ = group_norm(ho_ref[row : row + size], m0, m1)
        old = nh_ref[token : token + size, pl.ds(w0, WIN)].astype(F32)
        nh_ref[token : token + size, pl.ds(w0, WIN)] = jnp.where(from_first, unit * gain, old).astype(BF16)
    hook(step, 2)


def bwd_kernel(
    hook, mix_ref, qkv_ref, t_ref, gn_ref, jj_ref, dn_ref, att_ref, pre_ref, qs_ref, ho_ref,
    dqkv_ref, ggn_ref, gmix_ref, gconv_ref,
    dist_ref, dh_ref, mx_ref, dm_ref, dc_ref, es_ref, dqx_ref, dk_ref, dv_ref,
):
    side, t, g = pl.program_id(0), pl.program_id(1), pl.program_id(2)
    mix0 = 8 * side + 4 * g
    step = (side * 2 + t) * 2 + g
    hook(step, 0)
    w0 = pl.multiple_of(g * 128, 128)
    m0, m1, from_first = head_masks(g)
    both = m0 | m1
    fill_distance(jj_ref, dist_ref)
    gain = gn_ref[0:1, pl.ds(w0, WIN)]
    gn_sum = jnp.zeros((1, WIN), F32)
    for token, size, row, _, _ in SEGS:
        unit, inv, stat = group_norm(ho_ref[row : row + size], m0, m1)
        dn = jnp.where(both, dn_ref[token : token + size, pl.ds(w0, WIN)].astype(F32), 0.0)
        gn_sum = gn_sum + jnp.sum(dn * unit, axis=0, keepdims=True)
        scaled = dn * gain
        d_head = inv * (scaled - stat(scaled) - unit * stat(scaled * unit))
        dh_ref[0, row : row + size] = jnp.where(m0, d_head, 0.0).astype(BF16)
        dh_ref[1, row : row + size] = jnp.where(m1, d_head, 0.0).astype(BF16)

    @pl.when((t == 0) & (g == 0))
    def _():
        ggn_ref[...] = jnp.zeros_like(ggn_ref)

    ggn_ref[0:1, pl.ds(w0, WIN)] += gn_sum
    k0, v0 = w0 + 384, w0 + 768
    for c in range(2):
        mx_ref[c] = (mix_ref[mix0 + 2 * c] * att_ref[0] + mix_ref[mix0 + 2 * c + 1] * att_ref[1]).astype(BF16)

    def add_keys(acc_ref, b, c, grads):
        acc_ref[0:TRUNK] += grads[0:TRUNK]
        branch = pl.ds(pl.multiple_of(TRUNK + SEG * b, SEG), SEG)
        if c == 0:
            acc_ref[branch] = grads[TRUNK : TRUNK + SEG]
        else:
            acc_ref[branch] += grads[TRUNK : TRUNK + SEG]
        acc_ref[pl.ds(pl.multiple_of(320 + 64 * b + SEG * c, SEG), SEG)] = grads[TRUNK + SEG :]

    def value_part(rows, size, values):
        heads = dh_ref[:, rows].reshape(2 * size, WIN)
        dm_ref[:, rows] = nt(heads, values).reshape(2, size, WIN)
        return tn(mx_ref[:, rows].reshape(2 * size, WIN), heads)

    dv_ref[0:TRUNK] = value_part(pl.ds(0, TRUNK), TRUNK, path_rows(qkv_ref, None, 0, v0))[0:TRUNK]

    def fam_values(b, carry):
        for c in range(2):
            rows, size = fam_rows(b, c)
            add_keys(dv_ref, b, c, value_part(rows, size, path_rows(qkv_ref, b, c, v0)))
        return carry

    lax.fori_loop(0, 4, fam_values, 0)

    def soft_part(block, sums):
        rows = pl.ds(pl.multiple_of(block * FAM, 32), FAM)
        dm = [dm_ref[c, rows] for c in range(2)]
        att = [att_ref[e, rows] for e in range(2)]
        out = []
        for e in range(2):
            d_att = mix_ref[mix0 + e] * dm[0] + mix_ref[mix0 + 2 + e] * dm[1]
            d_conv = att[e] * (d_att - jnp.sum(d_att * att[e], axis=-1, keepdims=True))
            dc_ref[e, rows] = d_conv.astype(BF16)
        for c in range(2):
            for e in range(2):
                out.append(sums[2 * c + e] + jnp.sum(dm[c] * att[e], axis=0, keepdims=True))
        return tuple(out)

    mix_sums = lax.fori_loop(0, 6, soft_part, tuple(jnp.zeros((1, WIN), F32) for _ in range(4)))
    gmix_ref[...] = jnp.zeros_like(gmix_ref)
    gconv_ref[...] = jnp.zeros_like(gconv_ref)
    for index in range(4):
        gmix_ref[index : index + 1] = mix_sums[index]
    mirror = lax.broadcasted_iota(jnp.int32, (WIN, WIN), 0) + lax.broadcasted_iota(jnp.int32, (WIN, WIN), 1) - (WIN - 1)
    band = jnp.abs(mirror) <= CK // 2
    hook(step, 1)
    flip = jnp.where(mirror == 0, 1.0, 0.0).astype(BF16)
    for e in range(2):
        flipped = nn(dc_ref[e], flip).astype(BF16)
        for a in range(CQ):
            cols = slice(a * WIN, (a + 1) * WIN)
            products = jnp.where(band, tn(flipped, pre_ref[e, :, cols]), 0.0)
            rolled = pltpu.roll(products, 24, 1, stride=1, stride_axis=0)
            gconv_ref[e, a : a + 1] = jnp.sum(rolled, axis=0, keepdims=True)
            grads = nt(dc_ref[e], t_ref[e, cols, :])
            es_ref[e, a] = jnp.where(dist_ref[...] >= a, grads, 0.0).astype(BF16)

    def score_part(rows, size, keys):
        grads = es_ref[:, :, rows].reshape(2 * CQ * size, WIN)
        back = nn(grads, keys).reshape(2, CQ, size, WIN)
        d_query = [jnp.where(m0, back[0, a], jnp.where(m1, back[1, a], 0.0)) for a in range(CQ)]
        return d_query, tn(grads, qs_ref[:, :, rows].reshape(2 * CQ * size, WIN))

    def shifted_sum(parts, start, size):
        zeros = jnp.zeros((8, WIN), F32)
        total = None
        for a in range(CQ):
            padded = jnp.concatenate([zeros, parts[a][start : start + size]], axis=0)
            if a:
                padded = pltpu.roll(padded, size + 8 - a, 0)
            total = padded if total is None else total + padded
        return total

    d_query, d_keys = score_part(pl.ds(0, TRUNK), TRUNK, path_rows(qkv_ref, None, 0, k0))
    dqx_ref[0:200] = shifted_sum(d_query, 0, TRUNK)
    dk_ref[0:TRUNK] = d_keys[0:TRUNK]

    def fam_scores(b, carry):
        ext = 200 + 120 * b
        for c in range(2):
            rows, size = fam_rows(b, c)
            d_query, d_keys = score_part(rows, size, path_rows(qkv_ref, b, c, k0))
            add_keys(dk_ref, b, c, d_keys)
            if c == 0:
                dqx_ref[pl.ds(pl.multiple_of(ext, 8), 40)] = shifted_sum(d_query, 0, SEG)
                dqx_ref[pl.ds(pl.multiple_of(ext + 40, 8), 40)] = shifted_sum(d_query, SEG, SEG)
            else:
                dqx_ref[pl.ds(pl.multiple_of(ext + 80, 8), 40)] = shifted_sum(d_query, 0, SEG)
        return carry

    lax.fori_loop(0, 4, fam_scores, 0)
    for b in range(4):
        ext = 200 + 120 * b
        dqx_ref[192:200] += dqx_ref[ext : ext + 8]
        dqx_ref[ext + 32 : ext + 40] += dqx_ref[ext + 40 : ext + 48] + dqx_ref[ext + 80 : ext + 88]

    def put(token, size, column, value):
        old = dqkv_ref[token : token + size, pl.ds(column, WIN)].astype(F32)
        dqkv_ref[token : token + size, pl.ds(column, WIN)] = jnp.where(from_first, value, old).astype(BF16)

    for token, size, _, ext, _ in SEGS:
        put(token, size, w0, dqx_ref[ext + 8 : ext + 8 + size])
        put(token, size, k0, dk_ref[token : token + size])
        put(token, size, v0, dv_ref[token : token + size])
    hook(step, 2)


def by_group(shape):
    tail = (0,) * (len(shape) - 3)
    return pl.BlockSpec((None, None, None) + shape[3:], lambda s, t, g: (s, t, g) + tail)


def by_side(shape):
    return pl.BlockSpec((None,) + shape, lambda s, t, g: (s, 0, 0))


def common_specs(first=None):
    return [
        pl.BlockSpec(memory_space=pltpu.SMEM),
        *(first or [pl.BlockSpec((TREE, 1152), lambda s, t, g: (t, s))]),
        pl.BlockSpec((None, None, 2, CQ * WIN, WIN), lambda s, t, g: (s, g, 0, 0, 0)),
        by_side((8, 384)),
        pl.BlockSpec((None, 16, WIN), lambda s, t, g: (t, 0, 0)),
    ]


PARAMS = dict(vmem_limit_bytes=60 * 1024 * 1024, dimension_semantics=("arbitrary",) * 3)


def saved_shapes(trees):
    lead = (2, trees, 2)
    return [lead + (2, TREE, WIN), lead + (2, TREE, CQ * WIN), lead + (2, CQ, TREE, WIN), lead + (TREE, WIN)]


def attention_forward(mix, normed, weight, toeplitz, gains, jj, gather=None):
    trees, width = normed.shape[0] // TREE, normed.shape[1]
    shapes = saved_shapes(trees)
    kinds = (F32, BF16, BF16, F32)
    weights, wide, count, collective = gather if gather else ((), (), 0, {})
    many, held = len(weights), len(wide)

    def kernel(*refs):
        inputs, loads, refs = refs[:6], refs[6 : 6 + many], refs[6 + many :]
        outs, full, refs = refs[:6], refs[6 : 6 + held], refs[6 + held :]
        work = Gather(DIRECT, LATER, loads, full, *refs[3:]) if gather else None

        def hook(step, place):
            if work:
                background(work, step, place)

        fwd_kernel(hook, *inputs, *outs, *refs[:3])

    anywhere = pl.BlockSpec(memory_space=pl.ANY)
    first = [pl.BlockSpec((TREE, width), lambda s, t, g: (t, 0)), pl.BlockSpec((width, 1152), lambda s, t, g: (0, s))]
    result = pl.pallas_call(
        kernel,
        grid=(2, trees, 2),
        in_specs=common_specs(first) + [anywhere] * many,
        out_specs=[pl.BlockSpec((TREE, 384), lambda s, t, g: (t, s))]
        + [by_group(s) for s in shapes]
        + [pl.BlockSpec((TREE, 1152), lambda s, t, g: (t, s))]
        + [anywhere] * held,
        out_shape=[jax.ShapeDtypeStruct((trees * TREE, 768), BF16)]
        + [jax.ShapeDtypeStruct(s, k) for s, k in zip(shapes, kinds)]
        + [jax.ShapeDtypeStruct((trees * TREE, 2304), BF16)]
        + [jax.ShapeDtypeStruct((width, w), BF16) for w in wide],
        scratch_shapes=[pltpu.VMEM((TREE, WIN), jnp.int32), pltpu.VMEM((EXT, WIN), F32), pltpu.VMEM((2, TREE, WIN), BF16)]
        + gather_scratch(weights, count),
        compiler_params=pltpu.CompilerParams(**PARAMS, **collective),
        cost_estimate=pl.CostEstimate(flops=90_000_000_000, bytes_accessed=120_000_000, transcendentals=0),
    )(mix, normed, weight, toeplitz, gains, jj, *weights)
    return result[0], result[1:5], result[5], result[6:]


def attention_backward(mix, qkv, toeplitz, gains, jj, d_normed, saved, sums=None):
    trees = qkv.shape[0] // TREE
    shapes = saved_shapes(trees)
    collective = dict(collective_id=4, has_side_effects=True) if sums else {}
    many = len(sums or ())

    def kernel(*refs):
        inputs, extra, refs = refs[:10], refs[10 : 10 + many], refs[10 + many :]
        outs, full, refs = refs[:4], refs[4 : 4 + many], refs[4 + many :]
        work = Finish(BESIDE, extra, None, full, None, refs[9:]) if sums else None

        def hook(step, place):
            if work:
                beside(work, step, place)

        bwd_kernel(hook, *inputs, *outs, *refs[:9])

    anywhere = pl.BlockSpec(memory_space=pl.ANY)
    extra_in = [pl.BlockSpec((384, 2048), lambda s, t, g: (0, 0))] if sums else []
    result = pl.pallas_call(
        kernel,
        grid=(2, trees, 2),
        in_specs=common_specs() + [pl.BlockSpec((TREE, 384), lambda s, t, g: (t, s))] + [by_group(s) for s in shapes] + extra_in,
        out_specs=[
            pl.BlockSpec((TREE, 1152), lambda s, t, g: (t, s)),
            by_side((8, 384)),
            by_group((2, trees, 2, 8, WIN)),
            by_group((2, trees, 2, 2, 8, WIN)),
        ]
        + [anywhere] * many,
        out_shape=[
            jax.ShapeDtypeStruct((trees * TREE, 2304), BF16),
            jax.ShapeDtypeStruct((2, 8, 384), F32),
            jax.ShapeDtypeStruct((2, trees, 2, 8, WIN), F32),
            jax.ShapeDtypeStruct((2, trees, 2, 2, 8, WIN), F32),
        ]
        + [jax.ShapeDtypeStruct((1536, n), BF16) for n in (1024,)[:many]],
        scratch_shapes=[
            pltpu.VMEM((TREE, WIN), jnp.int32),
            pltpu.VMEM((2, TREE, WIN), BF16),
            pltpu.VMEM((2, TREE, WIN), BF16),
            pltpu.VMEM((2, TREE, WIN), F32),
            pltpu.VMEM((2, TREE, WIN), BF16),
            pltpu.VMEM((2, CQ, TREE, WIN), BF16),
            pltpu.VMEM((EXT, WIN), F32),
            pltpu.VMEM((TREE, WIN), F32),
            pltpu.VMEM((TREE, WIN), F32),
        ]
        + (finish_scratch(BESIDE, 128) if sums else []),
        compiler_params=pltpu.CompilerParams(**PARAMS, **collective),
        cost_estimate=pl.CostEstimate(flops=1_000_000_000, bytes_accessed=1_000_000, transcendentals=0),
    )(mix, qkv, toeplitz, gains, jj, d_normed, *saved, *(sums or ()))
    return result[:4], result[4:]


def band_rows(conv_w):
    rows = conv_w.reshape(-1, CK) * (1.0 / math.sqrt(HD))
    middle = jnp.zeros((rows.shape[0], WIN - CK), F32)
    return jnp.concatenate([rows[:, CK // 2 :], middle, rows[:, : CK // 2]], axis=1)


def fill_toeplitz(rows_ref, side, out_ref):
    offset = lax.broadcasted_iota(jnp.int32, (WIN, WIN), 1) - lax.broadcasted_iota(jnp.int32, (WIN, WIN), 0)
    band = jnp.abs(offset) <= CK // 2
    for head in range(4):
        for a in range(CQ):
            row = rows_ref[side, head * CQ + a : head * CQ + a + 1, :]
            rolled = pltpu.roll(jnp.broadcast_to(row, (WIN, WIN)), 0, 1, stride=1, stride_axis=0)
            out_ref[side, head // 2, head % 2, a * WIN : (a + 1) * WIN, :] = jnp.where(band, rolled, 0.0).astype(BF16)


def key_positions(valid):
    trees = valid.shape[0] // TREE
    valid = valid.reshape(trees, TREE)
    far = jnp.int32(1 << 20)

    def places(part, start):
        return jnp.where(part > 0, lax.broadcasted_iota(jnp.int32, part.shape, 1) + start, far)

    trunk = places(valid[:, :TRUNK], 0)
    empty = jnp.full((trees, SEG), far, jnp.int32)
    rows = [jnp.concatenate([trunk, empty, empty], axis=1)]
    for b in range(4):
        branch = places(valid[:, TRUNK + SEG * b : TRUNK + SEG * (b + 1)], TRUNK)
        rows.append(jnp.concatenate([trunk, branch, empty], axis=1))
        for c in range(2):
            first = 320 + 64 * b + SEG * c
            leaf = places(valid[:, first : first + SEG], TRUNK + SEG)
            rows.append(jnp.concatenate([trunk, branch, leaf], axis=1))
    rows += [jnp.zeros((trees, WIN), jnp.int32)] * 3
    return jnp.stack(rows, axis=1)


def conv_grads(gconv):
    lanes = gconv[..., :CQ, 18:29][..., ::-1] * (1.0 / math.sqrt(HD))
    return jnp.sum(lanes, axis=1).reshape(2, -1)


def mix_grads(gmix):
    return jnp.sum(gmix[:, :, :, :4], axis=(1, 4)).reshape(2, -1)


MESH = pl.DeviceIdType.MESH

FIRST = ((0, 0, 0, 0, 1152, 384), (1, 0, 0, 384, 1536, 384), (2, 0, 0, 768, 1920, 384))
LATER = (
    (0, 0, 0, 0, 384, 384),
    (1, 1, 0, 0, 2048, 512),
    (2, 1, 0, 512, 2560, 512),
    (1, 1, 512, 1024, 3072, 512),
    (2, 1, 512, 1536, 3584, 512),
    (3, 2, 0, 0, 1024, 512),
    (3, 2, 512, 512, 1536, 512),
)
WHOLE = 5
DIRECT = 0
LAST = ((0, 0, 0, 0, 1024, 512), (0, 0, 512, 512, 1536, 512))


def greet(peers):
    sem = pltpu.get_barrier_semaphore()
    for peer in peers:
        pl.semaphore_signal(sem, inc=1, device_id=peer, device_id_type=MESH)
    pl.semaphore_wait(sem, len(peers))


class Gather:
    def __init__(self, direct, items, weights, fulls, send, recv, local, *held):
        self.direct = direct
        self.items, self.weights, self.fulls, self.held = items, weights, fulls, held
        self.send, self.recv, self.local = send, recv, local
        q, c, z = lax.axis_index("plane"), lax.axis_index("core"), lax.axis_index("tensor")
        self.home = (z // 2) == c
        self.q = q
        self.core = (q, 1 - c, z)
        self.far = (q, 1 - c, (z + 2) % 4)
        self.near = (q, c, (z // 2) * 2 + (1 - z % 2))
        self.by_x = ((q // 2) * 2 + (1 - q % 2), c, z)
        self.by_y = ((q + 2) % 4, c, z)

    def away(self, action):
        pl.when(jnp.logical_not(self.home))(action)

    def whole(self, item, side):
        _, out, _, first, second, size = self.items[item]
        return self.fulls[out], pl.ds((first, second)[side], size)

    def z_copy(self, item, side, relay=False):
        weight, _, source_col, _, _, size = self.items[item]
        mine = pl.ds(pl.multiple_of(self.q * 384, 128), 384)
        ref, cols = self.whole(item, side)
        source = ref.at[mine, self.whole(item, 0)[1]] if relay else self.weights[weight].at[mine, pl.ds(source_col, size)]
        return pltpu.make_async_remote_copy(
            src_ref=source, dst_ref=ref.at[mine, cols], send_sem=self.send.at[item, side],
            recv_sem=self.recv.at[item, side], device_id=(self.far, self.near)[side], device_id_type=MESH)

    def plane_copy(self, item, side, step):
        ref, cols = self.whole(item, side)
        if step < 2:
            owner, first, size = self.q, 0, 384
        elif step == 2:
            owner, first, size = self.by_x[0], 0, 192
        else:
            owner, first, size = self.by_y[0], 192, 192
        span = pl.ds(pl.multiple_of(owner * 384 + first, 64), size)
        slot = 2 + 4 * side + step
        return pltpu.make_async_remote_copy(
            src_ref=ref.at[span, cols], dst_ref=ref.at[span, cols], send_sem=self.send.at[item, slot], recv_sem=self.recv.at[item, slot],
            device_id=(self.by_x, self.by_y, self.by_y, self.by_x)[step], device_id_type=MESH)

    def own_load(self, weight):
        return pltpu.make_async_copy(self.weights[weight], self.held[weight], self.local.at[weight, 0])

    def own_stores(self, weight):
        copies = []
        for number, (index, out, source_col, first, _, size) in enumerate(self.items):
            if index == weight:
                source = self.held[weight].at[:, pl.ds(source_col, size)]
                copies.append(pltpu.make_async_copy(source, self.fulls[out].at[:, pl.ds(first, size)], self.local.at[number, 1]))
        return copies

    def own(self):
        @pl.when(self.home)
        def _():
            for weight in range(len(self.weights)):
                self.own_load(weight).start()

    def pass_own(self, weight):
        @pl.when(self.home)
        def _():
            self.own_load(weight).wait()
            for copy in self.own_stores(weight):
                copy.start()

    def wait_own(self):
        @pl.when(self.home)
        def _():
            for weight in range(len(self.weights)):
                for copy in self.own_stores(weight):
                    copy.wait()

    def each(self, action):
        action(1)

        @self.away
        def _():
            action(0)

    def across_copy(self, item):
        weight, _, source_col, _, _, size = self.items[item]
        span = pl.ds(pl.multiple_of((3 - self.q) * 384, 128), 384)
        ref, cols = self.whole(item, 1)
        return pltpu.make_async_remote_copy(
            src_ref=self.weights[weight].at[span, pl.ds(source_col, size)], dst_ref=ref.at[span, cols], send_sem=self.send.at[item, 8],
            recv_sem=self.recv.at[item, 8], device_id=self.near, device_id_type=MESH)

    def start_z(self, item):
        @pl.when(self.home)
        def _():
            self.z_copy(item, 1).start()
            if item < self.direct:
                self.across_copy(item).start()

        @self.away
        def _():
            self.z_copy(item, 0).start()

    def relay_z(self, item):
        @self.away
        def _():
            self.z_copy(item, 0).wait_recv()
            self.z_copy(item, 1, True).start()
            self.plane_copy(item, 0, 0).start()
            self.plane_copy(item, 0, 1).start()

    def relay_only(self, item):
        @self.away
        def _():
            self.z_copy(item, 0).wait_recv()
            self.z_copy(item, 1, True).start()

    def finish_z(self, item):
        self.z_copy(item, 1).wait_recv()
        self.each(lambda side: self.z_copy(item, side).wait_send())

    def start_both(self, item):
        def act(side):
            self.plane_copy(item, side, 0).start()
            self.plane_copy(item, side, 1).start()

        self.each(act)

    def start_plane(self, item):
        self.z_copy(item, 1).wait_recv()
        self.plane_copy(item, 1, 0).start()
        self.plane_copy(item, 1, 1).start()

    def forward(self, item):
        def act(side):
            self.plane_copy(item, side, 0).wait_recv()
            self.plane_copy(item, side, 2).start()
            self.plane_copy(item, side, 1).wait_recv()
            self.plane_copy(item, side, 3).start()

        if item < self.direct:

            @self.away
            def _():
                act(1)
                act(0)

        else:
            self.each(act)

    def finish(self, item):
        def act(side):
            self.plane_copy(item, side, 2).wait_recv()
            self.plane_copy(item, side, 3).wait_recv()
            if self.weights:
                self.z_copy(item, side).wait_send()
            for step in range(4):
                self.plane_copy(item, side, step).wait_send()

        if item >= self.direct:
            self.each(act)
            return

        @self.away
        def _():
            act(1)
            act(0)

        @pl.when(self.home)
        def _():
            self.z_copy(item, 1).wait_send()
            self.across_copy(item).wait()
            for step in range(2):
                self.plane_copy(item, 1, step).wait()


def gather_scratch(weights, count):
    if not weights:
        return []
    return [pltpu.SemaphoreType.DMA((count, 10)), pltpu.SemaphoreType.DMA((count, 10)), pltpu.SemaphoreType.DMA((max(count, len(weights)), 2))] + [
        pltpu.VMEM(w.shape, BF16) for w in weights
    ]


SLOTS = {
    1: (("relay_z", 0), ("start_z", 2), ("pass_own", 0)),
    2: (("start_plane", 0),),
    3: (("relay_z", 1), ("start_z", 3), ("pass_own", 1)),
    4: (("forward", 0), ("start_plane", 1)),
    5: (("relay_z", 2), ("start_z", 4), ("pass_own", 2)),
    6: (("forward", 1), ("start_plane", 2)),
    7: (("relay_z", 3), ("pass_own", 3)),
    8: (("forward", 2), ("start_plane", 3), ("start_z", 5)),
    9: (("relay_z", 4), ("start_z", 6)),
    10: (("forward", 3), ("start_plane", 4)),
    11: (("relay_only", 5),),
    12: (("forward", 4),),
    13: (("relay_only", 6),),
}


def background(work, step, place):
    if place == 2:

        @pl.when(step == 7)
        def _():
            for item in range(len(work.items)):
                if item < WHOLE:
                    work.finish(item)
                else:
                    work.finish_z(item)
            work.wait_own()

        return

    for turn in range(8):
        slot = 2 * turn + place

        @pl.when(step == turn)
        def _(slot=slot):
            if slot == 0:
                work.own()
                greet((work.near, work.far, work.by_x, work.by_y))
                for item in range(2):
                    work.start_z(item)
            for name, item in SLOTS.get(slot, ()):
                getattr(work, name)(item)


TILE = 512


def beside_gate(work, step, place):
    script = {(0, 0): (("start_both", 0), ("start_both", 1)), (1, 1): (("forward", 0),), (3, 0): (("forward", 1),)}
    for (turn, where), names in script.items():
        if where == place:

            @pl.when(step == turn)
            def _(names=names, turn=turn):
                if turn == 0:
                    greet((work.by_x, work.by_y))
                for name, item in names:
                    getattr(work, name)(item)


def gated_forward(normed, weight, part=None):
    rows, width = normed.shape
    units = weight.shape[1] // 2
    many = 0 if part is None else 1
    count = len(LAST)

    def kernel(x_ref, w_ref, *refs):
        hidden_ref, gate_ref, up_ref, refs = refs[many], refs[many + 1], refs[many + 2], refs[many + 3 :]
        step = pl.program_id(0)
        work = Gather(0, LAST, (), refs[:1], refs[1], refs[2], None) if many else None
        if work:
            beside_gate(work, step, 0)
        gate = nn(x_ref[...], w_ref[:, :TILE])
        gate_ref[...] = gate.astype(BF16)
        if work:
            beside_gate(work, step, 1)
        up = nn(x_ref[...], w_ref[:, TILE:])
        up_ref[...] = up.astype(BF16)
        hidden_ref[...] = (gate * jax.nn.sigmoid(gate) * up).astype(BF16)
        if work:

            @pl.when(step == units // TILE - 1)
            def _():
                for item in range(count):
                    work.finish(item)

    anywhere = pl.BlockSpec(memory_space=pl.ANY)
    tile = pl.BlockSpec((rows, TILE), lambda j: (0, j))
    collective = dict(collective_id=5, has_side_effects=True) if many else {}
    extra = [] if part is None else [part]
    result = pl.pallas_call(
        kernel,
        grid=(units // TILE,),
        in_specs=[pl.BlockSpec((rows, width), lambda j: (0, 0)), pl.BlockSpec((width, 2 * TILE), lambda j: (0, j))] + [anywhere] * many,
        out_specs=[tile] * 3 + [anywhere] * many,
        out_shape=[jax.ShapeDtypeStruct((rows, units), BF16)] * 3 + [jax.ShapeDtypeStruct(p.shape, BF16) for p in extra],
        scratch_shapes=[pltpu.SemaphoreType.DMA((count, 10))] * 2 * many,
        input_output_aliases={2: 3} if many else {},
        compiler_params=pltpu.CompilerParams(vmem_limit_bytes=60 * 1024 * 1024, **collective),
    )(normed, weight, *extra)
    return result[:3], result[3:]


def gated_backward(d_out, down, gate, up, normed):
    rows, width = d_out.shape
    units = gate.shape[1]

    def kernel(d_ref, down_ref, gate_ref, up_ref, x_ref, d_gu_ref, grads_ref):
        d_hidden = nn(d_ref[...], down_ref[...])
        gate_value, up_value = gate_ref[...].astype(F32), up_ref[...].astype(F32)
        s = jax.nn.sigmoid(gate_value)
        d_gu_ref[:, :TILE] = (d_hidden * up_value * s * (1.0 + gate_value * (1.0 - s))).astype(BF16)
        d_gu_ref[:, TILE:] = (d_hidden * gate_value * s).astype(BF16)
        grads_ref[...] = tn(x_ref[...], d_gu_ref[...]).astype(BF16)

    whole = pl.BlockSpec((rows, width), lambda j: (0, 0))
    tile = pl.BlockSpec((rows, TILE), lambda j: (0, j))
    return pl.pallas_call(
        kernel,
        grid=(units // TILE,),
        in_specs=[whole, pl.BlockSpec((width, TILE), lambda j: (0, j)), tile, tile, whole],
        out_specs=[pl.BlockSpec((rows, 2 * TILE), lambda j: (0, j)), pl.BlockSpec((width, 2 * TILE), lambda j: (0, j))],
        out_shape=[jax.ShapeDtypeStruct((rows, 2 * units), BF16), jax.ShapeDtypeStruct((width, 2 * units), BF16)],
        compiler_params=pltpu.CompilerParams(vmem_limit_bytes=60 * 1024 * 1024),
        cost_estimate=pl.CostEstimate(flops=22_000_000_000, bytes_accessed=40_000_000, transcendentals=0),
    )(d_out, down, gate, up, normed)


def opening_kernel(tokens_ref, gain_ref, small_ref, wq_ref, wk_ref, wv_ref, full_ref, normed_ref, toep_ref, both_ref, send, recv, local, held0, held1, held2, extra_send, extra_recv):
    work = Gather(3, FIRST, (wq_ref, wk_ref, wv_ref), (full_ref,), send, recv, local, held0, held1, held2)
    rows = tokens_ref.shape[0]

    def extra(source, target, index, peer):
        return pltpu.make_async_remote_copy(
            src_ref=source, dst_ref=target, send_sem=extra_send.at[index], recv_sem=extra_recv.at[index], device_id=peer, device_id_type=MESH)

    far_small = extra(small_ref, both_ref.at[0], 0, work.far)
    near_small = extra(both_ref.at[0], both_ref.at[1], 1, work.near)
    normed_out = extra(normed_ref.at[0:rows], normed_ref.at[rows : 2 * rows], 2, work.core)
    work.own()
    greet((work.near, work.far, work.by_x, work.by_y, work.core))

    @work.away
    def _():
        far_small.start()

    @pl.when(work.home)
    def _():
        both_ref[0] = small_ref[...]
        near_small.start()

    for item in range(3):
        work.start_z(item)
    for start in range(0, rows, 96):
        x = tokens_ref[start : start + 96].astype(F32)
        inv = lax.rsqrt(jnp.mean(x * x, axis=-1, keepdims=True) + 1e-06)
        normed_ref[start : start + 96] = (x * inv * gain_ref[...]).astype(BF16)
    normed_out.start()

    @work.away
    def _():
        far_small.wait_recv()
        near_small.start()

    work.relay_z(0)
    work.start_plane(0)
    fill_toeplitz(both_ref, 0, toep_ref)
    work.relay_z(1)
    work.start_plane(1)
    work.forward(0)
    for weight in range(3):
        work.pass_own(weight)
    near_small.wait_recv()
    work.relay_z(2)
    work.start_plane(2)
    work.forward(1)
    fill_toeplitz(both_ref, 1, toep_ref)
    work.forward(2)
    for item in range(3):
        work.finish(item)
    work.wait_own()
    near_small.wait_send()

    @work.away
    def _():
        far_small.wait_send()

    normed_out.wait()


def opening(tokens, gain, small, weights, collective_id):
    vmem = pl.BlockSpec(memory_space=pltpu.VMEM)
    anywhere = pl.BlockSpec(memory_space=pl.ANY)
    rows, width = tokens.shape
    return pl.pallas_call(
        opening_kernel,
        in_specs=[vmem] * 3 + [anywhere] * 3,
        out_specs=[anywhere] + [vmem] * 3,
        out_shape=[
            jax.ShapeDtypeStruct((width, 2304), BF16),
            jax.ShapeDtypeStruct((2 * rows, width), BF16),
            jax.ShapeDtypeStruct((2, 2, 2, CQ * WIN, WIN), BF16),
            jax.ShapeDtypeStruct((2,) + small.shape, F32),
        ],
        scratch_shapes=gather_scratch(weights, 3) + [pltpu.SemaphoreType.DMA((3,)), pltpu.SemaphoreType.DMA((3,))],
        compiler_params=pltpu.CompilerParams(collective_id=collective_id, has_side_effects=True, vmem_limit_bytes=60 * 1024 * 1024),
    )(tokens, gain, small, *weights)


class Finish:
    def __init__(self, plan, parts, raw, outs, small, bufs, made=False):
        self.made = made
        q, c, z = lax.axis_index("plane"), lax.axis_index("core"), lax.axis_index("tensor")
        self.q, self.c = q, c
        self.home = (z // 2) == c
        self.by_x = ((q // 2) * 2 + (1 - q % 2), c, z)
        self.by_y = ((q + 2) % 4, c, z)
        self.core = (q, 1 - c, z)
        self.near = (q, c, (z // 2) * 2 + (1 - z % 2))
        self.far = (q, 1 - c, (z + 2) % 4)
        self.across = (q, c, (z + 2) % 4)
        self.plan, self.parts, self.raw, self.outs, self.small = plan, parts, raw, outs, small
        (self.near_buf, self.far_buf, self.core_buf, self.here_buf, self.raw_part, self.raw_own, self.raw_first,
         self.raw_second, self.send, self.recv, self.raw_send, self.raw_recv, self.local) = bufs[:13]
        if small is not None:
            self.small_buf, self.small_in, self.small_send, self.small_recv = bufs[13:]

    def remote(self, src, dst, sems, index, peer):
        return pltpu.make_async_remote_copy(
            src_ref=src, dst_ref=dst, send_sem=sems[0].at[index], recv_sem=sems[1].at[index], device_id=peer, device_id_type=MESH)

    def columns(self, item):
        _, first_a, first_b, size, _, _, at = self.plan[item]
        return pl.ds(first_a, size), pl.ds(first_b, size), pl.ds(at, size)

    def part(self, item):
        source = self.plan[item][0]
        if source >= 0:
            return self.parts[source]
        return self.raw.at[self.rows(self.q)] if self.made else self.raw_part

    def away(self, action):
        pl.when(jnp.logical_not(self.home))(action)

    def rows(self, owner):
        return pl.ds(pl.multiple_of(owner * 384, 128), 384)

    def raw_copies(self, item):
        cols_a, cols_b, _ = self.columns(item)
        sems = (self.raw_send, self.raw_recv)
        across = 3 - self.q
        x, y = self.by_x[0], self.by_y[0]
        remote = [
            self.remote(self.raw.at[self.rows(x), cols_a], self.raw_first.at[0, :, cols_a], sems, (item, 0), self.by_x),
            self.remote(self.raw.at[self.rows(across), cols_a], self.raw_first.at[1, :, cols_a], sems, (item, 1), self.by_x),
            self.remote(self.raw.at[self.rows(y), cols_b], self.raw_first.at[0, :, cols_b], sems, (item, 2), self.by_y),
            self.remote(self.raw.at[self.rows(across), cols_b], self.raw_first.at[1, :, cols_b], sems, (item, 3), self.by_y),
        ]
        if self.made:
            return remote, []
        return remote, [
            pltpu.make_async_copy(self.raw.at[self.rows(self.q), cols_a], self.raw_own.at[0, :, cols_a], self.local.at[item, 0]),
            pltpu.make_async_copy(self.raw.at[self.rows(y), cols_a], self.raw_own.at[1, :, cols_a], self.local.at[item, 1]),
            pltpu.make_async_copy(self.raw.at[self.rows(self.q), cols_b], self.raw_own.at[0, :, cols_b], self.local.at[item, 2]),
            pltpu.make_async_copy(self.raw.at[self.rows(x), cols_b], self.raw_own.at[1, :, cols_b], self.local.at[item, 3]),
        ]

    def raw_place(self, which, side, cols):
        if self.made:
            owner = self.q if which == 0 else (self.by_y[0], self.by_x[0])[side]
            return self.raw, (self.rows(owner), cols)
        return self.raw_own, (which, slice(None), cols)

    def raw_second_copies(self, item):
        sems = (self.raw_send, self.raw_recv)
        copies = []
        for side, cols in enumerate(self.columns(item)[:2]):
            ref, place = self.raw_place(1, side, cols)
            copies.append(self.remote(ref.at[place], self.raw_second.at[:, cols], sems, (item, 4 + side), (self.by_y, self.by_x)[side]))
        return copies

    def r1_side(self, item, side):
        for copy in self.raw_copies(item)[0][2 * side : 2 * side + 2]:
            copy.start()

    def r1(self, item):
        for group in self.raw_copies(item):
            for copy in group:
                copy.start()

    def r2(self, item):
        remote, own = self.raw_copies(item)
        for copy in own:
            copy.wait()
        for side, cols in enumerate(self.columns(item)[:2]):
            remote[2 * side + 1].wait_recv()
            ref, place = self.raw_place(1, side, cols)
            ref[place] = added(ref[place], self.raw_first[1, :, cols])
            self.raw_second_copies(item)[side].start()

    def r3(self, item):
        remote, _ = self.raw_copies(item)
        for side, cols in enumerate(self.columns(item)[:2]):
            remote[2 * side].wait_recv()
            self.raw_second_copies(item)[side].wait_recv()
            ref, place = self.raw_place(0, side, cols)
            total = ref[place].astype(F32) + self.raw_first[0, :, cols].astype(F32) + self.raw_second[:, cols].astype(F32)
            self.part(item)[:, cols] = total.astype(BF16)

    def near_copy(self, item):
        _, cols_b, at = self.columns(item)
        return self.remote(self.part(item).at[:, cols_b], self.near_buf.at[:, self.spot(item)], (self.send, self.recv), (item, 0), self.near)

    def spot(self, item):
        return pl.ds(self.plan[item][5], self.plan[item][3])

    def far_copy(self, item):
        spot = self.spot(item)
        return self.remote(self.here_buf.at[:, spot], self.far_buf.at[:, spot], (self.send, self.recv), (item, 1), self.far)

    def core_copy(self, item, relayed):
        spot = self.spot(item)
        source = self.far_buf if relayed else self.here_buf
        return self.remote(source.at[:, spot], self.core_buf.at[:, spot], (self.send, self.recv), (item, 2), self.core)

    def s1(self, item):
        self.near_copy(item).start()

    def s2(self, item):
        spot, cols_a = self.spot(item), self.columns(item)[0]
        self.near_copy(item).wait_recv()
        self.here_buf[:, spot] = added(self.part(item)[:, cols_a], self.near_buf[:, spot])

        @pl.when(self.home)
        def _():
            self.core_copy(item, False).start()

        @self.away
        def _():
            self.far_copy(item).start()

    def s3(self, item):
        @self.away
        def _():
            self.far_copy(item).wait_recv()
            self.core_copy(item, True).start()

    def plane_copies(self, item):
        out = self.outs[self.plan[item][4]]
        at, spot = self.columns(item)[2], self.spot(item)
        sems = (self.send, self.recv)
        half = self.c * 192

        def rows(owner, first, size):
            return pl.ds(pl.multiple_of(owner * 384 + half + first, 32), size)

        mine = self.core_buf.at[pl.ds(pl.multiple_of(half, 32), 192), spot]
        x, y, across = self.by_x[0], self.by_y[0], 3 - self.q
        own = out.at[rows(self.q, 0, 192), at]
        top, low = out.at[rows(x, 0, 96), at], out.at[rows(y, 96, 96), at]
        return [
            self.remote(mine, own, sems, (item, 3), self.by_x),
            self.remote(mine, own, sems, (item, 4), self.by_y),
            self.remote(top, top, sems, (item, 5), self.by_y),
            self.remote(low, low, sems, (item, 6), self.by_x),
        ] + [
            self.remote(out.at[rows(o, 0, 192), at], out.at[rows(o, 0, 192), at], sems, (item, 7 + i), self.core)
            for i, o in enumerate((x, y, across))
        ]

    def own_copy(self, item):
        out = self.outs[self.plan[item][4]]
        rows = pl.ds(pl.multiple_of(self.q * 384, 128), 384)
        return pltpu.make_async_copy(self.core_buf.at[:, self.spot(item)], out.at[rows, self.columns(item)[2]], self.local.at[item, 4])

    def s4(self, item):
        spot = self.spot(item)

        @pl.when(self.home)
        def _():
            self.core_copy(item, False).wait_recv()
            self.core_buf[:, spot] = added(self.here_buf[:, spot], self.core_buf[:, spot])

        @self.away
        def _():
            self.core_copy(item, True).wait_recv()
            self.core_buf[:, spot] = added(self.far_buf[:, spot], self.core_buf[:, spot])

        self.own_copy(item).start()
        copies = self.plane_copies(item)
        copies[0].start()
        copies[1].start()

    def s5(self, item):
        copies = self.plane_copies(item)
        copies[0].wait_recv()
        copies[2].start()
        copies[4].start()
        copies[1].wait_recv()
        copies[3].start()
        copies[5].start()

    def s6(self, item):
        copies = self.plane_copies(item)
        copies[2].wait_recv()
        copies[3].wait_recv()
        copies[6].start()

    def s7(self, item):
        copies = self.plane_copies(item)
        self.own_copy(item).wait()
        for copy in copies[4:]:
            copy.wait_recv()
        for copy in copies:
            copy.wait_send()
        self.near_copy(item).wait_send()

        @pl.when(self.home)
        def _():
            self.core_copy(item, False).wait_send()

        @self.away
        def _():
            self.core_copy(item, True).wait_send()
            self.far_copy(item).wait_send()

        if self.plan[item][0] < 0:
            for copy in self.raw_copies(item)[0] + self.raw_second_copies(item):
                copy.wait_send()

    def small_copy(self, turn):
        peer = (self.core, self.by_x, self.by_y, self.near, self.across)[turn]
        return self.remote(self.small_buf.at[turn], self.small_in.at[turn], (self.small_send, self.small_recv), turn, peer)

    def small_start(self):
        self.small_copy(0).start()

    def small_next(self, turn):
        self.small_copy(turn).wait_recv()
        self.small_buf[turn + 1] = self.small_buf[turn] + self.small_in[turn]
        if turn < 4:
            self.small_copy(turn + 1).start()

    def small_done(self, out):
        for turn in range(5):
            self.small_copy(turn).wait_send()
        out[...] = self.small_buf[5]


def added(left, right):
    return (left.astype(F32) + right.astype(F32)).astype(BF16)


FINISH = (
    (0, 0, 2048, 512, 0, 0, 0),
    (0, 512, 2560, 512, 1, 512, 0),
    (0, 1024, 3072, 512, 0, 1024, 512),
    (0, 1536, 3584, 512, 1, 1536, 512),
    (-1, 0, 1152, 384, 2, 2048, 0),
    (-1, 384, 1536, 384, 2, 2432, 384),
    (-1, 768, 1920, 384, 2, 2816, 768),
)
LONE = ((-1, 0, 384, 384, 0, 0, 0),)
BESIDE = (
    (0, 0, 1024, 512, 0, 0, 0),
    (0, 512, 1536, 512, 0, 512, 512),
)
BESIDE_STEPS = (
    (("greet", 0), ("s1", 0), ("s1", 1)),
    (),
    (("s2", 0),),
    (("s2", 1),),
    (("s3", 0),),
    (("s3", 1),),
    (("s4", 0),),
    (("s4", 1),),
    (),
    (),
    (("s5", 0),),
    (("s5", 1),),
    (),
    (("s6", 0),),
    (("s6", 1),),
)


def finish_scratch(plan, raw_width, made=False):
    count, width = len(plan), sum(item[3] for item in plan)
    return (
        [pltpu.VMEM((384, width), BF16)] * 4
        + [pltpu.VMEM((384, 128 if made else raw_width), BF16)]
        + [pltpu.VMEM((2, 384, 128 if made else raw_width), BF16), pltpu.VMEM((2, 384, raw_width), BF16)]
        + [pltpu.VMEM((384, raw_width), BF16)]
        + [pltpu.SemaphoreType.DMA((count, 10))] * 2
        + [pltpu.SemaphoreType.DMA((count, 6))] * 2
        + [pltpu.SemaphoreType.DMA((count, 5))]
    )


def beside(work, step, place):
    if place == 2:

        @pl.when(step == 7)
        def _():
            for item in range(len(work.plan)):
                work.s7(item)

        return

    for slot, names in enumerate(BESIDE_STEPS):
        if slot % 2 == place:

            @pl.when(step == slot // 2)
            def _(names=names):
                for name, item in names:
                    if name == "greet":
                        greet((work.near, work.far, work.by_x, work.by_y, work.core))
                    else:
                        getattr(work, name)(item)


def finish_kernel(
    small, gu, out, normed, d_qkv, weight, tokens, gain, d_hidden, small_out, d_input, o_gate, o_up, o_qkv, o_out,
    made, partner, arrived, loaded, load_sem, hidden_buf, tokens_buf, hidden_sem, core_send, core_recv, *bufs,
):
    lone = Finish(LONE, (), out, (o_out,), None, bufs[-13:])
    work = Finish(FINISH, (gu,), made, (o_gate, o_up, o_qkv), small, bufs[:-13], True)
    rows = tokens.shape[0]

    def load(part):
        return pltpu.make_async_copy(weight.at[384 * part : 384 * (part + 1)], loaded.at[part % 2], load_sem.at[part % 2])

    def exchange(part):
        cols = pl.ds(384 * part, 384)
        return work.remote(partner.at[:, cols], arrived.at[:, cols], (core_send, core_recv), part, work.core)

    def load_hidden(part):
        span = pl.ds(64 * part, 64)
        return (
            pltpu.make_async_copy(d_hidden.at[span], hidden_buf.at[part % 2], hidden_sem.at[0, part % 2]),
            pltpu.make_async_copy(tokens.at[span], tokens_buf.at[part % 2], hidden_sem.at[1, part % 2]),
        )

    load(0).start()
    load(1).start()
    for copy in load_hidden(0):
        copy.start()
    greet((work.near, work.far, work.by_x, work.by_y, work.core, work.across))
    lone.r1(0)
    work.s1(0)
    work.s1(1)

    def make(side, owner):
        cols = slice(1152 * side, 1152 * (side + 1))
        made[work.rows(owner), cols] = tn(normed[:, work.rows(owner)], d_qkv[:, cols]).astype(BF16)

    across = 3 - work.q
    for side, owners in enumerate(((across, work.by_x[0]), (across, work.by_y[0]))):
        for owner in owners:
            make(side, owner)
        for item in (4, 5, 6):
            work.r1_side(item, side)
    work.s2(0)
    work.s1(2)
    lone.r2(0)
    make(0, work.by_y[0])
    work.s2(1)
    work.s1(3)
    make(1, work.by_x[0])
    work.s3(0)
    make(0, work.q)
    work.s2(2)
    work.s3(1)
    make(1, work.q)
    work.r2(4)
    lone.r3(0)
    lone.s1(0)
    work.s4(0)

    def back(part):
        cols = slice(384 * part, 384 * (part + 1))
        load(part).wait()
        both = nt(d_qkv[...], loaded[part % 2])
        d_input[:, cols] = both[:rows]
        partner[:, cols] = both[rows:].astype(BF16)
        if part < 2:
            load(part + 2).start()
        exchange(part).start()

    back(0)
    work.r2(5)
    work.s2(3)
    work.s4(1)
    back(1)
    work.r2(6)
    work.r3(4)
    work.s1(4)
    work.s3(2)
    work.s5(0)
    back(2)
    lone.s2(0)
    work.r3(5)
    work.s1(5)
    work.s3(3)
    work.s4(2)
    work.s5(1)
    back(3)
    work.s2(4)
    work.r3(6)
    work.s1(6)
    work.s4(3)
    work.s6(0)
    for part in range(4):
        exchange(part).wait_recv()
    gain_sum = jnp.zeros((1, tokens.shape[1]), F32)
    for part in range(rows // 64):
        span = slice(64 * part, 64 * (part + 1))
        if part + 1 < rows // 64:
            for copy in load_hidden(part + 1):
                copy.start()
        for copy in load_hidden(part):
            copy.wait()
        x = tokens_buf[part % 2].astype(F32)
        inv = lax.rsqrt(jnp.mean(x * x, axis=-1, keepdims=True) + 1e-06)
        d_normed = d_input[span] + arrived[span].astype(F32)
        scaled = d_normed * gain[...]
        gain_sum = gain_sum + jnp.sum(d_normed * x * inv, axis=0, keepdims=True)
        d_input[span] = hidden_buf[part % 2] + inv * scaled - x * inv**3 * jnp.mean(scaled * x, axis=-1, keepdims=True)
    work.small_buf[0] = small[...]
    work.small_buf[0, 0:1] = gain_sum
    work.small_start()
    script = (
        ("s3", 4), ("s2", 5), ("s3", 7), ("s6", 1), ("s5", 2), ("m", 0),
        ("s4", 4), ("s3", 5), ("s2", 6), ("s4", 7), ("s5", 3), ("s6", 2), ("m", 1),
        ("s5", 4), ("s4", 5), ("s3", 6), ("s5", 7), ("s6", 3), ("m", 2),
        ("s6", 4), ("s5", 5), ("s4", 6), ("s6", 7), ("m", 3), ("s6", 5), ("s5", 6), ("m", 4), ("s6", 6),
    )
    for name, item in script:
        if name == "m":
            work.small_next(item)
        elif item == 7:
            getattr(lone, name)(0)
        else:
            getattr(work, name)(item)
    for item in range(len(FINISH)):
        work.s7(item)
    lone.s7(0)
    for part in range(4):
        exchange(part).wait_send()
    work.small_done(small_out)


def finish_gradients(small, gu, out, normed, d_qkv, weight, tokens, gain, d_hidden, collective_id):
    vmem = pl.BlockSpec(memory_space=pltpu.VMEM)
    anywhere = pl.BlockSpec(memory_space=pl.ANY)
    rows, width = tokens.shape
    return pl.pallas_call(
        finish_kernel,
        in_specs=[vmem] * 2 + [anywhere] + [vmem] * 2 + [anywhere] * 2 + [vmem] + [anywhere],
        out_specs=[vmem] * 2 + [anywhere] * 4,
        out_shape=[jax.ShapeDtypeStruct(small.shape, F32), jax.ShapeDtypeStruct((rows, width), F32)]
        + [jax.ShapeDtypeStruct((1536, n), BF16) for n in (1024, 1024, 1152, 384)],
        scratch_shapes=[
            pltpu.VMEM((1536, 2304), BF16),
            pltpu.VMEM((rows, width), BF16),
            pltpu.VMEM((rows, width), BF16),
            pltpu.VMEM((2, 384, 2304), BF16),
            pltpu.SemaphoreType.DMA((2,)),
            pltpu.VMEM((2, 64, width), F32),
            pltpu.VMEM((2, 64, width), BF16),
            pltpu.SemaphoreType.DMA((2, 2)),
            pltpu.SemaphoreType.DMA((4,)),
            pltpu.SemaphoreType.DMA((4,)),
        ]
        + finish_scratch(FINISH, 2304, True)
        + [pltpu.VMEM((6,) + small.shape, F32), pltpu.VMEM((5,) + small.shape, F32)]
        + [pltpu.SemaphoreType.DMA((5,))] * 2
        + finish_scratch(LONE, 768),
        compiler_params=pltpu.CompilerParams(collective_id=collective_id, has_side_effects=True, vmem_limit_bytes=60 * 1024 * 1024),
    )(small, gu, out, normed, d_qkv, weight, tokens, gain, d_hidden)


def rows_dot(lhs, rhs):
    return tn(lhs, rhs).astype(BF16)


def toeplitz_alone(both):
    def kernel(rows_ref, out_ref):
        fill_toeplitz(rows_ref, 0, out_ref)
        fill_toeplitz(rows_ref, 1, out_ref)

    return pl.pallas_call(
        kernel,
        out_shape=jax.ShapeDtypeStruct((2, 2, 2, CQ * WIN, WIN), BF16),
        compiler_params=pltpu.CompilerParams(vmem_limit_bytes=60 * 1024 * 1024),
    )(both)


def make_local(planes, tensors):
    every = ("plane", "core", "tensor")
    sides = [(c, z) for c in range(2) for z in range(tensors)]

    def spot(q, c, z):
        return (q * 2 + c) * tensors + z

    def is_home(c, z):
        return z // 2 == c

    far_pairs = [(spot(q, c, z), spot(q, 1 - c, z ^ 2)) for q in range(planes) for c, z in sides if not is_home(c, z)]
    near_pairs = [
        (spot(q, c, z), spot(q, c, z ^ 1) if is_home(c, z) else spot(q, 1 - c, z ^ 3)) for q in range(planes) for c, z in sides
    ]

    def over_core(value):
        return lax.ppermute(value, "core", [(0, 1), (1, 0)])

    def first_from(value):
        return lax.ppermute(value, every, far_pairs)

    def second_from(value):
        return lax.ppermute(value, every, near_pairs)

    square = planes == 4

    def local(
        tokens, teacher, valid_mask, norm1_gain, w_query, w_key, w_value, conv_weight, head_mix, gn_gain, w_out, norm2_gain,
        w_gate, w_up, w_down,
    ):
        q, c, z = lax.axis_index("plane"), lax.axis_index("core"), lax.axis_index("tensor")
        own_rows, width = tokens.shape
        home = (z // 2) == c
        wide = w_query.shape[1]

        def collect(weights):
            pairs = []
            for weight in weights:
                pairs.append(jnp.where(home, weight, first_from(weight)))
                pairs.append(second_from(weight))
            return pairs

        fused = square and tensors == 4
        units = w_gate.shape[1]

        def plane_sum(grads):
            return lax.psum_scatter(grads, "plane", scatter_dimension=0, tiled=True)

        def reduce(first, second):
            here = added(first, lax.ppermute(second, "tensor", [(i, i ^ 1) for i in range(tensors)]))
            here = jnp.where(home, here, first_from(here))
            total = added(here, over_core(here))
            return lax.all_gather(total, "plane", axis=0, tiled=True)

        small = jnp.concatenate(
            [
                band_rows(conv_weight),
                jnp.pad(head_mix.reshape(1, -1), ((0, 0), (0, WIN - head_mix.size))),
                jnp.pad(gn_gain.reshape(1, -1), ((0, 0), (0, 2 * WIN - wide))).reshape(2, WIN),
                jnp.zeros((5, WIN), F32),
            ]
        )
        conv_size, mix_size = conv_weight.size, head_mix.size
        small_size = conv_size + mix_size + wide
        gain_one, gain_two = norm1_gain, norm2_gain
        own_valid = lax.dynamic_slice_in_dim(valid_mask, z * own_rows, own_rows, 0)
        jj = key_positions(jnp.concatenate([own_valid, over_core(own_valid)]))

        def with_partner(value):
            return jnp.concatenate([value, over_core(value)], axis=0)

        def summed(left, right):
            sent = over_core(nt(left[own_rows:], right).astype(BF16))
            return nt(left[:own_rows], right) + sent.astype(F32)

        inputs = tokens.astype(F32)
        inv_one = lax.rsqrt(jnp.mean(inputs * inputs, axis=-1, keepdims=True) + 1e-06)
        if fused:
            qkv_weight, normed_one, toep, both_small = opening(tokens, gain_one[None], small, [w_query, w_key, w_value], 1)
            gather = ([w_out, w_gate, w_up, w_down], (768, 4096, 2048), len(LATER), dict(collective_id=3, has_side_effects=True))
        else:
            both_small = jnp.stack([jnp.where(home, small, first_from(small)), second_from(small)])
            toep = toeplitz_alone(both_small)
            normed_one = with_partner((inputs * inv_one * gain_one).astype(BF16))
            parts = collect([w_query, w_key, w_value])
            qkv_weight = jnp.concatenate(parts[0::2] + parts[1::2], axis=1)
            gather = None
        mix = both_small[:, 24, :mix_size].reshape(-1)
        gains = jnp.broadcast_to(both_small[:, 25:27].reshape(2, 1, 2 * WIN)[:, :, :wide], (2, 8, wide))
        heads_out, saved, qkv, later = attention_forward(mix, normed_one, qkv_weight, toep, gains, jj, gather)
        if fused:
            out_weight, gu_weight, down_weight = later
        else:
            out_weight = jnp.concatenate(collect([w_out]), axis=1)
            pieces = collect([w_gate, w_up])
            pieces = [pieces[2 * kind + side][:, start : start + TILE] for side in range(2) for start in range(0, units, TILE) for kind in range(2)]
            gu_weight = jnp.concatenate(pieces, axis=1)
        hidden_in = inputs + summed(heads_out, out_weight)
        inv_two = lax.rsqrt(jnp.mean(hidden_in * hidden_in, axis=-1, keepdims=True) + 1e-06)
        normed_two = with_partner((hidden_in * inv_two * gain_two).astype(BF16))
        (hidden, gate, up), last = gated_forward(normed_two, gu_weight, down_weight if fused else None)
        down_weight = last[0] if fused else jnp.concatenate(collect([w_down]), axis=1)
        final_rows = hidden_in + summed(hidden, down_weight)
        output = final_rows.astype(BF16)
        own_mask = own_valid.astype(F32)
        error = own_mask[:, None] * (final_rows - teacher.astype(F32))
        squared_sum = jnp.sum(error * error)
        count_sum = jnp.sum(own_mask)

        d_all = with_partner(error.astype(BF16))
        down_grads = rows_dot(d_all, hidden)
        down_grads, d_all = lax.optimization_barrier((down_grads, d_all))
        down_part = plane_sum(down_grads)
        d_gu, gu_grads = gated_backward(d_all, down_weight, gate, up, normed_two)
        gu_grads, d_gu = lax.optimization_barrier((gu_grads, d_gu))
        gu_part = plane_sum(gu_grads)
        d_normed_two = summed(d_gu, gu_weight)
        scaled_two = d_normed_two * gain_two
        grad_gain_two = jnp.sum(d_normed_two * hidden_in * inv_two, axis=0)
        d_hidden_in = (
            error + inv_two * scaled_two - hidden_in * inv_two**3 * jnp.mean(scaled_two * hidden_in, axis=-1, keepdims=True)
        )
        d_attn = with_partner(d_hidden_in.astype(BF16))
        out_grads = rows_dot(d_attn, heads_out)
        out_grads, d_attn = lax.optimization_barrier((out_grads, d_attn))
        d_normed = nn(d_attn, out_weight)
        d_normed, down_part = lax.optimization_barrier((d_normed, down_part))
        (d_qkv, ggn, gmix, gconv), done = attention_backward(
            mix, qkv, toep, gains, jj, d_normed, saved, (down_part,) if fused else None
        )
        small_grads = jnp.concatenate([conv_grads(gconv), mix_grads(gmix), ggn[:, 0]], axis=1)
        table = jnp.zeros((tensors, small_size), F32)
        table = lax.dynamic_update_slice(table, small_grads[:1], (2 * c + z % 2, 0))
        table = lax.dynamic_update_slice(table, small_grads[1:], (2 * c + 1 - z % 2, 0))
        table = jnp.pad(table.reshape(-1), (0, 4 * width - table.size)).reshape(4, width)
        last = jnp.pad(jnp.stack([squared_sum, count_sum]), (0, 2 * width - 2)).reshape(2, width)
        packed = jnp.concatenate([jnp.zeros((1, width), F32), grad_gain_two[None], table, last])
        if fused:
            packed, grad_input, sum_gate, sum_up, sum_qkv, sum_out = finish_gradients(
                packed, gu_part, out_grads, normed_one, d_qkv, qkv_weight, tokens, gain_one[None], d_hidden_in, 2
            )
            sums = [done[0], sum_gate, sum_up, sum_out, sum_qkv]
        else:
            qkv_grads = rows_dot(normed_one, d_qkv)
            d_normed_one = summed(d_qkv, qkv_weight)
            scaled_one = d_normed_one * gain_one
            packed = packed.at[0].set(jnp.sum(d_normed_one * inputs * inv_one, axis=0))
            grad_input = (
                d_hidden_in + inv_one * scaled_one - inputs * inv_one**3 * jnp.mean(scaled_one * inputs, axis=-1, keepdims=True)
            )
            packed = lax.psum(packed, every)
            out_part, qkv_part = plane_sum(out_grads), plane_sum(qkv_grads)
            sums = [reduce(part[:, : part.shape[1] // 2], part[:, part.shape[1] // 2 :]) for part in (down_part, out_part, qkv_part)]
            sum_gu = reduce(gu_part[:, : 2 * units], gu_part[:, 2 * units :])
            for kind in range(2):
                places = range(kind * TILE, 2 * units, 2 * TILE)
                sums.insert(1 + kind, jnp.concatenate([sum_gu[:, i : i + TILE] for i in places], axis=1))
        grad_down, grad_gate, grad_up, grad_out, grad_qkv = [value.astype(F32) for value in sums]
        small_sum = lax.dynamic_slice_in_dim(packed[2:6].reshape(-1), z * small_size, small_size, 0)
        gain_slice = width // tensors
        gain_one_out = lax.dynamic_slice_in_dim(packed[0], z * gain_slice, gain_slice, 0)
        gain_two_out = lax.dynamic_slice_in_dim(packed[1], z * gain_slice, gain_slice, 0)
        loss = packed[6, 0] / (packed[6, 1] * width)
        return (
            output,
            loss,
            grad_input,
            gain_one_out,
            grad_qkv[:, :wide],
            grad_qkv[:, wide : 2 * wide],
            grad_qkv[:, 2 * wide :],
            small_sum[:conv_size].reshape(conv_weight.shape),
            small_sum[conv_size : conv_size + mix_size].reshape(head_mix.shape),
            small_sum[conv_size + mix_size :].reshape(gn_gain.shape),
            grad_out,
            gain_two_out,
            grad_gate,
            grad_up,
            grad_down,
        )

    return local


def solution(mesh):
    tensors = mesh.shape["tensor"]
    planes = mesh.shape["dp"] // 2
    inner = jax.sharding.Mesh(mesh.devices.reshape(planes, 2, tensors), ("plane", "core", "tensor"))
    rows = P(("plane", "core", "tensor"), None)
    columns = P(None, "tensor")
    cube = P("tensor", None, None)
    return jax.shard_map(
        make_local(planes, tensors),
        mesh=inner,
        in_specs=(
            rows, rows, P(("plane", "core")), P(), columns, columns, columns, cube, cube, P("tensor", None), columns, P(),
            columns, columns, columns,
        ),
        out_specs=(
            rows, P(), rows, P("tensor"), columns, columns, columns, cube, cube, P("tensor", None), columns, P("tensor"),
            columns, columns, columns,
        ),
        check_vma=False,
    )
```

```python
import math
import jax
import jax.numpy as jnp
from jax import lax
from jax.experimental import pallas as pl
from jax.experimental.pallas import tpu as pltpu
from jax.sharding import PartitionSpec as P

HD = 96
CQ = 6
CK = 11
TRUNK = 192
SEG = 32
TREE = 576
WIN = 256
FAM = 96
EXT = 680
F32 = jnp.float32
BF16 = jnp.bfloat16


def segments():
    rows = [(0, TRUNK, 0, 0, -1)]
    for b in range(4):
        base, ext = TRUNK + FAM * b, 200 + 120 * b
        rows.append((TRUNK + SEG * b, SEG, base, ext, TRUNK - 8))
        for c in range(2):
            rows.append((320 + 64 * b + SEG * c, SEG, base + SEG * (c + 1), ext + 40 * (c + 1), TRUNK + SEG * b + SEG - 8))
    return rows


SEGS = segments()


def nn(a, b):
    return lax.dot_general(a, b, (((1,), (0,)), ((), ())), preferred_element_type=F32)


def nt(a, b):
    return lax.dot_general(a, b, (((1,), (1,)), ((), ())), preferred_element_type=F32)


def tn(a, b):
    return lax.dot_general(a, b, (((0,), (0,)), ((), ())), preferred_element_type=F32)


def head_masks(g):
    lane = lax.broadcasted_iota(jnp.int32, (1, WIN), 1)
    first = 64 * g
    m0 = (lane >= first) & (lane < first + HD)
    m1 = (lane >= first + HD) & (lane < first + 2 * HD)
    return m0, m1, lane >= first


def fill_distance(jj_ref, dist_ref):
    for index, (_, size, row, _, _) in enumerate(SEGS):
        start = 0 if index == 0 else (TRUNK if (index - 1) % 3 == 0 else TRUNK + SEG)
        pos = lax.broadcasted_iota(jnp.int32, (size, WIN), 0) + start
        dist_ref[row : row + size] = pos - jj_ref[index : index + 1, :]


def path_rows(ref, b, c, column):
    if b is None:
        parts = [ref[0:TRUNK, pl.ds(column, WIN)], ref[TRUNK : TRUNK + SEG, pl.ds(column, WIN)], ref[320 : 320 + SEG, pl.ds(column, WIN)]]
    else:
        parts = [
            ref[0:TRUNK, pl.ds(column, WIN)],
            ref[pl.ds(pl.multiple_of(TRUNK + SEG * b, SEG), SEG), pl.ds(column, WIN)],
            ref[pl.ds(pl.multiple_of(320 + 64 * b + SEG * c, SEG), SEG), pl.ds(column, WIN)],
        ]
    return jnp.concatenate(parts, axis=0)


def fam_rows(b, c):
    base = TRUNK + FAM * b
    return (pl.ds(pl.multiple_of(base, 32), 64), 64) if c == 0 else (pl.ds(pl.multiple_of(base + 64, 32), SEG), SEG)


def group_norm(ho, m0, m1):
    def stat(v):
        s0 = jnp.sum(jnp.where(m0, v, 0.0), axis=-1, keepdims=True) * (1.0 / HD)
        s1 = jnp.sum(jnp.where(m1, v, 0.0), axis=-1, keepdims=True) * (1.0 / HD)
        return jnp.where(m0, s0, s1)

    centered = jnp.where(m0 | m1, ho - stat(ho), 0.0)
    inv = lax.rsqrt(stat(centered * centered) + 1e-05)
    return centered * inv, inv, stat


def fwd_kernel(
    hook, mix_ref, normed_ref, weight_ref, t_ref, gn_ref, jj_ref, nh_ref, att_ref, pre_ref, qs_ref, ho_ref, qkv_ref, dist_ref, qx_ref, mx_ref
):
    side, t, g = pl.program_id(0), pl.program_id(1), pl.program_id(2)
    step = (side * 2 + t) * 2 + g
    mix0 = 8 * side + 4 * g
    hook(step, 0)

    @pl.when(g == 0)
    def _():
        for part in range(3):
            cols = slice(384 * part, 384 * (part + 1))
            qkv_ref[:, cols] = nn(normed_ref[...], weight_ref[:, cols]).astype(BF16)

    w0 = pl.multiple_of(g * 128, 128)
    m0, m1, from_first = head_masks(g)
    m0f, m1f = m0.astype(F32), m1.astype(F32)
    fill_distance(jj_ref, dist_ref)
    qx_ref[0:8] = jnp.zeros((8, WIN), F32)
    for token, size, _, ext, parent in SEGS:
        if parent >= 0:
            low = qkv_ref[parent - 8 : parent + 8, pl.ds(w0, WIN)].astype(F32)
            qx_ref[ext : ext + 8] = low[8:16]
        qx_ref[ext + 8 : ext + 8 + size] = qkv_ref[token : token + size, pl.ds(w0, WIN)].astype(F32)
    for a in range(CQ):
        for _, size, row, ext, _ in SEGS:
            part = qx_ref[ext + 8 - a : ext + 8 - a + size]
            qs_ref[0, a, row : row + size] = (part * m0f).astype(BF16)
            qs_ref[1, a, row : row + size] = (part * m1f).astype(BF16)
    k0, v0 = w0 + 384, w0 + 768
    k_trunk = path_rows(qkv_ref, None, 0, k0)

    def trunk_scores(a, carry):
        scores = nt(qs_ref[:, a, 0:TRUNK].reshape(2 * TRUNK, WIN), k_trunk).reshape(2, TRUNK, WIN)
        kept = dist_ref[0:TRUNK] >= a
        for e in range(2):
            pre_ref[e, 0:TRUNK, pl.ds(pl.multiple_of(a * WIN, WIN), WIN)] = jnp.where(kept, scores[e], 0.0).astype(BF16)
        return carry

    lax.fori_loop(0, CQ, trunk_scores, 0)

    def fam_scores(b, carry):
        for c in range(2):
            rows, size = fam_rows(b, c)
            keys = path_rows(qkv_ref, b, c, k0)
            scores = nt(qs_ref[:, :, rows].reshape(2 * CQ * size, WIN), keys).reshape(2, CQ, size, WIN)
            dist = dist_ref[rows]
            for a in range(CQ):
                kept = dist >= a
                for e in range(2):
                    pre_ref[e, rows, a * WIN : (a + 1) * WIN] = jnp.where(kept, scores[e, a], 0.0).astype(BF16)
        return carry

    lax.fori_loop(0, 4, fam_scores, 0)
    hook(step, 1)
    for e in range(2):
        conv = nn(pre_ref[e], t_ref[e])
        logits = jnp.where(dist_ref[...] >= 0, conv, -1e30)
        shifted = jnp.exp(logits - jnp.max(logits, axis=-1, keepdims=True))
        att_ref[e] = shifted / jnp.sum(shifted, axis=-1, keepdims=True)
    for c in range(2):
        mx_ref[c] = (mix_ref[mix0 + 2 * c] * att_ref[0] + mix_ref[mix0 + 2 * c + 1] * att_ref[1]).astype(BF16)

    def put_out(rows, size, values):
        out = nn(mx_ref[:, rows].reshape(2 * size, WIN), values).reshape(2, size, WIN)
        ho_ref[rows] = jnp.where(m0, out[0], jnp.where(m1, out[1], 0.0))

    put_out(pl.ds(0, TRUNK), TRUNK, path_rows(qkv_ref, None, 0, v0))

    def fam_out(b, carry):
        for c in range(2):
            rows, size = fam_rows(b, c)
            put_out(rows, size, path_rows(qkv_ref, b, c, v0))
        return carry

    lax.fori_loop(0, 4, fam_out, 0)
    gain = gn_ref[0:1, pl.ds(w0, WIN)]
    for token, size, row, _, _ in SEGS:
        unit, _, _ = group_norm(ho_ref[row : row + size], m0, m1)
        old = nh_ref[token : token + size, pl.ds(w0, WIN)].astype(F32)
        nh_ref[token : token + size, pl.ds(w0, WIN)] = jnp.where(from_first, unit * gain, old).astype(BF16)
    hook(step, 2)


def bwd_kernel(
    hook, mix_ref, qkv_ref, t_ref, gn_ref, jj_ref, dn_ref, att_ref, pre_ref, qs_ref, ho_ref,
    dqkv_ref, ggn_ref, gmix_ref, gconv_ref,
    dist_ref, dh_ref, mx_ref, dm_ref, dc_ref, es_ref, dqx_ref, dk_ref, dv_ref,
):
    side, t, g = pl.program_id(0), pl.program_id(1), pl.program_id(2)
    mix0 = 8 * side + 4 * g
    step = (side * 2 + t) * 2 + g
    hook(step, 0)
    w0 = pl.multiple_of(g * 128, 128)
    m0, m1, from_first = head_masks(g)
    both = m0 | m1
    fill_distance(jj_ref, dist_ref)
    gain = gn_ref[0:1, pl.ds(w0, WIN)]
    gn_sum = jnp.zeros((1, WIN), F32)
    for token, size, row, _, _ in SEGS:
        unit, inv, stat = group_norm(ho_ref[row : row + size], m0, m1)
        dn = jnp.where(both, dn_ref[token : token + size, pl.ds(w0, WIN)].astype(F32), 0.0)
        gn_sum = gn_sum + jnp.sum(dn * unit, axis=0, keepdims=True)
        scaled = dn * gain
        d_head = inv * (scaled - stat(scaled) - unit * stat(scaled * unit))
        dh_ref[0, row : row + size] = jnp.where(m0, d_head, 0.0).astype(BF16)
        dh_ref[1, row : row + size] = jnp.where(m1, d_head, 0.0).astype(BF16)

    @pl.when((t == 0) & (g == 0))
    def _():
        ggn_ref[...] = jnp.zeros_like(ggn_ref)

    ggn_ref[0:1, pl.ds(w0, WIN)] += gn_sum
    k0, v0 = w0 + 384, w0 + 768
    for c in range(2):
        mx_ref[c] = (mix_ref[mix0 + 2 * c] * att_ref[0] + mix_ref[mix0 + 2 * c + 1] * att_ref[1]).astype(BF16)

    def add_keys(acc_ref, b, c, grads):
        acc_ref[0:TRUNK] += grads[0:TRUNK]
        branch = pl.ds(pl.multiple_of(TRUNK + SEG * b, SEG), SEG)
        if c == 0:
            acc_ref[branch] = grads[TRUNK : TRUNK + SEG]
        else:
            acc_ref[branch] += grads[TRUNK : TRUNK + SEG]
        acc_ref[pl.ds(pl.multiple_of(320 + 64 * b + SEG * c, SEG), SEG)] = grads[TRUNK + SEG :]

    def value_part(rows, size, values):
        heads = dh_ref[:, rows].reshape(2 * size, WIN)
        dm_ref[:, rows] = nt(heads, values).reshape(2, size, WIN)
        return tn(mx_ref[:, rows].reshape(2 * size, WIN), heads)

    dv_ref[0:TRUNK] = value_part(pl.ds(0, TRUNK), TRUNK, path_rows(qkv_ref, None, 0, v0))[0:TRUNK]

    def fam_values(b, carry):
        for c in range(2):
            rows, size = fam_rows(b, c)
            add_keys(dv_ref, b, c, value_part(rows, size, path_rows(qkv_ref, b, c, v0)))
        return carry

    lax.fori_loop(0, 4, fam_values, 0)

    def soft_part(block, sums):
        rows = pl.ds(pl.multiple_of(block * FAM, 32), FAM)
        dm = [dm_ref[c, rows] for c in range(2)]
        att = [att_ref[e, rows] for e in range(2)]
        out = []
        for e in range(2):
            d_att = mix_ref[mix0 + e] * dm[0] + mix_ref[mix0 + 2 + e] * dm[1]
            d_conv = att[e] * (d_att - jnp.sum(d_att * att[e], axis=-1, keepdims=True))
            dc_ref[e, rows] = d_conv.astype(BF16)
        for c in range(2):
            for e in range(2):
                out.append(sums[2 * c + e] + jnp.sum(dm[c] * att[e], axis=0, keepdims=True))
        return tuple(out)

    mix_sums = lax.fori_loop(0, 6, soft_part, tuple(jnp.zeros((1, WIN), F32) for _ in range(4)))
    gmix_ref[...] = jnp.zeros_like(gmix_ref)
    gconv_ref[...] = jnp.zeros_like(gconv_ref)
    for index in range(4):
        gmix_ref[index : index + 1] = mix_sums[index]
    mirror = lax.broadcasted_iota(jnp.int32, (WIN, WIN), 0) + lax.broadcasted_iota(jnp.int32, (WIN, WIN), 1) - (WIN - 1)
    band = jnp.abs(mirror) <= CK // 2
    hook(step, 1)
    flip = jnp.where(mirror == 0, 1.0, 0.0).astype(BF16)
    for e in range(2):
        flipped = nn(dc_ref[e], flip).astype(BF16)
        for a in range(CQ):
            cols = slice(a * WIN, (a + 1) * WIN)
            products = jnp.where(band, tn(flipped, pre_ref[e, :, cols]), 0.0)
            rolled = pltpu.roll(products, 24, 1, stride=1, stride_axis=0)
            gconv_ref[e, a : a + 1] = jnp.sum(rolled, axis=0, keepdims=True)
            grads = nt(dc_ref[e], t_ref[e, cols, :])
            es_ref[e, a] = jnp.where(dist_ref[...] >= a, grads, 0.0).astype(BF16)

    def score_part(rows, size, keys):
        grads = es_ref[:, :, rows].reshape(2 * CQ * size, WIN)
        back = nn(grads, keys).reshape(2, CQ, size, WIN)
        d_query = [jnp.where(m0, back[0, a], jnp.where(m1, back[1, a], 0.0)) for a in range(CQ)]
        return d_query, tn(grads, qs_ref[:, :, rows].reshape(2 * CQ * size, WIN))

    def shifted_sum(parts, start, size):
        zeros = jnp.zeros((8, WIN), F32)
        total = None
        for a in range(CQ):
            padded = jnp.concatenate([zeros, parts[a][start : start + size]], axis=0)
            if a:
                padded = pltpu.roll(padded, size + 8 - a, 0)
            total = padded if total is None else total + padded
        return total

    d_query, d_keys = score_part(pl.ds(0, TRUNK), TRUNK, path_rows(qkv_ref, None, 0, k0))
    dqx_ref[0:200] = shifted_sum(d_query, 0, TRUNK)
    dk_ref[0:TRUNK] = d_keys[0:TRUNK]

    def fam_scores(b, carry):
        ext = 200 + 120 * b
        for c in range(2):
            rows, size = fam_rows(b, c)
            d_query, d_keys = score_part(rows, size, path_rows(qkv_ref, b, c, k0))
            add_keys(dk_ref, b, c, d_keys)
            if c == 0:
                dqx_ref[pl.ds(pl.multiple_of(ext, 8), 40)] = shifted_sum(d_query, 0, SEG)
                dqx_ref[pl.ds(pl.multiple_of(ext + 40, 8), 40)] = shifted_sum(d_query, SEG, SEG)
            else:
                dqx_ref[pl.ds(pl.multiple_of(ext + 80, 8), 40)] = shifted_sum(d_query, 0, SEG)
        return carry

    lax.fori_loop(0, 4, fam_scores, 0)
    for b in range(4):
        ext = 200 + 120 * b
        dqx_ref[192:200] += dqx_ref[ext : ext + 8]
        dqx_ref[ext + 32 : ext + 40] += dqx_ref[ext + 40 : ext + 48] + dqx_ref[ext + 80 : ext + 88]

    def put(token, size, column, value):
        old = dqkv_ref[token : token + size, pl.ds(column, WIN)].astype(F32)
        dqkv_ref[token : token + size, pl.ds(column, WIN)] = jnp.where(from_first, value, old).astype(BF16)

    for token, size, _, ext, _ in SEGS:
        put(token, size, w0, dqx_ref[ext + 8 : ext + 8 + size])
        put(token, size, k0, dk_ref[token : token + size])
        put(token, size, v0, dv_ref[token : token + size])
    hook(step, 2)


def by_group(shape):
    tail = (0,) * (len(shape) - 3)
    return pl.BlockSpec((None, None, None) + shape[3:], lambda s, t, g: (s, t, g) + tail)


def by_side(shape):
    return pl.BlockSpec((None,) + shape, lambda s, t, g: (s, 0, 0))


def common_specs(first=None):
    return [
        pl.BlockSpec(memory_space=pltpu.SMEM),
        *(first or [pl.BlockSpec((TREE, 1152), lambda s, t, g: (t, s))]),
        pl.BlockSpec((None, None, 2, CQ * WIN, WIN), lambda s, t, g: (s, g, 0, 0, 0)),
        by_side((8, 384)),
        pl.BlockSpec((None, 16, WIN), lambda s, t, g: (t, 0, 0)),
    ]


PARAMS = dict(vmem_limit_bytes=60 * 1024 * 1024, dimension_semantics=("arbitrary",) * 3)


def saved_shapes(trees):
    lead = (2, trees, 2)
    return [lead + (2, TREE, WIN), lead + (2, TREE, CQ * WIN), lead + (2, CQ, TREE, WIN), lead + (TREE, WIN)]


def attention_forward(mix, normed, weight, toeplitz, gains, jj, gather=None):
    trees, width = normed.shape[0] // TREE, normed.shape[1]
    shapes = saved_shapes(trees)
    kinds = (F32, BF16, BF16, F32)
    weights, wide, count, collective = gather if gather else ((), (), 0, {})
    many, held = len(weights), len(wide)

    def kernel(*refs):
        inputs, loads, refs = refs[:6], refs[6 : 6 + many], refs[6 + many :]
        outs, full, refs = refs[:6], refs[6 : 6 + held], refs[6 + held :]
        work = Gather(DIRECT, LATER, loads, full, *refs[3:]) if gather else None

        def hook(step, place):
            if work:
                background(work, step, place)

        fwd_kernel(hook, *inputs, *outs, *refs[:3])

    anywhere = pl.BlockSpec(memory_space=pl.ANY)
    first = [pl.BlockSpec((TREE, width), lambda s, t, g: (t, 0)), pl.BlockSpec((width, 1152), lambda s, t, g: (0, s))]
    result = pl.pallas_call(
        kernel,
        grid=(2, trees, 2),
        in_specs=common_specs(first) + [anywhere] * many,
        out_specs=[pl.BlockSpec((TREE, 384), lambda s, t, g: (t, s))]
        + [by_group(s) for s in shapes]
        + [pl.BlockSpec((TREE, 1152), lambda s, t, g: (t, s))]
        + [anywhere] * held,
        out_shape=[jax.ShapeDtypeStruct((trees * TREE, 768), BF16)]
        + [jax.ShapeDtypeStruct(s, k) for s, k in zip(shapes, kinds)]
        + [jax.ShapeDtypeStruct((trees * TREE, 2304), BF16)]
        + [jax.ShapeDtypeStruct((width, w), BF16) for w in wide],
        scratch_shapes=[pltpu.VMEM((TREE, WIN), jnp.int32), pltpu.VMEM((EXT, WIN), F32), pltpu.VMEM((2, TREE, WIN), BF16)]
        + gather_scratch(weights, count),
        compiler_params=pltpu.CompilerParams(**PARAMS, **collective),
        cost_estimate=pl.CostEstimate(flops=90_000_000_000, bytes_accessed=120_000_000, transcendentals=0),
    )(mix, normed, weight, toeplitz, gains, jj, *weights)
    return result[0], result[1:5], result[5], result[6:]


def attention_backward(mix, qkv, toeplitz, gains, jj, d_normed, saved, sums=None):
    trees = qkv.shape[0] // TREE
    shapes = saved_shapes(trees)
    collective = dict(collective_id=4, has_side_effects=True) if sums else {}
    many = len(sums or ())

    def kernel(*refs):
        inputs, extra, refs = refs[:10], refs[10 : 10 + many], refs[10 + many :]
        outs, full, refs = refs[:4], refs[4 : 4 + many], refs[4 + many :]
        work = Finish(BESIDE, extra, None, full, None, refs[9:]) if sums else None

        def hook(step, place):
            if work:
                beside(work, step, place)

        bwd_kernel(hook, *inputs, *outs, *refs[:9])

    anywhere = pl.BlockSpec(memory_space=pl.ANY)
    extra_in = [pl.BlockSpec((384, 2048), lambda s, t, g: (0, 0))] if sums else []
    result = pl.pallas_call(
        kernel,
        grid=(2, trees, 2),
        in_specs=common_specs() + [pl.BlockSpec((TREE, 384), lambda s, t, g: (t, s))] + [by_group(s) for s in shapes] + extra_in,
        out_specs=[
            pl.BlockSpec((TREE, 1152), lambda s, t, g: (t, s)),
            by_side((8, 384)),
            by_group((2, trees, 2, 8, WIN)),
            by_group((2, trees, 2, 2, 8, WIN)),
        ]
        + [anywhere] * many,
        out_shape=[
            jax.ShapeDtypeStruct((trees * TREE, 2304), BF16),
            jax.ShapeDtypeStruct((2, 8, 384), F32),
            jax.ShapeDtypeStruct((2, trees, 2, 8, WIN), F32),
            jax.ShapeDtypeStruct((2, trees, 2, 2, 8, WIN), F32),
        ]
        + [jax.ShapeDtypeStruct((1536, n), BF16) for n in (1024,)[:many]],
        scratch_shapes=[
            pltpu.VMEM((TREE, WIN), jnp.int32),
            pltpu.VMEM((2, TREE, WIN), BF16),
            pltpu.VMEM((2, TREE, WIN), BF16),
            pltpu.VMEM((2, TREE, WIN), F32),
            pltpu.VMEM((2, TREE, WIN), BF16),
            pltpu.VMEM((2, CQ, TREE, WIN), BF16),
            pltpu.VMEM((EXT, WIN), F32),
            pltpu.VMEM((TREE, WIN), F32),
            pltpu.VMEM((TREE, WIN), F32),
        ]
        + (finish_scratch(BESIDE, 128) if sums else []),
        compiler_params=pltpu.CompilerParams(**PARAMS, **collective),
        cost_estimate=pl.CostEstimate(flops=1_000_000_000, bytes_accessed=1_000_000, transcendentals=0),
    )(mix, qkv, toeplitz, gains, jj, d_normed, *saved, *(sums or ()))
    return result[:4], result[4:]


def band_rows(conv_w):
    rows = conv_w.reshape(-1, CK) * (1.0 / math.sqrt(HD))
    middle = jnp.zeros((rows.shape[0], WIN - CK), F32)
    return jnp.concatenate([rows[:, CK // 2 :], middle, rows[:, : CK // 2]], axis=1)


def fill_toeplitz(rows_ref, side, out_ref):
    offset = lax.broadcasted_iota(jnp.int32, (WIN, WIN), 1) - lax.broadcasted_iota(jnp.int32, (WIN, WIN), 0)
    band = jnp.abs(offset) <= CK // 2
    for head in range(4):
        for a in range(CQ):
            row = rows_ref[side, head * CQ + a : head * CQ + a + 1, :]
            rolled = pltpu.roll(jnp.broadcast_to(row, (WIN, WIN)), 0, 1, stride=1, stride_axis=0)
            out_ref[side, head // 2, head % 2, a * WIN : (a + 1) * WIN, :] = jnp.where(band, rolled, 0.0).astype(BF16)


def key_positions(valid):
    trees = valid.shape[0] // TREE
    valid = valid.reshape(trees, TREE)
    far = jnp.int32(1 << 20)

    def places(part, start):
        return jnp.where(part > 0, lax.broadcasted_iota(jnp.int32, part.shape, 1) + start, far)

    trunk = places(valid[:, :TRUNK], 0)
    empty = jnp.full((trees, SEG), far, jnp.int32)
    rows = [jnp.concatenate([trunk, empty, empty], axis=1)]
    for b in range(4):
        branch = places(valid[:, TRUNK + SEG * b : TRUNK + SEG * (b + 1)], TRUNK)
        rows.append(jnp.concatenate([trunk, branch, empty], axis=1))
        for c in range(2):
            first = 320 + 64 * b + SEG * c
            leaf = places(valid[:, first : first + SEG], TRUNK + SEG)
            rows.append(jnp.concatenate([trunk, branch, leaf], axis=1))
    rows += [jnp.zeros((trees, WIN), jnp.int32)] * 3
    return jnp.stack(rows, axis=1)


def conv_grads(gconv):
    lanes = gconv[..., :CQ, 18:29][..., ::-1] * (1.0 / math.sqrt(HD))
    return jnp.sum(lanes, axis=1).reshape(2, -1)


def mix_grads(gmix):
    return jnp.sum(gmix[:, :, :, :4], axis=(1, 4)).reshape(2, -1)


MESH = pl.DeviceIdType.MESH

FIRST = ((0, 0, 0, 0, 1152, 384), (1, 0, 0, 384, 1536, 384), (2, 0, 0, 768, 1920, 384))
LATER = (
    (0, 0, 0, 0, 384, 384),
    (1, 1, 0, 0, 2048, 512),
    (2, 1, 0, 512, 2560, 512),
    (1, 1, 512, 1024, 3072, 512),
    (2, 1, 512, 1536, 3584, 512),
    (3, 2, 0, 0, 1024, 512),
    (3, 2, 512, 512, 1536, 512),
)
WHOLE = 5
DIRECT = 0
LAST = ((0, 0, 0, 0, 1024, 512), (0, 0, 512, 512, 1536, 512))


def greet(peers):
    sem = pltpu.get_barrier_semaphore()
    for peer in peers:
        pl.semaphore_signal(sem, inc=1, device_id=peer, device_id_type=MESH)
    pl.semaphore_wait(sem, len(peers))


class Gather:
    def __init__(self, direct, items, weights, fulls, send, recv, local, *held):
        self.direct = direct
        self.items, self.weights, self.fulls, self.held = items, weights, fulls, held
        self.send, self.recv, self.local = send, recv, local
        q, c, z = lax.axis_index("plane"), lax.axis_index("core"), lax.axis_index("tensor")
        self.home = (z // 2) == c
        self.q = q
        self.core = (q, 1 - c, z)
        self.far = (q, 1 - c, (z + 2) % 4)
        self.near = (q, c, (z // 2) * 2 + (1 - z % 2))
        self.by_x = ((q // 2) * 2 + (1 - q % 2), c, z)
        self.by_y = ((q + 2) % 4, c, z)

    def away(self, action):
        pl.when(jnp.logical_not(self.home))(action)

    def whole(self, item, side):
        _, out, _, first, second, size = self.items[item]
        return self.fulls[out], pl.ds((first, second)[side], size)

    def z_copy(self, item, side, relay=False):
        weight, _, source_col, _, _, size = self.items[item]
        mine = pl.ds(pl.multiple_of(self.q * 384, 128), 384)
        ref, cols = self.whole(item, side)
        source = ref.at[mine, self.whole(item, 0)[1]] if relay else self.weights[weight].at[mine, pl.ds(source_col, size)]
        return pltpu.make_async_remote_copy(
            src_ref=source, dst_ref=ref.at[mine, cols], send_sem=self.send.at[item, side],
            recv_sem=self.recv.at[item, side], device_id=(self.far, self.near)[side], device_id_type=MESH)

    def plane_copy(self, item, side, step):
        ref, cols = self.whole(item, side)
        if step < 2:
            owner, first, size = self.q, 0, 384
        elif step == 2:
            owner, first, size = self.by_x[0], 0, 192
        else:
            owner, first, size = self.by_y[0], 192, 192
        span = pl.ds(pl.multiple_of(owner * 384 + first, 64), size)
        slot = 2 + 4 * side + step
        return pltpu.make_async_remote_copy(
            src_ref=ref.at[span, cols], dst_ref=ref.at[span, cols], send_sem=self.send.at[item, slot], recv_sem=self.recv.at[item, slot],
            device_id=(self.by_x, self.by_y, self.by_y, self.by_x)[step], device_id_type=MESH)

    def own_load(self, weight):
        return pltpu.make_async_copy(self.weights[weight], self.held[weight], self.local.at[weight, 0])

    def own_stores(self, weight):
        copies = []
        for number, (index, out, source_col, first, _, size) in enumerate(self.items):
            if index == weight:
                source = self.held[weight].at[:, pl.ds(source_col, size)]
                copies.append(pltpu.make_async_copy(source, self.fulls[out].at[:, pl.ds(first, size)], self.local.at[number, 1]))
        return copies

    def own(self):
        @pl.when(self.home)
        def _():
            for weight in range(len(self.weights)):
                self.own_load(weight).start()

    def pass_own(self, weight):
        @pl.when(self.home)
        def _():
            self.own_load(weight).wait()
            for copy in self.own_stores(weight):
                copy.start()

    def wait_own(self):
        @pl.when(self.home)
        def _():
            for weight in range(len(self.weights)):
                for copy in self.own_stores(weight):
                    copy.wait()

    def each(self, action):
        action(1)

        @self.away
        def _():
            action(0)

    def across_copy(self, item):
        weight, _, source_col, _, _, size = self.items[item]
        span = pl.ds(pl.multiple_of((3 - self.q) * 384, 128), 384)
        ref, cols = self.whole(item, 1)
        return pltpu.make_async_remote_copy(
            src_ref=self.weights[weight].at[span, pl.ds(source_col, size)], dst_ref=ref.at[span, cols], send_sem=self.send.at[item, 8],
            recv_sem=self.recv.at[item, 8], device_id=self.near, device_id_type=MESH)

    def start_z(self, item):
        @pl.when(self.home)
        def _():
            self.z_copy(item, 1).start()
            if item < self.direct:
                self.across_copy(item).start()

        @self.away
        def _():
            self.z_copy(item, 0).start()

    def relay_z(self, item):
        @self.away
        def _():
            self.z_copy(item, 0).wait_recv()
            self.z_copy(item, 1, True).start()
            self.plane_copy(item, 0, 0).start()
            self.plane_copy(item, 0, 1).start()

    def relay_only(self, item):
        @self.away
        def _():
            self.z_copy(item, 0).wait_recv()
            self.z_copy(item, 1, True).start()

    def finish_z(self, item):
        self.z_copy(item, 1).wait_recv()
        self.each(lambda side: self.z_copy(item, side).wait_send())

    def start_both(self, item):
        def act(side):
            self.plane_copy(item, side, 0).start()
            self.plane_copy(item, side, 1).start()

        self.each(act)

    def start_plane(self, item):
        self.z_copy(item, 1).wait_recv()
        self.plane_copy(item, 1, 0).start()
        self.plane_copy(item, 1, 1).start()

    def forward(self, item):
        def act(side):
            self.plane_copy(item, side, 0).wait_recv()
            self.plane_copy(item, side, 2).start()
            self.plane_copy(item, side, 1).wait_recv()
            self.plane_copy(item, side, 3).start()

        if item < self.direct:

            @self.away
            def _():
                act(1)
                act(0)

        else:
            self.each(act)

    def finish(self, item):
        def act(side):
            self.plane_copy(item, side, 2).wait_recv()
            self.plane_copy(item, side, 3).wait_recv()
            if self.weights:
                self.z_copy(item, side).wait_send()
            for step in range(4):
                self.plane_copy(item, side, step).wait_send()

        if item >= self.direct:
            self.each(act)
            return

        @self.away
        def _():
            act(1)
            act(0)

        @pl.when(self.home)
        def _():
            self.z_copy(item, 1).wait_send()
            self.across_copy(item).wait()
            for step in range(2):
                self.plane_copy(item, 1, step).wait()


def gather_scratch(weights, count):
    if not weights:
        return []
    return [pltpu.SemaphoreType.DMA((count, 10)), pltpu.SemaphoreType.DMA((count, 10)), pltpu.SemaphoreType.DMA((max(count, len(weights)), 2))] + [
        pltpu.VMEM(w.shape, BF16) for w in weights
    ]


SLOTS = {
    1: (("relay_z", 0), ("start_z", 2), ("pass_own", 0)),
    2: (("start_plane", 0),),
    3: (("relay_z", 1), ("start_z", 3), ("pass_own", 1)),
    4: (("start_plane", 1), ("forward", 0)),
    5: (("relay_z", 2), ("start_z", 4), ("pass_own", 2)),
    6: (("start_plane", 2), ("forward", 1)),
    7: (("relay_z", 3), ("pass_own", 3)),
    8: (("start_plane", 3), ("forward", 2), ("start_z", 5)),
    9: (("relay_z", 4), ("start_z", 6)),
    10: (("start_plane", 4), ("forward", 3)),
    11: (("forward", 4),),
    12: (("relay_only", 5),),
    13: (("relay_only", 6),),
}


def background(work, step, place):
    if place == 2:

        @pl.when(step == 7)
        def _():
            for item in range(len(work.items)):
                if item < WHOLE:
                    work.finish(item)
                else:
                    work.finish_z(item)
            work.wait_own()

        return

    for turn in range(8):
        slot = 2 * turn + place

        @pl.when(step == turn)
        def _(slot=slot):
            if slot == 0:
                work.own()
                greet((work.near, work.far, work.by_x, work.by_y))
                for item in range(2):
                    work.start_z(item)
            for name, item in SLOTS.get(slot, ()):
                getattr(work, name)(item)


TILE = 512


def beside_gate(work, step, place):
    script = {(0, 0): (("start_both", 0), ("start_both", 1)), (1, 1): (("forward", 0),), (3, 0): (("forward", 1),)}
    for (turn, where), names in script.items():
        if where == place:

            @pl.when(step == turn)
            def _(names=names, turn=turn):
                if turn == 0:
                    greet((work.by_x, work.by_y))
                for name, item in names:
                    getattr(work, name)(item)


def gated_forward(normed, weight, part=None):
    rows, width = normed.shape
    units = weight.shape[1] // 2
    many = 0 if part is None else 1
    count = len(LAST)

    def kernel(x_ref, w_ref, *refs):
        hidden_ref, gate_ref, up_ref, refs = refs[many], refs[many + 1], refs[many + 2], refs[many + 3 :]
        step = pl.program_id(0)
        work = Gather(0, LAST, (), refs[:1], refs[1], refs[2], None) if many else None
        if work:
            beside_gate(work, step, 0)
        gate = nn(x_ref[...], w_ref[:, :TILE])
        gate_ref[...] = gate.astype(BF16)
        if work:
            beside_gate(work, step, 1)
        up = nn(x_ref[...], w_ref[:, TILE:])
        up_ref[...] = up.astype(BF16)
        hidden_ref[...] = (gate * jax.nn.sigmoid(gate) * up).astype(BF16)
        if work:

            @pl.when(step == units // TILE - 1)
            def _():
                for item in range(count):
                    work.finish(item)

    anywhere = pl.BlockSpec(memory_space=pl.ANY)
    tile = pl.BlockSpec((rows, TILE), lambda j: (0, j))
    collective = dict(collective_id=5, has_side_effects=True) if many else {}
    extra = [] if part is None else [part]
    result = pl.pallas_call(
        kernel,
        grid=(units // TILE,),
        in_specs=[pl.BlockSpec((rows, width), lambda j: (0, 0)), pl.BlockSpec((width, 2 * TILE), lambda j: (0, j))] + [anywhere] * many,
        out_specs=[tile] * 3 + [anywhere] * many,
        out_shape=[jax.ShapeDtypeStruct((rows, units), BF16)] * 3 + [jax.ShapeDtypeStruct(p.shape, BF16) for p in extra],
        scratch_shapes=[pltpu.SemaphoreType.DMA((count, 10))] * 2 * many,
        input_output_aliases={2: 3} if many else {},
        compiler_params=pltpu.CompilerParams(vmem_limit_bytes=60 * 1024 * 1024, **collective),
    )(normed, weight, *extra)
    return result[:3], result[3:]


def gated_backward(d_out, down, gate, up, normed):
    rows, width = d_out.shape
    units = gate.shape[1]

    def kernel(d_ref, down_ref, gate_ref, up_ref, x_ref, d_gu_ref, grads_ref):
        d_hidden = nn(d_ref[...], down_ref[...])
        gate_value, up_value = gate_ref[...].astype(F32), up_ref[...].astype(F32)
        s = jax.nn.sigmoid(gate_value)
        d_gu_ref[:, :TILE] = (d_hidden * up_value * s * (1.0 + gate_value * (1.0 - s))).astype(BF16)
        d_gu_ref[:, TILE:] = (d_hidden * gate_value * s).astype(BF16)
        grads_ref[...] = tn(x_ref[...], d_gu_ref[...]).astype(BF16)

    whole = pl.BlockSpec((rows, width), lambda j: (0, 0))
    tile = pl.BlockSpec((rows, TILE), lambda j: (0, j))
    return pl.pallas_call(
        kernel,
        grid=(units // TILE,),
        in_specs=[whole, pl.BlockSpec((width, TILE), lambda j: (0, j)), tile, tile, whole],
        out_specs=[pl.BlockSpec((rows, 2 * TILE), lambda j: (0, j)), pl.BlockSpec((width, 2 * TILE), lambda j: (0, j))],
        out_shape=[jax.ShapeDtypeStruct((rows, 2 * units), BF16), jax.ShapeDtypeStruct((width, 2 * units), BF16)],
        compiler_params=pltpu.CompilerParams(vmem_limit_bytes=60 * 1024 * 1024),
        cost_estimate=pl.CostEstimate(flops=22_000_000_000, bytes_accessed=40_000_000, transcendentals=0),
    )(d_out, down, gate, up, normed)


def opening_kernel(tokens_ref, gain_ref, small_ref, wq_ref, wk_ref, wv_ref, full_ref, normed_ref, toep_ref, both_ref, send, recv, local, held0, held1, held2, extra_send, extra_recv):
    work = Gather(3, FIRST, (wq_ref, wk_ref, wv_ref), (full_ref,), send, recv, local, held0, held1, held2)
    rows = tokens_ref.shape[0]

    def extra(source, target, index, peer):
        return pltpu.make_async_remote_copy(
            src_ref=source, dst_ref=target, send_sem=extra_send.at[index], recv_sem=extra_recv.at[index], device_id=peer, device_id_type=MESH)

    far_small = extra(small_ref, both_ref.at[0], 0, work.far)
    near_small = extra(both_ref.at[0], both_ref.at[1], 1, work.near)
    normed_out = extra(normed_ref.at[0:rows], normed_ref.at[rows : 2 * rows], 2, work.core)
    work.own()
    greet((work.near, work.far, work.by_x, work.by_y, work.core))

    @work.away
    def _():
        far_small.start()

    @pl.when(work.home)
    def _():
        both_ref[0] = small_ref[...]
        near_small.start()

    for item in range(3):
        work.start_z(item)
    for start in range(0, rows, 96):
        x = tokens_ref[start : start + 96].astype(F32)
        inv = lax.rsqrt(jnp.mean(x * x, axis=-1, keepdims=True) + 1e-06)
        normed_ref[start : start + 96] = (x * inv * gain_ref[...]).astype(BF16)
    normed_out.start()

    @work.away
    def _():
        far_small.wait_recv()
        near_small.start()

    work.relay_z(0)
    work.start_plane(0)
    fill_toeplitz(both_ref, 0, toep_ref)
    work.relay_z(1)
    work.start_plane(1)
    work.forward(0)
    for weight in range(3):
        work.pass_own(weight)
    near_small.wait_recv()
    work.relay_z(2)
    work.start_plane(2)
    work.forward(1)
    fill_toeplitz(both_ref, 1, toep_ref)
    work.forward(2)
    for item in range(3):
        work.finish(item)
    work.wait_own()
    near_small.wait_send()

    @work.away
    def _():
        far_small.wait_send()

    normed_out.wait()


def opening(tokens, gain, small, weights, collective_id):
    vmem = pl.BlockSpec(memory_space=pltpu.VMEM)
    anywhere = pl.BlockSpec(memory_space=pl.ANY)
    rows, width = tokens.shape
    return pl.pallas_call(
        opening_kernel,
        in_specs=[vmem] * 3 + [anywhere] * 3,
        out_specs=[anywhere] + [vmem] * 3,
        out_shape=[
            jax.ShapeDtypeStruct((width, 2304), BF16),
            jax.ShapeDtypeStruct((2 * rows, width), BF16),
            jax.ShapeDtypeStruct((2, 2, 2, CQ * WIN, WIN), BF16),
            jax.ShapeDtypeStruct((2,) + small.shape, F32),
        ],
        scratch_shapes=gather_scratch(weights, 3) + [pltpu.SemaphoreType.DMA((3,)), pltpu.SemaphoreType.DMA((3,))],
        compiler_params=pltpu.CompilerParams(collective_id=collective_id, has_side_effects=True, vmem_limit_bytes=60 * 1024 * 1024),
    )(tokens, gain, small, *weights)


class Finish:
    def __init__(self, plan, parts, raw, outs, small, bufs, made=False):
        self.made = made
        q, c, z = lax.axis_index("plane"), lax.axis_index("core"), lax.axis_index("tensor")
        self.q, self.c = q, c
        self.home = (z // 2) == c
        self.by_x = ((q // 2) * 2 + (1 - q % 2), c, z)
        self.by_y = ((q + 2) % 4, c, z)
        self.core = (q, 1 - c, z)
        self.near = (q, c, (z // 2) * 2 + (1 - z % 2))
        self.far = (q, 1 - c, (z + 2) % 4)
        self.across = (q, c, (z + 2) % 4)
        self.plan, self.parts, self.raw, self.outs, self.small = plan, parts, raw, outs, small
        (self.near_buf, self.far_buf, self.core_buf, self.here_buf, self.raw_part, self.raw_own, self.raw_first,
         self.raw_second, self.send, self.recv, self.raw_send, self.raw_recv, self.local) = bufs[:13]
        if small is not None:
            self.small_buf, self.small_in, self.small_send, self.small_recv = bufs[13:]

    def remote(self, src, dst, sems, index, peer):
        return pltpu.make_async_remote_copy(
            src_ref=src, dst_ref=dst, send_sem=sems[0].at[index], recv_sem=sems[1].at[index], device_id=peer, device_id_type=MESH)

    def columns(self, item):
        _, first_a, first_b, size, _, _, at = self.plan[item]
        return pl.ds(first_a, size), pl.ds(first_b, size), pl.ds(at, size)

    def part(self, item):
        source = self.plan[item][0]
        if source >= 0:
            return self.parts[source]
        return self.raw.at[self.rows(self.q)] if self.made else self.raw_part

    def away(self, action):
        pl.when(jnp.logical_not(self.home))(action)

    def rows(self, owner):
        return pl.ds(pl.multiple_of(owner * 384, 128), 384)

    def raw_copies(self, item):
        cols_a, cols_b, _ = self.columns(item)
        sems = (self.raw_send, self.raw_recv)
        across = 3 - self.q
        x, y = self.by_x[0], self.by_y[0]
        remote = [
            self.remote(self.raw.at[self.rows(x), cols_a], self.raw_first.at[0, :, cols_a], sems, (item, 0), self.by_x),
            self.remote(self.raw.at[self.rows(across), cols_a], self.raw_first.at[1, :, cols_a], sems, (item, 1), self.by_x),
            self.remote(self.raw.at[self.rows(y), cols_b], self.raw_first.at[0, :, cols_b], sems, (item, 2), self.by_y),
            self.remote(self.raw.at[self.rows(across), cols_b], self.raw_first.at[1, :, cols_b], sems, (item, 3), self.by_y),
        ]
        if self.made:
            return remote, []
        return remote, [
            pltpu.make_async_copy(self.raw.at[self.rows(self.q), cols_a], self.raw_own.at[0, :, cols_a], self.local.at[item, 0]),
            pltpu.make_async_copy(self.raw.at[self.rows(y), cols_a], self.raw_own.at[1, :, cols_a], self.local.at[item, 1]),
            pltpu.make_async_copy(self.raw.at[self.rows(self.q), cols_b], self.raw_own.at[0, :, cols_b], self.local.at[item, 2]),
            pltpu.make_async_copy(self.raw.at[self.rows(x), cols_b], self.raw_own.at[1, :, cols_b], self.local.at[item, 3]),
        ]

    def raw_place(self, which, side, cols):
        if self.made:
            owner = self.q if which == 0 else (self.by_y[0], self.by_x[0])[side]
            return self.raw, (self.rows(owner), cols)
        return self.raw_own, (which, slice(None), cols)

    def raw_second_copies(self, item):
        sems = (self.raw_send, self.raw_recv)
        copies = []
        for side, cols in enumerate(self.columns(item)[:2]):
            ref, place = self.raw_place(1, side, cols)
            copies.append(self.remote(ref.at[place], self.raw_second.at[:, cols], sems, (item, 4 + side), (self.by_y, self.by_x)[side]))
        return copies

    def r1_side(self, item, side):
        for copy in self.raw_copies(item)[0][2 * side : 2 * side + 2]:
            copy.start()

    def r1(self, item):
        for group in self.raw_copies(item):
            for copy in group:
                copy.start()

    def r2(self, item):
        remote, own = self.raw_copies(item)
        for copy in own:
            copy.wait()
        for side, cols in enumerate(self.columns(item)[:2]):
            remote[2 * side + 1].wait_recv()
            ref, place = self.raw_place(1, side, cols)
            ref[place] = added(ref[place], self.raw_first[1, :, cols])
            self.raw_second_copies(item)[side].start()

    def r3(self, item):
        remote, _ = self.raw_copies(item)
        for side, cols in enumerate(self.columns(item)[:2]):
            remote[2 * side].wait_recv()
            self.raw_second_copies(item)[side].wait_recv()
            ref, place = self.raw_place(0, side, cols)
            total = ref[place].astype(F32) + self.raw_first[0, :, cols].astype(F32) + self.raw_second[:, cols].astype(F32)
            self.part(item)[:, cols] = total.astype(BF16)

    def near_copy(self, item):
        _, cols_b, at = self.columns(item)
        return self.remote(self.part(item).at[:, cols_b], self.near_buf.at[:, self.spot(item)], (self.send, self.recv), (item, 0), self.near)

    def spot(self, item):
        return pl.ds(self.plan[item][5], self.plan[item][3])

    def far_copy(self, item):
        spot = self.spot(item)
        return self.remote(self.here_buf.at[:, spot], self.far_buf.at[:, spot], (self.send, self.recv), (item, 1), self.far)

    def core_copy(self, item, relayed):
        spot = self.spot(item)
        source = self.far_buf if relayed else self.here_buf
        return self.remote(source.at[:, spot], self.core_buf.at[:, spot], (self.send, self.recv), (item, 2), self.core)

    def s1(self, item):
        self.near_copy(item).start()

    def s2(self, item):
        spot, cols_a = self.spot(item), self.columns(item)[0]
        self.near_copy(item).wait_recv()
        self.here_buf[:, spot] = added(self.part(item)[:, cols_a], self.near_buf[:, spot])

        @pl.when(self.home)
        def _():
            self.core_copy(item, False).start()

        @self.away
        def _():
            self.far_copy(item).start()

    def s3(self, item):
        @self.away
        def _():
            self.far_copy(item).wait_recv()
            self.core_copy(item, True).start()

    def plane_copies(self, item):
        out = self.outs[self.plan[item][4]]
        at, spot = self.columns(item)[2], self.spot(item)
        sems = (self.send, self.recv)
        half = self.c * 192

        def rows(owner, first, size):
            return pl.ds(pl.multiple_of(owner * 384 + half + first, 32), size)

        mine = self.core_buf.at[pl.ds(pl.multiple_of(half, 32), 192), spot]
        x, y, across = self.by_x[0], self.by_y[0], 3 - self.q
        own = out.at[rows(self.q, 0, 192), at]
        top, low = out.at[rows(x, 0, 96), at], out.at[rows(y, 96, 96), at]
        return [
            self.remote(mine, own, sems, (item, 3), self.by_x),
            self.remote(mine, own, sems, (item, 4), self.by_y),
            self.remote(top, top, sems, (item, 5), self.by_y),
            self.remote(low, low, sems, (item, 6), self.by_x),
        ] + [
            self.remote(out.at[rows(o, 0, 192), at], out.at[rows(o, 0, 192), at], sems, (item, 7 + i), self.core)
            for i, o in enumerate((x, y, across))
        ]

    def own_copy(self, item):
        out = self.outs[self.plan[item][4]]
        rows = pl.ds(pl.multiple_of(self.q * 384, 128), 384)
        return pltpu.make_async_copy(self.core_buf.at[:, self.spot(item)], out.at[rows, self.columns(item)[2]], self.local.at[item, 4])

    def s4(self, item):
        spot = self.spot(item)

        @pl.when(self.home)
        def _():
            self.core_copy(item, False).wait_recv()
            self.core_buf[:, spot] = added(self.here_buf[:, spot], self.core_buf[:, spot])

        @self.away
        def _():
            self.core_copy(item, True).wait_recv()
            self.core_buf[:, spot] = added(self.far_buf[:, spot], self.core_buf[:, spot])

        self.own_copy(item).start()
        copies = self.plane_copies(item)
        copies[0].start()
        copies[1].start()

    def s5(self, item):
        copies = self.plane_copies(item)
        copies[0].wait_recv()
        copies[2].start()
        copies[4].start()
        copies[1].wait_recv()
        copies[3].start()
        copies[5].start()

    def s6(self, item):
        copies = self.plane_copies(item)
        copies[2].wait_recv()
        copies[3].wait_recv()
        copies[6].start()

    def s7(self, item):
        copies = self.plane_copies(item)
        self.own_copy(item).wait()
        for copy in copies[4:]:
            copy.wait_recv()
        for copy in copies:
            copy.wait_send()
        self.near_copy(item).wait_send()

        @pl.when(self.home)
        def _():
            self.core_copy(item, False).wait_send()

        @self.away
        def _():
            self.core_copy(item, True).wait_send()
            self.far_copy(item).wait_send()

        if self.plan[item][0] < 0:
            for copy in self.raw_copies(item)[0] + self.raw_second_copies(item):
                copy.wait_send()

    def small_copy(self, turn):
        peer = (self.core, self.by_x, self.by_y, self.near, self.across)[turn]
        return self.remote(self.small_buf.at[turn], self.small_in.at[turn], (self.small_send, self.small_recv), turn, peer)

    def small_start(self):
        self.small_copy(0).start()

    def small_next(self, turn):
        self.small_copy(turn).wait_recv()
        self.small_buf[turn + 1] = self.small_buf[turn] + self.small_in[turn]
        if turn < 4:
            self.small_copy(turn + 1).start()

    def small_done(self, out):
        for turn in range(5):
            self.small_copy(turn).wait_send()
        out[...] = self.small_buf[5]


def added(left, right):
    return (left.astype(F32) + right.astype(F32)).astype(BF16)


FINISH = (
    (0, 0, 2048, 512, 0, 0, 0),
    (0, 512, 2560, 512, 1, 512, 0),
    (0, 1024, 3072, 512, 0, 1024, 512),
    (0, 1536, 3584, 512, 1, 1536, 512),
    (-1, 0, 1152, 384, 2, 2048, 0),
    (-1, 384, 1536, 384, 2, 2432, 384),
    (-1, 768, 1920, 384, 2, 2816, 768),
)
LONE = ((-1, 0, 384, 384, 0, 0, 0),)
BESIDE = (
    (0, 0, 1024, 512, 0, 0, 0),
    (0, 512, 1536, 512, 0, 512, 512),
)
BESIDE_STEPS = (
    (("greet", 0), ("s1", 0), ("s1", 1)),
    (),
    (("s2", 0),),
    (("s2", 1),),
    (("s3", 0),),
    (("s3", 1),),
    (("s4", 0),),
    (("s4", 1),),
    (),
    (),
    (("s5", 0),),
    (("s5", 1),),
    (),
    (("s6", 0),),
    (("s6", 1),),
)


def finish_scratch(plan, raw_width, made=False):
    count, width = len(plan), sum(item[3] for item in plan)
    return (
        [pltpu.VMEM((384, width), BF16)] * 4
        + [pltpu.VMEM((384, 128 if made else raw_width), BF16)]
        + [pltpu.VMEM((2, 384, 128 if made else raw_width), BF16), pltpu.VMEM((2, 384, raw_width), BF16)]
        + [pltpu.VMEM((384, raw_width), BF16)]
        + [pltpu.SemaphoreType.DMA((count, 10))] * 2
        + [pltpu.SemaphoreType.DMA((count, 6))] * 2
        + [pltpu.SemaphoreType.DMA((count, 5))]
    )


def beside(work, step, place):
    if place == 2:

        @pl.when(step == 7)
        def _():
            for item in range(len(work.plan)):
                work.s7(item)

        return

    for slot, names in enumerate(BESIDE_STEPS):
        if slot % 2 == place:

            @pl.when(step == slot // 2)
            def _(names=names):
                for name, item in names:
                    if name == "greet":
                        greet((work.near, work.far, work.by_x, work.by_y, work.core))
                    else:
                        getattr(work, name)(item)


def finish_kernel(
    small, gu, out, normed, d_qkv, weight, tokens, gain, d_hidden, small_out, d_input, o_gate, o_up, o_qkv, o_out,
    made, partner, arrived, loaded, load_sem, hidden_buf, tokens_buf, hidden_sem, core_send, core_recv, *bufs,
):
    lone = Finish(LONE, (), out, (o_out,), None, bufs[-13:])
    work = Finish(FINISH, (gu,), made, (o_gate, o_up, o_qkv), small, bufs[:-13], True)
    rows = tokens.shape[0]

    def load(part):
        return pltpu.make_async_copy(weight.at[384 * part : 384 * (part + 1)], loaded.at[part % 2], load_sem.at[part % 2])

    def exchange(part):
        cols = pl.ds(384 * part, 384)
        return work.remote(partner.at[:, cols], arrived.at[:, cols], (core_send, core_recv), part, work.core)

    def load_hidden(part):
        span = pl.ds(64 * part, 64)
        return (
            pltpu.make_async_copy(d_hidden.at[span], hidden_buf.at[part % 2], hidden_sem.at[0, part % 2]),
            pltpu.make_async_copy(tokens.at[span], tokens_buf.at[part % 2], hidden_sem.at[1, part % 2]),
        )

    load(0).start()
    load(1).start()
    for copy in load_hidden(0):
        copy.start()
    greet((work.near, work.far, work.by_x, work.by_y, work.core, work.across))
    lone.r1(0)
    work.s1(0)
    work.s1(1)

    def make(side, owner):
        cols = slice(1152 * side, 1152 * (side + 1))
        made[work.rows(owner), cols] = tn(normed[:, work.rows(owner)], d_qkv[:, cols]).astype(BF16)

    across = 3 - work.q
    for side, owners in enumerate(((across, work.by_x[0]), (across, work.by_y[0]))):
        for owner in owners:
            make(side, owner)
        for item in (4, 5, 6):
            work.r1_side(item, side)
    work.s2(0)
    work.s1(2)
    lone.r2(0)
    make(0, work.by_y[0])
    work.s2(1)
    work.s1(3)
    make(1, work.by_x[0])
    work.s3(0)
    make(0, work.q)
    work.s2(2)
    work.s3(1)
    make(1, work.q)
    work.r2(4)
    lone.r3(0)
    lone.s1(0)
    work.s4(0)

    def back(part):
        cols = slice(384 * part, 384 * (part + 1))
        load(part).wait()
        both = nt(d_qkv[...], loaded[part % 2])
        d_input[:, cols] = both[:rows]
        partner[:, cols] = both[rows:].astype(BF16)
        if part < 2:
            load(part + 2).start()
        exchange(part).start()

    back(0)
    work.r2(5)
    work.s2(3)
    work.s4(1)
    back(1)
    work.r2(6)
    work.r3(4)
    work.s1(4)
    work.s3(2)
    work.s5(0)
    back(2)
    lone.s2(0)
    work.r3(5)
    work.s1(5)
    work.s3(3)
    work.s4(2)
    work.s5(1)
    back(3)
    work.s2(4)
    work.r3(6)
    work.s1(6)
    work.s4(3)
    work.s6(0)
    for part in range(4):
        exchange(part).wait_recv()
    gain_sum = jnp.zeros((1, tokens.shape[1]), F32)
    for part in range(rows // 64):
        span = slice(64 * part, 64 * (part + 1))
        if part + 1 < rows // 64:
            for copy in load_hidden(part + 1):
                copy.start()
        for copy in load_hidden(part):
            copy.wait()
        x = tokens_buf[part % 2].astype(F32)
        inv = lax.rsqrt(jnp.mean(x * x, axis=-1, keepdims=True) + 1e-06)
        d_normed = d_input[span] + arrived[span].astype(F32)
        scaled = d_normed * gain[...]
        gain_sum = gain_sum + jnp.sum(d_normed * x * inv, axis=0, keepdims=True)
        d_input[span] = hidden_buf[part % 2] + inv * scaled - x * inv**3 * jnp.mean(scaled * x, axis=-1, keepdims=True)
    work.small_buf[0] = small[...]
    work.small_buf[0, 0:1] = gain_sum
    work.small_start()
    script = (
        ("s3", 4), ("s2", 5), ("s3", 7), ("s6", 1), ("s5", 2), ("m", 0),
        ("s4", 4), ("s3", 5), ("s2", 6), ("s4", 7), ("s5", 3), ("s6", 2), ("m", 1),
        ("s5", 4), ("s4", 5), ("s3", 6), ("s5", 7), ("s6", 3), ("m", 2),
        ("s6", 4), ("s5", 5), ("s4", 6), ("s6", 7), ("m", 3), ("s6", 5), ("s5", 6), ("m", 4), ("s6", 6),
    )
    for name, item in script:
        if name == "m":
            work.small_next(item)
        elif item == 7:
            getattr(lone, name)(0)
        else:
            getattr(work, name)(item)
    for item in range(len(FINISH)):
        work.s7(item)
    lone.s7(0)
    for part in range(4):
        exchange(part).wait_send()
    work.small_done(small_out)


def finish_gradients(small, gu, out, normed, d_qkv, weight, tokens, gain, d_hidden, collective_id):
    vmem = pl.BlockSpec(memory_space=pltpu.VMEM)
    anywhere = pl.BlockSpec(memory_space=pl.ANY)
    rows, width = tokens.shape
    return pl.pallas_call(
        finish_kernel,
        in_specs=[vmem] * 2 + [anywhere] + [vmem] * 2 + [anywhere] * 2 + [vmem] + [anywhere],
        out_specs=[vmem] * 2 + [anywhere] * 4,
        out_shape=[jax.ShapeDtypeStruct(small.shape, F32), jax.ShapeDtypeStruct((rows, width), F32)]
        + [jax.ShapeDtypeStruct((1536, n), BF16) for n in (1024, 1024, 1152, 384)],
        scratch_shapes=[
            pltpu.VMEM((1536, 2304), BF16),
            pltpu.VMEM((rows, width), BF16),
            pltpu.VMEM((rows, width), BF16),
            pltpu.VMEM((2, 384, 2304), BF16),
            pltpu.SemaphoreType.DMA((2,)),
            pltpu.VMEM((2, 64, width), F32),
            pltpu.VMEM((2, 64, width), BF16),
            pltpu.SemaphoreType.DMA((2, 2)),
            pltpu.SemaphoreType.DMA((4,)),
            pltpu.SemaphoreType.DMA((4,)),
        ]
        + finish_scratch(FINISH, 2304, True)
        + [pltpu.VMEM((6,) + small.shape, F32), pltpu.VMEM((5,) + small.shape, F32)]
        + [pltpu.SemaphoreType.DMA((5,))] * 2
        + finish_scratch(LONE, 768),
        compiler_params=pltpu.CompilerParams(collective_id=collective_id, has_side_effects=True, vmem_limit_bytes=60 * 1024 * 1024),
    )(small, gu, out, normed, d_qkv, weight, tokens, gain, d_hidden)


def rows_dot(lhs, rhs):
    return tn(lhs, rhs).astype(BF16)


def toeplitz_alone(both):
    def kernel(rows_ref, out_ref):
        fill_toeplitz(rows_ref, 0, out_ref)
        fill_toeplitz(rows_ref, 1, out_ref)

    return pl.pallas_call(
        kernel,
        out_shape=jax.ShapeDtypeStruct((2, 2, 2, CQ * WIN, WIN), BF16),
        compiler_params=pltpu.CompilerParams(vmem_limit_bytes=60 * 1024 * 1024),
    )(both)


def make_local(planes, tensors):
    every = ("plane", "core", "tensor")
    sides = [(c, z) for c in range(2) for z in range(tensors)]

    def spot(q, c, z):
        return (q * 2 + c) * tensors + z

    def is_home(c, z):
        return z // 2 == c

    far_pairs = [(spot(q, c, z), spot(q, 1 - c, z ^ 2)) for q in range(planes) for c, z in sides if not is_home(c, z)]
    near_pairs = [
        (spot(q, c, z), spot(q, c, z ^ 1) if is_home(c, z) else spot(q, 1 - c, z ^ 3)) for q in range(planes) for c, z in sides
    ]

    def over_core(value):
        return lax.ppermute(value, "core", [(0, 1), (1, 0)])

    def first_from(value):
        return lax.ppermute(value, every, far_pairs)

    def second_from(value):
        return lax.ppermute(value, every, near_pairs)

    square = planes == 4

    def local(
        tokens, teacher, valid_mask, norm1_gain, w_query, w_key, w_value, conv_weight, head_mix, gn_gain, w_out, norm2_gain,
        w_gate, w_up, w_down,
    ):
        q, c, z = lax.axis_index("plane"), lax.axis_index("core"), lax.axis_index("tensor")
        own_rows, width = tokens.shape
        home = (z // 2) == c
        wide = w_query.shape[1]

        def collect(weights):
            pairs = []
            for weight in weights:
                pairs.append(jnp.where(home, weight, first_from(weight)))
                pairs.append(second_from(weight))
            return pairs

        fused = square and tensors == 4
        units = w_gate.shape[1]

        def plane_sum(grads):
            return lax.psum_scatter(grads, "plane", scatter_dimension=0, tiled=True)

        def reduce(first, second):
            here = added(first, lax.ppermute(second, "tensor", [(i, i ^ 1) for i in range(tensors)]))
            here = jnp.where(home, here, first_from(here))
            total = added(here, over_core(here))
            return lax.all_gather(total, "plane", axis=0, tiled=True)

        small = jnp.concatenate(
            [
                band_rows(conv_weight),
                jnp.pad(head_mix.reshape(1, -1), ((0, 0), (0, WIN - head_mix.size))),
                jnp.pad(gn_gain.reshape(1, -1), ((0, 0), (0, 2 * WIN - wide))).reshape(2, WIN),
                jnp.zeros((5, WIN), F32),
            ]
        )
        conv_size, mix_size = conv_weight.size, head_mix.size
        small_size = conv_size + mix_size + wide
        gain_one, gain_two = norm1_gain, norm2_gain
        own_valid = lax.dynamic_slice_in_dim(valid_mask, z * own_rows, own_rows, 0)
        jj = key_positions(jnp.concatenate([own_valid, over_core(own_valid)]))

        def with_partner(value):
            return jnp.concatenate([value, over_core(value)], axis=0)

        def summed(left, right):
            sent = over_core(nt(left[own_rows:], right).astype(BF16))
            return nt(left[:own_rows], right) + sent.astype(F32)

        inputs = tokens.astype(F32)
        inv_one = lax.rsqrt(jnp.mean(inputs * inputs, axis=-1, keepdims=True) + 1e-06)
        if fused:
            qkv_weight, normed_one, toep, both_small = opening(tokens, gain_one[None], small, [w_query, w_key, w_value], 1)
            gather = ([w_out, w_gate, w_up, w_down], (768, 4096, 2048), len(LATER), dict(collective_id=3, has_side_effects=True))
        else:
            both_small = jnp.stack([jnp.where(home, small, first_from(small)), second_from(small)])
            toep = toeplitz_alone(both_small)
            normed_one = with_partner((inputs * inv_one * gain_one).astype(BF16))
            parts = collect([w_query, w_key, w_value])
            qkv_weight = jnp.concatenate(parts[0::2] + parts[1::2], axis=1)
            gather = None
        mix = both_small[:, 24, :mix_size].reshape(-1)
        gains = jnp.broadcast_to(both_small[:, 25:27].reshape(2, 1, 2 * WIN)[:, :, :wide], (2, 8, wide))
        heads_out, saved, qkv, later = attention_forward(mix, normed_one, qkv_weight, toep, gains, jj, gather)
        if fused:
            out_weight, gu_weight, down_weight = later
        else:
            out_weight = jnp.concatenate(collect([w_out]), axis=1)
            pieces = collect([w_gate, w_up])
            pieces = [pieces[2 * kind + side][:, start : start + TILE] for side in range(2) for start in range(0, units, TILE) for kind in range(2)]
            gu_weight = jnp.concatenate(pieces, axis=1)
        hidden_in = inputs + summed(heads_out, out_weight)
        inv_two = lax.rsqrt(jnp.mean(hidden_in * hidden_in, axis=-1, keepdims=True) + 1e-06)
        normed_two = with_partner((hidden_in * inv_two * gain_two).astype(BF16))
        (hidden, gate, up), last = gated_forward(normed_two, gu_weight, down_weight if fused else None)
        down_weight = last[0] if fused else jnp.concatenate(collect([w_down]), axis=1)
        final_rows = hidden_in + summed(hidden, down_weight)
        output = final_rows.astype(BF16)
        own_mask = own_valid.astype(F32)
        error = own_mask[:, None] * (final_rows - teacher.astype(F32))
        squared_sum = jnp.sum(error * error)
        count_sum = jnp.sum(own_mask)

        d_all = with_partner(error.astype(BF16))
        down_grads = rows_dot(d_all, hidden)
        down_grads, d_all = lax.optimization_barrier((down_grads, d_all))
        down_part = plane_sum(down_grads)
        d_gu, gu_grads = gated_backward(d_all, down_weight, gate, up, normed_two)
        gu_grads, d_gu = lax.optimization_barrier((gu_grads, d_gu))
        gu_part = plane_sum(gu_grads)
        d_normed_two = summed(d_gu, gu_weight)
        scaled_two = d_normed_two * gain_two
        grad_gain_two = jnp.sum(d_normed_two * hidden_in * inv_two, axis=0)
        d_hidden_in = (
            error + inv_two * scaled_two - hidden_in * inv_two**3 * jnp.mean(scaled_two * hidden_in, axis=-1, keepdims=True)
        )
        d_attn = with_partner(d_hidden_in.astype(BF16))
        out_grads = rows_dot(d_attn, heads_out)
        out_grads, d_attn = lax.optimization_barrier((out_grads, d_attn))
        d_normed = nn(d_attn, out_weight)
        d_normed, down_part = lax.optimization_barrier((d_normed, down_part))
        (d_qkv, ggn, gmix, gconv), done = attention_backward(
            mix, qkv, toep, gains, jj, d_normed, saved, (down_part,) if fused else None
        )
        small_grads = jnp.concatenate([conv_grads(gconv), mix_grads(gmix), ggn[:, 0]], axis=1)
        table = jnp.zeros((tensors, small_size), F32)
        table = lax.dynamic_update_slice(table, small_grads[:1], (2 * c + z % 2, 0))
        table = lax.dynamic_update_slice(table, small_grads[1:], (2 * c + 1 - z % 2, 0))
        table = jnp.pad(table.reshape(-1), (0, 4 * width - table.size)).reshape(4, width)
        last = jnp.pad(jnp.stack([squared_sum, count_sum]), (0, 2 * width - 2)).reshape(2, width)
        packed = jnp.concatenate([jnp.zeros((1, width), F32), grad_gain_two[None], table, last])
        if fused:
            packed, grad_input, sum_gate, sum_up, sum_qkv, sum_out = finish_gradients(
                packed, gu_part, out_grads, normed_one, d_qkv, qkv_weight, tokens, gain_one[None], d_hidden_in, 2
            )
            sums = [done[0], sum_gate, sum_up, sum_out, sum_qkv]
        else:
            qkv_grads = rows_dot(normed_one, d_qkv)
            d_normed_one = summed(d_qkv, qkv_weight)
            scaled_one = d_normed_one * gain_one
            packed = packed.at[0].set(jnp.sum(d_normed_one * inputs * inv_one, axis=0))
            grad_input = (
                d_hidden_in + inv_one * scaled_one - inputs * inv_one**3 * jnp.mean(scaled_one * inputs, axis=-1, keepdims=True)
            )
            packed = lax.psum(packed, every)
            out_part, qkv_part = plane_sum(out_grads), plane_sum(qkv_grads)
            sums = [reduce(part[:, : part.shape[1] // 2], part[:, part.shape[1] // 2 :]) for part in (down_part, out_part, qkv_part)]
            sum_gu = reduce(gu_part[:, : 2 * units], gu_part[:, 2 * units :])
            for kind in range(2):
                places = range(kind * TILE, 2 * units, 2 * TILE)
                sums.insert(1 + kind, jnp.concatenate([sum_gu[:, i : i + TILE] for i in places], axis=1))
        grad_down, grad_gate, grad_up, grad_out, grad_qkv = [value.astype(F32) for value in sums]
        small_sum = lax.dynamic_slice_in_dim(packed[2:6].reshape(-1), z * small_size, small_size, 0)
        gain_slice = width // tensors
        gain_one_out = lax.dynamic_slice_in_dim(packed[0], z * gain_slice, gain_slice, 0)
        gain_two_out = lax.dynamic_slice_in_dim(packed[1], z * gain_slice, gain_slice, 0)
        loss = packed[6, 0] / (packed[6, 1] * width)
        return (
            output,
            loss,
            grad_input,
            gain_one_out,
            grad_qkv[:, :wide],
            grad_qkv[:, wide : 2 * wide],
            grad_qkv[:, 2 * wide :],
            small_sum[:conv_size].reshape(conv_weight.shape),
            small_sum[conv_size : conv_size + mix_size].reshape(head_mix.shape),
            small_sum[conv_size + mix_size :].reshape(gn_gain.shape),
            grad_out,
            gain_two_out,
            grad_gate,
            grad_up,
            grad_down,
        )

    return local


def solution(mesh):
    tensors = mesh.shape["tensor"]
    planes = mesh.shape["dp"] // 2
    inner = jax.sharding.Mesh(mesh.devices.reshape(planes, 2, tensors), ("plane", "core", "tensor"))
    rows = P(("plane", "core", "tensor"), None)
    columns = P(None, "tensor")
    cube = P("tensor", None, None)
    return jax.shard_map(
        make_local(planes, tensors),
        mesh=inner,
        in_specs=(
            rows, rows, P(("plane", "core")), P(), columns, columns, columns, cube, cube, P("tensor", None), columns, P(),
            columns, columns, columns,
        ),
        out_specs=(
            rows, P(), rows, P("tensor"), columns, columns, columns, cube, cube, P("tensor", None), columns, P("tensor"),
            columns, columns, columns,
        ),
        check_vma=False,
    )
```
